32 devices in a mesh: wide: 8 (over y, x, core), narrow: 4 (over z).
Axes of the slice: x: 2, y: 2, z: 4, core: 2. Of those that a mesh axis runs over, the one named last changes fastest.
Arguments:
- tokens: bfloat16 [16384, 1024], P(('wide', 'narrow')), may hold values from -6 to 6
- w_query: bfloat16 [1024, 1024], P(('wide', 'narrow')), may hold values from -0.0234375 to 0.0234375
- w_key: bfloat16 [1024, 1024], P(('wide', 'narrow')), may hold values from -0.1875 to 0.1875
- w_value: bfloat16 [1024, 1024], P(('wide', 'narrow')), may hold values from -0.1875 to 0.1875
- w_output: bfloat16 [1024, 1024], P(('wide', 'narrow')), may hold values from -1.5 to 1.5
- w_gate: bfloat16 [1024, 2816], P(('wide', 'narrow')), may hold values from -0.1875 to 0.1875
- w_up: bfloat16 [1024, 2816], P(('wide', 'narrow')), may hold values from -0.1875 to 0.1875
- w_down: bfloat16 [2816, 1024], P(('wide', 'narrow')), may hold values from -0.109375 to 0.109375
- gain_attn: bfloat16 [1024], P(('wide', 'narrow')), may hold values from 0.5 to 1.5
- gain_ffn: bfloat16 [1024], P(('wide', 'narrow')), may hold values from 0.5 to 1.5
- rel_table: bfloat16 [512], P(('wide', 'narrow')), may hold values from -4 to 4
- lay_table: bfloat16 [512], P(('wide', 'narrow')), may hold values from -4 to 4
- ocr_counts: int32 [32], P(('wide', 'narrow')), may hold values from 50 to 316, as said below
- rel_bucket: int32 [16384, 512], P(('wide', 'narrow')), may hold values from 0 to 31
- lay_bucket: int32 [16384, 512], P(('wide', 'narrow')), may hold values from 0 to 31
- cotangent: bfloat16 [16384, 1024], P(('wide', 'narrow')), may hold values from -6 to 6
Outputs:
- output: bfloat16 [16384, 1024], P(('wide', 'narrow'))
- grad_tokens: float32 [16384, 1024], P(('wide', 'narrow'))
- grad_query: float32 [1024, 1024], P(('wide', 'narrow'))
- grad_key: float32 [1024, 1024], P(('wide', 'narrow'))
- grad_value: float32 [1024, 1024], P(('wide', 'narrow'))
- grad_output: float32 [1024, 1024], P(('wide', 'narrow'))
- grad_gate: float32 [1024, 2816], P(('wide', 'narrow'))
- grad_up: float32 [1024, 2816], P(('wide', 'narrow'))
- grad_down: float32 [2816, 1024], P(('wide', 'narrow'))
- grad_gain_attn: float32 [1024], P(('wide', 'narrow'))
- grad_gain_ffn: float32 [1024], P(('wide', 'narrow'))
- grad_rel: float32 [512], P(('wide', 'narrow'))
- grad_lay: float32 [512], P(('wide', 'narrow'))
The draws below stay inside these ranges and needn't reach their ends.
Inputs may be any that keep to these rules, and one draw needn't show every extreme that they name: `ocr_counts`: one page in every draw holds exactly 316 OCR tokens.
All inputs are finite; a program needn't handle non-finite values.
Results may differ from the reference program's by a relative error of at most 0.035.
Values may be sent and summed in bfloat16 or wider, within the bound.
A program may use at most 320 MiB of HBM per device.

```python
import jax
import jax.numpy as jnp
from jax import lax

D = 1024
H = 16
HD = 64
FF = 2816
NB = 32
SLOT = 512
IMG = 196
OCR_MIN = 50
OCR_MAX = 316
PAGES = 32
TOKENS = 16384


def draw_ocr_counts(key, part):
    key = jax.random.fold_in(key, 7)
    first_key, second_key = jax.random.split(key)
    counts = jax.random.randint(first_key, (PAGES,), OCR_MIN, OCR_MAX + 1)
    fullest = jax.random.randint(second_key, (), 0, PAGES)
    return jnp.where(jnp.arange(PAGES) == fullest, OCR_MAX, counts).astype(jnp.int32)


def plant(values, stream_key, low, top_value):
    index_at = [jax.random.randint(jax.random.fold_in(stream_key, axis), (), 0, length) for axis, length in enumerate(values.shape)]
    longest = values.shape.index(max(values.shape))
    next_to = index_at[:longest] + [(index_at[longest] + 1) % values.shape[longest]] + index_at[longest + 1:]
    return values.at[tuple(index_at)].set(low).at[tuple(next_to)].set(top_value)


def levels(own_key, dims, pieces, low, top_value):
    def one(dim, parts):
        heights = jax.random.uniform(jax.random.fold_in(jax.random.fold_in(own_key, 6), dim), (parts,), jnp.float32, low / len(pieces), top_value / len(pieces))
        return jnp.repeat(jnp.exp(heights), dims[dim] // parts).reshape((-1,) + (1,) * (len(dims) - dim - 1))

    factor_of = one(*pieces[0])
    for cut in pieces[1:]:
        factor_of = factor_of * one(*cut)
    return factor_of


def gaussian(rng, dims, scale, reach, shards=(), held_as=jnp.bfloat16):
    entries = scale * jax.random.normal(rng, dims, jnp.float32)
    if shards:
        entries = entries * levels(rng, dims, shards, -0.22, 0.18)
    return jnp.clip(entries, -reach, reach).astype(held_as)


def setup_inputs(seed: int = 0) -> dict:
    splits = jax.random.split(jax.random.key(seed), 17)
    return {
        "tokens": gaussian(splits[0], (TOKENS, D), 1.0, 6.0, ((0, 32),)),
        "w_query": gaussian(splits[1], (D, D), (D * HD) ** -0.5, 0.0234375, ((0, 32),)),
        "w_key": gaussian(splits[2], (D, D), D ** -0.5, 0.1875, ((0, 32),)),
        "w_value": gaussian(splits[3], (D, D), D ** -0.5, 0.1875, ((0, 32),)),
        "w_output": gaussian(splits[4], (D, D), 16 ** -0.5, 1.5, ((0, 32),)),
        "w_gate": gaussian(splits[5], (D, FF), D ** -0.5, 0.1875, ((0, 32),)),
        "w_up": gaussian(splits[6], (D, FF), D ** -0.5, 0.1875, ((0, 32),)),
        "w_down": gaussian(splits[7], (FF, D), FF ** -0.5, 0.109375, ((0, 32),)),
        "gain_attn": jnp.clip(1.0 + 0.1 * jax.random.normal(splits[8], (D,), jnp.float32), 0.5, 1.5).astype(jnp.bfloat16),
        "gain_ffn": jnp.clip(1.0 + 0.1 * jax.random.normal(splits[9], (D,), jnp.float32), 0.5, 1.5).astype(jnp.bfloat16),
        "rel_table": gaussian(splits[10], (NB * H,), 0.7, 4.0, ((0, 32),)),
        "lay_table": gaussian(splits[11], (NB * H,), 0.7, 4.0, ((0, 32),)),
        "ocr_counts": draw_ocr_counts(jax.random.fold_in(splits[16], 71), 0),
        "rel_bucket": plant(jax.random.randint(splits[13], (TOKENS, SLOT), 0, NB), jax.random.fold_in(splits[13], 1), 0, NB - 1).astype(jnp.int32),
        "lay_bucket": plant(jax.random.randint(splits[14], (TOKENS, SLOT), 0, NB), jax.random.fold_in(splits[14], 1), 0, NB - 1).astype(jnp.int32),
        "cotangent": gaussian(splits[15], (TOKENS, D), 1.0, 6.0, ((0, 32),)),
    }


RMS_EPSILON = 1e-06
MASK_SCORE = -1000000000.0

@jax.custom_vjp
def low(v):
    return lax.optimization_barrier(v.astype(jnp.bfloat16)).astype(jnp.float32)

@jax.custom_vjp
def low_back(v):
    return v

def low_keep(v):
    return (low(v), None)

def low_pass(kept, grad):
    return (grad,)

def back_keep(v):
    return (v, None)

def back_low(kept, grad):
    return (low(grad),)
low.defvjp(low_keep, low_pass)
low_back.defvjp(back_keep, back_low)

def matmul(left, right):
    return jnp.dot(left, right, precision=lax.Precision.HIGHEST)

def rms_scale(values, gain):
    return values * lax.rsqrt(lax.optimization_barrier(jnp.mean(values * values, axis=-1, keepdims=True)) + RMS_EPSILON) * gain

def page_layer(page_rows, params, count, rel_ids, lay_ids):
    w_query, w_key, w_value, w_output, w_gate, w_up, w_down, gain_attn, gain_ffn, rel_table, lay_table = params
    slot = page_rows.shape[0]
    valid = jnp.arange(slot) < count + IMG
    normed_attn = low(rms_scale(page_rows, gain_attn))
    queries = low_back(low(matmul(normed_attn, w_query))).reshape(slot, H, HD)
    keys_all = low_back(low(matmul(normed_attn, w_key))).reshape(slot, H, HD)
    values_all = low_back(low(matmul(normed_attn, w_value))).reshape(slot, H, HD)
    scores = jnp.einsum('ihd,jhd->hij', queries, keys_all, precision=lax.Precision.HIGHEST)
    bias = rel_table.reshape(NB, H)[rel_ids] + lay_table.reshape(NB, H)[lay_ids]
    scores = scores + jnp.transpose(bias, (2, 0, 1))
    scores = jnp.where(valid[None, None, :], scores, MASK_SCORE)
    scores = low_back(scores)
    probs = low(jax.nn.softmax(scores, axis=-1))
    attended = jnp.einsum('hij,jhd->ihd', probs, values_all, precision=lax.Precision.HIGHEST)
    attended = low_back(low(attended.reshape(slot, H * HD)))
    hidden_one = page_rows + low_back(matmul(attended, w_output))
    normed_ffn = low(rms_scale(hidden_one, gain_ffn))
    gate_act = low_back(matmul(normed_ffn, w_gate))
    up_proj = low_back(matmul(normed_ffn, w_up))
    mixed = low(jax.nn.gelu(gate_act, approximate=True) * up_proj)
    result = hidden_one + matmul(mixed, w_down)
    return jnp.where(valid[:, None], result, 0.0)

def reference(tokens, w_query, w_key, w_value, w_output, w_gate, w_up, w_down, gain_attn, gain_ffn, rel_table, lay_table, ocr_counts, rel_bucket, lay_bucket, cotangent):
    params = tuple((weight.astype(jnp.float32) for weight in (w_query, w_key, w_value, w_output, w_gate, w_up, w_down, gain_attn, gain_ffn, rel_table, lay_table)))
    pages = tokens.astype(jnp.float32).reshape(PAGES, SLOT, D)
    cot_pages = cotangent.astype(jnp.float32).reshape(PAGES, SLOT, D)
    rel_pages = rel_bucket.reshape(PAGES, SLOT, SLOT)
    lay_pages = lay_bucket.reshape(PAGES, SLOT, SLOT)

    def one_page(totals, item):
        page_rows, page_cot, count, rel_ids, lay_ids = item
        result, pull = jax.vjp(lambda rows, weights: page_layer(rows, weights, count, rel_ids, lay_ids), page_rows, params)
        grad_rows, grad_params = pull(page_cot)
        totals = jax.tree.map(lambda first, second: first + second, totals, grad_params)
        return (totals, (result.astype(jnp.bfloat16), grad_rows))
    zeros_set = tuple((jnp.zeros_like(weight) for weight in params))
    totals, (outputs, grad_rows) = lax.scan(one_page, zeros_set, (pages, cot_pages, ocr_counts, rel_pages, lay_pages))
    return (outputs.reshape(TOKENS, D), grad_rows.reshape(TOKENS, D), totals[0], totals[1], totals[2], totals[3], totals[4], totals[5], totals[6], totals[7], totals[8], totals[9], totals[10])
```

```python
import functools

import jax
import jax.numpy as jnp
from jax import lax
from jax.experimental import pallas as pl
from jax.experimental.pallas import tpu as pltpu
from jax.sharding import PartitionSpec as P

H = 16
HD = 64
NB = 32
IMG = 196
RING = 6
SCATTER_COPIES = 10


RMS_EPSILON = 1e-06
MASK_SCORE = -1000000000.0
HEAD_GROUP = 4


def rms_scale(values, gain):
    return (
        values * lax.rsqrt(jnp.mean(values * values, axis=-1, keepdims=True) + RMS_EPSILON) * gain
    )


def gated_product(gate_act, up_proj):
    return jax.nn.gelu(gate_act, approximate=True) * up_proj


def product(left, right):
    return jnp.dot(left, right, preferred_element_type=jnp.float32)


def contract_rows(left, right):
    return lax.dot_general(
        left, right, (((0,), (0,)), ((), ())), preferred_element_type=jnp.float32
    )


def contract_cols(left, right):
    return lax.dot_general(
        left, right, (((1,), (1,)), ((), ())), preferred_element_type=jnp.float32
    )


def split_heads(matrix):
    return jnp.moveaxis(matrix.reshape(matrix.shape[0], H // HEAD_GROUP, HEAD_GROUP, HD), 1, 0)


def join_heads(stacked):
    return jnp.moveaxis(stacked, 0, 1).reshape(stacked.shape[1], H * HD)


def group_tables(table_all):
    return jnp.moveaxis(table_all.reshape(2 * NB, H // HEAD_GROUP, HEAD_GROUP), 1, 0)


def group_scores(query_group, key_group, table_group, onehot, valid):
    scores = jnp.einsum("ihd,jhd->hij", query_group, key_group, preferred_element_type=jnp.float32)
    scores = scores + jnp.einsum(
        "ijb,bh->hij", onehot, table_group, preferred_element_type=jnp.float32
    )
    return jnp.where(valid[None, None, :], scores, MASK_SCORE)


def gather_weights(
    w_query,
    w_key,
    w_value,
    w_output,
    w_gate,
    w_up,
    w_down,
    gain_attn,
    gain_ffn,
    rel_table,
    lay_table,
):
    return (
        lax.all_gather(w_query, ("wide", "narrow"), axis=0, tiled=True),
        lax.all_gather(w_key, ("wide", "narrow"), axis=0, tiled=True),
        lax.all_gather(w_value, ("wide", "narrow"), axis=0, tiled=True),
        lax.all_gather(w_output, ("wide", "narrow"), axis=0, tiled=True),
        lax.all_gather(w_gate, ("wide", "narrow"), axis=0, tiled=True),
        lax.all_gather(w_up, ("wide", "narrow"), axis=0, tiled=True),
        lax.all_gather(w_down, ("wide", "narrow"), axis=0, tiled=True),
        lax.all_gather(gain_attn, ("wide", "narrow"), axis=0, tiled=True),
        lax.all_gather(gain_ffn, ("wide", "narrow"), axis=0, tiled=True),
        lax.all_gather(rel_table, ("wide", "narrow"), axis=0, tiled=True),
        lax.all_gather(lay_table, ("wide", "narrow"), axis=0, tiled=True),
    )


def table_pair(full_rel, full_lay):
    return jnp.concatenate([full_rel.reshape(NB, H), full_lay.reshape(NB, H)], axis=0)


def forward_pass(tokens_f, weights, onehot, valid):
    (
        full_query,
        full_key,
        full_value,
        full_output,
        full_gate,
        full_up,
        full_down,
        full_gain_attn,
        full_gain_ffn,
        full_rel,
        full_lay,
    ) = weights
    normed_attn = rms_scale(tokens_f, full_gain_attn.astype(jnp.float32)).astype(jnp.bfloat16)
    queries = product(normed_attn, full_query).astype(jnp.bfloat16)
    keys_all = product(normed_attn, full_key).astype(jnp.bfloat16)
    values_all = product(normed_attn, full_value).astype(jnp.bfloat16)

    def forward_one_group(operands):
        query_group, key_group, value_group, table_group = operands
        scores = group_scores(query_group, key_group, table_group, onehot, valid)
        peak = jnp.max(scores, axis=-1, keepdims=True)
        expo = jnp.exp(scores - peak)
        total = jnp.sum(expo, axis=-1, keepdims=True)
        probs_low = (expo / total).astype(jnp.bfloat16)
        attended_group = jnp.einsum(
            "hij,jhd->ihd", probs_low, value_group, preferred_element_type=jnp.float32
        )
        return (attended_group.astype(jnp.bfloat16), (peak + jnp.log(total))[..., 0])

    stacked, log_totals = lax.map(
        forward_one_group,
        (
            split_heads(queries),
            split_heads(keys_all),
            split_heads(values_all),
            group_tables(table_pair(full_rel, full_lay)),
        ),
    )
    attended = join_heads(stacked)
    hidden_one = tokens_f + product(attended, full_output)
    normed_ffn = rms_scale(hidden_one, full_gain_ffn.astype(jnp.float32)).astype(jnp.bfloat16)
    gate_act = product(normed_ffn, full_gate)
    up_proj = product(normed_ffn, full_up)
    mixed = gated_product(gate_act, up_proj).astype(jnp.bfloat16)
    result = hidden_one + product(mixed, full_down)
    return (
        result,
        (
            normed_attn,
            queries,
            keys_all,
            values_all,
            log_totals,
            attended,
            hidden_one,
            normed_ffn,
            gate_act,
            up_proj,
            mixed,
        ),
    )


def attention_backward(
    queries, keys_all, values_all, log_totals, grad_attended, table_all, onehot, valid
):

    def attention_one_group(operands):
        query_group, key_group, value_group, table_group, lse_group, grad_group = operands
        scores = group_scores(query_group, key_group, table_group, onehot, valid)
        probs = jnp.exp(scores - lse_group[..., None])
        probs_low = probs.astype(jnp.bfloat16)
        grad_values = jnp.einsum(
            "hij,ihd->jhd", probs_low, grad_group, preferred_element_type=jnp.float32
        )
        grad_probs = jnp.einsum(
            "ihd,jhd->hij", grad_group, value_group, preferred_element_type=jnp.float32
        )
        grad_scores = (
            probs * (grad_probs - jnp.sum(probs * grad_probs, axis=-1, keepdims=True))
        ).astype(jnp.bfloat16)
        grad_queries = jnp.einsum(
            "hij,jhd->ihd", grad_scores, key_group, preferred_element_type=jnp.float32
        )
        grad_keys = jnp.einsum(
            "hij,ihd->jhd", grad_scores, query_group, preferred_element_type=jnp.float32
        )
        grad_table = jnp.einsum(
            "hij,ijb->bh", grad_scores, onehot, preferred_element_type=jnp.float32
        )
        return (
            grad_queries.astype(jnp.bfloat16),
            grad_keys.astype(jnp.bfloat16),
            grad_values.astype(jnp.bfloat16),
            grad_table,
        )

    grad_q_all, grad_k_all, grad_v_all, grad_tables = lax.map(
        attention_one_group,
        (
            split_heads(queries),
            split_heads(keys_all),
            split_heads(values_all),
            group_tables(table_all),
            log_totals,
            split_heads(grad_attended),
        ),
    )
    grad_table_all = jnp.moveaxis(grad_tables, 0, 1).reshape(2 * NB, H)
    return (join_heads(grad_q_all), join_heads(grad_k_all), join_heads(grad_v_all), grad_table_all)


MESH_ID = pl.DeviceIdType.MESH
BF = jnp.bfloat16
F32 = jnp.float32
X_BIT = 2
Y_BIT = 4
PARTS = ((X_BIT, Y_BIT), (Y_BIT, X_BIT))


class Links:
    def __init__(self, nn, send_sem, recv_sem):
        self.nn = nn
        self.w = lax.axis_index("wide")
        self.z = lax.axis_index("narrow")
        self.send_sem = send_sem
        self.recv_sem = recv_sem
        self.used = 0
        self.sent = []

    def fresh(self):
        self.used += 1
        return self.used - 1

    def wide(self, bit):
        return (jnp.bitwise_xor(self.w, bit), self.z)

    def along(self, step):
        return (self.w, lax.rem(self.z + step, self.nn))

    def copy(self, src, dst, number, device):
        return pltpu.make_async_remote_copy(
            src_ref=src,
            dst_ref=dst,
            send_sem=self.send_sem.at[number],
            recv_sem=self.recv_sem.at[number],
            device_id=device,
            device_id_type=MESH_ID,
        )

    def send(self, src, dst, number, device):
        copy = self.copy(src, dst, number, device)
        copy.start()
        self.sent.append(copy)

    def greet(self):
        barrier = pltpu.get_barrier_semaphore()
        others = [self.wide(bit) for bit in (1, X_BIT, Y_BIT)]
        others += [self.along(step) for step in range(1, self.nn)]
        for other in others:
            pl.semaphore_signal(barrier, inc=1, device_id=other, device_id_type=MESH_ID)
        pl.semaphore_wait(barrier, len(others))

    def finish(self):
        for copy in self.sent:
            copy.wait_send()


class Gather:
    def __init__(self, links, shard, full, rows, parts, local_sem, line=None, merged=None):
        self.links, self.shard, self.full, self.rows, self.parts = links, shard, full, rows, parts
        self.local_sem, self.line, self.merged = local_sem, line, merged
        nn = links.nn
        self.block = rows * nn
        self.line_ids = [links.fresh() for _ in range(1, nn)]
        self.part_ids = {
            (p, mask): links.fresh()
            for p in range(len(parts))
            for mask in (X_BIT, Y_BIT, X_BIT | Y_BIT)
        }
        self.core_ids = {mask: links.fresh() for mask in (0, X_BIT, Y_BIT, X_BIT | Y_BIT)}

    def place(self, w, z):
        if self.line is not None:
            return self.line.at[z]
        return self.full.at[pl.ds((w * self.links.nn + z) * self.rows, self.rows)]

    def span(self, mask, part=None):
        rows = pl.ds(jnp.bitwise_xor(self.links.w, mask) * self.block, self.block)
        if part is None:
            return self.full.at[rows]
        low, size = self.parts[part][:2]
        return self.full.at[rows, pl.ds(low, size)]

    def own(self):
        return pltpu.make_async_copy(
            self.shard, self.place(self.links.w, self.links.z), self.local_sem
        )

    def start(self):
        k = self.links
        self.own().start()
        for step in range(1, k.nn):
            k.send(self.shard, self.place(k.w, k.z), self.line_ids[step - 1], k.along(step))

    def spread(self):
        k = self.links
        self.own().wait()
        for step in range(1, k.nn):
            came = lax.rem(k.z - step + k.nn, k.nn)
            k.copy(
                self.shard, self.place(k.w, came), self.line_ids[step - 1], k.along(step)
            ).wait_recv()
        if self.line is not None:
            whole = jnp.concatenate(
                [self.line[z, : self.rows].astype(F32) for z in range(k.nn)], axis=0
            )
            self.merged[...] = whole.astype(BF)
            move = pltpu.make_async_copy(self.merged, self.span(0), self.local_sem)
            move.start()
            move.wait()
        for p, part in enumerate(self.parts):
            for bit in part[2]:
                k.send(self.span(0, p), self.span(0, p), self.part_ids[p, bit], k.wide(bit))
        k.send(self.span(0), self.span(0), self.core_ids[0], k.wide(1))

    def arrive(self, p, mask):
        k = self.links
        k.copy(
            self.span(mask, p), self.span(mask, p), self.part_ids[p, mask], k.wide(X_BIT)
        ).wait_recv()

    def forward(self):
        k = self.links
        for p, part in enumerate(self.parts):
            first, second = part[2]
            self.arrive(p, first)
            both = first | second
            k.send(self.span(first, p), self.span(first, p), self.part_ids[p, both], k.wide(second))
        for p, part in enumerate(self.parts):
            self.arrive(p, part[2][1])
        for mask in (X_BIT, Y_BIT):
            k.send(self.span(mask), self.span(mask), self.core_ids[mask], k.wide(1))

    def last(self):
        k = self.links
        both = X_BIT | Y_BIT
        for p in range(len(self.parts)):
            self.arrive(p, both)
        k.send(self.span(both), self.span(both), self.core_ids[both], k.wide(1))

    def done(self):
        k = self.links
        for mask, number in self.core_ids.items():
            place = self.span(mask | 1)
            k.copy(place, place, number, k.wide(1)).wait_recv()


def halves(columns):
    low = columns // 256 * 128
    return ((0, low, PARTS[0]), (low, columns - low, PARTS[1]))


def gather_kernel(nn, shapes, *refs):
    count = len(shapes)
    shards, fulls = refs[:count], refs[count : 2 * count]
    line, merged, send_sem, recv_sem, local_sem = refs[2 * count :]
    links = Links(nn, send_sem, recv_sem)
    links.greet()
    gathers = []
    for index, (rows, columns) in enumerate(shapes):
        odd = rows % 16 != 0 and columns > 128
        gathers.append(
            Gather(
                links,
                shards[index],
                fulls[index],
                rows,
                halves(columns) if columns > 128 else ((0, columns, PARTS[0]),),
                local_sem.at[index],
                line if odd else None,
                merged if odd else None,
            )
        )
    gathers[0].start()
    gathers[1].start()
    for index in range(count + 3):
        if index < count:
            gathers[index].spread()
            if index + 2 < count:
                gathers[index + 2].start()
        if 0 <= index - 1 < count:
            gathers[index - 1].forward()
        if 0 <= index - 2 < count:
            gathers[index - 2].last()
        if 0 <= index - 3 < count:
            gathers[index - 3].done()
    links.finish()


def gather_all(nw, nn, shards, odd_rows):
    devices = nw * nn
    shapes = []
    for index, shard in enumerate(shards):
        rows = odd_rows if index == len(shards) - 1 else shard.shape[0]
        shapes.append((rows, shard.shape[1]))
    copies = len(shards) * (nn - 1 + 6 + 4)
    return pl.pallas_call(
        functools.partial(gather_kernel, nn, shapes),
        out_shape=[
            jax.ShapeDtypeStruct((rows * devices, columns), shard.dtype)
            for (rows, columns), shard in zip(shapes, shards)
        ],
        in_specs=[pl.BlockSpec(memory_space=pl.ANY)] * len(shards),
        out_specs=[pl.BlockSpec(memory_space=pl.ANY)] * len(shards),
        scratch_shapes=[
            pltpu.VMEM((nn,) + shards[-1].shape, BF),
            pltpu.VMEM((nn * odd_rows, shards[-1].shape[1]), BF),
            pltpu.SemaphoreType.DMA((copies,)),
            pltpu.SemaphoreType.DMA((copies,)),
            pltpu.SemaphoreType.DMA((len(shards),)),
        ],
        compiler_params=pltpu.CompilerParams(collective_id=0, has_side_effects=True),
    )(*shards)


class Scatter:
    def __init__(self, links, chunks, rows, columns, grads, came, slots, base):
        self.links, self.chunks, self.rows, self.columns = links, chunks, rows, columns
        self.grads, self.came = grads, came
        (self.held, self.other, self.round, self.out_line, self.in_line, self.load_sem) = slots
        self.base = base
        self.block = rows * links.nn
        self.parts = halves(columns)
        self.core = lax.rem(links.w, 2)
        self.ring = self.held.shape[0]

    def number(self, chunk, kind):
        return self.base + chunk * SCATTER_COPIES + kind

    def core_copy(self, chunk):
        return self.links.copy(
            self.grads.at[chunk, :, 1 - self.core],
            self.came.at[chunk],
            self.number(chunk, 0),
            self.links.wide(1),
        )

    def trade(self, chunk):
        self.core_copy(chunk).start()

    def loads(self, chunk):
        slot, turn = lax.rem(chunk, self.ring), lax.rem(chunk, 2)
        return (
            pltpu.make_async_copy(
                self.grads.at[chunk, :, self.core], self.held.at[slot], self.load_sem.at[turn, 0]
            ),
            pltpu.make_async_copy(
                self.came.at[chunk], self.other.at[turn], self.load_sem.at[turn, 1]
            ),
        )

    def fetch(self, chunk):
        self.core_copy(chunk).wait_recv()
        for load in self.loads(chunk):
            load.start()

    def square(self, mask):
        return jnp.bitwise_xor(self.links.w, mask) // 2

    def hop(self, chunk, p, mask):
        slot = lax.rem(chunk, self.ring)
        low, size, order = self.parts[p]
        bit = order[1] if mask & order[1] else order[0]
        kind = 1 + p * 3 + (X_BIT, Y_BIT, X_BIT | Y_BIT).index(mask)
        return self.links.copy(
            self.held.at[slot, self.square(mask), :, pl.ds(low, size)],
            self.round.at[slot, kind - 1, :, pl.ds(0, size)],
            self.number(chunk, kind),
            self.links.wide(bit),
        )

    def landed(self, chunk, p, mask):
        return self.round.at[
            lax.rem(chunk, self.ring), p * 3 + (X_BIT, Y_BIT, X_BIT | Y_BIT).index(mask)
        ]

    def add_core(self, chunk):
        for load in self.loads(chunk):
            load.wait()
        slot, turn = lax.rem(chunk, self.ring), lax.rem(chunk, 2)

        def one(square, carry):
            self.held[slot, square] = (
                self.held[slot, square].astype(F32) + self.other[turn, square].astype(F32)
            ).astype(BF)
            return carry

        lax.fori_loop(0, self.held.shape[1], one, 0)
        for p, part in enumerate(self.parts):
            self.hop(chunk, p, X_BIT | Y_BIT).start()
        for p, part in enumerate(self.parts):
            self.hop(chunk, p, part[2][1]).start()

    def add_corner(self, chunk):
        slot = lax.rem(chunk, self.ring)
        for p, (low, size, order) in enumerate(self.parts):
            self.hop(chunk, p, X_BIT | Y_BIT).wait_recv()
            square = self.square(order[0])
            came = self.landed(chunk, p, X_BIT | Y_BIT)
            self.held[slot, square, :, low : low + size] = (
                self.held[slot, square, :, low : low + size].astype(F32)
                + came[:, :size].astype(F32)
            ).astype(BF)
        for p, part in enumerate(self.parts):
            self.hop(chunk, p, part[2][0]).start()

    def line_copy(self, chunk, step):
        k = self.links
        slot = lax.rem(chunk, self.ring)
        return k.copy(
            self.out_line.at[slot, lax.rem(k.z + step, k.nn)],
            self.in_line.at[slot, step - 1],
            self.number(chunk, 6 + step),
            k.along(step),
        )

    def add_square(self, chunk):
        slot = lax.rem(chunk, self.ring)
        home = self.square(0)
        for p, (low, size, order) in enumerate(self.parts):
            total = self.held[slot, home, :, low : low + size].astype(F32)
            for mask in order:
                self.hop(chunk, p, mask).wait_recv()
                total = total + self.landed(chunk, p, mask)[:, :size].astype(F32)
            for z in range(self.links.nn):
                self.out_line[slot, z, : self.rows, low : low + size] = total[
                    z * self.rows : (z + 1) * self.rows
                ].astype(BF)
        for step in range(1, self.links.nn):
            self.line_copy(chunk, step).start()

    def total(self, chunk):
        slot = lax.rem(chunk, self.ring)
        total = self.out_line[slot, self.links.z, : self.rows].astype(F32)
        for step in range(1, self.links.nn):
            self.line_copy(chunk, step).wait_recv()
            total = total + self.in_line[slot, step - 1, : self.rows].astype(F32)
        return total

    def wait_sent(self, chunk):
        self.core_copy(chunk).wait_send()
        for p, part in enumerate(self.parts):
            for mask in (X_BIT, Y_BIT, X_BIT | Y_BIT):
                self.hop(chunk, p, mask).wait_send()
        for step in range(1, self.links.nn):
            self.line_copy(chunk, step).wait_send()


def scatter_kernel(nn, few, many, few_ref, many_ref, small_ref, few_out, many_out, small_out, few_came, many_came, *refs):
    few_slots, many_slots = refs[:6], refs[6:12]
    small_came, small_round, small_line, small_mine, send_sem, recv_sem = refs[12:]
    links = Links(nn, send_sem, recv_sem)
    links.greet()
    sets = []
    base = 0
    for (chunks, rows, columns), grads, came, slots in (
        (few, few_ref, few_came, few_slots),
        (many, many_ref, many_came, many_slots),
    ):
        sets.append(Scatter(links, chunks, rows, columns, grads, came, slots, base))
        base += chunks * SCATTER_COPIES
    links.used = base

    def run(scatter, out):
        chunks = scatter.chunks

        def each(chunk, carry):
            scatter.trade(chunk)
            return carry

        lax.fori_loop(0, chunks, each, 0)

        def step(index, carry):
            for lag, action in enumerate(
                (scatter.fetch, scatter.add_core, scatter.add_corner, scatter.add_square)
            ):
                chunk = index - lag

                @pl.when(jnp.logical_and(chunk >= 0, chunk < chunks))
                def _(chunk=chunk, action=action):
                    action(chunk)

            chunk = index - 4

            @pl.when(chunk >= 0)
            def _(chunk=chunk):
                out[chunk] = scatter.total(chunk)
                scatter.wait_sent(chunk)

            return carry

        lax.fori_loop(0, chunks + 4, step, 0)

    run(sets[0], few_out)
    run(sets[1], many_out)
    scatter_small(links, small_ref, small_out, small_came, small_round, small_line, small_mine)
    links.finish()


def scatter_small(links, grads, out, came, round_in, line_in, mine):
    core = lax.rem(links.w, 2)
    home = links.w // 2
    number = links.fresh()
    links.send(grads.at[:, 1 - core], came, number, links.wide(1))
    links.sent[-1].wait_recv()
    mine[...] = grads[:, core] + came[...]
    masks = (X_BIT, Y_BIT, X_BIT | Y_BIT)
    copies = []
    for index, mask in enumerate(masks):
        number = links.fresh()
        links.send(
            mine.at[jnp.bitwise_xor(links.w, mask) // 2], round_in.at[index], number, links.wide(mask)
        )
        copies.append(links.sent[-1])
    for copy in copies:
        copy.wait()
    del links.sent[-3:]
    mine[home] = mine[home] + round_in[0] + round_in[1] + round_in[2]
    copies = []
    for step in range(1, links.nn):
        number = links.fresh()
        links.send(
            mine.at[home, pl.ds(lax.rem(links.z + step, links.nn) * 8, 8)],
            line_in.at[step - 1],
            number,
            links.along(step),
        )
        copies.append(links.sent[-1])
    total = mine[home, pl.ds(pl.multiple_of(links.z * 8, 8), 8)]
    for step in range(1, links.nn):
        copies[step - 1].wait_recv()
        total = total + line_in[step - 1]
    out[...] = total


def padded(rows):
    return (rows + 15) // 16 * 16


def scatter_slots(squares, nn, rows, columns):
    half = columns // 2
    return [
        pltpu.VMEM((RING, squares, nn * rows, columns), BF),
        pltpu.VMEM((2, squares, nn * rows, columns), BF),
        pltpu.VMEM((RING, 6, nn * rows, half), BF),
        pltpu.VMEM((RING, nn, padded(rows), columns), BF),
        pltpu.VMEM((RING, nn - 1, padded(rows), columns), BF),
        pltpu.SemaphoreType.DMA((2, 2)),
    ]


def scatter_all(nw, nn, few_grads, many_grads, small):
    squares = nw // 2

    def facts(grads):
        return (grads.shape[0], grads.shape[1] // (nw * nn), grads.shape[2])

    few, many = facts(few_grads), facts(many_grads)
    outs = []
    for chunks, rows, columns in (few, many):
        outs.append(jax.ShapeDtypeStruct((chunks, rows, columns), F32))
    outs.append(jax.ShapeDtypeStruct((8, 128), F32))
    for chunks, rows, columns in (few, many):
        outs.append(jax.ShapeDtypeStruct((chunks, squares, nn * rows, columns), BF))
    copies = (few[0] + many[0]) * SCATTER_COPIES + 16
    vmem = pl.BlockSpec(memory_space=pltpu.VMEM)
    hbm = pl.BlockSpec(memory_space=pl.ANY)
    given = [
        grads.reshape(grads.shape[0], squares, 2, -1, grads.shape[2])
        for grads in (few_grads, many_grads)
    ]
    return pl.pallas_call(
        functools.partial(scatter_kernel, nn, few, many),
        out_shape=outs,
        in_specs=[hbm, hbm, vmem],
        out_specs=[vmem, vmem, vmem, hbm, hbm],
        scratch_shapes=scatter_slots(squares, nn, few[1], few[2])
        + scatter_slots(squares, nn, many[1], many[2])
        + [
            pltpu.VMEM((squares, nn * 8, 128), F32),
            pltpu.VMEM((3, nn * 8, 128), F32),
            pltpu.VMEM((nn - 1, 8, 128), F32),
            pltpu.VMEM((squares, nn * 8, 128), F32),
            pltpu.SemaphoreType.DMA((copies,)),
            pltpu.SemaphoreType.DMA((copies,)),
        ],
        compiler_params=pltpu.CompilerParams(
            collective_id=1, has_side_effects=True, vmem_limit_bytes=60 * 2**20
        ),
    )(*given, small.reshape(squares, 2, nn * 8, 128))[:3]

def gather_fast(
    nw,
    nn,
    w_query,
    w_key,
    w_value,
    w_output,
    w_gate,
    w_up,
    w_down,
    gain_attn,
    gain_ffn,
    rel_table,
    lay_table,
):
    small = jnp.concatenate([gain_attn, gain_ffn, rel_table, lay_table]).astype(F32)
    small = jnp.zeros((8, 128), F32).at[0, : small.shape[0]].set(small)
    down = jnp.pad(w_down, ((0, padded(w_down.shape[0]) - w_down.shape[0]), (0, 0)))
    full = gather_all(
        nw,
        nn,
        [small, w_query, w_key, w_value, w_output, w_gate, w_up, down],
        w_down.shape[0],
    )
    rows = full[0].reshape(nw * nn, 8, 128)[:, 0]
    cuts, at = [], 0
    for part in (gain_attn, gain_ffn, rel_table, lay_table):
        size = part.shape[0]
        cuts.append(rows[:, at : at + size].reshape(-1).astype(BF))
        at += size
    return tuple(full[1:]) + tuple(cuts)


def scatter_fast(
    nw,
    nn,
    grad_query,
    grad_key,
    grad_value,
    grad_output,
    grad_gate,
    grad_up,
    grad_down,
    grad_gain_attn,
    grad_gain_ffn,
    grad_rel,
    grad_lay,
):
    devices = nw * nn

    def columns(grad, width):
        return jnp.moveaxis(
            grad.astype(BF).reshape(grad.shape[0], grad.shape[1] // width, width), 1, 0
        )

    few = columns(grad_down, 256)
    pairs = jnp.concatenate([columns(grad_gate, 256), columns(grad_up, 256)], axis=2)
    many = jnp.concatenate(
        [pairs] + [columns(grad, 512) for grad in (grad_output, grad_query, grad_key, grad_value)]
    )
    parts = [
        part.reshape(devices, -1) for part in (grad_gain_attn, grad_gain_ffn, grad_rel, grad_lay)
    ]
    small = jnp.concatenate(parts, axis=1)
    small = jnp.zeros((devices, 8, 128), F32).at[:, 0, : small.shape[1]].set(small)
    few_sum, many_sum, small_sum = scatter_all(nw, nn, few, many, small)

    def join(stack):
        return jnp.moveaxis(stack, 0, 1).reshape(stack.shape[1], -1)

    tiles = pairs.shape[0]
    owned = []
    for index in range(4):
        at = tiles + 2 * index
        owned.append(join(many_sum[at : at + 2]))
    gate, up = join(many_sum[:tiles, :, :256]), join(many_sum[:tiles, :, 256:])
    at, cuts = 0, []
    for part in parts:
        cuts.append(small_sum[0, at : at + part.shape[1]])
        at += part.shape[1]
    return (owned[1], owned[2], owned[3], owned[0], gate, up, join(few_sum)) + tuple(cuts)


def local(
    nw,
    nn,
    tokens,
    w_query,
    w_key,
    w_value,
    w_output,
    w_gate,
    w_up,
    w_down,
    gain_attn,
    gain_ffn,
    rel_table,
    lay_table,
    ocr_counts,
    rel_bucket,
    lay_bucket,
    cotangent,
):
    slot = tokens.shape[0]
    valid = jnp.arange(slot) < ocr_counts[0] + IMG
    buckets = jnp.arange(NB)
    onehot = jnp.concatenate(
        [
            (rel_bucket[:, :, None] == buckets).astype(jnp.bfloat16),
            (lay_bucket[:, :, None] == buckets).astype(jnp.bfloat16),
        ],
        axis=2,
    )
    tokens_f = tokens.astype(jnp.float32)
    fast = nw == 8 and w_query.shape[0] % 16 == 0
    if fast:
        weights = gather_fast(
            nw,
            nn,
            w_query,
            w_key,
            w_value,
            w_output,
            w_gate,
            w_up,
            w_down,
            gain_attn,
            gain_ffn,
            rel_table,
            lay_table,
        )
    else:
        weights = gather_weights(
            w_query,
            w_key,
            w_value,
            w_output,
            w_gate,
            w_up,
            w_down,
            gain_attn,
            gain_ffn,
            rel_table,
            lay_table,
        )
    result, saved = forward_pass(tokens_f, weights, onehot, valid)
    output = jnp.where(valid[:, None], result, 0.0).astype(jnp.bfloat16)
    (
        full_query,
        full_key,
        full_value,
        full_output,
        full_gate,
        full_up,
        full_down,
        full_gain_attn,
        full_gain_ffn,
        full_rel,
        full_lay,
    ) = weights
    (
        normed_attn,
        queries,
        keys_all,
        values_all,
        log_totals,
        attended,
        hidden_one,
        normed_ffn,
        gate_act,
        up_proj,
        mixed,
    ) = saved
    grad_result = jnp.where(valid[:, None], cotangent.astype(jnp.float32), 0.0)
    grad_low = grad_result.astype(jnp.bfloat16)
    grad_down = contract_rows(mixed, grad_low)
    grad_mixed = contract_cols(grad_low, full_down)
    gated_value, gated_pull = jax.vjp(gated_product, gate_act, up_proj)
    grad_gate_act, grad_up_proj = gated_pull(grad_mixed)
    gate_low = grad_gate_act.astype(jnp.bfloat16)
    up_low = grad_up_proj.astype(jnp.bfloat16)
    grad_gate = contract_rows(normed_ffn, gate_low)
    grad_up = contract_rows(normed_ffn, up_low)
    grad_normed_ffn = contract_cols(gate_low, full_gate) + contract_cols(up_low, full_up)
    norm_value, norm_pull = jax.vjp(rms_scale, hidden_one, full_gain_ffn.astype(jnp.float32))
    grad_hidden_part, grad_gain_ffn = norm_pull(grad_normed_ffn)
    grad_hidden = grad_result + grad_hidden_part
    branch_low = grad_hidden.astype(jnp.bfloat16)
    grad_output = contract_rows(attended, branch_low)
    grad_attended = contract_cols(branch_low, full_output).astype(jnp.bfloat16)
    grad_queries, grad_keys, grad_values, grad_table_all = attention_backward(
        queries,
        keys_all,
        values_all,
        log_totals,
        grad_attended,
        table_pair(full_rel, full_lay),
        onehot,
        valid,
    )
    grad_rel = grad_table_all[:NB].reshape(NB * H)
    grad_lay = grad_table_all[NB:].reshape(NB * H)
    grad_query = contract_rows(normed_attn, grad_queries)
    grad_key = contract_rows(normed_attn, grad_keys)
    grad_value = contract_rows(normed_attn, grad_values)
    grad_normed_attn = (
        contract_cols(grad_queries, full_query)
        + contract_cols(grad_keys, full_key)
        + contract_cols(grad_values, full_value)
    )
    input_value, input_pull = jax.vjp(rms_scale, tokens_f, full_gain_attn.astype(jnp.float32))
    grad_input_part, grad_gain_attn = input_pull(grad_normed_attn)
    grad_tokens = grad_hidden + grad_input_part
    if fast:
        owned = scatter_fast(
            nw,
            nn,
            grad_query,
            grad_key,
            grad_value,
            grad_output,
            grad_gate,
            grad_up,
            grad_down,
            grad_gain_attn,
            grad_gain_ffn,
            grad_rel,
            grad_lay,
        )
        return (output, grad_tokens) + owned
    owned = (
        lax.psum_scatter(grad_query, ("wide", "narrow"), scatter_dimension=0, tiled=True),
        lax.psum_scatter(grad_key, ("wide", "narrow"), scatter_dimension=0, tiled=True),
        lax.psum_scatter(grad_value, ("wide", "narrow"), scatter_dimension=0, tiled=True),
        lax.psum_scatter(grad_output, ("wide", "narrow"), scatter_dimension=0, tiled=True),
        lax.psum_scatter(grad_gate, ("wide", "narrow"), scatter_dimension=0, tiled=True),
        lax.psum_scatter(grad_up, ("wide", "narrow"), scatter_dimension=0, tiled=True),
        lax.psum_scatter(grad_down, ("wide", "narrow"), scatter_dimension=0, tiled=True),
        lax.psum_scatter(grad_gain_attn, ("wide", "narrow"), scatter_dimension=0, tiled=True),
        lax.psum_scatter(grad_gain_ffn, ("wide", "narrow"), scatter_dimension=0, tiled=True),
        lax.psum_scatter(grad_rel, ("wide", "narrow"), scatter_dimension=0, tiled=True),
        lax.psum_scatter(grad_lay, ("wide", "narrow"), scatter_dimension=0, tiled=True),
    )
    return (
        output,
        grad_tokens,
        owned[0],
        owned[1],
        owned[2],
        owned[3],
        owned[4],
        owned[5],
        owned[6],
        owned[7],
        owned[8],
        owned[9],
        owned[10],
    )


def solution(mesh):
    placed = (
        P(("wide", "narrow"), None),
        P(("wide", "narrow"), None),
        P(("wide", "narrow"), None),
        P(("wide", "narrow"), None),
        P(("wide", "narrow"), None),
        P(("wide", "narrow"), None),
        P(("wide", "narrow"), None),
        P(("wide", "narrow"), None),
        P(("wide", "narrow")),
        P(("wide", "narrow")),
        P(("wide", "narrow")),
        P(("wide", "narrow")),
        P(("wide", "narrow")),
        P(("wide", "narrow"), None),
        P(("wide", "narrow"), None),
        P(("wide", "narrow"), None),
    )
    return jax.shard_map(
        functools.partial(local, mesh.shape["wide"], mesh.shape["narrow"]),
        mesh=mesh,
        in_specs=placed,
        out_specs=(
            P(("wide", "narrow"), None),
            P(("wide", "narrow"), None),
            P(("wide", "narrow"), None),
            P(("wide", "narrow"), None),
            P(("wide", "narrow"), None),
            P(("wide", "narrow"), None),
            P(("wide", "narrow"), None),
            P(("wide", "narrow"), None),
            P(("wide", "narrow"), None),
            P(("wide", "narrow")),
            P(("wide", "narrow")),
            P(("wide", "narrow")),
            P(("wide", "narrow")),
        ),
        check_vma=False,
    )
```

```python
import functools

import jax
import jax.numpy as jnp
from jax import lax
from jax.experimental import pallas as pl
from jax.experimental.pallas import tpu as pltpu
from jax.sharding import PartitionSpec as P

H = 16
HD = 64
NB = 32
IMG = 196
RING = 6
SCATTER_COPIES = 10
TILE = 256
QB = 8
GELU_SCALE = 0.7978845608028654
GELU_CUBE = 0.044715


RMS_EPSILON = 1e-06
MASK_SCORE = -1000000000.0
HEAD_GROUP = 4


def rms_scale(values, gain):
    return (
        values * lax.rsqrt(jnp.mean(values * values, axis=-1, keepdims=True) + RMS_EPSILON) * gain
    )


def gated_product(gate_act, up_proj):
    return jax.nn.gelu(gate_act, approximate=True) * up_proj


def product(left, right):
    return jnp.dot(left, right, preferred_element_type=jnp.float32)


def contract_rows(left, right):
    return lax.dot_general(
        left, right, (((0,), (0,)), ((), ())), preferred_element_type=jnp.float32
    )


def contract_cols(left, right):
    return lax.dot_general(
        left, right, (((1,), (1,)), ((), ())), preferred_element_type=jnp.float32
    )


def split_heads(matrix):
    return jnp.moveaxis(matrix.reshape(matrix.shape[0], H // HEAD_GROUP, HEAD_GROUP, HD), 1, 0)


def join_heads(stacked):
    return jnp.moveaxis(stacked, 0, 1).reshape(stacked.shape[1], H * HD)


def group_tables(table_all):
    return jnp.moveaxis(table_all.reshape(2 * NB, H // HEAD_GROUP, HEAD_GROUP), 1, 0)


def group_scores(query_group, key_group, table_group, onehot, valid):
    scores = jnp.einsum("ihd,jhd->hij", query_group, key_group, preferred_element_type=jnp.float32)
    scores = scores + jnp.einsum(
        "ijb,bh->hij", onehot, table_group, preferred_element_type=jnp.float32
    )
    return jnp.where(valid[None, None, :], scores, MASK_SCORE)


def gather_weights(
    w_query,
    w_key,
    w_value,
    w_output,
    w_gate,
    w_up,
    w_down,
    gain_attn,
    gain_ffn,
    rel_table,
    lay_table,
):
    return (
        lax.all_gather(w_query, ("wide", "narrow"), axis=0, tiled=True),
        lax.all_gather(w_key, ("wide", "narrow"), axis=0, tiled=True),
        lax.all_gather(w_value, ("wide", "narrow"), axis=0, tiled=True),
        lax.all_gather(w_output, ("wide", "narrow"), axis=0, tiled=True),
        lax.all_gather(w_gate, ("wide", "narrow"), axis=0, tiled=True),
        lax.all_gather(w_up, ("wide", "narrow"), axis=0, tiled=True),
        lax.all_gather(w_down, ("wide", "narrow"), axis=0, tiled=True),
        lax.all_gather(gain_attn, ("wide", "narrow"), axis=0, tiled=True),
        lax.all_gather(gain_ffn, ("wide", "narrow"), axis=0, tiled=True),
        lax.all_gather(rel_table, ("wide", "narrow"), axis=0, tiled=True),
        lax.all_gather(lay_table, ("wide", "narrow"), axis=0, tiled=True),
    )


def table_pair(full_rel, full_lay):
    return jnp.concatenate([full_rel.reshape(NB, H), full_lay.reshape(NB, H)], axis=0)


def forward_pass(tokens_f, weights, onehot, valid):
    (
        full_query,
        full_key,
        full_value,
        full_output,
        full_gate,
        full_up,
        full_down,
        full_gain_attn,
        full_gain_ffn,
        full_rel,
        full_lay,
    ) = weights
    normed_attn = rms_scale(tokens_f, full_gain_attn.astype(jnp.float32)).astype(jnp.bfloat16)
    queries = product(normed_attn, full_query).astype(jnp.bfloat16)
    keys_all = product(normed_attn, full_key).astype(jnp.bfloat16)
    values_all = product(normed_attn, full_value).astype(jnp.bfloat16)

    def forward_one_group(operands):
        query_group, key_group, value_group, table_group = operands
        scores = group_scores(query_group, key_group, table_group, onehot, valid)
        peak = jnp.max(scores, axis=-1, keepdims=True)
        expo = jnp.exp(scores - peak)
        total = jnp.sum(expo, axis=-1, keepdims=True)
        probs_low = (expo / total).astype(jnp.bfloat16)
        attended_group = jnp.einsum(
            "hij,jhd->ihd", probs_low, value_group, preferred_element_type=jnp.float32
        )
        return (attended_group.astype(jnp.bfloat16), (peak + jnp.log(total))[..., 0])

    stacked, log_totals = lax.map(
        forward_one_group,
        (
            split_heads(queries),
            split_heads(keys_all),
            split_heads(values_all),
            group_tables(table_pair(full_rel, full_lay)),
        ),
    )
    attended = join_heads(stacked)
    hidden_one = tokens_f + product(attended, full_output)
    normed_ffn = rms_scale(hidden_one, full_gain_ffn.astype(jnp.float32)).astype(jnp.bfloat16)
    gate_act = product(normed_ffn, full_gate)
    up_proj = product(normed_ffn, full_up)
    mixed = gated_product(gate_act, up_proj).astype(jnp.bfloat16)
    result = hidden_one + product(mixed, full_down)
    return (
        result,
        (
            normed_attn,
            queries,
            keys_all,
            values_all,
            log_totals,
            attended,
            hidden_one,
            normed_ffn,
            gate_act,
            up_proj,
            mixed,
        ),
    )


def attention_backward(
    queries, keys_all, values_all, log_totals, grad_attended, table_all, onehot, valid
):

    def attention_one_group(operands):
        query_group, key_group, value_group, table_group, lse_group, grad_group = operands
        scores = group_scores(query_group, key_group, table_group, onehot, valid)
        probs = jnp.exp(scores - lse_group[..., None])
        probs_low = probs.astype(jnp.bfloat16)
        grad_values = jnp.einsum(
            "hij,ihd->jhd", probs_low, grad_group, preferred_element_type=jnp.float32
        )
        grad_probs = jnp.einsum(
            "ihd,jhd->hij", grad_group, value_group, preferred_element_type=jnp.float32
        )
        grad_scores = (
            probs * (grad_probs - jnp.sum(probs * grad_probs, axis=-1, keepdims=True))
        ).astype(jnp.bfloat16)
        grad_queries = jnp.einsum(
            "hij,jhd->ihd", grad_scores, key_group, preferred_element_type=jnp.float32
        )
        grad_keys = jnp.einsum(
            "hij,ihd->jhd", grad_scores, query_group, preferred_element_type=jnp.float32
        )
        grad_table = jnp.einsum(
            "hij,ijb->bh", grad_scores, onehot, preferred_element_type=jnp.float32
        )
        return (
            grad_queries.astype(jnp.bfloat16),
            grad_keys.astype(jnp.bfloat16),
            grad_values.astype(jnp.bfloat16),
            grad_table,
        )

    grad_q_all, grad_k_all, grad_v_all, grad_tables = lax.map(
        attention_one_group,
        (
            split_heads(queries),
            split_heads(keys_all),
            split_heads(values_all),
            group_tables(table_all),
            log_totals,
            split_heads(grad_attended),
        ),
    )
    grad_table_all = jnp.moveaxis(grad_tables, 0, 1).reshape(2 * NB, H)
    return (join_heads(grad_q_all), join_heads(grad_k_all), join_heads(grad_v_all), grad_table_all)


MESH_ID = pl.DeviceIdType.MESH
BF = jnp.bfloat16
F32 = jnp.float32
X_BIT = 2
Y_BIT = 4
PARTS = ((X_BIT, Y_BIT), (Y_BIT, X_BIT))


class Links:
    def __init__(self, nn, send_sem, recv_sem):
        self.nn = nn
        self.w = lax.axis_index("wide")
        self.z = lax.axis_index("narrow")
        self.send_sem = send_sem
        self.recv_sem = recv_sem
        self.used = 0
        self.sent = []

    def fresh(self):
        self.used += 1
        return self.used - 1

    def wide(self, bit):
        return (jnp.bitwise_xor(self.w, bit), self.z)

    def along(self, step):
        return (self.w, lax.rem(self.z + step, self.nn))

    def copy(self, src, dst, number, device):
        return pltpu.make_async_remote_copy(
            src_ref=src,
            dst_ref=dst,
            send_sem=self.send_sem.at[number],
            recv_sem=self.recv_sem.at[number],
            device_id=device,
            device_id_type=MESH_ID,
        )

    def send(self, src, dst, number, device):
        copy = self.copy(src, dst, number, device)
        copy.start()
        self.sent.append(copy)

    def greet(self):
        barrier = pltpu.get_barrier_semaphore()
        others = [self.wide(bit) for bit in (1, X_BIT, Y_BIT)]
        others += [self.along(step) for step in range(1, self.nn)]
        for other in others:
            pl.semaphore_signal(barrier, inc=1, device_id=other, device_id_type=MESH_ID)
        pl.semaphore_wait(barrier, len(others))

    def finish(self):
        for copy in self.sent:
            copy.wait_send()


class Gather:
    def __init__(self, links, shard, full, rows, parts, local_sem, line=None, merged=None):
        self.links, self.shard, self.full, self.rows, self.parts = links, shard, full, rows, parts
        self.local_sem, self.line, self.merged = local_sem, line, merged
        nn = links.nn
        self.block = rows * nn
        self.line_ids = [links.fresh() for _ in range(1, nn)]
        self.part_ids = {
            (p, mask): links.fresh()
            for p in range(len(parts))
            for mask in (X_BIT, Y_BIT, X_BIT | Y_BIT)
        }
        self.core_ids = {mask: links.fresh() for mask in (0, X_BIT, Y_BIT, X_BIT | Y_BIT)}

    def place(self, w, z):
        if self.line is not None:
            return self.line.at[z]
        return self.full.at[pl.ds((w * self.links.nn + z) * self.rows, self.rows)]

    def span(self, mask, part=None):
        rows = pl.ds(jnp.bitwise_xor(self.links.w, mask) * self.block, self.block)
        if part is None:
            return self.full.at[rows]
        low, size = self.parts[part][:2]
        return self.full.at[rows, pl.ds(low, size)]

    def own(self):
        return pltpu.make_async_copy(
            self.shard, self.place(self.links.w, self.links.z), self.local_sem
        )

    def start(self):
        k = self.links
        self.own().start()
        for step in range(1, k.nn):
            k.send(self.shard, self.place(k.w, k.z), self.line_ids[step - 1], k.along(step))

    def spread(self):
        k = self.links
        self.own().wait()
        for step in range(1, k.nn):
            came = lax.rem(k.z - step + k.nn, k.nn)
            k.copy(
                self.shard, self.place(k.w, came), self.line_ids[step - 1], k.along(step)
            ).wait_recv()
        if self.line is not None:
            whole = jnp.concatenate(
                [self.line[z, : self.rows].astype(F32) for z in range(k.nn)], axis=0
            )
            self.merged[...] = whole.astype(BF)
            move = pltpu.make_async_copy(self.merged, self.span(0), self.local_sem)
            move.start()
            move.wait()
        for p, part in enumerate(self.parts):
            for bit in part[2]:
                k.send(self.span(0, p), self.span(0, p), self.part_ids[p, bit], k.wide(bit))
        k.send(self.span(0), self.span(0), self.core_ids[0], k.wide(1))

    def arrive(self, p, mask):
        k = self.links
        k.copy(
            self.span(mask, p), self.span(mask, p), self.part_ids[p, mask], k.wide(X_BIT)
        ).wait_recv()

    def forward(self):
        k = self.links
        for p, part in enumerate(self.parts):
            first, second = part[2]
            self.arrive(p, first)
            both = first | second
            k.send(self.span(first, p), self.span(first, p), self.part_ids[p, both], k.wide(second))
        for p, part in enumerate(self.parts):
            self.arrive(p, part[2][1])
        for mask in (X_BIT, Y_BIT):
            k.send(self.span(mask), self.span(mask), self.core_ids[mask], k.wide(1))

    def last(self):
        k = self.links
        both = X_BIT | Y_BIT
        for p in range(len(self.parts)):
            self.arrive(p, both)
        k.send(self.span(both), self.span(both), self.core_ids[both], k.wide(1))

    def done(self):
        k = self.links
        for mask, number in self.core_ids.items():
            place = self.span(mask | 1)
            k.copy(place, place, number, k.wide(1)).wait_recv()


def halves(columns):
    low = columns // 256 * 128
    return ((0, low, PARTS[0]), (low, columns - low, PARTS[1]))


def dot(left, right):
    return jnp.dot(left, right, preferred_element_type=F32)


def dot_nt(left, right):
    return lax.dot_general(left, right, (((1,), (1,)), ((), ())), preferred_element_type=F32)


def dot_tn(left, right):
    return lax.dot_general(left, right, (((0,), (0,)), ((), ())), preferred_element_type=F32)


def iota(shape, dimension):
    return lax.broadcasted_iota(jnp.int32, shape, dimension)


def ones_where(mask):
    return jnp.where(mask, 1.0, 0.0).astype(BF)


def unpack_row(rows, first, each, total):
    devices = rows.shape[0]
    pick = ones_where(iota((128, total), 0) == first + lax.rem(iota((128, total), 1), each))
    spread = dot(rows.astype(BF), pick)
    mine = iota((devices, total), 1) // each == iota((devices, total), 0)
    return jnp.sum(jnp.where(mine, spread, 0.0), axis=0, keepdims=True)


def table_block(rows, first):
    pick_shape = (H * QB, 128)
    total = None
    for index in range(2):
        lane = first + H * index + iota(pick_shape, 0) // QB
        pick = ones_where(iota(pick_shape, 1) == lane)
        table = dot_nt(pick, rows.astype(BF)).astype(BF)
        wide = (NB, QB * 2 * NB)
        spread = dot(table, ones_where(lax.rem(iota(wide, 1), 2 * NB) == iota(wide, 0) + NB * index))
        total = spread if total is None else total + spread
    shape = (H * QB, QB * 2 * NB)
    mine = lax.rem(iota(shape, 0), QB) == iota(shape, 1) // (2 * NB)
    return jnp.where(mine, total, 0.0).astype(BF)


def bucket_ones(rel, lay, onehot, block):
    width = rel.shape[1]
    rows = iota((NB, width), 0)
    for query in range(QB):
        for index, bucket in enumerate((rel, lay)):
            row = bucket[pl.ds(block * QB + query, 1), :]
            low = (query * 2 + index) * NB
            onehot[low : low + NB, :] = ones_where(jnp.broadcast_to(row, (NB, width)) == rows)


def forward_kernel(nn, shapes, *refs):
    count = len(shapes)
    occupied, tokens, rel_hbm, lay_hbm = refs[:4]
    shards = refs[4 : 4 + count]
    refs = refs[4 + count :]
    fulls, refs = refs[:count], refs[count:]
    saved, refs = refs[:10], refs[10:]
    (out_h, na_h, q_h, k_h, v_h, att_h, hid_h, nf_h, mix_h, probs_h) = saved
    (slope_h, act_h), refs = refs[:2], refs[2:]
    (
        line,
        merged,
        x,
        rel,
        lay,
        small,
        lhs,
        onehot,
        bias,
        na,
        q,
        k,
        v,
        att,
        hid,
        nf,
        mix,
        slope,
        act,
        probs,
        w_one,
        w_wide,
        w_down,
        gains,
        send_sem,
        recv_sem,
        gather_sem,
        local_sem,
        ring_sem,
    ) = refs
    slots, width = x.shape
    links = Links(nn, send_sem, recv_sem)
    numbers = iter(range(64))

    def move(src, dst):
        copy = pltpu.make_async_copy(src, dst, local_sem.at[next(numbers)])
        copy.start()
        return copy

    arriving = [move(tokens, x), move(rel_hbm, rel), move(lay_hbm, lay)]
    links.greet()
    g = []
    for index, (rows, columns) in enumerate(shapes):
        odd = rows % 16 != 0 and columns > 128
        g.append(
            Gather(
                links,
                shards[index],
                fulls[index],
                rows,
                halves(columns) if columns > 128 else ((0, columns, PARTS[0]),),
                gather_sem.at[index],
                line if odd else None,
                merged if odd else None,
            )
        )
    SMALL, Q, K, V, O, GATE, UP, DOWN = range(8)
    g[SMALL].start()
    g[Q].start()
    g[K].start()
    g[SMALL].spread()
    g[SMALL].forward()
    g[SMALL].last()
    g[SMALL].done()
    small_in = move(fulls[SMALL], small)
    g[Q].spread()
    g[V].start()
    leaving = []
    for copy in arriving:
        copy.wait()
    small_in.wait()
    rows = small.reshape(small.shape[0] // 8, 8, 128)[:, 0, :]
    each = width // rows.shape[0]
    gains[0:1, :] = unpack_row(rows, 0, each, width)
    gains[1:2, :] = unpack_row(rows, each, each, width)
    lhs[...] = table_block(rows, 2 * each)

    def normalise(index, carry):
        at = pl.ds(pl.multiple_of(index * 64, 64), 64)
        values = x[at, :].astype(F32)
        scale = lax.rsqrt(jnp.mean(values * values, axis=-1, keepdims=True) + RMS_EPSILON)
        na[at, :] = (values * scale * gains[0:1, :]).astype(BF)
        return carry

    lax.fori_loop(0, slots // 64, normalise, 0)
    leaving.append(move(na, na_h))
    valid = iota((1, slots), 1) < occupied[0] + IMG

    def bias_block(block, carry):
        bucket_ones(rel, lay, onehot, block)
        found = jnp.where(valid, dot(lhs[...], onehot[...]), MASK_SCORE)
        bias[:, pl.ds(pl.multiple_of(block * QB, QB), QB), :] = found.reshape(H, QB, slots)
        return carry

    blocks = slots // QB
    lax.fori_loop(0, blocks // 4, bias_block, 0)
    g[K].spread()
    g[O].start()
    g[Q].forward()
    lax.fori_loop(blocks // 4, blocks // 2, bias_block, 0)
    g[V].spread()
    g[GATE].start()
    g[K].forward()
    g[Q].last()
    lax.fori_loop(blocks // 2, 3 * blocks // 4, bias_block, 0)
    g[O].spread()
    g[V].forward()
    g[K].last()
    g[Q].done()
    fetch = move(fulls[Q], w_one.at[0])
    lax.fori_loop(3 * blocks // 4, blocks, bias_block, 0)
    fetch.wait()

    def project(slot, target):
        def one(tile, carry):
            at = pl.ds(pl.multiple_of(tile * TILE, TILE), TILE)
            target[:, at] = dot(na[...], w_one[slot, :, at]).astype(BF)
            return carry

        lax.fori_loop(0, width // TILE, one, 0)

    project(0, q)
    leaving.append(move(q, q_h))
    g[GATE].spread()
    g[UP].start()
    g[O].forward()
    g[V].last()
    g[K].done()
    fetch = move(fulls[K], w_one.at[1])
    fetch.wait()
    project(1, k)
    leaving.append(move(k, k_h))
    g[O].last()
    g[V].done()
    fetch = move(fulls[V], w_one.at[0])
    fetch.wait()
    project(0, v)
    leaving.append(move(v, v_h))

    def probs_out(pair):
        turn = lax.rem(pair, 2)
        return pltpu.make_async_copy(probs.at[turn], probs_h.at[pl.ds(pair * 2, 2)], ring_sem.at[turn])

    def attend(pair, carry):
        @pl.when(pair >= 2)
        def _():
            probs_out(pair - 2).wait()

        at = pl.ds(pl.multiple_of(pair * 128, 128), 128)
        low = iota((slots, 128), 1) < HD
        queries = q[:, at]
        keys = k[:, at]
        found = []
        for side in range(2):
            mine = jnp.where(low if side == 0 else jnp.logical_not(low), queries, 0)
            scores = dot_nt(mine, keys) + bias[pair * 2 + side]
            peak = jnp.max(scores, axis=-1, keepdims=True)
            expo = jnp.exp(scores - peak)
            total = jnp.sum(expo, axis=-1, keepdims=True)
            share = (expo * (1.0 / total)).astype(BF)
            probs[lax.rem(pair, 2), side] = share
            found.append(dot(share, v[:, at]))
        att[:, at] = jnp.where(low, found[0], found[1]).astype(BF)
        probs_out(pair).start()
        return carry

    pairs = H // 2
    lax.fori_loop(0, 2, attend, 0)
    g[UP].spread()
    g[DOWN].start()
    g[GATE].forward()
    g[O].done()
    fetch_o = move(fulls[O], w_one.at[1])
    lax.fori_loop(2, 5, attend, 0)
    g[GATE].last()
    lax.fori_loop(5, pairs, attend, 0)
    leaving.append(move(att, att_h))
    g[DOWN].spread()
    g[UP].forward()
    g[GATE].done()
    fetch_gate = move(fulls[GATE], w_wide.at[0])
    fetch_o.wait()

    def output_tile(tile, carry):
        at = pl.ds(pl.multiple_of(tile * TILE, TILE), TILE)
        hid[:, at] = x[:, at].astype(F32) + dot(att[...], w_one[1, :, at])
        return carry

    lax.fori_loop(0, width // TILE, output_tile, 0)
    leaving.append(move(hid, hid_h))

    def normalise_two(index, carry):
        at = pl.ds(pl.multiple_of(index * 64, 64), 64)
        values = hid[at, :]
        scale = lax.rsqrt(jnp.mean(values * values, axis=-1, keepdims=True) + RMS_EPSILON)
        nf[at, :] = (values * scale * gains[1:2, :]).astype(BF)
        return carry

    lax.fori_loop(0, slots // 64, normalise_two, 0)
    leaving.append(move(nf, nf_h))
    g[UP].last()
    g[DOWN].forward()
    g[UP].done()
    fetch_up = move(fulls[UP], w_wide.at[1])
    fetch_gate.wait()
    fetch_up.wait()

    def ffn_out(tile):
        turn = lax.rem(tile, 2)
        at = pl.ds(pl.multiple_of(tile * TILE, TILE), TILE)
        return (
            pltpu.make_async_copy(slope.at[turn], slope_h.at[:, at], ring_sem.at[2 + turn]),
            pltpu.make_async_copy(act.at[turn], act_h.at[:, at], ring_sem.at[4 + turn]),
        )

    def ffn_tile(tile, carry):
        @pl.when(tile >= 2)
        def _():
            for copy in ffn_out(tile - 2):
                copy.wait()

        at = pl.ds(pl.multiple_of(tile * TILE, TILE), TILE)
        turn = lax.rem(tile, 2)
        gate = dot(nf[...], w_wide[0, :, at])
        up = dot(nf[...], w_wide[1, :, at])
        square = gate * gate
        inner = GELU_SCALE * gate * (1.0 + GELU_CUBE * square)
        bend = jnp.tanh(inner)
        half = 0.5 * (1.0 + bend)
        active = gate * half
        rise = half + 0.5 * gate * (1.0 - bend * bend) * GELU_SCALE * (1.0 + 3.0 * GELU_CUBE * square)
        mix[:, at] = (active * up).astype(BF)
        act[turn] = active.astype(BF)
        slope[turn] = (up * rise).astype(BF)
        for copy in ffn_out(tile):
            copy.start()
        return carry

    tiles = mix.shape[1] // TILE
    lax.fori_loop(0, tiles // 2, ffn_tile, 0)
    g[DOWN].last()
    lax.fori_loop(tiles // 2, tiles, ffn_tile, 0)
    leaving.append(move(mix, mix_h))
    g[DOWN].done()
    move(fulls[DOWN], w_down).wait()
    valid_rows = iota((slots, 1), 0) < occupied[0] + IMG

    def down_tile(tile, carry):
        at = pl.ds(pl.multiple_of(tile * TILE, TILE), TILE)
        result = hid[:, at] + dot(mix[...], w_down[:, at])
        na[:, at] = jnp.where(valid_rows, result, 0.0).astype(BF)
        return carry

    leaving[0].wait()
    lax.fori_loop(0, width // TILE, down_tile, 0)
    move(na, out_h).wait()
    for copy in leaving[1:]:
        copy.wait()
    for pair in (pairs - 2, pairs - 1):
        probs_out(pair).wait()
    for tile in (tiles - 2, tiles - 1):
        for copy in ffn_out(tile):
            copy.wait()
    links.finish()


def forward_all(nw, nn, counts, tokens, rel, lay, shards, odd_rows):
    devices = nw * nn
    shapes = []
    for index, shard in enumerate(shards):
        rows = odd_rows if index == len(shards) - 1 else shard.shape[0]
        shapes.append((rows, shard.shape[1]))
    copies = len(shards) * (nn - 1 + 6 + 4)
    slots, width = tokens.shape
    ffn = shapes[5][1]
    low = jax.ShapeDtypeStruct((slots, width), BF)
    wide = jax.ShapeDtypeStruct((slots, ffn), BF)
    full = jax.ShapeDtypeStruct((slots, width), F32)
    out_shape = [
        jax.ShapeDtypeStruct((rows * devices, columns), shard.dtype)
        for (rows, columns), shard in zip(shapes, shards)
    ]
    out_shape += [low] * 6 + [full, low, wide]
    out_shape += [jax.ShapeDtypeStruct((H, slots, slots), BF), wide, wide]
    hbm = pl.BlockSpec(memory_space=pl.ANY)
    page = pltpu.VMEM((slots, width), BF)
    return pl.pallas_call(
        functools.partial(forward_kernel, nn, shapes),
        out_shape=out_shape,
        in_specs=[pl.BlockSpec(memory_space=pltpu.SMEM)] + [hbm] * (3 + len(shards)),
        out_specs=[hbm] * len(out_shape),
        scratch_shapes=[
            pltpu.VMEM((nn,) + shards[-1].shape, BF),
            pltpu.VMEM((nn * odd_rows, shards[-1].shape[1]), BF),
            page,
            pltpu.VMEM((slots, slots), jnp.int32),
            pltpu.VMEM((slots, slots), jnp.int32),
            pltpu.VMEM((devices * 8, 128), F32),
            pltpu.VMEM((H * QB, QB * 2 * NB), BF),
            pltpu.VMEM((QB * 2 * NB, slots), BF),
            pltpu.VMEM((H, slots, slots), F32),
            page,
            page,
            page,
            page,
            page,
            pltpu.VMEM((slots, width), F32),
            page,
            pltpu.VMEM((slots, ffn), BF),
            pltpu.VMEM((2, slots, TILE), BF),
            pltpu.VMEM((2, slots, TILE), BF),
            pltpu.VMEM((2, 2, slots, slots), BF),
            pltpu.VMEM((2, width, width), BF),
            pltpu.VMEM((2, width, ffn), BF),
            pltpu.VMEM((ffn, width), BF),
            pltpu.VMEM((8, width), F32),
            pltpu.SemaphoreType.DMA((copies,)),
            pltpu.SemaphoreType.DMA((copies,)),
            pltpu.SemaphoreType.DMA((len(shards),)),
            pltpu.SemaphoreType.DMA((64,)),
            pltpu.SemaphoreType.DMA((6,)),
        ],
        compiler_params=pltpu.CompilerParams(
            collective_id=0, has_side_effects=True, vmem_limit_bytes=63 * 2**20
        ),
    )(counts, tokens, rel, lay, *shards)


class Scatter:
    def __init__(self, links, chunks, rows, columns, grads, came, slots, base):
        self.links, self.chunks, self.rows, self.columns = links, chunks, rows, columns
        self.grads, self.came = grads, came
        (self.held, self.other, self.round, self.out_line, self.in_line, self.load_sem) = slots
        self.base = base
        self.block = rows * links.nn
        self.parts = halves(columns)
        self.core = lax.rem(links.w, 2)
        self.ring = self.held.shape[0]

    def number(self, chunk, kind):
        return self.base + chunk * SCATTER_COPIES + kind

    def core_copy(self, chunk):
        return self.links.copy(
            self.grads.at[chunk, :, 1 - self.core],
            self.came.at[chunk],
            self.number(chunk, 0),
            self.links.wide(1),
        )

    def trade(self, chunk):
        self.core_copy(chunk).start()

    def loads(self, chunk):
        slot, turn = lax.rem(chunk, self.ring), lax.rem(chunk, 2)
        return (
            pltpu.make_async_copy(
                self.grads.at[chunk, :, self.core], self.held.at[slot], self.load_sem.at[turn, 0]
            ),
            pltpu.make_async_copy(
                self.came.at[chunk], self.other.at[turn], self.load_sem.at[turn, 1]
            ),
        )

    def fetch(self, chunk):
        self.core_copy(chunk).wait_recv()
        for load in self.loads(chunk):
            load.start()

    def square(self, mask):
        return jnp.bitwise_xor(self.links.w, mask) // 2

    def hop(self, chunk, p, mask):
        slot = lax.rem(chunk, self.ring)
        low, size, order = self.parts[p]
        bit = order[1] if mask & order[1] else order[0]
        kind = 1 + p * 3 + (X_BIT, Y_BIT, X_BIT | Y_BIT).index(mask)
        return self.links.copy(
            self.held.at[slot, self.square(mask), :, pl.ds(low, size)],
            self.round.at[slot, kind - 1, :, pl.ds(0, size)],
            self.number(chunk, kind),
            self.links.wide(bit),
        )

    def landed(self, chunk, p, mask):
        return self.round.at[
            lax.rem(chunk, self.ring), p * 3 + (X_BIT, Y_BIT, X_BIT | Y_BIT).index(mask)
        ]

    def add_core(self, chunk):
        for load in self.loads(chunk):
            load.wait()
        slot, turn = lax.rem(chunk, self.ring), lax.rem(chunk, 2)

        def one(square, carry):
            self.held[slot, square] = (
                self.held[slot, square].astype(F32) + self.other[turn, square].astype(F32)
            ).astype(BF)
            return carry

        lax.fori_loop(0, self.held.shape[1], one, 0)
        for p, part in enumerate(self.parts):
            self.hop(chunk, p, X_BIT | Y_BIT).start()
        for p, part in enumerate(self.parts):
            self.hop(chunk, p, part[2][1]).start()

    def add_corner(self, chunk):
        slot = lax.rem(chunk, self.ring)
        for p, (low, size, order) in enumerate(self.parts):
            self.hop(chunk, p, X_BIT | Y_BIT).wait_recv()
            square = self.square(order[0])
            came = self.landed(chunk, p, X_BIT | Y_BIT)
            self.held[slot, square, :, low : low + size] = (
                self.held[slot, square, :, low : low + size].astype(F32)
                + came[:, :size].astype(F32)
            ).astype(BF)
        for p, part in enumerate(self.parts):
            self.hop(chunk, p, part[2][0]).start()

    def line_copy(self, chunk, step):
        k = self.links
        slot = lax.rem(chunk, self.ring)
        return k.copy(
            self.out_line.at[slot, lax.rem(k.z + step, k.nn)],
            self.in_line.at[slot, step - 1],
            self.number(chunk, 6 + step),
            k.along(step),
        )

    def add_square(self, chunk):
        slot = lax.rem(chunk, self.ring)
        home = self.square(0)
        for p, (low, size, order) in enumerate(self.parts):
            total = self.held[slot, home, :, low : low + size].astype(F32)
            for mask in order:
                self.hop(chunk, p, mask).wait_recv()
                total = total + self.landed(chunk, p, mask)[:, :size].astype(F32)
            for z in range(self.links.nn):
                self.out_line[slot, z, : self.rows, low : low + size] = total[
                    z * self.rows : (z + 1) * self.rows
                ].astype(BF)
        for step in range(1, self.links.nn):
            self.line_copy(chunk, step).start()

    def total(self, chunk):
        slot = lax.rem(chunk, self.ring)
        total = self.out_line[slot, self.links.z, : self.rows].astype(F32)
        for step in range(1, self.links.nn):
            self.line_copy(chunk, step).wait_recv()
            total = total + self.in_line[slot, step - 1, : self.rows].astype(F32)
        return total

    def wait_sent(self, chunk):
        self.core_copy(chunk).wait_send()
        for p, part in enumerate(self.parts):
            for mask in (X_BIT, Y_BIT, X_BIT | Y_BIT):
                self.hop(chunk, p, mask).wait_send()
        for step in range(1, self.links.nn):
            self.line_copy(chunk, step).wait_send()


def scatter_kernel(nn, few, many, few_ref, many_ref, small_ref, few_out, many_out, small_out, few_came, many_came, *refs):
    few_slots, many_slots = refs[:6], refs[6:12]
    small_came, small_round, small_line, small_mine, send_sem, recv_sem = refs[12:]
    links = Links(nn, send_sem, recv_sem)
    links.greet()
    sets = []
    base = 0
    for (chunks, rows, columns), grads, came, slots in (
        (few, few_ref, few_came, few_slots),
        (many, many_ref, many_came, many_slots),
    ):
        sets.append(Scatter(links, chunks, rows, columns, grads, came, slots, base))
        base += chunks * SCATTER_COPIES
    links.used = base

    def run(scatter, out):
        chunks = scatter.chunks

        def each(chunk, carry):
            scatter.trade(chunk)
            return carry

        lax.fori_loop(0, chunks, each, 0)

        def step(index, carry):
            for lag, action in enumerate(
                (scatter.fetch, scatter.add_core, scatter.add_corner, scatter.add_square)
            ):
                chunk = index - lag

                @pl.when(jnp.logical_and(chunk >= 0, chunk < chunks))
                def _(chunk=chunk, action=action):
                    action(chunk)

            chunk = index - 4

            @pl.when(chunk >= 0)
            def _(chunk=chunk):
                out[chunk] = scatter.total(chunk)
                scatter.wait_sent(chunk)

            return carry

        lax.fori_loop(0, chunks + 4, step, 0)

    run(sets[0], few_out)
    run(sets[1], many_out)
    scatter_small(links, small_ref, small_out, small_came, small_round, small_line, small_mine)
    links.finish()


def scatter_small(links, grads, out, came, round_in, line_in, mine):
    core = lax.rem(links.w, 2)
    home = links.w // 2
    number = links.fresh()
    links.send(grads.at[:, 1 - core], came, number, links.wide(1))
    links.sent[-1].wait_recv()
    mine[...] = grads[:, core] + came[...]
    masks = (X_BIT, Y_BIT, X_BIT | Y_BIT)
    copies = []
    for index, mask in enumerate(masks):
        number = links.fresh()
        links.send(
            mine.at[jnp.bitwise_xor(links.w, mask) // 2], round_in.at[index], number, links.wide(mask)
        )
        copies.append(links.sent[-1])
    for copy in copies:
        copy.wait()
    del links.sent[-3:]
    mine[home] = mine[home] + round_in[0] + round_in[1] + round_in[2]
    copies = []
    for step in range(1, links.nn):
        number = links.fresh()
        links.send(
            mine.at[home, pl.ds(lax.rem(links.z + step, links.nn) * 8, 8)],
            line_in.at[step - 1],
            number,
            links.along(step),
        )
        copies.append(links.sent[-1])
    total = mine[home, pl.ds(pl.multiple_of(links.z * 8, 8), 8)]
    for step in range(1, links.nn):
        copies[step - 1].wait_recv()
        total = total + line_in[step - 1]
    out[...] = total


def padded(rows):
    return (rows + 15) // 16 * 16


def scatter_slots(squares, nn, rows, columns):
    half = columns // 2
    return [
        pltpu.VMEM((RING, squares, nn * rows, columns), BF),
        pltpu.VMEM((2, squares, nn * rows, columns), BF),
        pltpu.VMEM((RING, 6, nn * rows, half), BF),
        pltpu.VMEM((RING, nn, padded(rows), columns), BF),
        pltpu.VMEM((RING, nn - 1, padded(rows), columns), BF),
        pltpu.SemaphoreType.DMA((2, 2)),
    ]


def scatter_all(nw, nn, few_grads, many_grads, small):
    squares = nw // 2

    def facts(grads):
        return (grads.shape[0], grads.shape[1] // (nw * nn), grads.shape[2])

    few, many = facts(few_grads), facts(many_grads)
    outs = []
    for chunks, rows, columns in (few, many):
        outs.append(jax.ShapeDtypeStruct((chunks, rows, columns), F32))
    outs.append(jax.ShapeDtypeStruct((8, 128), F32))
    for chunks, rows, columns in (few, many):
        outs.append(jax.ShapeDtypeStruct((chunks, squares, nn * rows, columns), BF))
    copies = (few[0] + many[0]) * SCATTER_COPIES + 16
    vmem = pl.BlockSpec(memory_space=pltpu.VMEM)
    hbm = pl.BlockSpec(memory_space=pl.ANY)
    given = [
        grads.reshape(grads.shape[0], squares, 2, -1, grads.shape[2])
        for grads in (few_grads, many_grads)
    ]
    return pl.pallas_call(
        functools.partial(scatter_kernel, nn, few, many),
        out_shape=outs,
        in_specs=[hbm, hbm, vmem],
        out_specs=[vmem, vmem, vmem, hbm, hbm],
        scratch_shapes=scatter_slots(squares, nn, few[1], few[2])
        + scatter_slots(squares, nn, many[1], many[2])
        + [
            pltpu.VMEM((squares, nn * 8, 128), F32),
            pltpu.VMEM((3, nn * 8, 128), F32),
            pltpu.VMEM((nn - 1, 8, 128), F32),
            pltpu.VMEM((squares, nn * 8, 128), F32),
            pltpu.SemaphoreType.DMA((copies,)),
            pltpu.SemaphoreType.DMA((copies,)),
        ],
        compiler_params=pltpu.CompilerParams(
            collective_id=1, has_side_effects=True, vmem_limit_bytes=60 * 2**20
        ),
    )(*given, small.reshape(squares, 2, nn * 8, 128))[:3]

def local_fast(
    nw,
    nn,
    tokens,
    w_query,
    w_key,
    w_value,
    w_output,
    w_gate,
    w_up,
    w_down,
    gain_attn,
    gain_ffn,
    rel_table,
    lay_table,
    ocr_counts,
    rel_bucket,
    lay_bucket,
    cotangent,
):
    small = jnp.concatenate([gain_attn, gain_ffn, rel_table, lay_table]).astype(F32)
    small = jnp.pad(small[None], ((0, 7), (0, 128 - small.shape[0])))
    down = jnp.pad(w_down, ((0, padded(w_down.shape[0]) - w_down.shape[0]), (0, 0)))
    (
        full_small,
        full_query,
        full_key,
        full_value,
        full_output,
        full_gate,
        full_up,
        full_down,
        output,
        normed_attn,
        queries,
        keys_all,
        values_all,
        attended,
        hidden_one,
        normed_ffn,
        mixed,
        probs,
        slope,
        active,
    ) = forward_all(
        nw,
        nn,
        ocr_counts,
        tokens,
        rel_bucket,
        lay_bucket,
        [small, w_query, w_key, w_value, w_output, w_gate, w_up, down],
        w_down.shape[0],
    )
    rows = full_small.reshape(nw * nn, 8, 128)[:, 0]
    each = gain_attn.shape[0]
    full_gain_attn = rows[:, :each].reshape(-1)
    full_gain_ffn = rows[:, each : 2 * each].reshape(-1)
    slot = tokens.shape[0]
    valid = jnp.arange(slot) < ocr_counts[0] + IMG
    buckets = jnp.arange(NB)
    onehot = jnp.concatenate(
        [
            (rel_bucket[:, :, None] == buckets).astype(jnp.bfloat16),
            (lay_bucket[:, :, None] == buckets).astype(jnp.bfloat16),
        ],
        axis=2,
    )
    tokens_f = tokens.astype(F32)
    grad_result = jnp.where(valid[:, None], cotangent.astype(jnp.float32), 0.0)
    grad_low = grad_result.astype(jnp.bfloat16)
    grad_down = contract_rows(mixed, grad_low)
    grad_mixed = contract_cols(grad_low, full_down)
    gate_low = (grad_mixed * slope.astype(F32)).astype(BF)
    up_low = (grad_mixed * active.astype(F32)).astype(BF)
    grad_gate = contract_rows(normed_ffn, gate_low)
    grad_up = contract_rows(normed_ffn, up_low)
    grad_normed_ffn = contract_cols(gate_low, full_gate) + contract_cols(up_low, full_up)
    norm_value, norm_pull = jax.vjp(rms_scale, hidden_one, full_gain_ffn)
    grad_hidden_part, grad_gain_ffn = norm_pull(grad_normed_ffn)
    grad_hidden = grad_result + grad_hidden_part
    branch_low = grad_hidden.astype(jnp.bfloat16)
    grad_output = contract_rows(attended, branch_low)
    grad_attended = contract_cols(branch_low, full_output).astype(jnp.bfloat16)

    def one_group(operands):
        query_group, key_group, value_group, grad_group, probs_low = operands
        part = functools.partial(jnp.einsum, preferred_element_type=F32)
        grad_values = part("hij,ihd->jhd", probs_low, grad_group)
        grad_probs = part("ihd,jhd->hij", grad_group, value_group)
        share = probs_low.astype(F32)
        grad_scores = (
            share * (grad_probs - jnp.sum(share * grad_probs, axis=-1, keepdims=True))
        ).astype(BF)
        return (
            part("hij,jhd->ihd", grad_scores, key_group).astype(BF),
            part("hij,ihd->jhd", grad_scores, query_group).astype(BF),
            grad_values.astype(BF),
            part("hij,ijb->bh", grad_scores, onehot),
        )

    grad_q, grad_k, grad_v, grad_tables = lax.map(
        one_group,
        (
            split_heads(queries),
            split_heads(keys_all),
            split_heads(values_all),
            split_heads(grad_attended),
            probs.reshape(H // HEAD_GROUP, HEAD_GROUP, slot, slot),
        ),
    )
    grad_table_all = jnp.moveaxis(grad_tables, 0, 1).reshape(2 * NB, H)
    grad_queries, grad_keys, grad_values = join_heads(grad_q), join_heads(grad_k), join_heads(grad_v)
    grad_rel = grad_table_all[:NB].reshape(NB * H)
    grad_lay = grad_table_all[NB:].reshape(NB * H)
    grad_query = contract_rows(normed_attn, grad_queries)
    grad_key = contract_rows(normed_attn, grad_keys)
    grad_value = contract_rows(normed_attn, grad_values)
    grad_normed_attn = (
        contract_cols(grad_queries, full_query)
        + contract_cols(grad_keys, full_key)
        + contract_cols(grad_values, full_value)
    )
    input_value, input_pull = jax.vjp(rms_scale, tokens_f, full_gain_attn)
    grad_input_part, grad_gain_attn = input_pull(grad_normed_attn)
    grad_tokens = grad_hidden + grad_input_part
    return (output, grad_tokens) + scatter_fast(
        nw,
        nn,
        grad_query,
        grad_key,
        grad_value,
        grad_output,
        grad_gate,
        grad_up,
        grad_down,
        grad_gain_attn,
        grad_gain_ffn,
        grad_rel,
        grad_lay,
    )


def scatter_fast(
    nw,
    nn,
    grad_query,
    grad_key,
    grad_value,
    grad_output,
    grad_gate,
    grad_up,
    grad_down,
    grad_gain_attn,
    grad_gain_ffn,
    grad_rel,
    grad_lay,
):
    devices = nw * nn

    def columns(grad, width):
        return jnp.moveaxis(
            grad.astype(BF).reshape(grad.shape[0], grad.shape[1] // width, width), 1, 0
        )

    few = columns(grad_down, 256)
    pairs = jnp.concatenate([columns(grad_gate, 256), columns(grad_up, 256)], axis=2)
    many = jnp.concatenate(
        [pairs] + [columns(grad, 512) for grad in (grad_output, grad_query, grad_key, grad_value)]
    )
    parts = [
        part.reshape(devices, -1) for part in (grad_gain_attn, grad_gain_ffn, grad_rel, grad_lay)
    ]
    small = jnp.concatenate(parts, axis=1)
    small = jnp.zeros((devices, 8, 128), F32).at[:, 0, : small.shape[1]].set(small)
    few_sum, many_sum, small_sum = scatter_all(nw, nn, few, many, small)

    def join(stack):
        return jnp.moveaxis(stack, 0, 1).reshape(stack.shape[1], -1)

    tiles = pairs.shape[0]
    owned = []
    for index in range(4):
        at = tiles + 2 * index
        owned.append(join(many_sum[at : at + 2]))
    gate, up = join(many_sum[:tiles, :, :256]), join(many_sum[:tiles, :, 256:])
    at, cuts = 0, []
    for part in parts:
        cuts.append(small_sum[0, at : at + part.shape[1]])
        at += part.shape[1]
    return (owned[1], owned[2], owned[3], owned[0], gate, up, join(few_sum)) + tuple(cuts)


def local(
    tokens,
    w_query,
    w_key,
    w_value,
    w_output,
    w_gate,
    w_up,
    w_down,
    gain_attn,
    gain_ffn,
    rel_table,
    lay_table,
    ocr_counts,
    rel_bucket,
    lay_bucket,
    cotangent,
):
    slot = tokens.shape[0]
    valid = jnp.arange(slot) < ocr_counts[0] + IMG
    buckets = jnp.arange(NB)
    onehot = jnp.concatenate(
        [
            (rel_bucket[:, :, None] == buckets).astype(jnp.bfloat16),
            (lay_bucket[:, :, None] == buckets).astype(jnp.bfloat16),
        ],
        axis=2,
    )
    tokens_f = tokens.astype(jnp.float32)
    weights = gather_weights(
        w_query,
        w_key,
        w_value,
        w_output,
        w_gate,
        w_up,
        w_down,
        gain_attn,
        gain_ffn,
        rel_table,
        lay_table,
    )
    result, saved = forward_pass(tokens_f, weights, onehot, valid)
    output = jnp.where(valid[:, None], result, 0.0).astype(jnp.bfloat16)
    (
        full_query,
        full_key,
        full_value,
        full_output,
        full_gate,
        full_up,
        full_down,
        full_gain_attn,
        full_gain_ffn,
        full_rel,
        full_lay,
    ) = weights
    (
        normed_attn,
        queries,
        keys_all,
        values_all,
        log_totals,
        attended,
        hidden_one,
        normed_ffn,
        gate_act,
        up_proj,
        mixed,
    ) = saved
    grad_result = jnp.where(valid[:, None], cotangent.astype(jnp.float32), 0.0)
    grad_low = grad_result.astype(jnp.bfloat16)
    grad_down = contract_rows(mixed, grad_low)
    grad_mixed = contract_cols(grad_low, full_down)
    gated_value, gated_pull = jax.vjp(gated_product, gate_act, up_proj)
    grad_gate_act, grad_up_proj = gated_pull(grad_mixed)
    gate_low = grad_gate_act.astype(jnp.bfloat16)
    up_low = grad_up_proj.astype(jnp.bfloat16)
    grad_gate = contract_rows(normed_ffn, gate_low)
    grad_up = contract_rows(normed_ffn, up_low)
    grad_normed_ffn = contract_cols(gate_low, full_gate) + contract_cols(up_low, full_up)
    norm_value, norm_pull = jax.vjp(rms_scale, hidden_one, full_gain_ffn.astype(jnp.float32))
    grad_hidden_part, grad_gain_ffn = norm_pull(grad_normed_ffn)
    grad_hidden = grad_result + grad_hidden_part
    branch_low = grad_hidden.astype(jnp.bfloat16)
    grad_output = contract_rows(attended, branch_low)
    grad_attended = contract_cols(branch_low, full_output).astype(jnp.bfloat16)
    grad_queries, grad_keys, grad_values, grad_table_all = attention_backward(
        queries,
        keys_all,
        values_all,
        log_totals,
        grad_attended,
        table_pair(full_rel, full_lay),
        onehot,
        valid,
    )
    grad_rel = grad_table_all[:NB].reshape(NB * H)
    grad_lay = grad_table_all[NB:].reshape(NB * H)
    grad_query = contract_rows(normed_attn, grad_queries)
    grad_key = contract_rows(normed_attn, grad_keys)
    grad_value = contract_rows(normed_attn, grad_values)
    grad_normed_attn = (
        contract_cols(grad_queries, full_query)
        + contract_cols(grad_keys, full_key)
        + contract_cols(grad_values, full_value)
    )
    input_value, input_pull = jax.vjp(rms_scale, tokens_f, full_gain_attn.astype(jnp.float32))
    grad_input_part, grad_gain_attn = input_pull(grad_normed_attn)
    grad_tokens = grad_hidden + grad_input_part
    owned = (
        lax.psum_scatter(grad_query, ("wide", "narrow"), scatter_dimension=0, tiled=True),
        lax.psum_scatter(grad_key, ("wide", "narrow"), scatter_dimension=0, tiled=True),
        lax.psum_scatter(grad_value, ("wide", "narrow"), scatter_dimension=0, tiled=True),
        lax.psum_scatter(grad_output, ("wide", "narrow"), scatter_dimension=0, tiled=True),
        lax.psum_scatter(grad_gate, ("wide", "narrow"), scatter_dimension=0, tiled=True),
        lax.psum_scatter(grad_up, ("wide", "narrow"), scatter_dimension=0, tiled=True),
        lax.psum_scatter(grad_down, ("wide", "narrow"), scatter_dimension=0, tiled=True),
        lax.psum_scatter(grad_gain_attn, ("wide", "narrow"), scatter_dimension=0, tiled=True),
        lax.psum_scatter(grad_gain_ffn, ("wide", "narrow"), scatter_dimension=0, tiled=True),
        lax.psum_scatter(grad_rel, ("wide", "narrow"), scatter_dimension=0, tiled=True),
        lax.psum_scatter(grad_lay, ("wide", "narrow"), scatter_dimension=0, tiled=True),
    )
    return (
        output,
        grad_tokens,
        owned[0],
        owned[1],
        owned[2],
        owned[3],
        owned[4],
        owned[5],
        owned[6],
        owned[7],
        owned[8],
        owned[9],
        owned[10],
    )


def solution(mesh):
    nw, nn = mesh.shape["wide"], mesh.shape["narrow"]

    def body(*args):
        if nw == 8 and nw * nn == NB and args[1].shape[0] % 16 == 0:
            return local_fast(nw, nn, *args)
        return local(*args)

    placed = (
        P(("wide", "narrow"), None),
        P(("wide", "narrow"), None),
        P(("wide", "narrow"), None),
        P(("wide", "narrow"), None),
        P(("wide", "narrow"), None),
        P(("wide", "narrow"), None),
        P(("wide", "narrow"), None),
        P(("wide", "narrow"), None),
        P(("wide", "narrow")),
        P(("wide", "narrow")),
        P(("wide", "narrow")),
        P(("wide", "narrow")),
        P(("wide", "narrow")),
        P(("wide", "narrow"), None),
        P(("wide", "narrow"), None),
        P(("wide", "narrow"), None),
    )
    return jax.shard_map(
        body,
        mesh=mesh,
        in_specs=placed,
        out_specs=(
            P(("wide", "narrow"), None),
            P(("wide", "narrow"), None),
            P(("wide", "narrow"), None),
            P(("wide", "narrow"), None),
            P(("wide", "narrow"), None),
            P(("wide", "narrow"), None),
            P(("wide", "narrow"), None),
            P(("wide", "narrow"), None),
            P(("wide", "narrow"), None),
            P(("wide", "narrow")),
            P(("wide", "narrow")),
            P(("wide", "narrow")),
            P(("wide", "narrow")),
        ),
        check_vma=False,
    )
```

```python
import functools

import jax
import jax.numpy as jnp
from jax import lax
from jax.experimental import pallas as pl
from jax.experimental.pallas import tpu as pltpu
from jax.sharding import PartitionSpec as P

H = 16
HD = 64
NB = 32
IMG = 196
RING = 6
SCATTER_COPIES = 10
LAGS = 4
FFN_LAG = 8
BACK_QB = 16
TILE = 256
QB = 8
GELU_SCALE = 0.7978845608028654
GELU_CUBE = 0.044715


RMS_EPSILON = 1e-06
MASK_SCORE = -1000000000.0
HEAD_GROUP = 4


def rms_scale(values, gain):
    return (
        values * lax.rsqrt(jnp.mean(values * values, axis=-1, keepdims=True) + RMS_EPSILON) * gain
    )


def gated_product(gate_act, up_proj):
    return jax.nn.gelu(gate_act, approximate=True) * up_proj


def product(left, right):
    return jnp.dot(left, right, preferred_element_type=jnp.float32)


def contract_rows(left, right):
    return lax.dot_general(
        left, right, (((0,), (0,)), ((), ())), preferred_element_type=jnp.float32
    )


def contract_cols(left, right):
    return lax.dot_general(
        left, right, (((1,), (1,)), ((), ())), preferred_element_type=jnp.float32
    )


def split_heads(matrix):
    return jnp.moveaxis(matrix.reshape(matrix.shape[0], H // HEAD_GROUP, HEAD_GROUP, HD), 1, 0)


def join_heads(stacked):
    return jnp.moveaxis(stacked, 0, 1).reshape(stacked.shape[1], H * HD)


def group_tables(table_all):
    return jnp.moveaxis(table_all.reshape(2 * NB, H // HEAD_GROUP, HEAD_GROUP), 1, 0)


def group_scores(query_group, key_group, table_group, onehot, valid):
    scores = jnp.einsum("ihd,jhd->hij", query_group, key_group, preferred_element_type=jnp.float32)
    scores = scores + jnp.einsum(
        "ijb,bh->hij", onehot, table_group, preferred_element_type=jnp.float32
    )
    return jnp.where(valid[None, None, :], scores, MASK_SCORE)


def gather_weights(
    w_query,
    w_key,
    w_value,
    w_output,
    w_gate,
    w_up,
    w_down,
    gain_attn,
    gain_ffn,
    rel_table,
    lay_table,
):
    return (
        lax.all_gather(w_query, ("wide", "narrow"), axis=0, tiled=True),
        lax.all_gather(w_key, ("wide", "narrow"), axis=0, tiled=True),
        lax.all_gather(w_value, ("wide", "narrow"), axis=0, tiled=True),
        lax.all_gather(w_output, ("wide", "narrow"), axis=0, tiled=True),
        lax.all_gather(w_gate, ("wide", "narrow"), axis=0, tiled=True),
        lax.all_gather(w_up, ("wide", "narrow"), axis=0, tiled=True),
        lax.all_gather(w_down, ("wide", "narrow"), axis=0, tiled=True),
        lax.all_gather(gain_attn, ("wide", "narrow"), axis=0, tiled=True),
        lax.all_gather(gain_ffn, ("wide", "narrow"), axis=0, tiled=True),
        lax.all_gather(rel_table, ("wide", "narrow"), axis=0, tiled=True),
        lax.all_gather(lay_table, ("wide", "narrow"), axis=0, tiled=True),
    )


def table_pair(full_rel, full_lay):
    return jnp.concatenate([full_rel.reshape(NB, H), full_lay.reshape(NB, H)], axis=0)


def forward_pass(tokens_f, weights, onehot, valid):
    (
        full_query,
        full_key,
        full_value,
        full_output,
        full_gate,
        full_up,
        full_down,
        full_gain_attn,
        full_gain_ffn,
        full_rel,
        full_lay,
    ) = weights
    normed_attn = rms_scale(tokens_f, full_gain_attn.astype(jnp.float32)).astype(jnp.bfloat16)
    queries = product(normed_attn, full_query).astype(jnp.bfloat16)
    keys_all = product(normed_attn, full_key).astype(jnp.bfloat16)
    values_all = product(normed_attn, full_value).astype(jnp.bfloat16)

    def forward_one_group(operands):
        query_group, key_group, value_group, table_group = operands
        scores = group_scores(query_group, key_group, table_group, onehot, valid)
        peak = jnp.max(scores, axis=-1, keepdims=True)
        expo = jnp.exp(scores - peak)
        total = jnp.sum(expo, axis=-1, keepdims=True)
        probs_low = (expo / total).astype(jnp.bfloat16)
        attended_group = jnp.einsum(
            "hij,jhd->ihd", probs_low, value_group, preferred_element_type=jnp.float32
        )
        return (attended_group.astype(jnp.bfloat16), (peak + jnp.log(total))[..., 0])

    stacked, log_totals = lax.map(
        forward_one_group,
        (
            split_heads(queries),
            split_heads(keys_all),
            split_heads(values_all),
            group_tables(table_pair(full_rel, full_lay)),
        ),
    )
    attended = join_heads(stacked)
    hidden_one = tokens_f + product(attended, full_output)
    normed_ffn = rms_scale(hidden_one, full_gain_ffn.astype(jnp.float32)).astype(jnp.bfloat16)
    gate_act = product(normed_ffn, full_gate)
    up_proj = product(normed_ffn, full_up)
    mixed = gated_product(gate_act, up_proj).astype(jnp.bfloat16)
    result = hidden_one + product(mixed, full_down)
    return (
        result,
        (
            normed_attn,
            queries,
            keys_all,
            values_all,
            log_totals,
            attended,
            hidden_one,
            normed_ffn,
            gate_act,
            up_proj,
            mixed,
        ),
    )


def attention_backward(
    queries, keys_all, values_all, log_totals, grad_attended, table_all, onehot, valid
):

    def attention_one_group(operands):
        query_group, key_group, value_group, table_group, lse_group, grad_group = operands
        scores = group_scores(query_group, key_group, table_group, onehot, valid)
        probs = jnp.exp(scores - lse_group[..., None])
        probs_low = probs.astype(jnp.bfloat16)
        grad_values = jnp.einsum(
            "hij,ihd->jhd", probs_low, grad_group, preferred_element_type=jnp.float32
        )
        grad_probs = jnp.einsum(
            "ihd,jhd->hij", grad_group, value_group, preferred_element_type=jnp.float32
        )
        grad_scores = (
            probs * (grad_probs - jnp.sum(probs * grad_probs, axis=-1, keepdims=True))
        ).astype(jnp.bfloat16)
        grad_queries = jnp.einsum(
            "hij,jhd->ihd", grad_scores, key_group, preferred_element_type=jnp.float32
        )
        grad_keys = jnp.einsum(
            "hij,ihd->jhd", grad_scores, query_group, preferred_element_type=jnp.float32
        )
        grad_table = jnp.einsum(
            "hij,ijb->bh", grad_scores, onehot, preferred_element_type=jnp.float32
        )
        return (
            grad_queries.astype(jnp.bfloat16),
            grad_keys.astype(jnp.bfloat16),
            grad_values.astype(jnp.bfloat16),
            grad_table,
        )

    grad_q_all, grad_k_all, grad_v_all, grad_tables = lax.map(
        attention_one_group,
        (
            split_heads(queries),
            split_heads(keys_all),
            split_heads(values_all),
            group_tables(table_all),
            log_totals,
            split_heads(grad_attended),
        ),
    )
    grad_table_all = jnp.moveaxis(grad_tables, 0, 1).reshape(2 * NB, H)
    return (join_heads(grad_q_all), join_heads(grad_k_all), join_heads(grad_v_all), grad_table_all)


MESH_ID = pl.DeviceIdType.MESH
BF = jnp.bfloat16
F32 = jnp.float32
X_BIT = 2
Y_BIT = 4
PARTS = ((X_BIT, Y_BIT), (Y_BIT, X_BIT))


class Links:
    def __init__(self, nn, send_sem, recv_sem):
        self.nn = nn
        self.w = lax.axis_index("wide")
        self.z = lax.axis_index("narrow")
        self.send_sem = send_sem
        self.recv_sem = recv_sem
        self.used = 0
        self.sent = []

    def fresh(self):
        self.used += 1
        return self.used - 1

    def wide(self, bit):
        return (jnp.bitwise_xor(self.w, bit), self.z)

    def along(self, step):
        return (self.w, lax.rem(self.z + step, self.nn))

    def copy(self, src, dst, number, device):
        return pltpu.make_async_remote_copy(
            src_ref=src,
            dst_ref=dst,
            send_sem=self.send_sem.at[number],
            recv_sem=self.recv_sem.at[number],
            device_id=device,
            device_id_type=MESH_ID,
        )

    def send(self, src, dst, number, device):
        copy = self.copy(src, dst, number, device)
        copy.start()
        self.sent.append(copy)

    def greet(self):
        barrier = pltpu.get_barrier_semaphore()
        others = [self.wide(bit) for bit in (1, X_BIT, Y_BIT)]
        others += [self.along(step) for step in range(1, self.nn)]
        for other in others:
            pl.semaphore_signal(barrier, inc=1, device_id=other, device_id_type=MESH_ID)
        pl.semaphore_wait(barrier, len(others))

    def finish(self):
        for copy in self.sent:
            copy.wait_send()


class Gather:
    def __init__(self, links, shard, full, rows, parts, local_sem, line=None, merged=None):
        self.links, self.shard, self.full, self.rows, self.parts = links, shard, full, rows, parts
        self.local_sem, self.line, self.merged = local_sem, line, merged
        nn = links.nn
        self.block = rows * nn
        self.line_ids = [links.fresh() for _ in range(1, nn)]
        self.part_ids = {
            (p, mask): links.fresh()
            for p in range(len(parts))
            for mask in (X_BIT, Y_BIT, X_BIT | Y_BIT)
        }
        self.core_ids = {mask: links.fresh() for mask in (0, X_BIT, Y_BIT, X_BIT | Y_BIT)}

    def place(self, w, z):
        if self.line is not None:
            return self.line.at[z]
        return self.full.at[pl.ds((w * self.links.nn + z) * self.rows, self.rows)]

    def span(self, mask, part=None):
        rows = pl.ds(jnp.bitwise_xor(self.links.w, mask) * self.block, self.block)
        if part is None:
            return self.full.at[rows]
        low, size = self.parts[part][:2]
        return self.full.at[rows, pl.ds(low, size)]

    def own(self):
        return pltpu.make_async_copy(
            self.shard, self.place(self.links.w, self.links.z), self.local_sem
        )

    def start(self):
        k = self.links
        self.own().start()
        for step in range(1, k.nn):
            k.send(self.shard, self.place(k.w, k.z), self.line_ids[step - 1], k.along(step))

    def spread(self):
        k = self.links
        self.own().wait()
        for step in range(1, k.nn):
            came = lax.rem(k.z - step + k.nn, k.nn)
            k.copy(
                self.shard, self.place(k.w, came), self.line_ids[step - 1], k.along(step)
            ).wait_recv()
        if self.line is not None:
            whole = jnp.concatenate(
                [self.line[z, : self.rows].astype(F32) for z in range(k.nn)], axis=0
            )
            self.merged[...] = whole.astype(BF)
            move = pltpu.make_async_copy(self.merged, self.span(0), self.local_sem)
            move.start()
            move.wait()
        for p, part in enumerate(self.parts):
            for bit in part[2]:
                k.send(self.span(0, p), self.span(0, p), self.part_ids[p, bit], k.wide(bit))
        k.send(self.span(0), self.span(0), self.core_ids[0], k.wide(1))

    def arrive(self, p, mask):
        k = self.links
        k.copy(
            self.span(mask, p), self.span(mask, p), self.part_ids[p, mask], k.wide(X_BIT)
        ).wait_recv()

    def forward(self):
        k = self.links
        for p, part in enumerate(self.parts):
            first, second = part[2]
            self.arrive(p, first)
            both = first | second
            k.send(self.span(first, p), self.span(first, p), self.part_ids[p, both], k.wide(second))
        for p, part in enumerate(self.parts):
            self.arrive(p, part[2][1])
        for mask in (X_BIT, Y_BIT):
            k.send(self.span(mask), self.span(mask), self.core_ids[mask], k.wide(1))

    def last(self):
        k = self.links
        both = X_BIT | Y_BIT
        for p in range(len(self.parts)):
            self.arrive(p, both)
        k.send(self.span(both), self.span(both), self.core_ids[both], k.wide(1))

    def done(self):
        k = self.links
        for mask, number in self.core_ids.items():
            place = self.span(mask | 1)
            k.copy(place, place, number, k.wide(1)).wait_recv()


def halves(columns):
    low = columns // 256 * 128
    return ((0, low, PARTS[0]), (low, columns - low, PARTS[1]))


def dot(left, right):
    return jnp.dot(left, right, preferred_element_type=F32)


def dot_nt(left, right):
    return lax.dot_general(left, right, (((1,), (1,)), ((), ())), preferred_element_type=F32)


def dot_tn(left, right):
    return lax.dot_general(left, right, (((0,), (0,)), ((), ())), preferred_element_type=F32)


def iota(shape, dimension):
    return lax.broadcasted_iota(jnp.int32, shape, dimension)


def ones_where(mask):
    return jnp.where(mask, 1.0, 0.0).astype(BF)


def unpack_row(rows, first, each, total):
    devices = rows.shape[0]
    pick = ones_where(iota((128, total), 0) == first + lax.rem(iota((128, total), 1), each))
    spread = dot(rows.astype(BF), pick)
    mine = iota((devices, total), 1) // each == iota((devices, total), 0)
    return jnp.sum(jnp.where(mine, spread, 0.0), axis=0, keepdims=True)


def table_block(rows, first):
    pick_shape = (H * QB, 128)
    total = None
    for index in range(2):
        lane = first + H * index + iota(pick_shape, 0) // QB
        pick = ones_where(iota(pick_shape, 1) == lane)
        table = dot_nt(pick, rows.astype(BF)).astype(BF)
        wide = (NB, QB * 2 * NB)
        spread = dot(table, ones_where(lax.rem(iota(wide, 1), 2 * NB) == iota(wide, 0) + NB * index))
        total = spread if total is None else total + spread
    shape = (H * QB, QB * 2 * NB)
    mine = lax.rem(iota(shape, 0), QB) == iota(shape, 1) // (2 * NB)
    return jnp.where(mine, total, 0.0).astype(BF)


def bucket_ones(rel, lay, onehot, block):
    width = rel.shape[1]
    rows = iota((NB, width), 0)
    for query in range(QB):
        for index, bucket in enumerate((rel, lay)):
            row = bucket[pl.ds(block * QB + query, 1), :]
            low = (query * 2 + index) * NB
            onehot[low : low + NB, :] = ones_where(jnp.broadcast_to(row, (NB, width)) == rows)


def forward_kernel(nn, shapes, *refs):
    count = len(shapes)
    occupied, tokens, rel_hbm, lay_hbm = refs[:4]
    shards = refs[4 : 4 + count]
    refs = refs[4 + count :]
    fulls, refs = refs[:count], refs[count:]
    saved, refs = refs[:10], refs[10:]
    (out_h, na_t, q_t, k_h, v_h, att_t, hid_h, nf_t, mix_t, probs_h) = saved
    (slope_h, act_h), refs = refs[:2], refs[2:]
    (
        line,
        merged,
        x,
        rel,
        lay,
        small,
        lhs,
        onehot,
        bias,
        na,
        q,
        k,
        v,
        att,
        hid,
        nf,
        mix,
        slope,
        act,
        probs,
        w_one,
        w_wide,
        w_down,
        gains,
        turned,
        mixed_t,
        send_sem,
        recv_sem,
        gather_sem,
        local_sem,
        ring_sem,
    ) = refs
    slots, width = x.shape
    links = Links(nn, send_sem, recv_sem)
    numbers = iter(range(64))

    def move(src, dst):
        copy = pltpu.make_async_copy(src, dst, local_sem.at[next(numbers)])
        copy.start()
        return copy

    arriving = [move(tokens, x), move(rel_hbm, rel), move(lay_hbm, lay)]
    links.greet()
    g = []
    for index, (rows, columns) in enumerate(shapes):
        odd = rows % 16 != 0 and columns > 128
        g.append(
            Gather(
                links,
                shards[index],
                fulls[index],
                rows,
                halves(columns) if columns > 128 else ((0, columns, PARTS[0]),),
                gather_sem.at[index],
                line if odd else None,
                merged if odd else None,
            )
        )
    SMALL, Q, K, V, O, GATE, UP, DOWN = range(8)
    g[SMALL].start()
    g[Q].start()
    g[K].start()
    g[SMALL].spread()
    g[SMALL].forward()
    g[SMALL].last()
    g[SMALL].done()
    small_in = move(fulls[SMALL], small)
    g[Q].spread()
    g[V].start()
    leaving = []
    turning = {}

    def turn_out(slot, source, target):
        if slot in turning:
            turning[slot].wait()

        def one(tile, carry):
            at = pl.ds(pl.multiple_of(tile * TILE, TILE), TILE)
            turned[slot, at, :] = source[:, at].T
            return carry

        lax.fori_loop(0, width // TILE, one, 0)
        turning[slot] = move(turned.at[slot], target)

    for copy in arriving:
        copy.wait()
    small_in.wait()
    rows = small.reshape(small.shape[0] // 8, 8, 128)[:, 0, :]
    each = width // rows.shape[0]
    gains[0:1, :] = unpack_row(rows, 0, each, width)
    gains[1:2, :] = unpack_row(rows, each, each, width)
    lhs[...] = table_block(rows, 2 * each)

    def normalise(index, carry):
        at = pl.ds(pl.multiple_of(index * 64, 64), 64)
        values = x[at, :].astype(F32)
        scale = lax.rsqrt(jnp.mean(values * values, axis=-1, keepdims=True) + RMS_EPSILON)
        na[at, :] = (values * scale * gains[0:1, :]).astype(BF)
        return carry

    lax.fori_loop(0, slots // 64, normalise, 0)
    turn_out(0, na, na_t)
    valid = iota((1, slots), 1) < occupied[0] + IMG

    def bias_block(block, carry):
        bucket_ones(rel, lay, onehot, block)
        found = jnp.where(valid, dot(lhs[...], onehot[...]), MASK_SCORE)
        bias[:, pl.ds(pl.multiple_of(block * QB, QB), QB), :] = found.reshape(H, QB, slots)
        return carry

    blocks = slots // QB
    lax.fori_loop(0, blocks // 4, bias_block, 0)
    g[K].spread()
    g[O].start()
    g[Q].forward()
    lax.fori_loop(blocks // 4, blocks // 2, bias_block, 0)
    g[V].spread()
    g[GATE].start()
    g[K].forward()
    g[Q].last()
    lax.fori_loop(blocks // 2, 3 * blocks // 4, bias_block, 0)
    g[O].spread()
    g[V].forward()
    g[K].last()
    g[Q].done()
    fetch = move(fulls[Q], w_one.at[0])
    lax.fori_loop(3 * blocks // 4, blocks, bias_block, 0)
    fetch.wait()

    def project(slot, target):
        def one(tile, carry):
            at = pl.ds(pl.multiple_of(tile * TILE, TILE), TILE)
            target[:, at] = dot(na[...], w_one[slot, :, at]).astype(BF)
            return carry

        lax.fori_loop(0, width // TILE, one, 0)

    project(0, q)
    turn_out(1, q, q_t)
    g[GATE].spread()
    g[UP].start()
    g[O].forward()
    g[V].last()
    g[K].done()
    fetch = move(fulls[K], w_one.at[1])
    fetch.wait()
    project(1, k)
    leaving.append(move(k, k_h))
    g[O].last()
    g[V].done()
    fetch = move(fulls[V], w_one.at[0])
    fetch.wait()
    project(0, v)
    leaving.append(move(v, v_h))

    def probs_out(pair):
        turn = lax.rem(pair, 2)
        return pltpu.make_async_copy(probs.at[turn], probs_h.at[pl.ds(pair * 2, 2)], ring_sem.at[turn])

    def attend(pair, carry):
        @pl.when(pair >= 2)
        def _():
            probs_out(pair - 2).wait()

        at = pl.ds(pl.multiple_of(pair * 128, 128), 128)
        low = iota((slots, 128), 1) < HD
        queries = q[:, at]
        keys = k[:, at]
        found = []
        for side in range(2):
            mine = jnp.where(low if side == 0 else jnp.logical_not(low), queries, 0)
            scores = dot_nt(mine, keys) + bias[pair * 2 + side]
            peak = jnp.max(scores, axis=-1, keepdims=True)
            expo = jnp.exp(scores - peak)
            total = jnp.sum(expo, axis=-1, keepdims=True)
            share = (expo * (1.0 / total)).astype(BF)
            probs[lax.rem(pair, 2), side] = share
            found.append(dot(share, v[:, at]))
        att[:, at] = jnp.where(low, found[0], found[1]).astype(BF)
        probs_out(pair).start()
        return carry

    pairs = H // 2
    lax.fori_loop(0, 2, attend, 0)
    g[UP].spread()
    g[DOWN].start()
    g[GATE].forward()
    g[O].done()
    fetch_o = move(fulls[O], w_one.at[1])
    lax.fori_loop(2, 5, attend, 0)
    g[GATE].last()
    lax.fori_loop(5, pairs, attend, 0)
    turn_out(0, att, att_t)
    g[DOWN].spread()
    g[UP].forward()
    g[GATE].done()
    fetch_gate = move(fulls[GATE], w_wide.at[0])
    fetch_o.wait()

    def output_tile(tile, carry):
        at = pl.ds(pl.multiple_of(tile * TILE, TILE), TILE)
        hid[:, at] = x[:, at].astype(F32) + dot(att[...], w_one[1, :, at])
        return carry

    lax.fori_loop(0, width // TILE, output_tile, 0)
    leaving.append(move(hid, hid_h))

    def normalise_two(index, carry):
        at = pl.ds(pl.multiple_of(index * 64, 64), 64)
        values = hid[at, :]
        scale = lax.rsqrt(jnp.mean(values * values, axis=-1, keepdims=True) + RMS_EPSILON)
        nf[at, :] = (values * scale * gains[1:2, :]).astype(BF)
        return carry

    lax.fori_loop(0, slots // 64, normalise_two, 0)
    turn_out(1, nf, nf_t)
    g[UP].last()
    g[DOWN].forward()
    g[UP].done()
    fetch_up = move(fulls[UP], w_wide.at[1])
    fetch_gate.wait()
    fetch_up.wait()

    def ffn_out(tile):
        turn = lax.rem(tile, 2)
        at = pl.ds(pl.multiple_of(tile * TILE, TILE), TILE)
        return (
            pltpu.make_async_copy(slope.at[turn], slope_h.at[:, at], ring_sem.at[2 + turn]),
            pltpu.make_async_copy(act.at[turn], act_h.at[:, at], ring_sem.at[4 + turn]),
            pltpu.make_async_copy(mixed_t.at[turn], mix_t.at[at], ring_sem.at[6 + turn]),
        )

    def ffn_tile(tile, carry):
        @pl.when(tile >= 2)
        def _():
            for copy in ffn_out(tile - 2):
                copy.wait()

        at = pl.ds(pl.multiple_of(tile * TILE, TILE), TILE)
        turn = lax.rem(tile, 2)
        gate = dot(nf[...], w_wide[0, :, at])
        up = dot(nf[...], w_wide[1, :, at])
        square = gate * gate
        inner = GELU_SCALE * gate * (1.0 + GELU_CUBE * square)
        bend = jnp.tanh(inner)
        half = 0.5 * (1.0 + bend)
        active = gate * half
        rise = half + 0.5 * gate * (1.0 - bend * bend) * GELU_SCALE * (1.0 + 3.0 * GELU_CUBE * square)
        mixed = (active * up).astype(BF)
        mix[:, at] = mixed
        mixed_t[turn] = mixed.T
        act[turn] = active.astype(BF)
        slope[turn] = (up * rise).astype(BF)
        for copy in ffn_out(tile):
            copy.start()
        return carry

    tiles = mix.shape[1] // TILE
    lax.fori_loop(0, tiles // 2, ffn_tile, 0)
    g[DOWN].last()
    lax.fori_loop(tiles // 2, tiles, ffn_tile, 0)
    g[DOWN].done()
    move(fulls[DOWN], w_down).wait()
    valid_rows = iota((slots, 1), 0) < occupied[0] + IMG

    def down_tile(tile, carry):
        at = pl.ds(pl.multiple_of(tile * TILE, TILE), TILE)
        result = hid[:, at] + dot(mix[...], w_down[:, at])
        na[:, at] = jnp.where(valid_rows, result, 0.0).astype(BF)
        return carry

    lax.fori_loop(0, width // TILE, down_tile, 0)
    move(na, out_h).wait()
    for copy in leaving + list(turning.values()):
        copy.wait()
    for pair in (pairs - 2, pairs - 1):
        probs_out(pair).wait()
    for tile in (tiles - 2, tiles - 1):
        for copy in ffn_out(tile):
            copy.wait()
    links.finish()


def forward_all(nw, nn, counts, tokens, rel, lay, shards, odd_rows):
    devices = nw * nn
    shapes = []
    for index, shard in enumerate(shards):
        rows = odd_rows if index == len(shards) - 1 else shard.shape[0]
        shapes.append((rows, shard.shape[1]))
    copies = len(shards) * (nn - 1 + 6 + 4)
    slots, width = tokens.shape
    ffn = shapes[5][1]
    low = jax.ShapeDtypeStruct((slots, width), BF)
    wide = jax.ShapeDtypeStruct((slots, ffn), BF)
    full = jax.ShapeDtypeStruct((slots, width), F32)
    out_shape = [
        jax.ShapeDtypeStruct((rows * devices, columns), shard.dtype)
        for (rows, columns), shard in zip(shapes, shards)
    ]
    low_t = jax.ShapeDtypeStruct((width, slots), BF)
    wide_t = jax.ShapeDtypeStruct((ffn, slots), BF)
    out_shape += [low, low_t, low_t, low, low, low_t, full, low_t, wide_t]
    out_shape += [jax.ShapeDtypeStruct((H, slots, slots), BF), wide, wide]
    hbm = pl.BlockSpec(memory_space=pl.ANY)
    page = pltpu.VMEM((slots, width), BF)
    return pl.pallas_call(
        functools.partial(forward_kernel, nn, shapes),
        out_shape=out_shape,
        in_specs=[pl.BlockSpec(memory_space=pltpu.SMEM)] + [hbm] * (3 + len(shards)),
        out_specs=[hbm] * len(out_shape),
        scratch_shapes=[
            pltpu.VMEM((nn,) + shards[-1].shape, BF),
            pltpu.VMEM((nn * odd_rows, shards[-1].shape[1]), BF),
            page,
            pltpu.VMEM((slots, slots), jnp.int32),
            pltpu.VMEM((slots, slots), jnp.int32),
            pltpu.VMEM((devices * 8, 128), F32),
            pltpu.VMEM((H * QB, QB * 2 * NB), BF),
            pltpu.VMEM((QB * 2 * NB, slots), BF),
            pltpu.VMEM((H, slots, slots), F32),
            page,
            page,
            page,
            page,
            page,
            pltpu.VMEM((slots, width), F32),
            page,
            pltpu.VMEM((slots, ffn), BF),
            pltpu.VMEM((2, slots, TILE), BF),
            pltpu.VMEM((2, slots, TILE), BF),
            pltpu.VMEM((2, 2, slots, slots), BF),
            pltpu.VMEM((2, width, width), BF),
            pltpu.VMEM((2, width, ffn), BF),
            pltpu.VMEM((ffn, width), BF),
            pltpu.VMEM((8, width), F32),
            pltpu.VMEM((2, width, slots), BF),
            pltpu.VMEM((2, TILE, slots), BF),
            pltpu.SemaphoreType.DMA((copies,)),
            pltpu.SemaphoreType.DMA((copies,)),
            pltpu.SemaphoreType.DMA((len(shards),)),
            pltpu.SemaphoreType.DMA((64,)),
            pltpu.SemaphoreType.DMA((8,)),
        ],
        compiler_params=pltpu.CompilerParams(
            collective_id=0, has_side_effects=True, vmem_limit_bytes=63 * 2**20
        ),
    )(counts, tokens, rel, lay, *shards)


class Scatter:
    def __init__(self, links, chunks, rows, columns, grads, came, slots, base):
        self.links, self.chunks, self.rows, self.columns = links, chunks, rows, columns
        self.grads, self.came = grads, came
        (self.held, self.other, self.round, self.out_line, self.in_line, self.load_sem) = slots
        self.base = base
        self.block = rows * links.nn
        self.parts = halves(columns)
        self.core = lax.rem(links.w, 2)
        self.ring = self.held.shape[0]

    def number(self, chunk, kind):
        return self.base + chunk * SCATTER_COPIES + kind

    def core_copy(self, chunk):
        return self.links.copy(
            self.grads.at[chunk, :, 1 - self.core],
            self.came.at[chunk],
            self.number(chunk, 0),
            self.links.wide(1),
        )

    def trade(self, chunk):
        self.core_copy(chunk).start()

    def loads(self, chunk):
        slot, turn = lax.rem(chunk, self.ring), lax.rem(chunk, 2)
        return (
            pltpu.make_async_copy(
                self.grads.at[chunk, :, self.core], self.held.at[slot], self.load_sem.at[turn, 0]
            ),
            pltpu.make_async_copy(
                self.came.at[chunk], self.other.at[turn], self.load_sem.at[turn, 1]
            ),
        )

    def fetch(self, chunk):
        self.core_copy(chunk).wait_recv()
        for load in self.loads(chunk):
            load.start()

    def square(self, mask):
        return jnp.bitwise_xor(self.links.w, mask) // 2

    def hop(self, chunk, p, mask):
        slot = lax.rem(chunk, self.ring)
        low, size, order = self.parts[p]
        bit = order[1] if mask & order[1] else order[0]
        kind = 1 + p * 3 + (X_BIT, Y_BIT, X_BIT | Y_BIT).index(mask)
        return self.links.copy(
            self.held.at[slot, self.square(mask), :, pl.ds(low, size)],
            self.round.at[slot, kind - 1, :, pl.ds(0, size)],
            self.number(chunk, kind),
            self.links.wide(bit),
        )

    def landed(self, chunk, p, mask):
        return self.round.at[
            lax.rem(chunk, self.ring), p * 3 + (X_BIT, Y_BIT, X_BIT | Y_BIT).index(mask)
        ]

    def add_core(self, chunk):
        for load in self.loads(chunk):
            load.wait()
        slot, turn = lax.rem(chunk, self.ring), lax.rem(chunk, 2)

        def one(square, carry):
            self.held[slot, square] = (
                self.held[slot, square].astype(F32) + self.other[turn, square].astype(F32)
            ).astype(BF)
            return carry

        lax.fori_loop(0, self.held.shape[1], one, 0)
        for p, part in enumerate(self.parts):
            self.hop(chunk, p, X_BIT | Y_BIT).start()
        for p, part in enumerate(self.parts):
            self.hop(chunk, p, part[2][1]).start()

    def add_corner(self, chunk):
        slot = lax.rem(chunk, self.ring)
        for p, (low, size, order) in enumerate(self.parts):
            self.hop(chunk, p, X_BIT | Y_BIT).wait_recv()
            square = self.square(order[0])
            came = self.landed(chunk, p, X_BIT | Y_BIT)
            self.held[slot, square, :, low : low + size] = (
                self.held[slot, square, :, low : low + size].astype(F32)
                + came[:, :size].astype(F32)
            ).astype(BF)
        for p, part in enumerate(self.parts):
            self.hop(chunk, p, part[2][0]).start()

    def line_copy(self, chunk, step):
        k = self.links
        slot = lax.rem(chunk, self.ring)
        return k.copy(
            self.out_line.at[slot, lax.rem(k.z + step, k.nn)],
            self.in_line.at[slot, step - 1],
            self.number(chunk, 6 + step),
            k.along(step),
        )

    def add_square(self, chunk):
        slot = lax.rem(chunk, self.ring)
        home = self.square(0)
        for p, (low, size, order) in enumerate(self.parts):
            total = self.held[slot, home, :, low : low + size].astype(F32)
            for mask in order:
                self.hop(chunk, p, mask).wait_recv()
                total = total + self.landed(chunk, p, mask)[:, :size].astype(F32)
            for z in range(self.links.nn):
                self.out_line[slot, z, : self.rows, low : low + size] = total[
                    z * self.rows : (z + 1) * self.rows
                ].astype(BF)
        for step in range(1, self.links.nn):
            self.line_copy(chunk, step).start()

    def total(self, chunk):
        slot = lax.rem(chunk, self.ring)
        total = self.out_line[slot, self.links.z, : self.rows].astype(F32)
        for step in range(1, self.links.nn):
            self.line_copy(chunk, step).wait_recv()
            total = total + self.in_line[slot, step - 1, : self.rows].astype(F32)
        return total

    def pump(self, index, out, made=None):
        index = jnp.int32(index)
        made = self.chunks if made is None else made
        idle = index >= made if made < self.chunks else False
        for lag, action in enumerate((self.fetch, self.add_core, self.add_corner, self.add_square, self.finish)):
            chunk = index - lag
            ready = jnp.logical_and(chunk >= 0, chunk < self.chunks)
            if made < self.chunks:
                ready = jnp.logical_and(ready, jnp.logical_not(idle))

            @pl.when(ready)
            def _(chunk=chunk, action=action):
                action(chunk, out) if action == self.finish else action(chunk)

    def finish(self, chunk, out):
        out[chunk] = self.total(chunk)
        self.wait_sent(chunk)

    def wait_sent(self, chunk):
        self.core_copy(chunk).wait_send()
        for p, part in enumerate(self.parts):
            for mask in (X_BIT, Y_BIT, X_BIT | Y_BIT):
                self.hop(chunk, p, mask).wait_send()
        for step in range(1, self.links.nn):
            self.line_copy(chunk, step).wait_send()


def scatter_small(links, grads, out, came, round_in, line_in, mine):
    core = lax.rem(links.w, 2)
    home = links.w // 2
    number = links.fresh()
    links.send(grads.at[:, 1 - core], came, number, links.wide(1))
    links.sent[-1].wait_recv()
    mine[...] = grads[:, core] + came[...]
    masks = (X_BIT, Y_BIT, X_BIT | Y_BIT)
    copies = []
    for index, mask in enumerate(masks):
        number = links.fresh()
        links.send(
            mine.at[jnp.bitwise_xor(links.w, mask) // 2], round_in.at[index], number, links.wide(mask)
        )
        copies.append(links.sent[-1])
    for copy in copies:
        copy.wait()
    del links.sent[-3:]
    mine[home] = mine[home] + round_in[0] + round_in[1] + round_in[2]
    copies = []
    for step in range(1, links.nn):
        number = links.fresh()
        links.send(
            mine.at[home, pl.ds(lax.rem(links.z + step, links.nn) * 8, 8)],
            line_in.at[step - 1],
            number,
            links.along(step),
        )
        copies.append(links.sent[-1])
    total = mine[home, pl.ds(pl.multiple_of(links.z * 8, 8), 8)]
    for step in range(1, links.nn):
        copies[step - 1].wait_recv()
        total = total + line_in[step - 1]
    out[...] = total


def padded(rows):
    return (rows + 15) // 16 * 16


def scatter_slots(squares, nn, rows, columns, ring):
    half = columns // 2
    return [
        pltpu.VMEM((ring, squares, nn * rows, columns), BF),
        pltpu.VMEM((2, squares, nn * rows, columns), BF),
        pltpu.VMEM((ring, 6, nn * rows, half), BF),
        pltpu.VMEM((ring, nn, padded(rows), columns), BF),
        pltpu.VMEM((ring, nn - 1, padded(rows), columns), BF),
        pltpu.SemaphoreType.DMA((2, 2)),
    ]


def norm_pull(values, gain, grad):
    scale = lax.rsqrt(jnp.mean(values * values, axis=-1, keepdims=True) + RMS_EPSILON)
    scaled = grad * gain
    along = jnp.mean(scaled * values, axis=-1, keepdims=True)
    share = grad * values * scale
    return scale * scaled - values * (scale * scale * scale * along), share


def fold_rows(values):
    return jnp.sum(values.reshape(values.shape[0] // 8, 8, values.shape[1]), axis=0)


def pack_row(row, first, each, devices):
    total = row.shape[1]
    shape = (128, total)
    pick = jnp.where(iota(shape, 0) == first + lax.rem(iota(shape, 1), each), 1.0, 0.0)
    shape = (devices, total)
    mine = jnp.where(iota(shape, 1) // each == iota(shape, 0), row, 0.0)
    return lax.dot_general(
        mine,
        pick,
        (((1,), (1,)), ((), ())),
        preferred_element_type=F32,
        precision=lax.Precision.HIGHEST,
    )


def backward_kernel(nn, few_facts, many_facts, *refs):
    occupied, refs = refs[0], refs[1:]
    (
        tokens,
        rel_hbm,
        lay_hbm,
        cotangent,
        small_h,
        query_h,
        key_h,
        value_h,
        output_h,
        gate_h,
        up_h,
        down_h,
        na_t,
        q_t,
        k_h,
        v_h,
        att_t,
        hid_h,
        nf_t,
        mix_t,
        probs_h,
        slope_h,
        act_h,
    ) = refs[:23]
    refs = refs[23:]
    (rows_out, few_out, many_out, small_out, few_grads, many_grads, few_came, many_came) = refs[:8]
    few_slots, many_slots, refs = refs[8:14], refs[14:20], refs[20:]
    (
        x,
        rel,
        lay,
        small,
        gains,
        grad,
        left,
        left_att,
        acc,
        hid,
        wd_s,
        wg_s,
        wu_s,
        slope_s,
        act_s,
        few_stage,
        many_stage,
        branch,
        w_one,
        pull,
        pull_t,
        qt,
        k,
        v,
        probs,
        pieces,
        dq,
        dkt,
        dvt,
        onehot,
        table,
        sums,
        small_grads,
        small_came,
        small_round,
        small_line,
        small_mine,
        send_sem,
        recv_sem,
        local_sem,
        tile_sem,
        stage_sem,
        probs_sem,
    ) = refs
    slots, width = x.shape
    links = Links(nn, send_sem, recv_sem)
    numbers = iter(range(64))

    def move(src, dst):
        copy = pltpu.make_async_copy(src, dst, local_sem.at[next(numbers)])
        copy.start()
        return copy

    ffn = mix_t.shape[0]
    tiles = ffn // TILE
    mix_in = move(mix_t, pieces.at[pl.ds(0, ffn)])
    grad_in = move(cotangent, grad)
    nf_in = move(nf_t, left)

    def tile_copies(tile):
        turn = lax.rem(tile, 2)
        at = pl.ds(pl.multiple_of(tile * TILE, TILE), TILE)
        return [
            pltpu.make_async_copy(src, dst.at[turn], tile_sem.at[turn, index])
            for index, (src, dst) in enumerate(
                (
                    (down_h.at[at], wd_s),
                    (gate_h.at[:, at], wg_s),
                    (up_h.at[:, at], wu_s),
                    (slope_h.at[:, at], slope_s),
                    (act_h.at[:, at], act_s),
                )
            )
        ]

    for copy in tile_copies(0):
        copy.start()
    later = [move(hid_h, hid), move(small_h, small), move(att_t, left_att), move(output_h, w_one.at[0])]
    later += [move(q_t, qt), move(k_h, k), move(v_h, v)]
    last = [move(tokens, x), move(rel_hbm, rel), move(lay_hbm, lay), move(value_h, w_one.at[1])]
    links.greet()
    few = Scatter(links, *few_facts, few_grads, few_came, few_slots, 0)
    base = few_facts[0] * SCATTER_COPIES
    many = Scatter(links, *many_facts, many_grads, many_came, many_slots, base)
    links.used = base + many_facts[0] * SCATTER_COPIES

    def stage_copy(scatter, stage, chunk, first):
        turn = lax.rem(chunk, 2)
        return pltpu.make_async_copy(
            stage.at[turn], scatter.grads.at[chunk], stage_sem.at[first + turn]
        )

    def few_copy(chunk):
        return stage_copy(few, few_stage, chunk, 0)

    def many_copy(chunk):
        return stage_copy(many, many_stage, chunk, 2)

    grad_in.wait()
    valid_rows = iota((slots, 1), 0) < occupied[0] + IMG

    def keep_valid(tile, carry):
        at = pl.ds(pl.multiple_of(tile * TILE, TILE), TILE)
        grad[:, at] = jnp.where(valid_rows, grad[:, at].astype(F32), 0.0).astype(BF)
        return carry

    lax.fori_loop(0, width // TILE, keep_valid, 0)
    mix_in.wait()
    block = few.block

    def down_chunk(chunk, carry):
        at = pl.ds(pl.multiple_of(chunk * few.columns, few.columns), few.columns)
        turn = lax.rem(chunk, 2)

        def one(index, carry):
            rows = pl.ds(pl.multiple_of(index * block, 16), block)
            few_stage[turn, index // 2, lax.rem(index, 2)] = dot(pieces[rows, :], grad[:, at]).astype(BF)
            return carry

        lax.fori_loop(0, ffn // block, one, 0)
        few_copy(chunk).start()

        @pl.when(chunk >= 1)
        def _():
            few_copy(chunk - 1).wait()
            few.trade(chunk - 1)

        return carry

    lax.fori_loop(0, few.chunks, down_chunk, 0)
    few_copy(few.chunks - 1).wait()
    few.trade(few.chunks - 1)
    nf_in.wait()

    def put(chunk, low, value):
        shape = many_stage.shape[1:4]
        many_stage[lax.rem(chunk, 2), :, :, :, low : low + value.shape[1]] = value.astype(BF).reshape(
            shape + (value.shape[1],)
        )

    def ffn_tile(tile, carry):
        turn = lax.rem(tile, 2)

        @pl.when(tile + 1 < tiles)
        def _():
            for copy in tile_copies(tile + 1):
                copy.start()

        for copy in tile_copies(tile):
            copy.wait()
        grad_mixed = dot_nt(grad[...], wd_s[turn])
        gate_low = (grad_mixed * slope_s[turn].astype(F32)).astype(BF)
        up_low = (grad_mixed * act_s[turn].astype(F32)).astype(BF)
        put(tile, 0, dot(left[...], gate_low))
        put(tile, TILE, dot(left[...], up_low))
        many_copy(tile).start()

        @pl.when(tile >= 1)
        def _():
            many_copy(tile - 1).wait()
            many.trade(tile - 1)

        for part in range(width // TILE):
            at = slice(part * TILE, (part + 1) * TILE)
            more = dot_nt(gate_low, wg_s[turn, at, :]) + dot_nt(up_low, wu_s[turn, at, :])
            acc[:, at] = jnp.where(tile == 0, 0.0, acc[:, at]) + more
        few.pump(tile, few_out)
        many.pump(tile - FFN_LAG, many_out)
        return carry

    lax.fori_loop(0, tiles, ffn_tile, 0)
    many_copy(tiles - 1).wait()
    many.trade(tiles - 1)
    done = tiles - FFN_LAG
    for copy in later:
        copy.wait()
    na_in = move(na_t, left)
    rows = small.reshape(small.shape[0] // 8, 8, 128)[:, 0, :]
    devices = rows.shape[0]
    each = width // devices
    gains[0:1, :] = unpack_row(rows, 0, each, width)
    gains[1:2, :] = unpack_row(rows, each, each, width)

    def norm_two(index, total):
        at = pl.ds(pl.multiple_of(index * 64, 64), 64)
        part, share = norm_pull(hid[at, :], gains[1:2, :], acc[at, :])
        whole = grad[at, :].astype(F32) + part
        hid[at, :] = whole
        branch[at, :] = whole.astype(BF)
        return total + fold_rows(share)

    zero = jnp.zeros((8, width), F32)
    sums[0] = lax.fori_loop(0, slots // 64, norm_two, zero)

    def emit(chunk, value):
        put(chunk, 0, value)
        many_copy(chunk).start()

    def flush(chunk):
        many_copy(chunk).wait()
        many.trade(chunk)

    wide = many.columns
    for part in range(width // wide):
        emit(tiles + part, dot(left_att[...], branch[:, part * wide : (part + 1) * wide]))
    many.pump(done, many_out)
    done += 1

    def pull_tile(tile, carry):
        at = pl.ds(pl.multiple_of(tile * TILE, TILE), TILE)
        found = dot_nt(branch[...], w_one[0, at, :]).astype(BF)
        pull[:, at] = found
        pull_t[at, :] = found.T
        return carry

    lax.fori_loop(0, width // TILE, pull_tile, 0)
    for part in range(width // wide):
        flush(tiles + part)
    made = tiles + width // wide
    query_in = move(query_h, w_one.at[0])

    def probs_copy(pair):
        turn = lax.rem(pair, 2)
        return pltpu.make_async_copy(probs_h.at[pl.ds(pair * 2, 2)], probs.at[turn], probs_sem.at[turn])

    pairs = H // 2
    probs_copy(0).start()

    def attend_back(pair, carry):
        @pl.when(pair + 1 < pairs)
        def _():
            probs_copy(pair + 1).start()

        probs_copy(pair).wait()
        turn = lax.rem(pair, 2)
        at = pl.ds(pl.multiple_of(pair * 128, 128), 128)
        low = iota((slots, 128), 1) < HD
        keys, pulls, values = k[:, at], pull[:, at], v[:, at]
        found = []
        for side in range(2):
            head = pair * 2 + side
            mine = jnp.where(low if side == 0 else jnp.logical_not(low), pulls, 0)
            share = probs[turn, side]
            wanted = dot_nt(mine, values)
            share_f = share.astype(F32)
            joint = share_f * wanted
            piece = (joint - share_f * jnp.sum(joint, axis=-1, keepdims=True)).astype(BF)
            pieces[pl.ds(pl.multiple_of(head * slots, slots), slots), :] = piece
            found.append(dot(piece, keys))
            rows = pl.ds(pl.multiple_of(head * HD, HD), HD)
            dkt[rows, :] = dot(qt[rows, :], piece).astype(BF)
            dvt[rows, :] = dot(pull_t[rows, :], share).astype(BF)
        dq[:, at] = jnp.where(low, found[0], found[1]).astype(BF)
        many.pump(done + pair, many_out, made)
        return carry

    lax.fori_loop(0, pairs, attend_back, 0)
    done = min(done + pairs, made)
    for copy in last:
        copy.wait()
    na_in.wait()
    for index, (grads, turned) in enumerate(((dvt, True), (dq, False), (dkt, True))):
        for part in range(width // wide):
            at = slice(part * wide, (part + 1) * wide)
            chunk = made + index * (width // wide) + part
            if index or part:
                flush(chunk - 1)
            if turned:
                emit(chunk, dot_nt(left[...], grads[at, :]))
            else:
                emit(chunk, dot(left[...], grads[:, at]))
        many.pump(done, many_out, made)
        done = min(done + 1, made)
    flush(many.chunks - 1)
    table[...] = jnp.zeros_like(table)

    def table_block_back(index, carry):
        for query in range(BACK_QB):
            for which, bucket in enumerate((rel, lay)):
                row = bucket[pl.ds(index * BACK_QB + query, 1), :]
                first = (query * 2 + which) * NB
                onehot[first : first + NB, :] = ones_where(
                    jnp.broadcast_to(row, (NB, slots)) == iota((NB, slots), 0)
                )
        heads = [
            pieces[pl.ds(pl.multiple_of(head * slots + index * BACK_QB, BACK_QB), BACK_QB), :]
            for head in range(H)
        ]
        table[...] += dot_nt(onehot[...], jnp.concatenate(heads, axis=0))
        return carry

    blocks = slots // BACK_QB
    groups = 8

    def table_group(group, carry):
        lax.fori_loop(group * (blocks // groups), (group + 1) * (blocks // groups), table_block_back, 0)
        many.pump(done + group, many_out)
        return carry

    lax.fori_loop(0, groups, table_group, 0)
    done += groups
    query_in.wait()

    def turn_back(tile, carry):
        at = pl.ds(pl.multiple_of(tile * TILE, TILE), TILE)
        pull[:, at] = dvt[at, :].T
        branch[:, at] = dkt[at, :].T
        return carry

    lax.fori_loop(0, width // TILE, turn_back, 0)

    def first_two(tile, carry):
        at = pl.ds(pl.multiple_of(tile * TILE, TILE), TILE)
        acc[:, at] = dot_nt(pull[...], w_one[1, at, :]) + dot_nt(dq[...], w_one[0, at, :])
        return carry

    lax.fori_loop(0, width // TILE, first_two, 0)
    key_in = move(key_h, w_one.at[0])
    many.pump(done, many_out)
    done += 1
    key_in.wait()

    def third(tile, carry):
        at = pl.ds(pl.multiple_of(tile * TILE, TILE), TILE)
        acc[:, at] += dot_nt(branch[...], w_one[0, at, :])
        return carry

    lax.fori_loop(0, width // TILE, third, 0)
    many.pump(done, many_out)
    done += 1

    def norm_one(index, total):
        at = pl.ds(pl.multiple_of(index * 64, 64), 64)
        part, share = norm_pull(x[at, :].astype(F32), gains[0:1, :], acc[at, :])
        hid[at, :] += part
        return total + fold_rows(share)

    sums[1] = lax.fori_loop(0, slots // 64, norm_one, zero)
    rows_copy = move(hid, rows_out)
    total = table[...]
    mine = iota(total.shape, 0) // (2 * NB) == lax.rem(iota(total.shape, 1), BACK_QB)
    folded = jnp.sum(
        jnp.where(mine, total, 0.0).reshape(BACK_QB, 2 * NB, H * BACK_QB), axis=0
    )
    packed = pack_row(jnp.sum(sums[1], axis=0, keepdims=True), 0, each, devices)
    packed += pack_row(jnp.sum(sums[0], axis=0, keepdims=True), each, each, devices)
    for index in range(2):
        shape = (H * BACK_QB, 128)
        lane = 2 * each + H * index + iota(shape, 0) // BACK_QB
        pick = jnp.where(iota(shape, 1) == lane, 1.0, 0.0)
        packed += jnp.dot(
            folded[index * NB : (index + 1) * NB],
            pick,
            preferred_element_type=F32,
            precision=lax.Precision.HIGHEST,
        )
    small_grads[...] = jnp.zeros_like(small_grads)
    for device in range(devices):
        wide_at, z = divmod(device, nn)
        small_grads[wide_at // 2, wide_at % 2, z * 8 : z * 8 + 1, :] = packed[device : device + 1]
    scatter_small(links, small_grads, small_out, small_came, small_round, small_line, small_mine)

    def rest(index, carry):
        many.pump(index, many_out)
        return carry

    lax.fori_loop(done, many.chunks + LAGS, rest, 0)
    rows_copy.wait()
    links.finish()


def backward_all(nw, nn, counts, page, weights, saved):
    squares = nw // 2
    devices = nw * nn
    slots, width = page[0].shape
    ffn = weights[5].shape[1]
    few = (width // 256, ffn // devices, 256)
    many = (ffn // TILE + 8, width // devices, 2 * TILE)
    outs = [jax.ShapeDtypeStruct((slots, width), F32)]
    for chunks, rows, columns in (few, many):
        outs.append(jax.ShapeDtypeStruct((chunks, rows, columns), F32))
    outs.append(jax.ShapeDtypeStruct((8, 128), F32))
    for chunks, rows, columns in (few, many):
        outs.append(jax.ShapeDtypeStruct((chunks, squares, 2, nn * rows, columns), BF))
    for chunks, rows, columns in (few, many):
        outs.append(jax.ShapeDtypeStruct((chunks, squares, nn * rows, columns), BF))
    copies = (few[0] + many[0]) * SCATTER_COPIES + 16
    vmem = pl.BlockSpec(memory_space=pltpu.VMEM)
    hbm = pl.BlockSpec(memory_space=pl.ANY)
    low = pltpu.VMEM((slots, width), BF)
    turned = pltpu.VMEM((width, slots), BF)
    full = pltpu.VMEM((slots, width), F32)
    inputs = (counts,) + tuple(page) + tuple(weights) + tuple(saved)
    return pl.pallas_call(
        functools.partial(backward_kernel, nn, few, many),
        out_shape=outs,
        in_specs=[pl.BlockSpec(memory_space=pltpu.SMEM)] + [hbm] * (len(inputs) - 1),
        out_specs=[hbm, vmem, vmem, vmem, hbm, hbm, hbm, hbm],
        scratch_shapes=scatter_slots(squares, nn, few[1], few[2], few[0])
        + scatter_slots(squares, nn, many[1], many[2], RING)
        + [
            low,
            pltpu.VMEM((slots, slots), jnp.int32),
            pltpu.VMEM((slots, slots), jnp.int32),
            pltpu.VMEM((devices * 8, 128), F32),
            pltpu.VMEM((8, width), F32),
            low,
            turned,
            turned,
            full,
            full,
            pltpu.VMEM((2, TILE, width), BF),
            pltpu.VMEM((2, width, TILE), BF),
            pltpu.VMEM((2, width, TILE), BF),
            pltpu.VMEM((2, slots, TILE), BF),
            pltpu.VMEM((2, slots, TILE), BF),
            pltpu.VMEM((2, squares, 2, nn * few[1], few[2]), BF),
            pltpu.VMEM((2, squares, 2, nn * many[1], many[2]), BF),
            low,
            pltpu.VMEM((2, width, width), BF),
            low,
            turned,
            turned,
            low,
            low,
            pltpu.VMEM((2, 2, slots, slots), BF),
            pltpu.VMEM((H * slots, slots), BF),
            low,
            turned,
            turned,
            pltpu.VMEM((BACK_QB * 2 * NB, slots), BF),
            pltpu.VMEM((BACK_QB * 2 * NB, H * BACK_QB), F32),
            pltpu.VMEM((2, 8, width), F32),
            pltpu.VMEM((squares, 2, nn * 8, 128), F32),
            pltpu.VMEM((squares, nn * 8, 128), F32),
            pltpu.VMEM((3, nn * 8, 128), F32),
            pltpu.VMEM((nn - 1, 8, 128), F32),
            pltpu.VMEM((squares, nn * 8, 128), F32),
            pltpu.SemaphoreType.DMA((copies,)),
            pltpu.SemaphoreType.DMA((copies,)),
            pltpu.SemaphoreType.DMA((64,)),
            pltpu.SemaphoreType.DMA((2, 5)),
            pltpu.SemaphoreType.DMA((4,)),
            pltpu.SemaphoreType.DMA((2,)),
        ],
        compiler_params=pltpu.CompilerParams(
            collective_id=1, has_side_effects=True, vmem_limit_bytes=63 * 2**20
        ),
    )(*inputs)[:4]


def local_fast(
    nw,
    nn,
    tokens,
    w_query,
    w_key,
    w_value,
    w_output,
    w_gate,
    w_up,
    w_down,
    gain_attn,
    gain_ffn,
    rel_table,
    lay_table,
    ocr_counts,
    rel_bucket,
    lay_bucket,
    cotangent,
):
    small = jnp.concatenate([gain_attn, gain_ffn, rel_table, lay_table]).astype(F32)
    small = jnp.pad(small[None], ((0, 7), (0, 128 - small.shape[0])))
    down = jnp.pad(w_down, ((0, padded(w_down.shape[0]) - w_down.shape[0]), (0, 0)))
    page = (tokens, rel_bucket, lay_bucket)
    shards = [small, w_query, w_key, w_value, w_output, w_gate, w_up, down]
    found = forward_all(nw, nn, ocr_counts, *page, shards, w_down.shape[0])
    weights, output, saved = found[: len(shards)], found[len(shards)], found[len(shards) + 1 :]
    grad_tokens, few, many, small = backward_all(
        nw, nn, ocr_counts, page + (cotangent,), weights, saved
    )

    def join(stack):
        return jnp.moveaxis(stack, 0, 1).reshape(stack.shape[1], -1)

    tiles = w_gate.shape[1] // TILE
    grad_output, grad_value, grad_query, grad_key = (
        join(many[tiles + 2 * index : tiles + 2 * index + 2]) for index in range(4)
    )
    gate, up = join(many[:tiles, :, :TILE]), join(many[:tiles, :, TILE:])
    cuts, at = [], 0
    for part in (gain_attn, gain_ffn, rel_table, lay_table):
        cuts.append(small[0, at : at + part.shape[0]])
        at += part.shape[0]
    grads = (grad_query, grad_key, grad_value, grad_output, gate, up, join(few))
    return (output, grad_tokens) + grads + tuple(cuts)


def local(
    tokens,
    w_query,
    w_key,
    w_value,
    w_output,
    w_gate,
    w_up,
    w_down,
    gain_attn,
    gain_ffn,
    rel_table,
    lay_table,
    ocr_counts,
    rel_bucket,
    lay_bucket,
    cotangent,
):
    slot = tokens.shape[0]
    valid = jnp.arange(slot) < ocr_counts[0] + IMG
    buckets = jnp.arange(NB)
    onehot = jnp.concatenate(
        [
            (rel_bucket[:, :, None] == buckets).astype(jnp.bfloat16),
            (lay_bucket[:, :, None] == buckets).astype(jnp.bfloat16),
        ],
        axis=2,
    )
    tokens_f = tokens.astype(jnp.float32)
    weights = gather_weights(
        w_query,
        w_key,
        w_value,
        w_output,
        w_gate,
        w_up,
        w_down,
        gain_attn,
        gain_ffn,
        rel_table,
        lay_table,
    )
    result, saved = forward_pass(tokens_f, weights, onehot, valid)
    output = jnp.where(valid[:, None], result, 0.0).astype(jnp.bfloat16)
    (
        full_query,
        full_key,
        full_value,
        full_output,
        full_gate,
        full_up,
        full_down,
        full_gain_attn,
        full_gain_ffn,
        full_rel,
        full_lay,
    ) = weights
    (
        normed_attn,
        queries,
        keys_all,
        values_all,
        log_totals,
        attended,
        hidden_one,
        normed_ffn,
        gate_act,
        up_proj,
        mixed,
    ) = saved
    grad_result = jnp.where(valid[:, None], cotangent.astype(jnp.float32), 0.0)
    grad_low = grad_result.astype(jnp.bfloat16)
    grad_down = contract_rows(mixed, grad_low)
    grad_mixed = contract_cols(grad_low, full_down)
    gated_value, gated_pull = jax.vjp(gated_product, gate_act, up_proj)
    grad_gate_act, grad_up_proj = gated_pull(grad_mixed)
    gate_low = grad_gate_act.astype(jnp.bfloat16)
    up_low = grad_up_proj.astype(jnp.bfloat16)
    grad_gate = contract_rows(normed_ffn, gate_low)
    grad_up = contract_rows(normed_ffn, up_low)
    grad_normed_ffn = contract_cols(gate_low, full_gate) + contract_cols(up_low, full_up)
    norm_value, norm_pull = jax.vjp(rms_scale, hidden_one, full_gain_ffn.astype(jnp.float32))
    grad_hidden_part, grad_gain_ffn = norm_pull(grad_normed_ffn)
    grad_hidden = grad_result + grad_hidden_part
    branch_low = grad_hidden.astype(jnp.bfloat16)
    grad_output = contract_rows(attended, branch_low)
    grad_attended = contract_cols(branch_low, full_output).astype(jnp.bfloat16)
    grad_queries, grad_keys, grad_values, grad_table_all = attention_backward(
        queries,
        keys_all,
        values_all,
        log_totals,
        grad_attended,
        table_pair(full_rel, full_lay),
        onehot,
        valid,
    )
    grad_rel = grad_table_all[:NB].reshape(NB * H)
    grad_lay = grad_table_all[NB:].reshape(NB * H)
    grad_query = contract_rows(normed_attn, grad_queries)
    grad_key = contract_rows(normed_attn, grad_keys)
    grad_value = contract_rows(normed_attn, grad_values)
    grad_normed_attn = (
        contract_cols(grad_queries, full_query)
        + contract_cols(grad_keys, full_key)
        + contract_cols(grad_values, full_value)
    )
    input_value, input_pull = jax.vjp(rms_scale, tokens_f, full_gain_attn.astype(jnp.float32))
    grad_input_part, grad_gain_attn = input_pull(grad_normed_attn)
    grad_tokens = grad_hidden + grad_input_part
    owned = (
        lax.psum_scatter(grad_query, ("wide", "narrow"), scatter_dimension=0, tiled=True),
        lax.psum_scatter(grad_key, ("wide", "narrow"), scatter_dimension=0, tiled=True),
        lax.psum_scatter(grad_value, ("wide", "narrow"), scatter_dimension=0, tiled=True),
        lax.psum_scatter(grad_output, ("wide", "narrow"), scatter_dimension=0, tiled=True),
        lax.psum_scatter(grad_gate, ("wide", "narrow"), scatter_dimension=0, tiled=True),
        lax.psum_scatter(grad_up, ("wide", "narrow"), scatter_dimension=0, tiled=True),
        lax.psum_scatter(grad_down, ("wide", "narrow"), scatter_dimension=0, tiled=True),
        lax.psum_scatter(grad_gain_attn, ("wide", "narrow"), scatter_dimension=0, tiled=True),
        lax.psum_scatter(grad_gain_ffn, ("wide", "narrow"), scatter_dimension=0, tiled=True),
        lax.psum_scatter(grad_rel, ("wide", "narrow"), scatter_dimension=0, tiled=True),
        lax.psum_scatter(grad_lay, ("wide", "narrow"), scatter_dimension=0, tiled=True),
    )
    return (
        output,
        grad_tokens,
        owned[0],
        owned[1],
        owned[2],
        owned[3],
        owned[4],
        owned[5],
        owned[6],
        owned[7],
        owned[8],
        owned[9],
        owned[10],
    )


def solution(mesh):
    nw, nn = mesh.shape["wide"], mesh.shape["narrow"]

    def body(*args):
        if nw == 8 and nw * nn == NB and args[1].shape[0] % 16 == 0:
            return local_fast(nw, nn, *args)
        return local(*args)

    placed = (
        P(("wide", "narrow"), None),
        P(("wide", "narrow"), None),
        P(("wide", "narrow"), None),
        P(("wide", "narrow"), None),
        P(("wide", "narrow"), None),
        P(("wide", "narrow"), None),
        P(("wide", "narrow"), None),
        P(("wide", "narrow"), None),
        P(("wide", "narrow")),
        P(("wide", "narrow")),
        P(("wide", "narrow")),
        P(("wide", "narrow")),
        P(("wide", "narrow")),
        P(("wide", "narrow"), None),
        P(("wide", "narrow"), None),
        P(("wide", "narrow"), None),
    )
    return jax.shard_map(
        body,
        mesh=mesh,
        in_specs=placed,
        out_specs=(
            P(("wide", "narrow"), None),
            P(("wide", "narrow"), None),
            P(("wide", "narrow"), None),
            P(("wide", "narrow"), None),
            P(("wide", "narrow"), None),
            P(("wide", "narrow"), None),
            P(("wide", "narrow"), None),
            P(("wide", "narrow"), None),
            P(("wide", "narrow"), None),
            P(("wide", "narrow")),
            P(("wide", "narrow")),
            P(("wide", "narrow")),
            P(("wide", "narrow")),
        ),
        check_vma=False,
    )
```

```python
import functools

import jax
import jax.numpy as jnp
from jax import lax
from jax.experimental import pallas as pl
from jax.experimental.pallas import tpu as pltpu
from jax.sharding import PartitionSpec as P

H = 16
HD = 64
NB = 32
IMG = 196
RING = 6
SCATTER_COPIES = 10
LAG = (0, 1, 2, 4, 6)
LAGS = LAG[-1]
FFN_LAG = 4
BACK_QB = 16
DOWN_PIECE = 256
TILE = 256
QB = 8
GELU_SCALE = 0.7978845608028654
GELU_CUBE = 0.044715


RMS_EPSILON = 1e-06
MASK_SCORE = -1000000000.0
HEAD_GROUP = 4


def rms_scale(values, gain):
    return (
        values * lax.rsqrt(jnp.mean(values * values, axis=-1, keepdims=True) + RMS_EPSILON) * gain
    )


def gated_product(gate_act, up_proj):
    return jax.nn.gelu(gate_act, approximate=True) * up_proj


def product(left, right):
    return jnp.dot(left, right, preferred_element_type=jnp.float32)


def contract_rows(left, right):
    return lax.dot_general(
        left, right, (((0,), (0,)), ((), ())), preferred_element_type=jnp.float32
    )


def contract_cols(left, right):
    return lax.dot_general(
        left, right, (((1,), (1,)), ((), ())), preferred_element_type=jnp.float32
    )


def split_heads(matrix):
    return jnp.moveaxis(matrix.reshape(matrix.shape[0], H // HEAD_GROUP, HEAD_GROUP, HD), 1, 0)


def join_heads(stacked):
    return jnp.moveaxis(stacked, 0, 1).reshape(stacked.shape[1], H * HD)


def group_tables(table_all):
    return jnp.moveaxis(table_all.reshape(2 * NB, H // HEAD_GROUP, HEAD_GROUP), 1, 0)


def group_scores(query_group, key_group, table_group, onehot, valid):
    scores = jnp.einsum("ihd,jhd->hij", query_group, key_group, preferred_element_type=jnp.float32)
    scores = scores + jnp.einsum(
        "ijb,bh->hij", onehot, table_group, preferred_element_type=jnp.float32
    )
    return jnp.where(valid[None, None, :], scores, MASK_SCORE)


def gather_weights(
    w_query,
    w_key,
    w_value,
    w_output,
    w_gate,
    w_up,
    w_down,
    gain_attn,
    gain_ffn,
    rel_table,
    lay_table,
):
    return (
        lax.all_gather(w_query, ("wide", "narrow"), axis=0, tiled=True),
        lax.all_gather(w_key, ("wide", "narrow"), axis=0, tiled=True),
        lax.all_gather(w_value, ("wide", "narrow"), axis=0, tiled=True),
        lax.all_gather(w_output, ("wide", "narrow"), axis=0, tiled=True),
        lax.all_gather(w_gate, ("wide", "narrow"), axis=0, tiled=True),
        lax.all_gather(w_up, ("wide", "narrow"), axis=0, tiled=True),
        lax.all_gather(w_down, ("wide", "narrow"), axis=0, tiled=True),
        lax.all_gather(gain_attn, ("wide", "narrow"), axis=0, tiled=True),
        lax.all_gather(gain_ffn, ("wide", "narrow"), axis=0, tiled=True),
        lax.all_gather(rel_table, ("wide", "narrow"), axis=0, tiled=True),
        lax.all_gather(lay_table, ("wide", "narrow"), axis=0, tiled=True),
    )


def table_pair(full_rel, full_lay):
    return jnp.concatenate([full_rel.reshape(NB, H), full_lay.reshape(NB, H)], axis=0)


def forward_pass(tokens_f, weights, onehot, valid):
    (
        full_query,
        full_key,
        full_value,
        full_output,
        full_gate,
        full_up,
        full_down,
        full_gain_attn,
        full_gain_ffn,
        full_rel,
        full_lay,
    ) = weights
    normed_attn = rms_scale(tokens_f, full_gain_attn.astype(jnp.float32)).astype(jnp.bfloat16)
    queries = product(normed_attn, full_query).astype(jnp.bfloat16)
    keys_all = product(normed_attn, full_key).astype(jnp.bfloat16)
    values_all = product(normed_attn, full_value).astype(jnp.bfloat16)

    def forward_one_group(operands):
        query_group, key_group, value_group, table_group = operands
        scores = group_scores(query_group, key_group, table_group, onehot, valid)
        peak = jnp.max(scores, axis=-1, keepdims=True)
        expo = jnp.exp(scores - peak)
        total = jnp.sum(expo, axis=-1, keepdims=True)
        probs_low = (expo / total).astype(jnp.bfloat16)
        attended_group = jnp.einsum(
            "hij,jhd->ihd", probs_low, value_group, preferred_element_type=jnp.float32
        )
        return (attended_group.astype(jnp.bfloat16), (peak + jnp.log(total))[..., 0])

    stacked, log_totals = lax.map(
        forward_one_group,
        (
            split_heads(queries),
            split_heads(keys_all),
            split_heads(values_all),
            group_tables(table_pair(full_rel, full_lay)),
        ),
    )
    attended = join_heads(stacked)
    hidden_one = tokens_f + product(attended, full_output)
    normed_ffn = rms_scale(hidden_one, full_gain_ffn.astype(jnp.float32)).astype(jnp.bfloat16)
    gate_act = product(normed_ffn, full_gate)
    up_proj = product(normed_ffn, full_up)
    mixed = gated_product(gate_act, up_proj).astype(jnp.bfloat16)
    result = hidden_one + product(mixed, full_down)
    return (
        result,
        (
            normed_attn,
            queries,
            keys_all,
            values_all,
            log_totals,
            attended,
            hidden_one,
            normed_ffn,
            gate_act,
            up_proj,
            mixed,
        ),
    )


def attention_backward(
    queries, keys_all, values_all, log_totals, grad_attended, table_all, onehot, valid
):

    def attention_one_group(operands):
        query_group, key_group, value_group, table_group, lse_group, grad_group = operands
        scores = group_scores(query_group, key_group, table_group, onehot, valid)
        probs = jnp.exp(scores - lse_group[..., None])
        probs_low = probs.astype(jnp.bfloat16)
        grad_values = jnp.einsum(
            "hij,ihd->jhd", probs_low, grad_group, preferred_element_type=jnp.float32
        )
        grad_probs = jnp.einsum(
            "ihd,jhd->hij", grad_group, value_group, preferred_element_type=jnp.float32
        )
        grad_scores = (
            probs * (grad_probs - jnp.sum(probs * grad_probs, axis=-1, keepdims=True))
        ).astype(jnp.bfloat16)
        grad_queries = jnp.einsum(
            "hij,jhd->ihd", grad_scores, key_group, preferred_element_type=jnp.float32
        )
        grad_keys = jnp.einsum(
            "hij,ihd->jhd", grad_scores, query_group, preferred_element_type=jnp.float32
        )
        grad_table = jnp.einsum(
            "hij,ijb->bh", grad_scores, onehot, preferred_element_type=jnp.float32
        )
        return (
            grad_queries.astype(jnp.bfloat16),
            grad_keys.astype(jnp.bfloat16),
            grad_values.astype(jnp.bfloat16),
            grad_table,
        )

    grad_q_all, grad_k_all, grad_v_all, grad_tables = lax.map(
        attention_one_group,
        (
            split_heads(queries),
            split_heads(keys_all),
            split_heads(values_all),
            group_tables(table_all),
            log_totals,
            split_heads(grad_attended),
        ),
    )
    grad_table_all = jnp.moveaxis(grad_tables, 0, 1).reshape(2 * NB, H)
    return (join_heads(grad_q_all), join_heads(grad_k_all), join_heads(grad_v_all), grad_table_all)


MESH_ID = pl.DeviceIdType.MESH
BF = jnp.bfloat16
F32 = jnp.float32
X_BIT = 2
Y_BIT = 4
PARTS = ((X_BIT, Y_BIT), (Y_BIT, X_BIT))


class Links:
    def __init__(self, nn, send_sem, recv_sem):
        self.nn = nn
        self.w = lax.axis_index("wide")
        self.z = lax.axis_index("narrow")
        self.send_sem = send_sem
        self.recv_sem = recv_sem
        self.used = 0
        self.sent = []

    def fresh(self):
        self.used += 1
        return self.used - 1

    def wide(self, bit):
        return (jnp.bitwise_xor(self.w, bit), self.z)

    def along(self, step):
        return (self.w, lax.rem(self.z + step, self.nn))

    def copy(self, src, dst, number, device):
        return pltpu.make_async_remote_copy(
            src_ref=src,
            dst_ref=dst,
            send_sem=self.send_sem.at[number],
            recv_sem=self.recv_sem.at[number],
            device_id=device,
            device_id_type=MESH_ID,
        )

    def send(self, src, dst, number, device):
        copy = self.copy(src, dst, number, device)
        copy.start()
        self.sent.append(copy)

    def greet(self):
        barrier = pltpu.get_barrier_semaphore()
        others = [self.wide(bit) for bit in (1, X_BIT, Y_BIT)]
        others += [self.along(step) for step in range(1, self.nn)]
        for other in others:
            pl.semaphore_signal(barrier, inc=1, device_id=other, device_id_type=MESH_ID)
        pl.semaphore_wait(barrier, len(others))

    def finish(self):
        for copy in self.sent:
            copy.wait_send()


class Gather:
    def __init__(self, links, shard, full, rows, window, parts, local_sem, line=None, merged=None):
        self.links, self.shard, self.full, self.rows, self.parts = links, shard, full, rows, parts
        self.window = window
        self.local_sem, self.line, self.merged = local_sem, line, merged
        nn = links.nn
        self.block = rows * nn
        self.line_ids = [links.fresh() for _ in range(1, nn)]
        self.part_ids = {
            (p, mask): links.fresh()
            for p in range(len(parts))
            for mask in (X_BIT, Y_BIT, X_BIT | Y_BIT)
        }
        self.core_ids = {mask: links.fresh() for mask in (0, X_BIT, Y_BIT, X_BIT | Y_BIT)}

    def place(self, w, z):
        if self.line is not None:
            return self.line.at[z]
        return self.full.at[pl.ds((w * self.links.nn + z) * self.rows, self.rows), pl.ds(*self.window)]

    def span(self, mask, part=None):
        rows = pl.ds(jnp.bitwise_xor(self.links.w, mask) * self.block, self.block)
        low, size = self.window if part is None else self.parts[part][:2]
        return self.full.at[rows, pl.ds(low, size)]

    def own(self):
        return pltpu.make_async_copy(
            self.shard, self.place(self.links.w, self.links.z), self.local_sem
        )

    def start(self):
        k = self.links
        self.own().start()
        for step in range(1, k.nn):
            k.send(self.shard, self.place(k.w, k.z), self.line_ids[step - 1], k.along(step))

    def spread(self):
        k = self.links
        self.own().wait()
        for step in range(1, k.nn):
            came = lax.rem(k.z - step + k.nn, k.nn)
            k.copy(
                self.shard, self.place(k.w, came), self.line_ids[step - 1], k.along(step)
            ).wait_recv()
        if self.line is not None:
            whole = jnp.concatenate(
                [self.line[z, : self.rows].astype(F32) for z in range(k.nn)], axis=0
            )
            self.merged[...] = whole.astype(BF)
            move = pltpu.make_async_copy(self.merged, self.span(0), self.local_sem)
            move.start()
            move.wait()
        for p, part in enumerate(self.parts):
            for bit in part[2]:
                k.send(self.span(0, p), self.span(0, p), self.part_ids[p, bit], k.wide(bit))
        k.send(self.span(0), self.span(0), self.core_ids[0], k.wide(1))

    def arrive(self, p, mask):
        k = self.links
        k.copy(
            self.span(mask, p), self.span(mask, p), self.part_ids[p, mask], k.wide(X_BIT)
        ).wait_recv()

    def forward(self):
        k = self.links
        for p, part in enumerate(self.parts):
            first, second = part[2]
            self.arrive(p, first)
            both = first | second
            k.send(self.span(first, p), self.span(first, p), self.part_ids[p, both], k.wide(second))
        for p, part in enumerate(self.parts):
            self.arrive(p, part[2][1])
        for mask in (X_BIT, Y_BIT):
            k.send(self.span(mask), self.span(mask), self.core_ids[mask], k.wide(1))

    def last(self):
        k = self.links
        both = X_BIT | Y_BIT
        for p in range(len(self.parts)):
            self.arrive(p, both)
        k.send(self.span(both), self.span(both), self.core_ids[both], k.wide(1))

    def done(self):
        k = self.links
        for mask, number in self.core_ids.items():
            place = self.span(mask | 1)
            k.copy(place, place, number, k.wide(1)).wait_recv()


def halves(columns, first=0):
    low = columns // 256 * 128
    return ((first, low, PARTS[0]), (first + low, columns - low, PARTS[1]))


class GatherSquare:
    def __init__(self, links, shard, full, rows, window, local_sem, square, lines, merged):
        self.links, self.shard, self.full, self.rows, self.window = links, shard, full, rows, window
        self.square, self.lines, self.merged, self.local_sem = square, lines, merged, local_sem
        self.parts = halves(window[1])
        self.block = rows * links.nn
        self.part_ids = {
            (p, mask): links.fresh()
            for p in range(len(self.parts))
            for mask in (X_BIT, Y_BIT, X_BIT | Y_BIT)
        }
        self.line_ids = [links.fresh() for _ in range(1, links.nn)]
        self.core_ids = [links.fresh() for _ in range(square.shape[0])]

    def spot(self, mask, p):
        low, size = self.parts[p][:2]
        return self.square.at[jnp.bitwise_xor(self.links.w, mask) // 2, :, pl.ds(low, size)]

    def own(self):
        return pltpu.make_async_copy(
            self.shard, self.square.at[self.links.w // 2], self.local_sem.at[0]
        )

    def start(self):
        k = self.links
        self.own().start()
        for p, (low, size, order) in enumerate(self.parts):
            for bit in order:
                k.send(self.shard.at[:, pl.ds(low, size)], self.spot(0, p), self.part_ids[p, bit], k.wide(bit))

    def arrive(self, p, mask):
        k = self.links
        k.copy(self.spot(mask, p), self.spot(mask, p), self.part_ids[p, mask], k.wide(X_BIT)).wait_recv()

    def forward(self):
        k = self.links
        for p, (low, size, (first, second)) in enumerate(self.parts):
            self.arrive(p, first)
            k.send(self.spot(first, p), self.spot(first, p), self.part_ids[p, first | second], k.wide(second))
        for p, (low, size, (first, second)) in enumerate(self.parts):
            self.arrive(p, second)

    def keep(self):
        return pltpu.make_async_copy(self.square, self.lines.at[self.links.z], self.local_sem.at[0])

    def line(self):
        k = self.links
        self.own().wait()
        for p in range(len(self.parts)):
            self.arrive(p, X_BIT | Y_BIT)
        self.keep().start()
        for step in range(1, k.nn):
            k.send(self.square, self.lines.at[k.z], self.line_ids[step - 1], k.along(step))

    def rows_of(self, square, core):
        rows = pl.ds((square * 2 + core) * self.block, self.block)
        return self.full.at[rows, pl.ds(*self.window)]

    def out(self, square):
        core = lax.rem(self.links.w, 2)
        return pltpu.make_async_copy(
            self.merged.at[square], self.rows_of(square, core), self.local_sem.at[1 + square]
        )

    def join(self):
        k = self.links
        self.keep().wait()
        for step in range(1, k.nn):
            came = lax.rem(k.z - step + k.nn, k.nn)
            k.copy(self.square, self.lines.at[came], self.line_ids[step - 1], k.along(step)).wait_recv()

        def one(square, carry):
            whole = jnp.concatenate(
                [self.lines[z, square, : self.rows].astype(F32) for z in range(k.nn)], axis=0
            )
            self.merged[square] = whole.astype(BF)
            return carry

        lax.fori_loop(0, self.merged.shape[0], one, 0)
        core = lax.rem(k.w, 2)
        for square, number in enumerate(self.core_ids):
            self.out(square).start()
            k.send(self.merged.at[square], self.rows_of(square, core), number, k.wide(1))

    def done(self):
        k = self.links
        core = lax.rem(k.w, 2)
        for square, number in enumerate(self.core_ids):
            self.out(square).wait()
            k.copy(self.merged.at[square], self.rows_of(square, 1 - core), number, k.wide(1)).wait_recv()


def dot(left, right):
    return jnp.dot(left, right, preferred_element_type=F32)


def dot_nt(left, right):
    return lax.dot_general(left, right, (((1,), (1,)), ((), ())), preferred_element_type=F32)


def dot_tn(left, right):
    return lax.dot_general(left, right, (((0,), (0,)), ((), ())), preferred_element_type=F32)


def iota(shape, dimension):
    return lax.broadcasted_iota(jnp.int32, shape, dimension)


def ones_where(mask):
    return jnp.where(mask, 1.0, 0.0).astype(BF)


def unpack_row(rows, first, each, total):
    devices = rows.shape[0]
    pick = ones_where(iota((128, total), 0) == first + lax.rem(iota((128, total), 1), each))
    spread = dot(rows.astype(BF), pick)
    mine = iota((devices, total), 1) // each == iota((devices, total), 0)
    return jnp.sum(jnp.where(mine, spread, 0.0), axis=0, keepdims=True)


def table_block(rows, first):
    pick_shape = (H * QB, 128)
    total = None
    for index in range(2):
        lane = first + H * index + iota(pick_shape, 0) // QB
        pick = ones_where(iota(pick_shape, 1) == lane)
        table = dot_nt(pick, rows.astype(BF)).astype(BF)
        wide = (NB, QB * 2 * NB)
        spread = dot(table, ones_where(lax.rem(iota(wide, 1), 2 * NB) == iota(wide, 0) + NB * index))
        total = spread if total is None else total + spread
    shape = (H * QB, QB * 2 * NB)
    mine = lax.rem(iota(shape, 0), QB) == iota(shape, 1) // (2 * NB)
    return jnp.where(mine, total, 0.0).astype(BF)


def bucket_ones(rel, lay, onehot, block):
    width = rel.shape[1]
    rows = iota((NB, width), 0)
    for query in range(QB):
        for index, bucket in enumerate((rel, lay)):
            row = bucket[pl.ds(block * QB + query, 1), :]
            low = (query * 2 + index) * NB
            onehot[low : low + NB, :] = ones_where(jnp.broadcast_to(row, (NB, width)) == rows)


def forward_kernel(nn, shapes, *refs):
    count = len(shapes)
    occupied, tokens, rel_hbm, lay_hbm, cotangent = refs[:5]
    shards = refs[5 : 5 + count]
    refs = refs[5 + count :]
    fulls, refs = refs[:count], refs[count:]
    (grad_h, na_t, q_t, k_h, v_h, att_t, hid_h, nf_t, mix_h, probs_h, slope_h, act_h) = refs[:12]
    down_grads, down_came, refs = refs[12], refs[13], refs[14:]
    (
        line,
        merged,
        x,
        rel,
        lay,
        small,
        lhs,
        onehot,
        bias,
        na,
        q,
        k,
        v,
        att,
        hid,
        nf,
        mix,
        slope,
        act,
        probs,
        w_one,
        w_wide,
        grad,
        down_stage,
        gains,
        turned,
        mixed_t,
        send_sem,
        recv_sem,
        gather_sem,
        local_sem,
        ring_sem,
        rest_square,
        rest_lines,
        rest_merged,
        rest_sem,
    ) = refs
    slots, width = x.shape
    links = Links(nn, send_sem, recv_sem)
    numbers = iter(range(64))

    def move(src, dst):
        copy = pltpu.make_async_copy(src, dst, local_sem.at[next(numbers)])
        copy.start()
        return copy

    arriving = [move(tokens, x), move(rel_hbm, rel), move(lay_hbm, lay)]
    grad_in = move(cotangent, grad)
    links.greet()
    g = []
    for index, (rows, columns) in enumerate(shapes):
        odd = rows % 16 != 0 and columns > 128
        columns = columns // 2 if odd else columns
        g.append(
            Gather(
                links,
                shards[index].at[:, pl.ds(0, columns)] if odd else shards[index],
                fulls[index],
                rows,
                (0, columns),
                halves(columns) if columns > 128 else ((0, columns, PARTS[0]),),
                gather_sem.at[index],
                line if odd else None,
                merged if odd else None,
            )
        )
    rows, columns = shapes[-1]
    rest = GatherSquare(
        links,
        shards[-1].at[:, pl.ds(columns // 2, columns // 2)],
        fulls[-1],
        rows,
        (columns // 2, columns // 2),
        rest_sem,
        rest_square,
        rest_lines,
        rest_merged,
    )
    down_ids = [links.fresh() for _ in range(down_grads.shape[0])]
    SMALL, Q, K, V, O, GATE, UP, DOWN = range(8)
    g[SMALL].start()
    g[Q].start()
    rest.start()
    g[SMALL].spread()
    g[SMALL].forward()
    g[K].start()
    g[Q].spread()
    g[V].start()
    g[SMALL].last()
    g[SMALL].done()
    rest.forward()
    small_in = move(fulls[SMALL], small)
    leaving = []
    turning = {}

    def turn_out(slot, source, target):
        if slot in turning:
            turning[slot].wait()

        def one(tile, carry):
            at = pl.ds(pl.multiple_of(tile * TILE, TILE), TILE)
            turned[slot, at, :] = source[:, at].T
            return carry

        lax.fori_loop(0, width // TILE, one, 0)
        turning[slot] = move(turned.at[slot], target)

    for copy in arriving:
        copy.wait()
    small_in.wait()
    rows = small.reshape(small.shape[0] // 8, 8, 128)[:, 0, :]
    each = width // rows.shape[0]
    gains[0:1, :] = unpack_row(rows, 0, each, width)
    gains[1:2, :] = unpack_row(rows, each, each, width)
    lhs[...] = table_block(rows, 2 * each)

    def normalise(index, carry):
        at = pl.ds(pl.multiple_of(index * 64, 64), 64)
        values = x[at, :].astype(F32)
        scale = lax.rsqrt(jnp.mean(values * values, axis=-1, keepdims=True) + RMS_EPSILON)
        na[at, :] = (values * scale * gains[0:1, :]).astype(BF)
        return carry

    lax.fori_loop(0, slots // 64, normalise, 0)
    turn_out(0, na, na_t)
    valid = iota((1, slots), 1) < occupied[0] + IMG

    def bias_block(block, carry):
        bucket_ones(rel, lay, onehot, block)
        found = jnp.where(valid, dot(lhs[...], onehot[...]), MASK_SCORE)
        bias[:, pl.ds(pl.multiple_of(block * QB, QB), QB), :] = found.reshape(H, QB, slots)
        return carry

    blocks = slots // QB
    g[K].spread()
    g[O].start()
    g[GATE].start()
    g[Q].forward()
    lax.fori_loop(0, blocks // 3, bias_block, 0)
    g[V].spread()
    g[K].forward()
    g[Q].last()
    lax.fori_loop(blocks // 3, 2 * blocks // 3, bias_block, 0)
    g[O].spread()
    g[UP].start()
    g[V].forward()
    g[K].last()
    g[Q].done()
    fetch = move(fulls[Q], w_one.at[0])
    lax.fori_loop(2 * blocks // 3, blocks, bias_block, 0)
    fetch.wait()

    def project(slot, target):
        def one(tile, carry):
            at = pl.ds(pl.multiple_of(tile * TILE, TILE), TILE)
            target[:, at] = dot(na[...], w_one[slot, :, at]).astype(BF)
            return carry

        lax.fori_loop(0, width // TILE, one, 0)

    project(0, q)
    turn_out(1, q, q_t)
    g[GATE].spread()
    g[DOWN].start()
    g[O].forward()
    g[V].last()
    g[K].done()
    fetch = move(fulls[K], w_one.at[1])
    fetch.wait()
    project(1, k)
    leaving.append(move(k, k_h))
    g[V].done()
    fetch = move(fulls[V], w_one.at[0])
    fetch.wait()
    project(0, v)
    leaving.append(move(v, v_h))
    g[O].last()

    def probs_out(pair):
        turn = lax.rem(pair, 2)
        return pltpu.make_async_copy(probs.at[turn], probs_h.at[pl.ds(pair * 2, 2)], ring_sem.at[turn])

    def attend(pair, carry):
        @pl.when(pair >= 2)
        def _():
            probs_out(pair - 2).wait()

        at = pl.ds(pl.multiple_of(pair * 128, 128), 128)
        low = iota((slots, 128), 1) < HD
        queries = q[:, at]
        keys = k[:, at]
        found = []
        for side in range(2):
            mine = jnp.where(low if side == 0 else jnp.logical_not(low), queries, 0)
            scores = dot_nt(mine, keys) + bias[pair * 2 + side]
            peak = jnp.max(scores, axis=-1, keepdims=True)
            expo = jnp.exp(scores - peak)
            total = jnp.sum(expo, axis=-1, keepdims=True)
            share = (expo * (1.0 / total)).astype(BF)
            probs[lax.rem(pair, 2), side] = share
            found.append(dot(share, v[:, at]))
        att[:, at] = jnp.where(low, found[0], found[1]).astype(BF)
        probs_out(pair).start()
        return carry

    pairs = H // 2
    lax.fori_loop(0, 4, attend, 0)
    g[UP].spread()
    rest.line()
    g[GATE].forward()
    g[O].done()
    fetch_o = move(fulls[O], w_one.at[1])
    lax.fori_loop(4, pairs, attend, 0)
    turn_out(0, att, att_t)
    fetch_o.wait()

    def output_tile(tile, carry):
        at = pl.ds(pl.multiple_of(tile * TILE, TILE), TILE)
        hid[:, at] = x[:, at].astype(F32) + dot(att[...], w_one[1, :, at])
        return carry

    lax.fori_loop(0, width // TILE, output_tile, 0)
    leaving.append(move(hid, hid_h))

    def normalise_two(index, carry):
        at = pl.ds(pl.multiple_of(index * 64, 64), 64)
        values = hid[at, :]
        scale = lax.rsqrt(jnp.mean(values * values, axis=-1, keepdims=True) + RMS_EPSILON)
        nf[at, :] = (values * scale * gains[1:2, :]).astype(BF)
        return carry

    lax.fori_loop(0, slots // 64, normalise_two, 0)
    turn_out(1, nf, nf_t)
    g[UP].forward()
    g[DOWN].spread()
    g[GATE].last()
    g[GATE].done()
    fetch_gate = move(fulls[GATE], w_wide.at[0])
    grad_in.wait()
    valid_rows = iota((slots, 1), 0) < occupied[0] + IMG

    def keep_valid(tile, carry):
        at = pl.ds(pl.multiple_of(tile * TILE, TILE), TILE)
        grad[:, at] = jnp.where(valid_rows, grad[:, at].astype(F32), 0.0).astype(BF)
        return carry

    lax.fori_loop(0, width // TILE, keep_valid, 0)
    leaving.append(move(grad, grad_h))
    fetch_gate.wait()
    ffn = mixed_t.shape[0]
    tiles = ffn // TILE
    across = slots // TILE

    def gate_spot(tile, second):
        at = pl.ds(pl.multiple_of(lax.rem(tile, across) * TILE, TILE), TILE)
        return bias.at[tile // across + second * (-(-tiles // across)), :, at]

    def gate_tile(tile, carry):
        at = pl.ds(pl.multiple_of(tile * TILE, TILE), TILE)
        gate = dot(nf[...], w_wide[0, :, at])
        square = gate * gate
        inner = GELU_SCALE * gate * (1.0 + GELU_CUBE * square)
        bend = jnp.tanh(inner)
        half = 0.5 * (1.0 + bend)
        gate_spot(tile, 0)[...] = gate * half
        gate_spot(tile, 1)[...] = half + 0.5 * gate * (1.0 - bend * bend) * GELU_SCALE * (
            1.0 + 3.0 * GELU_CUBE * square
        )
        return carry

    lax.fori_loop(0, tiles, gate_tile, 0)
    g[UP].last()
    g[UP].done()
    fetch_up = move(fulls[UP], w_wide.at[1])
    fetch_up.wait()

    def ffn_out(tile):
        turn = lax.rem(tile, 2)
        at = pl.ds(pl.multiple_of(tile * TILE, TILE), TILE)
        return (
            pltpu.make_async_copy(slope.at[turn], slope_h.at[:, at], ring_sem.at[2 + turn]),
            pltpu.make_async_copy(act.at[turn], act_h.at[:, at], ring_sem.at[4 + turn]),
            pltpu.make_async_copy(mix.at[turn], mix_h.at[:, at], ring_sem.at[6 + turn]),
        )

    def ffn_tile(tile, carry):
        @pl.when(tile >= 2)
        def _():
            for copy in ffn_out(tile - 2):
                copy.wait()

        at = pl.ds(pl.multiple_of(tile * TILE, TILE), TILE)
        turn = lax.rem(tile, 2)
        up = dot(nf[...], w_wide[1, :, at])
        active = gate_spot(tile, 0)[...]
        rise = gate_spot(tile, 1)[...]
        mixed = (active * up).astype(BF)
        mix[turn] = mixed
        mixed_t[at, :] = mixed.T
        act[turn] = active.astype(BF)
        slope[turn] = (up * rise).astype(BF)
        for copy in ffn_out(tile):
            copy.start()
        return carry

    lax.fori_loop(0, tiles, ffn_tile, 0)
    g[DOWN].forward()
    block = down_stage.shape[3]
    piece = down_stage.shape[4]

    def down_copy(chunk):
        turn = lax.rem(chunk, 2)
        return pltpu.make_async_copy(down_stage.at[turn], down_grads.at[chunk], ring_sem.at[8 + turn])

    def down_chunk(chunk, carry):
        at = pl.ds(pl.multiple_of(chunk * piece, piece), piece)

        def one(index, carry):
            rows = pl.ds(pl.multiple_of(index * block, 16), block)
            down_stage[lax.rem(chunk, 2), index // 2, lax.rem(index, 2)] = dot(
                mixed_t[rows, :], grad[:, at]
            ).astype(BF)
            return carry

        lax.fori_loop(0, ffn // block, one, 0)
        down_copy(chunk).start()
        return carry

    def down_trade(chunk):
        core = lax.rem(links.w, 2)
        return links.copy(
            down_grads.at[chunk, :, 1 - core], down_came.at[chunk], down_ids[chunk], links.wide(1)
        )

    chunks = width // piece
    for chunk in range(chunks):
        down_chunk(jnp.int32(chunk), 0)
        if chunk == 1:
            rest.join()
        if chunk >= 1:
            down_copy(chunk - 1).wait()
            down_trade(chunk - 1).start()
    g[DOWN].last()
    down_copy(chunks - 1).wait()
    down_trade(chunks - 1).start()
    g[DOWN].done()
    rest.done()
    for chunk in range(chunks):
        down_trade(chunk).wait()
    for copy in leaving + list(turning.values()):
        copy.wait()
    for pair in (pairs - 2, pairs - 1):
        probs_out(pair).wait()
    for tile in (tiles - 2, tiles - 1):
        for copy in ffn_out(tile):
            copy.wait()
    links.finish()


def forward_all(nw, nn, counts, tokens, rel, lay, cotangent, shards, odd_rows):
    devices = nw * nn
    shapes = []
    for index, shard in enumerate(shards):
        rows = odd_rows if index == len(shards) - 1 else shard.shape[0]
        shapes.append((rows, shard.shape[1]))
    slots, width = tokens.shape
    copies = (len(shards) + 1) * (nn - 1 + 6 + nw // 2) + width // DOWN_PIECE
    ffn = shapes[5][1]
    low = jax.ShapeDtypeStruct((slots, width), BF)
    wide = jax.ShapeDtypeStruct((slots, ffn), BF)
    full = jax.ShapeDtypeStruct((slots, width), F32)
    out_shape = [
        jax.ShapeDtypeStruct((rows * devices, columns), shard.dtype)
        for (rows, columns), shard in zip(shapes, shards)
    ]
    low_t = jax.ShapeDtypeStruct((width, slots), BF)
    out_shape += [low, low_t, low_t, low, low, low_t, full, low_t, wide]
    out_shape += [jax.ShapeDtypeStruct((H, slots, slots), BF), wide, wide]
    down = (nw // 2, 2, nn * odd_rows, DOWN_PIECE)
    out_shape += [jax.ShapeDtypeStruct((width // DOWN_PIECE,) + down, BF)]
    out_shape += [jax.ShapeDtypeStruct((width // DOWN_PIECE, nw // 2, nn * odd_rows, DOWN_PIECE), BF)]
    half = (shards[-1].shape[0], shards[-1].shape[1] // 2)
    hbm = pl.BlockSpec(memory_space=pl.ANY)
    page = pltpu.VMEM((slots, width), BF)
    return pl.pallas_call(
        functools.partial(forward_kernel, nn, shapes),
        out_shape=out_shape,
        in_specs=[pl.BlockSpec(memory_space=pltpu.SMEM)] + [hbm] * (4 + len(shards)),
        out_specs=[hbm] * len(out_shape),
        scratch_shapes=[
            pltpu.VMEM((nn,) + half, BF),
            pltpu.VMEM((nn * odd_rows, half[1]), BF),
            page,
            pltpu.VMEM((slots, slots), jnp.int32),
            pltpu.VMEM((slots, slots), jnp.int32),
            pltpu.VMEM((devices * 8, 128), F32),
            pltpu.VMEM((H * QB, QB * 2 * NB), BF),
            pltpu.VMEM((QB * 2 * NB, slots), BF),
            pltpu.VMEM((H, slots, slots), F32),
            page,
            page,
            page,
            page,
            page,
            pltpu.VMEM((slots, width), F32),
            page,
            pltpu.VMEM((2, slots, TILE), BF),
            pltpu.VMEM((2, slots, TILE), BF),
            pltpu.VMEM((2, slots, TILE), BF),
            pltpu.VMEM((2, 2, slots, slots), BF),
            pltpu.VMEM((2, width, width), BF),
            pltpu.VMEM((2, width, ffn), BF),
            page,
            pltpu.VMEM((2,) + down, BF),
            pltpu.VMEM((8, width), F32),
            pltpu.VMEM((2, width, slots), BF),
            pltpu.VMEM((ffn, slots), BF),
            pltpu.SemaphoreType.DMA((copies,)),
            pltpu.SemaphoreType.DMA((copies,)),
            pltpu.SemaphoreType.DMA((len(shards),)),
            pltpu.SemaphoreType.DMA((64,)),
            pltpu.SemaphoreType.DMA((10,)),
            pltpu.VMEM((nw // 2,) + half, BF),
            pltpu.VMEM((nn, nw // 2) + half, BF),
            pltpu.VMEM((nw // 2, nn * odd_rows, half[1]), BF),
            pltpu.SemaphoreType.DMA((1 + nw // 2,)),
        ],
        compiler_params=pltpu.CompilerParams(
            collective_id=0, has_side_effects=True, vmem_limit_bytes=63 * 2**20
        ),
    )(counts, tokens, rel, lay, cotangent, *shards)


class Scatter:
    def __init__(self, links, chunks, rows, columns, grads, came, slots, base, traded=False):
        self.links, self.chunks, self.rows, self.columns = links, chunks, rows, columns
        self.grads, self.came = grads, came
        (self.held, self.other, self.round, self.out_line, self.in_line, self.load_sem) = slots
        self.base = base
        self.traded = traded
        self.block = rows * links.nn
        self.parts = halves(columns)
        self.core = lax.rem(links.w, 2)
        self.ring = self.held.shape[0]

    def number(self, chunk, kind):
        return self.base + chunk * SCATTER_COPIES + kind

    def core_copy(self, chunk):
        return self.links.copy(
            self.grads.at[chunk, :, 1 - self.core],
            self.came.at[chunk],
            self.number(chunk, 0),
            self.links.wide(1),
        )

    def trade(self, chunk):
        self.core_copy(chunk).start()

    def loads(self, chunk):
        slot, turn = lax.rem(chunk, self.ring), lax.rem(chunk, 2)
        return (
            pltpu.make_async_copy(
                self.grads.at[chunk, :, self.core], self.held.at[slot], self.load_sem.at[turn, 0]
            ),
            pltpu.make_async_copy(
                self.came.at[chunk], self.other.at[turn], self.load_sem.at[turn, 1]
            ),
        )

    def fetch(self, chunk):
        if not self.traded:
            self.core_copy(chunk).wait_recv()
        for load in self.loads(chunk):
            load.start()

    def square(self, mask):
        return jnp.bitwise_xor(self.links.w, mask) // 2

    def hop(self, chunk, p, mask):
        slot = lax.rem(chunk, self.ring)
        low, size, order = self.parts[p]
        bit = order[1] if mask & order[1] else order[0]
        kind = 1 + p * 3 + (X_BIT, Y_BIT, X_BIT | Y_BIT).index(mask)
        return self.links.copy(
            self.held.at[slot, self.square(mask), :, pl.ds(low, size)],
            self.round.at[slot, kind - 1, :, pl.ds(0, size)],
            self.number(chunk, kind),
            self.links.wide(bit),
        )

    def landed(self, chunk, p, mask):
        return self.round.at[
            lax.rem(chunk, self.ring), p * 3 + (X_BIT, Y_BIT, X_BIT | Y_BIT).index(mask)
        ]

    def add_core(self, chunk):
        for load in self.loads(chunk):
            load.wait()
        slot, turn = lax.rem(chunk, self.ring), lax.rem(chunk, 2)

        def one(square, carry):
            self.held[slot, square] = (
                self.held[slot, square].astype(F32) + self.other[turn, square].astype(F32)
            ).astype(BF)
            return carry

        lax.fori_loop(0, self.held.shape[1], one, 0)
        for p, part in enumerate(self.parts):
            self.hop(chunk, p, X_BIT | Y_BIT).start()
        for p, part in enumerate(self.parts):
            self.hop(chunk, p, part[2][1]).start()

    def add_corner(self, chunk):
        slot = lax.rem(chunk, self.ring)
        for p, (low, size, order) in enumerate(self.parts):
            self.hop(chunk, p, X_BIT | Y_BIT).wait_recv()
            square = self.square(order[0])
            came = self.landed(chunk, p, X_BIT | Y_BIT)
            self.held[slot, square, :, low : low + size] = (
                self.held[slot, square, :, low : low + size].astype(F32)
                + came[:, :size].astype(F32)
            ).astype(BF)
        for p, part in enumerate(self.parts):
            self.hop(chunk, p, part[2][0]).start()

    def line_copy(self, chunk, step):
        k = self.links
        slot = lax.rem(chunk, self.ring)
        return k.copy(
            self.out_line.at[slot, lax.rem(k.z + step, k.nn)],
            self.in_line.at[slot, step - 1],
            self.number(chunk, 6 + step),
            k.along(step),
        )

    def add_square(self, chunk):
        slot = lax.rem(chunk, self.ring)
        home = self.square(0)
        for p, (low, size, order) in enumerate(self.parts):
            total = self.held[slot, home, :, low : low + size].astype(F32)
            for mask in order:
                self.hop(chunk, p, mask).wait_recv()
                total = total + self.landed(chunk, p, mask)[:, :size].astype(F32)
            for z in range(self.links.nn):
                self.out_line[slot, z, : self.rows, low : low + size] = total[
                    z * self.rows : (z + 1) * self.rows
                ].astype(BF)
        for step in range(1, self.links.nn):
            self.line_copy(chunk, step).start()
        if not self.traded:
            self.core_copy(chunk).wait_send()
        for p in range(len(self.parts)):
            for mask in (X_BIT, Y_BIT, X_BIT | Y_BIT):
                self.hop(chunk, p, mask).wait_send()

    def total(self, chunk):
        slot = lax.rem(chunk, self.ring)
        total = self.out_line[slot, self.links.z, : self.rows].astype(F32)
        for step in range(1, self.links.nn):
            self.line_copy(chunk, step).wait_recv()
            total = total + self.in_line[slot, step - 1, : self.rows].astype(F32)
        return total

    def pump(self, index, out, made=None):
        index = jnp.int32(index)
        made = self.chunks if made is None else made
        idle = index >= made if made < self.chunks else False
        steps = (self.fetch, self.add_core, self.add_corner, self.add_square, self.finish)
        for lag, action in zip(LAG, steps):
            chunk = index - lag
            ready = jnp.logical_and(chunk >= 0, chunk < self.chunks)
            if made < self.chunks:
                ready = jnp.logical_and(ready, jnp.logical_not(idle))

            @pl.when(ready)
            def _(chunk=chunk, action=action):
                action(chunk, out) if action == self.finish else action(chunk)

    def finish(self, chunk, out):
        out[chunk] = self.total(chunk)
        for step in range(1, self.links.nn):
            self.line_copy(chunk, step).wait_send()


def scatter_small(links, grads, out, came, round_in, line_in, mine):
    core = lax.rem(links.w, 2)
    home = links.w // 2
    number = links.fresh()
    links.send(grads.at[:, 1 - core], came, number, links.wide(1))
    links.sent[-1].wait_recv()
    mine[...] = grads[:, core] + came[...]
    masks = (X_BIT, Y_BIT, X_BIT | Y_BIT)
    copies = []
    for index, mask in enumerate(masks):
        number = links.fresh()
        links.send(
            mine.at[jnp.bitwise_xor(links.w, mask) // 2], round_in.at[index], number, links.wide(mask)
        )
        copies.append(links.sent[-1])
    for copy in copies:
        copy.wait()
    del links.sent[-3:]
    mine[home] = mine[home] + round_in[0] + round_in[1] + round_in[2]
    copies = []
    for step in range(1, links.nn):
        number = links.fresh()
        links.send(
            mine.at[home, pl.ds(lax.rem(links.z + step, links.nn) * 8, 8)],
            line_in.at[step - 1],
            number,
            links.along(step),
        )
        copies.append(links.sent[-1])
    total = mine[home, pl.ds(pl.multiple_of(links.z * 8, 8), 8)]
    for step in range(1, links.nn):
        copies[step - 1].wait_recv()
        total = total + line_in[step - 1]
    out[...] = total


def padded(rows):
    return (rows + 15) // 16 * 16


def scatter_slots(squares, nn, rows, columns, ring):
    half = columns // 2
    return [
        pltpu.VMEM((ring, squares, nn * rows, columns), BF),
        pltpu.VMEM((2, squares, nn * rows, columns), BF),
        pltpu.VMEM((ring, 6, nn * rows, half), BF),
        pltpu.VMEM((ring, nn, padded(rows), columns), BF),
        pltpu.VMEM((ring, nn - 1, padded(rows), columns), BF),
        pltpu.SemaphoreType.DMA((2, 2)),
    ]


def norm_pull(values, gain, grad):
    scale = lax.rsqrt(jnp.mean(values * values, axis=-1, keepdims=True) + RMS_EPSILON)
    scaled = grad * gain
    along = jnp.mean(scaled * values, axis=-1, keepdims=True)
    share = grad * values * scale
    return scale * scaled - values * (scale * scale * scale * along), share


def fold_rows(values):
    return jnp.sum(values.reshape(values.shape[0] // 8, 8, values.shape[1]), axis=0)


def pack_row(row, first, each, devices):
    total = row.shape[1]
    shape = (128, total)
    pick = jnp.where(iota(shape, 0) == first + lax.rem(iota(shape, 1), each), 1.0, 0.0)
    shape = (devices, total)
    mine = jnp.where(iota(shape, 1) // each == iota(shape, 0), row, 0.0)
    return lax.dot_general(
        mine,
        pick,
        (((1,), (1,)), ((), ())),
        preferred_element_type=F32,
        precision=lax.Precision.HIGHEST,
    )


def backward_kernel(nn, few_facts, many_facts, *refs):
    occupied, refs = refs[0], refs[1:]
    (
        tokens,
        rel_hbm,
        lay_hbm,
        grad_h,
        small_h,
        query_h,
        key_h,
        value_h,
        output_h,
        gate_h,
        up_h,
        down_h,
        na_t,
        q_t,
        k_h,
        v_h,
        att_t,
        hid_h,
        nf_t,
        mix_h,
        probs_h,
        slope_h,
        act_h,
        few_grads,
        few_came,
    ) = refs[:25]
    refs = refs[25:]
    (out_h, rows_out, few_out, many_out, small_out, many_grads, many_came) = refs[:7]
    few_slots, many_slots, refs = refs[7:13], refs[13:19], refs[19:]
    (
        x,
        rel,
        lay,
        small,
        gains,
        grad,
        left,
        acc,
        hid,
        wd_s,
        wg_s,
        wu_s,
        slope_s,
        act_s,
        many_stage,
        branch,
        w_one,
        pull,
        pull_t,
        qt,
        k,
        v,
        probs,
        pieces,
        onehot,
        table,
        sums,
        small_grads,
        small_came,
        small_round,
        small_line,
        small_mine,
        send_sem,
        recv_sem,
        local_sem,
        tile_sem,
        stage_sem,
        probs_sem,
    ) = refs
    slots, width = x.shape
    links = Links(nn, send_sem, recv_sem)
    numbers = iter(range(64))

    def move(src, dst):
        copy = pltpu.make_async_copy(src, dst, local_sem.at[next(numbers)])
        copy.start()
        return copy

    ffn = mix_h.shape[1]
    tiles = ffn // TILE
    grad_in = move(grad_h, grad)
    nf_in = move(nf_t, left)

    def tile_copies(tile):
        turn = lax.rem(tile, 2)
        at = pl.ds(pl.multiple_of(tile * TILE, TILE), TILE)
        return [
            pltpu.make_async_copy(src, dst.at[turn], tile_sem.at[turn, index])
            for index, (src, dst) in enumerate(
                (
                    (down_h.at[at], wd_s),
                    (gate_h.at[:, at], wg_s),
                    (up_h.at[:, at], wu_s),
                    (slope_h.at[:, at], slope_s),
                    (act_h.at[:, at], act_s),
                )
            )
        ]

    for copy in tile_copies(0):
        copy.start()
    later = [move(hid_h, hid), move(small_h, small), move(att_t, pull_t), move(output_h, w_one.at[0])]
    later += [move(q_t, qt), move(k_h, k), move(v_h, v)]
    last = [move(tokens, x), move(rel_hbm, rel), move(lay_hbm, lay), move(value_h, w_one.at[1])]
    links.greet()
    few = Scatter(links, *few_facts, few_grads, few_came, few_slots, 0, traded=True)
    base = few_facts[0] * SCATTER_COPIES
    many = Scatter(links, *many_facts, many_grads, many_came, many_slots, base)
    links.used = base + many_facts[0] * SCATTER_COPIES

    def many_copy(chunk):
        turn = lax.rem(chunk, 2)
        return pltpu.make_async_copy(many_stage.at[turn], many.grads.at[chunk], stage_sem.at[turn])

    grad_in.wait()
    nf_in.wait()

    def put(chunk, low, value):
        shape = many_stage.shape[1:4]
        many_stage[lax.rem(chunk, 2), :, :, :, low : low + value.shape[1]] = value.astype(BF).reshape(
            shape + (value.shape[1],)
        )

    def ffn_tile(tile, carry):
        turn = lax.rem(tile, 2)

        @pl.when(tile + 1 < tiles)
        def _():
            for copy in tile_copies(tile + 1):
                copy.start()

        for copy in tile_copies(tile):
            copy.wait()
        grad_mixed = dot_nt(grad[...], wd_s[turn])
        gate_low = (grad_mixed * slope_s[turn].astype(F32)).astype(BF)
        up_low = (grad_mixed * act_s[turn].astype(F32)).astype(BF)
        put(tile, 0, dot(left[...], gate_low))
        put(tile, TILE, dot(left[...], up_low))
        many_copy(tile).start()

        @pl.when(tile >= 1)
        def _():
            many_copy(tile - 1).wait()
            many.trade(tile - 1)

        for part in range(width // TILE):
            at = slice(part * TILE, (part + 1) * TILE)
            more = dot_nt(gate_low, wg_s[turn, at, :]) + dot_nt(up_low, wu_s[turn, at, :])
            acc[:, at] = jnp.where(tile == 0, 0.0, acc[:, at]) + more
        few.pump(tile, few_out)
        many.pump(tile - FFN_LAG, many_out)
        return carry

    lax.fori_loop(0, tiles, ffn_tile, 0)
    many_copy(tiles - 1).wait()
    many.trade(tiles - 1)
    done = tiles - FFN_LAG
    for copy in later:
        copy.wait()
    na_in = move(na_t, left)
    rows = small.reshape(small.shape[0] // 8, 8, 128)[:, 0, :]
    devices = rows.shape[0]
    each = width // devices
    gains[0:1, :] = unpack_row(rows, 0, each, width)
    gains[1:2, :] = unpack_row(rows, each, each, width)

    def norm_two(index, total):
        at = pl.ds(pl.multiple_of(index * 64, 64), 64)
        part, share = norm_pull(hid[at, :], gains[1:2, :], acc[at, :])
        whole = grad[at, :].astype(F32) + part
        hid[at, :] = whole
        branch[at, :] = whole.astype(BF)
        return total + fold_rows(share)

    zero = jnp.zeros((8, width), F32)
    sums[0] = lax.fori_loop(0, slots // 64, norm_two, zero)

    def emit(chunk, value):
        put(chunk, 0, value)
        many_copy(chunk).start()

    def flush(chunk):
        many_copy(chunk).wait()
        many.trade(chunk)

    wide = many.columns
    for part in range(width // wide):
        emit(tiles + part, dot(pull_t[...], branch[:, part * wide : (part + 1) * wide]))
    many.pump(done, many_out)
    done += 1

    def pull_tile(tile, carry):
        at = pl.ds(pl.multiple_of(tile * TILE, TILE), TILE)
        found = dot_nt(branch[...], w_one[0, at, :]).astype(BF)
        pull[:, at] = found
        pull_t[at, :] = found.T
        return carry

    lax.fori_loop(0, width // TILE, pull_tile, 0)
    for part in range(width // wide):
        flush(tiles + part)
    made = tiles + width // wide
    query_in = move(query_h, w_one.at[0])

    def probs_copy(pair):
        turn = lax.rem(pair, 2)
        return pltpu.make_async_copy(probs_h.at[pl.ds(pair * 2, 2)], probs.at[turn], probs_sem.at[turn])

    pairs = H // 2
    probs_copy(0).start()

    def attend_back(pair, carry):
        @pl.when(pair + 1 < pairs)
        def _():
            probs_copy(pair + 1).start()

        probs_copy(pair).wait()
        turn = lax.rem(pair, 2)
        at = pl.ds(pl.multiple_of(pair * 128, 128), 128)
        low = iota((slots, 128), 1) < HD
        keys, pulls, values = k[:, at], pull[:, at], v[:, at]
        found = []
        for side in range(2):
            head = pair * 2 + side
            mine = jnp.where(low if side == 0 else jnp.logical_not(low), pulls, 0)
            share = probs[turn, side]
            wanted = dot_nt(mine, values)
            share_f = share.astype(F32)
            joint = share_f * wanted
            piece = (joint - share_f * jnp.sum(joint, axis=-1, keepdims=True)).astype(BF)
            pieces[pl.ds(pl.multiple_of(head * slots, slots), slots), :] = piece
            found.append(dot(piece, keys))
            rows = pl.ds(pl.multiple_of(head * HD, HD), HD)
            qt[rows, :] = dot(qt[rows, :], piece).astype(BF)
            pull_t[rows, :] = dot(pull_t[rows, :], share).astype(BF)
        pull[:, at] = jnp.where(low, found[0], found[1]).astype(BF)
        return carry

    for half in range(width // wide):
        heads = pairs * wide // width
        first = done - half * heads

        def attend_pump(pair, carry, first=first, made=made):
            attend_back(pair, 0)
            many.pump(first + pair, many_out, made)
            return carry

        lax.fori_loop(half * heads, (half + 1) * heads, attend_pump, 0)
        done = done + heads if made == many.chunks else min(done + heads, made)
        if half == 0:
            for copy in last:
                copy.wait()
            na_in.wait()
        at = slice(half * wide, (half + 1) * wide)
        for part, (grads, turned) in enumerate(((pull_t, True), (pull, False), (qt, True))):
            chunk = tiles + width // wide + half * 3 + part
            if part:
                flush(chunk - 1)
            if turned:
                emit(chunk, dot_nt(left[...], grads[at, :]))
            else:
                emit(chunk, dot(left[...], grads[:, at]))
        flush(chunk)
        many.pump(done, many_out, made)
        done = done + 1 if made == many.chunks else min(done + 1, made)
        made = min(made + 3, many.chunks)
    table[...] = jnp.zeros_like(table)

    def table_block_back(index, carry):
        for query in range(BACK_QB):
            for which, bucket in enumerate((rel, lay)):
                row = bucket[pl.ds(index * BACK_QB + query, 1), :]
                first = (query * 2 + which) * NB
                onehot[first : first + NB, :] = ones_where(
                    jnp.broadcast_to(row, (NB, slots)) == iota((NB, slots), 0)
                )
        heads = [
            pieces[pl.ds(pl.multiple_of(head * slots + index * BACK_QB, BACK_QB), BACK_QB), :]
            for head in range(H)
        ]
        table[...] += dot_nt(onehot[...], jnp.concatenate(heads, axis=0))
        return carry

    blocks = slots // BACK_QB
    groups = 4
    def table_group(group, carry):
        lax.fori_loop(group * (blocks // groups), (group + 1) * (blocks // groups), table_block_back, 0)
        many.pump(done + group, many_out)
        return carry

    lax.fori_loop(0, groups, table_group, 0)
    done += groups
    whole = ffn // slots
    output_in = [
        move(down_h.at[:, pl.ds(part * slots, slots)], pieces.at[pl.ds(part * ffn, ffn)])
        for part in range(width // slots)
    ]
    first_mix = width // slots * ffn
    output_in += [
        move(mix_h.at[:, pl.ds(part * slots, slots)], pieces.at[pl.ds(first_mix + part * slots, slots)])
        for part in range(whole)
    ]
    output_in.append(move(mix_h.at[:, pl.ds(whole * slots, TILE)], slope_s.at[0]))
    query_in.wait()

    def turn_back(tile, carry):
        at = pl.ds(pl.multiple_of(tile * TILE, TILE), TILE)
        v[:, at] = pull_t[at, :].T
        branch[:, at] = qt[at, :].T
        return carry

    lax.fori_loop(0, width // TILE, turn_back, 0)

    def first_two(tile, carry):
        at = pl.ds(pl.multiple_of(tile * TILE, TILE), TILE)
        acc[:, at] = dot_nt(v[...], w_one[1, at, :]) + dot_nt(pull[...], w_one[0, at, :])
        return carry

    lax.fori_loop(0, width // TILE, first_two, 0)
    key_in = move(key_h, w_one.at[0])
    many.pump(done, many_out)
    done += 1
    key_in.wait()

    def third(tile, carry):
        at = pl.ds(pl.multiple_of(tile * TILE, TILE), TILE)
        acc[:, at] += dot_nt(branch[...], w_one[0, at, :])
        return carry

    lax.fori_loop(0, width // TILE, third, 0)
    many.pump(done, many_out)
    done += 1

    def norm_one(index, total):
        at = pl.ds(pl.multiple_of(index * 64, 64), 64)
        part, share = norm_pull(x[at, :].astype(F32), gains[0:1, :], acc[at, :])
        hid[at, :] += part
        return total + fold_rows(share)

    sums[1] = lax.fori_loop(0, slots // 64, norm_one, zero)
    rows_copy = move(hid, rows_out)
    output_in.append(move(hid_h, acc))
    total = table[...]
    mine = iota(total.shape, 0) // (2 * NB) == lax.rem(iota(total.shape, 1), BACK_QB)
    folded = jnp.sum(
        jnp.where(mine, total, 0.0).reshape(BACK_QB, 2 * NB, H * BACK_QB), axis=0
    )
    packed = pack_row(jnp.sum(sums[1], axis=0, keepdims=True), 0, each, devices)
    packed += pack_row(jnp.sum(sums[0], axis=0, keepdims=True), each, each, devices)
    for index in range(2):
        shape = (H * BACK_QB, 128)
        lane = 2 * each + H * index + iota(shape, 0) // BACK_QB
        pick = jnp.where(iota(shape, 1) == lane, 1.0, 0.0)
        packed += jnp.dot(
            folded[index * NB : (index + 1) * NB],
            pick,
            preferred_element_type=F32,
            precision=lax.Precision.HIGHEST,
        )
    small_grads[...] = jnp.zeros_like(small_grads)
    for device in range(devices):
        wide_at, z = divmod(device, nn)
        small_grads[wide_at // 2, wide_at % 2, z * 8 : z * 8 + 1, :] = packed[device : device + 1]
    scatter_small(links, small_grads, small_out, small_came, small_round, small_line, small_mine)

    for copy in output_in:
        copy.wait()
    valid_rows = iota((slots, 1), 0) < occupied[0] + IMG

    def output_tile(tile, carry):
        at = pl.ds(pl.multiple_of(tile * TILE, TILE), TILE)
        part, column = tile // (slots // TILE), lax.rem(tile, slots // TILE) * TILE
        column = pl.ds(pl.multiple_of(column, TILE), TILE)
        total = acc[:, at]
        for index in range(whole):
            rows = pl.ds(pl.multiple_of(part * ffn + index * slots, TILE), slots)
            mixed = pieces[first_mix + index * slots : first_mix + (index + 1) * slots, :]
            total = total + dot(mixed, pieces[rows, column])
        rows = pl.ds(pl.multiple_of(part * ffn + whole * slots, TILE), TILE)
        total = total + dot(slope_s[0], pieces[rows, column])
        x[:, at] = jnp.where(valid_rows, total, 0.0).astype(BF)
        many.pump(done + tile, many_out)
        return carry

    lax.fori_loop(0, width // TILE, output_tile, 0)
    done += width // TILE
    out_copy = move(x, out_h)

    def rest(index, carry):
        many.pump(index, many_out)
        return carry

    lax.fori_loop(done, many.chunks + LAGS, rest, 0)
    rows_copy.wait()
    out_copy.wait()
    links.finish()


def backward_all(nw, nn, counts, page, weights, saved):
    squares = nw // 2
    devices = nw * nn
    slots, width = page[0].shape
    ffn = weights[5].shape[1]
    few = (width // DOWN_PIECE, ffn // devices, DOWN_PIECE)
    many = (ffn // TILE + 8, width // devices, 2 * TILE)
    outs = [jax.ShapeDtypeStruct((slots, width), BF), jax.ShapeDtypeStruct((slots, width), F32)]
    for chunks, rows, columns in (few, many):
        outs.append(jax.ShapeDtypeStruct((chunks, rows, columns), F32))
    outs.append(jax.ShapeDtypeStruct((8, 128), F32))
    chunks, rows, columns = many
    outs.append(jax.ShapeDtypeStruct((chunks, squares, 2, nn * rows, columns), BF))
    outs.append(jax.ShapeDtypeStruct((chunks, squares, nn * rows, columns), BF))
    copies = (few[0] + many[0]) * SCATTER_COPIES + 16
    vmem = pl.BlockSpec(memory_space=pltpu.VMEM)
    hbm = pl.BlockSpec(memory_space=pl.ANY)
    low = pltpu.VMEM((slots, width), BF)
    turned = pltpu.VMEM((width, slots), BF)
    full = pltpu.VMEM((slots, width), F32)
    inputs = (counts,) + tuple(page) + tuple(weights) + tuple(saved)
    return pl.pallas_call(
        functools.partial(backward_kernel, nn, few, many),
        out_shape=outs,
        in_specs=[pl.BlockSpec(memory_space=pltpu.SMEM)] + [hbm] * (len(inputs) - 1),
        out_specs=[hbm, hbm, vmem, vmem, vmem, hbm, hbm],
        scratch_shapes=scatter_slots(squares, nn, few[1], few[2], few[0])
        + scatter_slots(squares, nn, many[1], many[2], RING)
        + [
            low,
            pltpu.VMEM((slots, slots), jnp.int32),
            pltpu.VMEM((slots, slots), jnp.int32),
            pltpu.VMEM((devices * 8, 128), F32),
            pltpu.VMEM((8, width), F32),
            low,
            turned,
            full,
            full,
            pltpu.VMEM((2, TILE, width), BF),
            pltpu.VMEM((2, width, TILE), BF),
            pltpu.VMEM((2, width, TILE), BF),
            pltpu.VMEM((2, slots, TILE), BF),
            pltpu.VMEM((2, slots, TILE), BF),
            pltpu.VMEM((2, squares, 2, nn * many[1], many[2]), BF),
            low,
            pltpu.VMEM((2, width, width), BF),
            low,
            turned,
            turned,
            low,
            low,
            pltpu.VMEM((2, 2, slots, slots), BF),
            pltpu.VMEM((H * slots, slots), BF),
            pltpu.VMEM((BACK_QB * 2 * NB, slots), BF),
            pltpu.VMEM((BACK_QB * 2 * NB, H * BACK_QB), F32),
            pltpu.VMEM((2, 8, width), F32),
            pltpu.VMEM((squares, 2, nn * 8, 128), F32),
            pltpu.VMEM((squares, nn * 8, 128), F32),
            pltpu.VMEM((3, nn * 8, 128), F32),
            pltpu.VMEM((nn - 1, 8, 128), F32),
            pltpu.VMEM((squares, nn * 8, 128), F32),
            pltpu.SemaphoreType.DMA((copies,)),
            pltpu.SemaphoreType.DMA((copies,)),
            pltpu.SemaphoreType.DMA((64,)),
            pltpu.SemaphoreType.DMA((2, 5)),
            pltpu.SemaphoreType.DMA((2,)),
            pltpu.SemaphoreType.DMA((2,)),
        ],
        compiler_params=pltpu.CompilerParams(
            collective_id=1, has_side_effects=True, vmem_limit_bytes=63 * 2**20
        ),
    )(*inputs)[:5]


def local_fast(
    nw,
    nn,
    tokens,
    w_query,
    w_key,
    w_value,
    w_output,
    w_gate,
    w_up,
    w_down,
    gain_attn,
    gain_ffn,
    rel_table,
    lay_table,
    ocr_counts,
    rel_bucket,
    lay_bucket,
    cotangent,
):
    small = jnp.concatenate([gain_attn, gain_ffn, rel_table, lay_table]).astype(F32)
    small = jnp.pad(small[None], ((0, 7), (0, 128 - small.shape[0])))
    down = jnp.pad(w_down, ((0, padded(w_down.shape[0]) - w_down.shape[0]), (0, 0)))
    page = (tokens, rel_bucket, lay_bucket)
    shards = [small, w_query, w_key, w_value, w_output, w_gate, w_up, down]
    found = forward_all(nw, nn, ocr_counts, *page, cotangent, shards, w_down.shape[0])
    weights, grad, saved = found[: len(shards)], found[len(shards)], found[len(shards) + 1 :]
    output, grad_tokens, few, many, small = backward_all(
        nw, nn, ocr_counts, page + (grad,), weights, saved
    )

    def join(stack):
        return jnp.moveaxis(stack, 0, 1).reshape(stack.shape[1], -1)

    tiles = w_gate.shape[1] // TILE
    grad_output = join(many[tiles : tiles + 2])
    grad_value, grad_query, grad_key = (join(many[tiles + 2 + part :: 3]) for part in range(3))
    gate, up = join(many[:tiles, :, :TILE]), join(many[:tiles, :, TILE:])
    cuts, at = [], 0
    for part in (gain_attn, gain_ffn, rel_table, lay_table):
        cuts.append(small[0, at : at + part.shape[0]])
        at += part.shape[0]
    grads = (grad_query, grad_key, grad_value, grad_output, gate, up, join(few))
    return (output, grad_tokens) + grads + tuple(cuts)


def local(
    tokens,
    w_query,
    w_key,
    w_value,
    w_output,
    w_gate,
    w_up,
    w_down,
    gain_attn,
    gain_ffn,
    rel_table,
    lay_table,
    ocr_counts,
    rel_bucket,
    lay_bucket,
    cotangent,
):
    slot = tokens.shape[0]
    valid = jnp.arange(slot) < ocr_counts[0] + IMG
    buckets = jnp.arange(NB)
    onehot = jnp.concatenate(
        [
            (rel_bucket[:, :, None] == buckets).astype(jnp.bfloat16),
            (lay_bucket[:, :, None] == buckets).astype(jnp.bfloat16),
        ],
        axis=2,
    )
    tokens_f = tokens.astype(jnp.float32)
    weights = gather_weights(
        w_query,
        w_key,
        w_value,
        w_output,
        w_gate,
        w_up,
        w_down,
        gain_attn,
        gain_ffn,
        rel_table,
        lay_table,
    )
    result, saved = forward_pass(tokens_f, weights, onehot, valid)
    output = jnp.where(valid[:, None], result, 0.0).astype(jnp.bfloat16)
    (
        full_query,
        full_key,
        full_value,
        full_output,
        full_gate,
        full_up,
        full_down,
        full_gain_attn,
        full_gain_ffn,
        full_rel,
        full_lay,
    ) = weights
    (
        normed_attn,
        queries,
        keys_all,
        values_all,
        log_totals,
        attended,
        hidden_one,
        normed_ffn,
        gate_act,
        up_proj,
        mixed,
    ) = saved
    grad_result = jnp.where(valid[:, None], cotangent.astype(jnp.float32), 0.0)
    grad_low = grad_result.astype(jnp.bfloat16)
    grad_down = contract_rows(mixed, grad_low)
    grad_mixed = contract_cols(grad_low, full_down)
    gated_value, gated_pull = jax.vjp(gated_product, gate_act, up_proj)
    grad_gate_act, grad_up_proj = gated_pull(grad_mixed)
    gate_low = grad_gate_act.astype(jnp.bfloat16)
    up_low = grad_up_proj.astype(jnp.bfloat16)
    grad_gate = contract_rows(normed_ffn, gate_low)
    grad_up = contract_rows(normed_ffn, up_low)
    grad_normed_ffn = contract_cols(gate_low, full_gate) + contract_cols(up_low, full_up)
    norm_value, norm_pull = jax.vjp(rms_scale, hidden_one, full_gain_ffn.astype(jnp.float32))
    grad_hidden_part, grad_gain_ffn = norm_pull(grad_normed_ffn)
    grad_hidden = grad_result + grad_hidden_part
    branch_low = grad_hidden.astype(jnp.bfloat16)
    grad_output = contract_rows(attended, branch_low)
    grad_attended = contract_cols(branch_low, full_output).astype(jnp.bfloat16)
    grad_queries, grad_keys, grad_values, grad_table_all = attention_backward(
        queries,
        keys_all,
        values_all,
        log_totals,
        grad_attended,
        table_pair(full_rel, full_lay),
        onehot,
        valid,
    )
    grad_rel = grad_table_all[:NB].reshape(NB * H)
    grad_lay = grad_table_all[NB:].reshape(NB * H)
    grad_query = contract_rows(normed_attn, grad_queries)
    grad_key = contract_rows(normed_attn, grad_keys)
    grad_value = contract_rows(normed_attn, grad_values)
    grad_normed_attn = (
        contract_cols(grad_queries, full_query)
        + contract_cols(grad_keys, full_key)
        + contract_cols(grad_values, full_value)
    )
    input_value, input_pull = jax.vjp(rms_scale, tokens_f, full_gain_attn.astype(jnp.float32))
    grad_input_part, grad_gain_attn = input_pull(grad_normed_attn)
    grad_tokens = grad_hidden + grad_input_part
    owned = (
        lax.psum_scatter(grad_query, ("wide", "narrow"), scatter_dimension=0, tiled=True),
        lax.psum_scatter(grad_key, ("wide", "narrow"), scatter_dimension=0, tiled=True),
        lax.psum_scatter(grad_value, ("wide", "narrow"), scatter_dimension=0, tiled=True),
        lax.psum_scatter(grad_output, ("wide", "narrow"), scatter_dimension=0, tiled=True),
        lax.psum_scatter(grad_gate, ("wide", "narrow"), scatter_dimension=0, tiled=True),
        lax.psum_scatter(grad_up, ("wide", "narrow"), scatter_dimension=0, tiled=True),
        lax.psum_scatter(grad_down, ("wide", "narrow"), scatter_dimension=0, tiled=True),
        lax.psum_scatter(grad_gain_attn, ("wide", "narrow"), scatter_dimension=0, tiled=True),
        lax.psum_scatter(grad_gain_ffn, ("wide", "narrow"), scatter_dimension=0, tiled=True),
        lax.psum_scatter(grad_rel, ("wide", "narrow"), scatter_dimension=0, tiled=True),
        lax.psum_scatter(grad_lay, ("wide", "narrow"), scatter_dimension=0, tiled=True),
    )
    return (
        output,
        grad_tokens,
        owned[0],
        owned[1],
        owned[2],
        owned[3],
        owned[4],
        owned[5],
        owned[6],
        owned[7],
        owned[8],
        owned[9],
        owned[10],
    )


def solution(mesh):
    nw, nn = mesh.shape["wide"], mesh.shape["narrow"]

    def body(*args):
        if nw == 8 and nw * nn == NB and args[1].shape[0] % 16 == 0:
            return local_fast(nw, nn, *args)
        return local(*args)

    placed = (
        P(("wide", "narrow"), None),
        P(("wide", "narrow"), None),
        P(("wide", "narrow"), None),
        P(("wide", "narrow"), None),
        P(("wide", "narrow"), None),
        P(("wide", "narrow"), None),
        P(("wide", "narrow"), None),
        P(("wide", "narrow"), None),
        P(("wide", "narrow")),
        P(("wide", "narrow")),
        P(("wide", "narrow")),
        P(("wide", "narrow")),
        P(("wide", "narrow")),
        P(("wide", "narrow"), None),
        P(("wide", "narrow"), None),
        P(("wide", "narrow"), None),
    )
    return jax.shard_map(
        body,
        mesh=mesh,
        in_specs=placed,
        out_specs=(
            P(("wide", "narrow"), None),
            P(("wide", "narrow"), None),
            P(("wide", "narrow"), None),
            P(("wide", "narrow"), None),
            P(("wide", "narrow"), None),
            P(("wide", "narrow"), None),
            P(("wide", "narrow"), None),
            P(("wide", "narrow"), None),
            P(("wide", "narrow"), None),
            P(("wide", "narrow")),
            P(("wide", "narrow")),
            P(("wide", "narrow")),
            P(("wide", "narrow")),
        ),
        check_vma=False,
    )
```

```python
import functools

import jax
import jax.numpy as jnp
from jax import lax
from jax.experimental import pallas as pl
from jax.experimental.pallas import tpu as pltpu
from jax.sharding import PartitionSpec as P

H = 16
HD = 64
NB = 32
IMG = 196
RING = 6
SCATTER_COPIES = 10
LAG = (0, 1, 2, 4, 6)
LAGS = LAG[-1]
FFN_LAG = 6
BACK_QB = 16
WIDE = 512
DOWN_PIECE = 256
REST = 512
UP_TILES = 6
TILE = 256
QB = 8
GELU_SCALE = 0.7978845608028654
GELU_CUBE = 0.044715


RMS_EPSILON = 1e-06
MASK_SCORE = -1000000000.0
HEAD_GROUP = 4


def rms_scale(values, gain):
    return (
        values * lax.rsqrt(jnp.mean(values * values, axis=-1, keepdims=True) + RMS_EPSILON) * gain
    )


def gated_product(gate_act, up_proj):
    return jax.nn.gelu(gate_act, approximate=True) * up_proj


def product(left, right):
    return jnp.dot(left, right, preferred_element_type=jnp.float32)


def contract_rows(left, right):
    return lax.dot_general(
        left, right, (((0,), (0,)), ((), ())), preferred_element_type=jnp.float32
    )


def contract_cols(left, right):
    return lax.dot_general(
        left, right, (((1,), (1,)), ((), ())), preferred_element_type=jnp.float32
    )


def split_heads(matrix):
    return jnp.moveaxis(matrix.reshape(matrix.shape[0], H // HEAD_GROUP, HEAD_GROUP, HD), 1, 0)


def join_heads(stacked):
    return jnp.moveaxis(stacked, 0, 1).reshape(stacked.shape[1], H * HD)


def group_tables(table_all):
    return jnp.moveaxis(table_all.reshape(2 * NB, H // HEAD_GROUP, HEAD_GROUP), 1, 0)


def group_scores(query_group, key_group, table_group, onehot, valid):
    scores = jnp.einsum("ihd,jhd->hij", query_group, key_group, preferred_element_type=jnp.float32)
    scores = scores + jnp.einsum(
        "ijb,bh->hij", onehot, table_group, preferred_element_type=jnp.float32
    )
    return jnp.where(valid[None, None, :], scores, MASK_SCORE)


def gather_weights(
    w_query,
    w_key,
    w_value,
    w_output,
    w_gate,
    w_up,
    w_down,
    gain_attn,
    gain_ffn,
    rel_table,
    lay_table,
):
    return (
        lax.all_gather(w_query, ("wide", "narrow"), axis=0, tiled=True),
        lax.all_gather(w_key, ("wide", "narrow"), axis=0, tiled=True),
        lax.all_gather(w_value, ("wide", "narrow"), axis=0, tiled=True),
        lax.all_gather(w_output, ("wide", "narrow"), axis=0, tiled=True),
        lax.all_gather(w_gate, ("wide", "narrow"), axis=0, tiled=True),
        lax.all_gather(w_up, ("wide", "narrow"), axis=0, tiled=True),
        lax.all_gather(w_down, ("wide", "narrow"), axis=0, tiled=True),
        lax.all_gather(gain_attn, ("wide", "narrow"), axis=0, tiled=True),
        lax.all_gather(gain_ffn, ("wide", "narrow"), axis=0, tiled=True),
        lax.all_gather(rel_table, ("wide", "narrow"), axis=0, tiled=True),
        lax.all_gather(lay_table, ("wide", "narrow"), axis=0, tiled=True),
    )


def table_pair(full_rel, full_lay):
    return jnp.concatenate([full_rel.reshape(NB, H), full_lay.reshape(NB, H)], axis=0)


def forward_pass(tokens_f, weights, onehot, valid):
    (
        full_query,
        full_key,
        full_value,
        full_output,
        full_gate,
        full_up,
        full_down,
        full_gain_attn,
        full_gain_ffn,
        full_rel,
        full_lay,
    ) = weights
    normed_attn = rms_scale(tokens_f, full_gain_attn.astype(jnp.float32)).astype(jnp.bfloat16)
    queries = product(normed_attn, full_query).astype(jnp.bfloat16)
    keys_all = product(normed_attn, full_key).astype(jnp.bfloat16)
    values_all = product(normed_attn, full_value).astype(jnp.bfloat16)

    def forward_one_group(operands):
        query_group, key_group, value_group, table_group = operands
        scores = group_scores(query_group, key_group, table_group, onehot, valid)
        peak = jnp.max(scores, axis=-1, keepdims=True)
        expo = jnp.exp(scores - peak)
        total = jnp.sum(expo, axis=-1, keepdims=True)
        probs_low = (expo / total).astype(jnp.bfloat16)
        attended_group = jnp.einsum(
            "hij,jhd->ihd", probs_low, value_group, preferred_element_type=jnp.float32
        )
        return (attended_group.astype(jnp.bfloat16), (peak + jnp.log(total))[..., 0])

    stacked, log_totals = lax.map(
        forward_one_group,
        (
            split_heads(queries),
            split_heads(keys_all),
            split_heads(values_all),
            group_tables(table_pair(full_rel, full_lay)),
        ),
    )
    attended = join_heads(stacked)
    hidden_one = tokens_f + product(attended, full_output)
    normed_ffn = rms_scale(hidden_one, full_gain_ffn.astype(jnp.float32)).astype(jnp.bfloat16)
    gate_act = product(normed_ffn, full_gate)
    up_proj = product(normed_ffn, full_up)
    mixed = gated_product(gate_act, up_proj).astype(jnp.bfloat16)
    result = hidden_one + product(mixed, full_down)
    return (
        result,
        (
            normed_attn,
            queries,
            keys_all,
            values_all,
            log_totals,
            attended,
            hidden_one,
            normed_ffn,
            gate_act,
            up_proj,
            mixed,
        ),
    )


def attention_backward(
    queries, keys_all, values_all, log_totals, grad_attended, table_all, onehot, valid
):

    def attention_one_group(operands):
        query_group, key_group, value_group, table_group, lse_group, grad_group = operands
        scores = group_scores(query_group, key_group, table_group, onehot, valid)
        probs = jnp.exp(scores - lse_group[..., None])
        probs_low = probs.astype(jnp.bfloat16)
        grad_values = jnp.einsum(
            "hij,ihd->jhd", probs_low, grad_group, preferred_element_type=jnp.float32
        )
        grad_probs = jnp.einsum(
            "ihd,jhd->hij", grad_group, value_group, preferred_element_type=jnp.float32
        )
        grad_scores = (
            probs * (grad_probs - jnp.sum(probs * grad_probs, axis=-1, keepdims=True))
        ).astype(jnp.bfloat16)
        grad_queries = jnp.einsum(
            "hij,jhd->ihd", grad_scores, key_group, preferred_element_type=jnp.float32
        )
        grad_keys = jnp.einsum(
            "hij,ihd->jhd", grad_scores, query_group, preferred_element_type=jnp.float32
        )
        grad_table = jnp.einsum(
            "hij,ijb->bh", grad_scores, onehot, preferred_element_type=jnp.float32
        )
        return (
            grad_queries.astype(jnp.bfloat16),
            grad_keys.astype(jnp.bfloat16),
            grad_values.astype(jnp.bfloat16),
            grad_table,
        )

    grad_q_all, grad_k_all, grad_v_all, grad_tables = lax.map(
        attention_one_group,
        (
            split_heads(queries),
            split_heads(keys_all),
            split_heads(values_all),
            group_tables(table_all),
            log_totals,
            split_heads(grad_attended),
        ),
    )
    grad_table_all = jnp.moveaxis(grad_tables, 0, 1).reshape(2 * NB, H)
    return (join_heads(grad_q_all), join_heads(grad_k_all), join_heads(grad_v_all), grad_table_all)


MESH_ID = pl.DeviceIdType.MESH
BF = jnp.bfloat16
F32 = jnp.float32
X_BIT = 2
Y_BIT = 4
PARTS = ((X_BIT, Y_BIT), (Y_BIT, X_BIT))


class Links:
    def __init__(self, nn, send_sem, recv_sem):
        self.nn = nn
        self.w = lax.axis_index("wide")
        self.z = lax.axis_index("narrow")
        self.send_sem = send_sem
        self.recv_sem = recv_sem
        self.used = 0
        self.sent = []

    def fresh(self):
        self.used += 1
        return self.used - 1

    def wide(self, bit):
        return (jnp.bitwise_xor(self.w, bit), self.z)

    def along(self, step):
        return (self.w, lax.rem(self.z + step, self.nn))

    def copy(self, src, dst, number, device):
        return pltpu.make_async_remote_copy(
            src_ref=src,
            dst_ref=dst,
            send_sem=self.send_sem.at[number],
            recv_sem=self.recv_sem.at[number],
            device_id=device,
            device_id_type=MESH_ID,
        )

    def send(self, src, dst, number, device):
        copy = self.copy(src, dst, number, device)
        copy.start()
        self.sent.append(copy)

    def greet(self):
        barrier = pltpu.get_barrier_semaphore()
        others = [self.wide(bit) for bit in (1, X_BIT, Y_BIT)]
        others += [self.along(step) for step in range(1, self.nn)]
        for other in others:
            pl.semaphore_signal(barrier, inc=1, device_id=other, device_id_type=MESH_ID)
        pl.semaphore_wait(barrier, len(others))

    def finish(self):
        for copy in self.sent:
            copy.wait_send()


class Gather:
    def __init__(self, links, shard, full, rows, window, parts, local_sem, line=None, merged=None):
        self.links, self.shard, self.full, self.rows, self.parts = links, shard, full, rows, parts
        self.window = window
        self.local_sem, self.line, self.merged = local_sem, line, merged
        nn = links.nn
        self.block = rows * nn
        self.line_ids = [links.fresh() for _ in range(1, nn)]
        self.part_ids = {
            (p, mask): links.fresh()
            for p in range(len(parts))
            for mask in (X_BIT, Y_BIT, X_BIT | Y_BIT)
        }
        self.core_ids = {mask: links.fresh() for mask in (0, X_BIT, Y_BIT, X_BIT | Y_BIT)}

    def place(self, w, z):
        if self.line is not None:
            return self.line.at[z]
        return self.full.at[pl.ds((w * self.links.nn + z) * self.rows, self.rows), pl.ds(*self.window)]

    def span(self, mask, part=None):
        rows = pl.ds(jnp.bitwise_xor(self.links.w, mask) * self.block, self.block)
        low, size = self.window if part is None else self.parts[part][:2]
        return self.full.at[rows, pl.ds(low, size)]

    def own(self):
        return pltpu.make_async_copy(
            self.shard, self.place(self.links.w, self.links.z), self.local_sem
        )

    def start(self):
        k = self.links
        self.own().start()
        for step in range(1, k.nn):
            k.send(self.shard, self.place(k.w, k.z), self.line_ids[step - 1], k.along(step))

    def ready(self):
        k = self.links
        self.own().wait()
        for step in range(1, k.nn):
            came = lax.rem(k.z - step + k.nn, k.nn)
            k.copy(
                self.shard, self.place(k.w, came), self.line_ids[step - 1], k.along(step)
            ).wait_recv()
        if self.line is not None:
            whole = jnp.concatenate(
                [self.line[z, : self.rows].astype(F32) for z in range(k.nn)], axis=0
            )
            self.merged[...] = whole.astype(BF)
            move = pltpu.make_async_copy(self.merged, self.span(0), self.local_sem)
            move.start()
            move.wait()

    def spread(self):
        k = self.links
        for p, part in enumerate(self.parts):
            for bit in part[2]:
                k.send(self.span(0, p), self.span(0, p), self.part_ids[p, bit], k.wide(bit))
        k.send(self.span(0), self.span(0), self.core_ids[0], k.wide(1))

    def arrive(self, p, mask):
        k = self.links
        k.copy(
            self.span(mask, p), self.span(mask, p), self.part_ids[p, mask], k.wide(X_BIT)
        ).wait_recv()

    def forward(self):
        k = self.links
        for p, part in enumerate(self.parts):
            first, second = part[2]
            self.arrive(p, first)
            both = first | second
            k.send(self.span(first, p), self.span(first, p), self.part_ids[p, both], k.wide(second))

    def settle(self):
        k = self.links
        for p, part in enumerate(self.parts):
            self.arrive(p, part[2][1])
        for mask in (X_BIT, Y_BIT):
            k.send(self.span(mask), self.span(mask), self.core_ids[mask], k.wide(1))

    def last(self):
        k = self.links
        both = X_BIT | Y_BIT
        for p in range(len(self.parts)):
            self.arrive(p, both)
        k.send(self.span(both), self.span(both), self.core_ids[both], k.wide(1))

    def done(self):
        k = self.links
        for mask, number in self.core_ids.items():
            place = self.span(mask | 1)
            k.copy(place, place, number, k.wide(1)).wait_recv()


def halves(columns, first=0):
    low = columns // 256 * 128
    return ((first, low, PARTS[0]), (first + low, columns - low, PARTS[1]))


class GatherSquare:
    def __init__(self, links, shard, full, rows, window, local_sem, square, lines, merged):
        self.links, self.shard, self.full, self.rows, self.window = links, shard, full, rows, window
        self.square, self.lines, self.merged, self.local_sem = square, lines, merged, local_sem
        self.parts = halves(window[1])
        self.block = rows * links.nn
        self.part_ids = {
            (p, mask): links.fresh()
            for p in range(len(self.parts))
            for mask in (X_BIT, Y_BIT, X_BIT | Y_BIT)
        }
        self.line_ids = [links.fresh() for _ in range(1, links.nn)]
        self.core_ids = [links.fresh() for _ in range(square.shape[0])]

    def spot(self, mask, p):
        low, size = self.parts[p][:2]
        return self.square.at[jnp.bitwise_xor(self.links.w, mask) // 2, :, pl.ds(low, size)]

    def own(self):
        return pltpu.make_async_copy(
            self.shard, self.square.at[self.links.w // 2], self.local_sem.at[0]
        )

    def start(self):
        k = self.links
        self.own().start()
        for p, (low, size, order) in enumerate(self.parts):
            for bit in order:
                k.send(self.shard.at[:, pl.ds(low, size)], self.spot(0, p), self.part_ids[p, bit], k.wide(bit))

    def arrive(self, p, mask):
        k = self.links
        k.copy(self.spot(mask, p), self.spot(mask, p), self.part_ids[p, mask], k.wide(X_BIT)).wait_recv()

    def forward(self):
        k = self.links
        for p, (low, size, (first, second)) in enumerate(self.parts):
            self.arrive(p, first)
            k.send(self.spot(first, p), self.spot(first, p), self.part_ids[p, first | second], k.wide(second))
        for p, (low, size, (first, second)) in enumerate(self.parts):
            self.arrive(p, second)

    def keep(self):
        return pltpu.make_async_copy(self.square, self.lines.at[self.links.z], self.local_sem.at[0])

    def line(self):
        k = self.links
        self.own().wait()
        for p in range(len(self.parts)):
            self.arrive(p, X_BIT | Y_BIT)
        self.keep().start()
        for step in range(1, k.nn):
            k.send(self.square, self.lines.at[k.z], self.line_ids[step - 1], k.along(step))

    def rows_of(self, square, core):
        rows = pl.ds((square * 2 + core) * self.block, self.block)
        return self.full.at[rows, pl.ds(*self.window)]

    def out(self, square):
        core = lax.rem(self.links.w, 2)
        return pltpu.make_async_copy(
            self.merged.at[square], self.rows_of(square, core), self.local_sem.at[1 + square]
        )

    def join(self):
        k = self.links
        self.keep().wait()
        for step in range(1, k.nn):
            came = lax.rem(k.z - step + k.nn, k.nn)
            k.copy(self.square, self.lines.at[came], self.line_ids[step - 1], k.along(step)).wait_recv()

        def one(square, carry):
            whole = jnp.concatenate(
                [self.lines[z, square, : self.rows].astype(F32) for z in range(k.nn)], axis=0
            )
            self.merged[square] = whole.astype(BF)
            return carry

        lax.fori_loop(0, self.merged.shape[0], one, 0)
        core = lax.rem(k.w, 2)
        for square, number in enumerate(self.core_ids):
            self.out(square).start()
            k.send(self.merged.at[square], self.rows_of(square, core), number, k.wide(1))

    def done(self):
        k = self.links
        core = lax.rem(k.w, 2)
        for square, number in enumerate(self.core_ids):
            self.out(square).wait()
            k.copy(self.merged.at[square], self.rows_of(square, 1 - core), number, k.wide(1)).wait_recv()


def dot(left, right):
    return jnp.dot(left, right, preferred_element_type=F32)


def dot_nt(left, right):
    return lax.dot_general(left, right, (((1,), (1,)), ((), ())), preferred_element_type=F32)


def dot_tn(left, right):
    return lax.dot_general(left, right, (((0,), (0,)), ((), ())), preferred_element_type=F32)


def iota(shape, dimension):
    return lax.broadcasted_iota(jnp.int32, shape, dimension)


def ones_where(mask):
    return jnp.where(mask, 1.0, 0.0).astype(BF)


def unpack_row(rows, first, each, total):
    devices = rows.shape[0]
    pick = ones_where(iota((128, total), 0) == first + lax.rem(iota((128, total), 1), each))
    spread = dot(rows.astype(BF), pick)
    mine = iota((devices, total), 1) // each == iota((devices, total), 0)
    return jnp.sum(jnp.where(mine, spread, 0.0), axis=0, keepdims=True)


def table_block(rows, first):
    pick_shape = (H * QB, 128)
    total = None
    for index in range(2):
        lane = first + H * index + iota(pick_shape, 0) // QB
        pick = ones_where(iota(pick_shape, 1) == lane)
        table = dot_nt(pick, rows.astype(BF)).astype(BF)
        wide = (NB, QB * 2 * NB)
        spread = dot(table, ones_where(lax.rem(iota(wide, 1), 2 * NB) == iota(wide, 0) + NB * index))
        total = spread if total is None else total + spread
    shape = (H * QB, QB * 2 * NB)
    mine = lax.rem(iota(shape, 0), QB) == iota(shape, 1) // (2 * NB)
    return jnp.where(mine, total, 0.0).astype(BF)


def bucket_ones(rel, lay, onehot, block):
    width = rel.shape[1]
    rows = iota((NB, width), 0)
    for query in range(QB):
        for index, bucket in enumerate((rel, lay)):
            row = bucket[pl.ds(block * QB + query, 1), :]
            low = (query * 2 + index) * NB
            onehot[low : low + NB, :] = ones_where(jnp.broadcast_to(row, (NB, width)) == rows)


def forward_kernel(nn, shapes, *refs):
    count = len(shapes)
    occupied, tokens, rel_hbm, lay_hbm, cotangent = refs[:5]
    shards = refs[5 : 5 + count]
    refs = refs[5 + count :]
    fulls, refs = refs[:count], refs[count:]
    (grad_h, na_t, q_t, k_h, v_h, att_t, hid_h, nf_t, mix_h, probs_h, slope_h, act_h) = refs[:12]
    down_grads, down_came, refs = refs[12], refs[13], refs[14:]
    (
        line,
        merged,
        x,
        rel,
        lay,
        small,
        lhs,
        onehot,
        bias,
        na,
        q,
        k,
        v,
        att,
        hid,
        nf,
        mix,
        slope,
        act,
        probs,
        w_one,
        w_wide,
        grad,
        down_stage,
        gains,
        turned,
        mixed_t,
        send_sem,
        recv_sem,
        gather_sem,
        local_sem,
        ring_sem,
        rest_square,
        rest_lines,
        rest_merged,
        rest_sem,
    ) = refs
    slots, width = x.shape
    links = Links(nn, send_sem, recv_sem)
    numbers = iter(range(64))

    def move(src, dst):
        copy = pltpu.make_async_copy(src, dst, local_sem.at[next(numbers)])
        copy.start()
        return copy

    arriving = [move(tokens, x), move(rel_hbm, rel), move(lay_hbm, lay)]
    grad_in = move(cotangent, grad)
    links.greet()
    g = []
    first_up = UP_TILES * TILE
    cuts = [(0, columns) for rows, columns in shapes]
    cuts[6:] = [(0, first_up), (first_up, shapes[6][1] - first_up), (0, width - REST)]
    for number, (low, columns) in enumerate(cuts):
        index = min(number, 6) if number < 8 else 7
        rows = shapes[index][0]
        odd = index == 7
        g.append(
            Gather(
                links,
                shards[index].at[:, pl.ds(low, columns)],
                w_wide.at[index - 5] if index in (5, 6) else fulls[index],
                rows,
                (low, columns),
                halves(columns, low) if columns > 128 else ((0, columns, PARTS[0]),),
                gather_sem.at[number],
                line if odd else None,
                merged if odd else None,
            )
        )
    rows, columns = shapes[-1]
    rest = GatherSquare(
        links,
        shards[-1].at[:, pl.ds(columns - REST, REST)],
        fulls[-1],
        rows,
        (columns - REST, REST),
        rest_sem,
        rest_square,
        rest_lines,
        rest_merged,
    )
    down_ids = [[links.fresh() for _ in range(2)] for _ in range(down_grads.shape[0])]
    small_g, q_g, k_g, v_g, o_g, gate_g, up_g, up_two_g, down_g = g
    leaving = []
    turning = {}
    ffn = mixed_t.shape[0]
    tiles = ffn // TILE
    across = slots // TILE
    pairs = H // 2
    blocks = slots // QB
    block, piece = down_stage.shape[3:]
    chunks = width // piece
    squares = down_stage.shape[1]
    valid = iota((1, slots), 1) < occupied[0] + IMG

    def turn_out(slot, source, target):
        if slot in turning:
            turning[slot].wait()

        def one(tile, carry):
            at = pl.ds(pl.multiple_of(tile * TILE, TILE), TILE)
            turned[slot, at, :] = source[:, at].T
            return carry

        lax.fori_loop(0, width // TILE, one, 0)
        turning[slot] = move(turned.at[slot], target)

    def unpack():
        rows = small.reshape(small.shape[0] // 8, 8, 128)[:, 0, :]
        each = width // rows.shape[0]
        gains[0:1, :] = unpack_row(rows, 0, each, width)
        gains[1:2, :] = unpack_row(rows, each, each, width)
        lhs[...] = table_block(rows, 2 * each)

    def normalise(source, row, target):
        def one(index, carry):
            at = pl.ds(pl.multiple_of(index * 64, 64), 64)
            values = source[at, :].astype(F32)
            scale = lax.rsqrt(jnp.mean(values * values, axis=-1, keepdims=True) + RMS_EPSILON)
            target[at, :] = (values * scale * gains[row : row + 1, :]).astype(BF)
            return carry

        lax.fori_loop(0, slots // 64, one, 0)

    def bias_block(block, carry):
        bucket_ones(rel, lay, onehot, block)
        found = jnp.where(valid, dot(lhs[...], onehot[...]), MASK_SCORE)
        bias[:, pl.ds(pl.multiple_of(block * QB, QB), QB), :] = found.reshape(H, QB, slots)
        return carry

    def add_bias(part, parts):
        lax.fori_loop(part * blocks // parts, (part + 1) * blocks // parts, bias_block, 0)

    def project(slot, target):
        def one(tile, carry):
            at = pl.ds(pl.multiple_of(tile * WIDE, WIDE), WIDE)
            target[:, at] = dot(na[...], w_one[slot, :, at]).astype(BF)
            return carry

        lax.fori_loop(0, width // WIDE, one, 0)

    def probs_out(pair):
        turn = lax.rem(pair, 2)
        return pltpu.make_async_copy(probs.at[turn], probs_h.at[pl.ds(pair * 2, 2)], ring_sem.at[turn])

    def attend_pair(pair, carry):
        @pl.when(pair >= 2)
        def _():
            probs_out(pair - 2).wait()

        at = pl.ds(pl.multiple_of(pair * 128, 128), 128)
        low = iota((slots, 128), 1) < HD
        queries = q[:, at]
        keys = k[:, at]
        found = []
        for side in range(2):
            mine = jnp.where(low if side == 0 else jnp.logical_not(low), queries, 0)
            scores = dot_nt(mine, keys) + bias[pair * 2 + side]
            peak = jnp.max(scores, axis=-1, keepdims=True)
            expo = jnp.exp(scores - peak)
            total = jnp.sum(expo, axis=-1, keepdims=True)
            share = (expo * (1.0 / total)).astype(BF)
            probs[lax.rem(pair, 2), side] = share
            found.append(dot(share, v[:, at]))
        att[:, at] = jnp.where(low, found[0], found[1]).astype(BF)
        probs_out(pair).start()
        return carry

    def attend(first, last):
        lax.fori_loop(first, last, attend_pair, 0)

    def output():
        def one(tile, carry):
            at = pl.ds(pl.multiple_of(tile * WIDE, WIDE), WIDE)
            hid[:, at] = x[:, at].astype(F32) + dot(att[...], w_one[1, :, at])
            return carry

        lax.fori_loop(0, width // WIDE, one, 0)
        leaving.append(move(hid, hid_h))

    def keep_valid():
        valid_rows = iota((slots, 1), 0) < occupied[0] + IMG

        def one(tile, carry):
            at = pl.ds(pl.multiple_of(tile * TILE, TILE), TILE)
            grad[:, at] = jnp.where(valid_rows, grad[:, at].astype(F32), 0.0).astype(BF)
            return carry

        lax.fori_loop(0, width // TILE, one, 0)
        leaving.append(move(grad, grad_h))

    def gate_spot(tile, second):
        at = pl.ds(pl.multiple_of(lax.rem(tile, across) * TILE, TILE), TILE)
        return bias.at[tile // across + second * (-(-tiles // across)), :, at]

    def gate_tile(tile, carry):
        at = pl.ds(pl.multiple_of(tile * TILE, TILE), TILE)
        gate = dot(nf[...], w_wide[0, :, at])
        square = gate * gate
        inner = GELU_SCALE * gate * (1.0 + GELU_CUBE * square)
        bend = jnp.tanh(inner)
        half = 0.5 * (1.0 + bend)
        gate_spot(tile, 0)[...] = gate * half
        gate_spot(tile, 1)[...] = half + 0.5 * gate * (1.0 - bend * bend) * GELU_SCALE * (
            1.0 + 3.0 * GELU_CUBE * square
        )
        return carry

    def ffn_out(tile):
        turn = lax.rem(tile, 2)
        at = pl.ds(pl.multiple_of(tile * TILE, TILE), TILE)
        return (
            pltpu.make_async_copy(slope.at[turn], slope_h.at[:, at], ring_sem.at[2 + turn]),
            pltpu.make_async_copy(act.at[turn], act_h.at[:, at], ring_sem.at[4 + turn]),
            pltpu.make_async_copy(mix.at[turn], mix_h.at[:, at], ring_sem.at[6 + turn]),
        )

    def ffn_tile(tile, carry):
        @pl.when(tile >= 2)
        def _():
            for copy in ffn_out(tile - 2):
                copy.wait()

        at = pl.ds(pl.multiple_of(tile * TILE, TILE), TILE)
        turn = lax.rem(tile, 2)
        up = dot(nf[...], w_wide[1, :, at])
        active = gate_spot(tile, 0)[...]
        rise = gate_spot(tile, 1)[...]
        mixed = (active * up).astype(BF)
        mix[turn] = mixed
        mixed_t[at, :] = mixed.T
        act[turn] = active.astype(BF)
        slope[turn] = (up * rise).astype(BF)
        for copy in ffn_out(tile):
            copy.start()
        return carry

    def down_place(chunk, half):
        return down_grads.at[chunk, pl.ds(half * squares, squares)]

    def down_copy(unit):
        half, chunk = divmod(unit, chunks)
        turn = unit % 2
        return pltpu.make_async_copy(down_stage.at[turn], down_place(chunk, half), ring_sem.at[8 + turn])

    def down_trade(unit):
        half, chunk = divmod(unit, chunks)
        core = lax.rem(links.w, 2)
        there = pl.ds(half * squares, squares)
        return links.copy(
            down_grads.at[chunk, there, 1 - core],
            down_came.at[chunk, there],
            down_ids[chunk][half],
            links.wide(1),
        )

    def down_unit(unit):
        half, chunk = divmod(unit, chunks)

        rows = slice(half * 2 * squares * block, (half + 1) * 2 * squares * block)
        found = dot(mixed_t[rows, :], grad[:, chunk * piece : (chunk + 1) * piece])
        down_stage[unit % 2] = found.astype(BF).reshape(down_stage.shape[1:])
        down_copy(unit).start()
        if unit >= 1:
            down_copy(unit - 1).wait()
            down_trade(unit - 1).start()

    small_g.start()
    q_g.start()
    rest.start()
    small_g.ready()
    small_g.spread()
    k_g.start()
    q_g.ready()
    q_g.spread()
    v_g.start()
    small_g.forward()
    small_g.settle()
    small_g.last()
    small_g.done()
    small_in = move(fulls[0], small)
    rest.forward()
    for copy in arriving:
        copy.wait()
    k_g.ready()
    k_g.spread()
    o_g.start()
    gate_g.start()
    q_g.forward()
    small_in.wait()
    unpack()
    normalise(x, 0, na)
    turn_out(0, na, na_t)
    q_g.settle()
    add_bias(0, 4)
    v_g.ready()
    v_g.spread()
    k_g.forward()
    q_g.last()
    add_bias(1, 4)
    k_g.settle()
    o_g.ready()
    o_g.spread()
    up_g.start()
    v_g.forward()
    add_bias(2, 4)
    k_g.last()
    v_g.settle()
    q_g.done()
    fetch_q = move(fulls[1], w_one.at[0])
    add_bias(3, 4)
    gate_g.ready()
    gate_g.spread()
    up_two_g.start()
    o_g.forward()
    fetch_q.wait()
    project(0, q)
    turn_out(1, q, q_t)
    k_g.done()
    fetch_k = move(fulls[2], w_one.at[1])
    v_g.last()
    fetch_k.wait()
    project(1, k)
    leaving.append(move(k, k_h))
    v_g.done()
    fetch_v = move(fulls[3], w_one.at[0])
    o_g.settle()
    fetch_v.wait()
    project(0, v)
    leaving.append(move(v, v_h))
    attend(0, 3)
    up_g.ready()
    up_g.spread()
    down_g.start()
    o_g.last()
    gate_g.forward()
    o_g.done()
    fetch_o = move(fulls[4], w_one.at[1])
    attend(3, 6)
    gate_g.settle()
    rest.line()
    attend(6, pairs)
    turn_out(0, att, att_t)
    fetch_o.wait()
    output()
    normalise(hid, 1, nf)
    turn_out(1, nf, nf_t)
    up_g.forward()
    up_two_g.ready()
    up_two_g.spread()
    grad_in.wait()
    keep_valid()
    down_g.ready()
    up_g.settle()
    gate_g.last()
    gate_g.done()
    leaving.append(move(w_wide.at[0], fulls[5]))
    lax.fori_loop(0, tiles, gate_tile, 0)
    up_g.last()
    up_two_g.forward()
    down_g.spread()
    up_g.done()
    lax.fori_loop(0, UP_TILES, ffn_tile, 0)
    up_two_g.settle()
    down_unit(0)
    down_unit(1)
    down_unit(2)
    down_unit(3)
    up_two_g.last()
    down_g.forward()
    down_g.settle()
    up_two_g.done()
    leaving.append(move(w_wide.at[1], fulls[6]))
    lax.fori_loop(UP_TILES, tiles, ffn_tile, 0)
    down_unit(4)
    down_g.last()
    down_unit(5)
    rest.join()
    down_unit(6)
    down_unit(7)
    down_copy(2 * chunks - 1).wait()
    down_trade(2 * chunks - 1).start()
    down_g.done()
    rest.done()
    for unit in range(2 * chunks):
        down_trade(unit).wait()
    for copy in leaving + list(turning.values()):
        copy.wait()
    for pair in (pairs - 2, pairs - 1):
        probs_out(pair).wait()
    for tile in (tiles - 2, tiles - 1):
        for copy in ffn_out(tile):
            copy.wait()
    links.finish()


def forward_all(nw, nn, counts, tokens, rel, lay, cotangent, shards, odd_rows):
    devices = nw * nn
    shapes = []
    for index, shard in enumerate(shards):
        rows = odd_rows if index == len(shards) - 1 else shard.shape[0]
        shapes.append((rows, shard.shape[1]))
    slots, width = tokens.shape
    copies = (len(shards) + 2) * (nn - 1 + 6 + nw // 2) + 2 * (width // DOWN_PIECE)
    ffn = shapes[5][1]
    low = jax.ShapeDtypeStruct((slots, width), BF)
    wide = jax.ShapeDtypeStruct((slots, ffn), BF)
    full = jax.ShapeDtypeStruct((slots, width), F32)
    out_shape = [
        jax.ShapeDtypeStruct((rows * devices, columns), shard.dtype)
        for (rows, columns), shard in zip(shapes, shards)
    ]
    low_t = jax.ShapeDtypeStruct((width, slots), BF)
    out_shape += [low, low_t, low_t, low, low, low_t, full, low_t, wide]
    out_shape += [jax.ShapeDtypeStruct((H, slots, slots), BF), wide, wide]
    down = (nw // 2, 2, nn * odd_rows, DOWN_PIECE)
    out_shape += [jax.ShapeDtypeStruct((width // DOWN_PIECE,) + down, BF)]
    out_shape += [jax.ShapeDtypeStruct((width // DOWN_PIECE, nw // 2, nn * odd_rows, DOWN_PIECE), BF)]
    tile_rows = shards[-1].shape[0]
    half = (tile_rows, REST)
    hbm = pl.BlockSpec(memory_space=pl.ANY)
    page = pltpu.VMEM((slots, width), BF)
    return pl.pallas_call(
        functools.partial(forward_kernel, nn, shapes),
        out_shape=out_shape,
        in_specs=[pl.BlockSpec(memory_space=pltpu.SMEM)] + [hbm] * (4 + len(shards)),
        out_specs=[hbm] * len(out_shape),
        scratch_shapes=[
            pltpu.VMEM((nn, tile_rows, width - REST), BF),
            pltpu.VMEM((nn * odd_rows, width - REST), BF),
            page,
            pltpu.VMEM((slots, slots), jnp.int32),
            pltpu.VMEM((slots, slots), jnp.int32),
            pltpu.VMEM((devices * 8, 128), F32),
            pltpu.VMEM((H * QB, QB * 2 * NB), BF),
            pltpu.VMEM((QB * 2 * NB, slots), BF),
            pltpu.VMEM((H, slots, slots), F32),
            page,
            page,
            page,
            page,
            page,
            pltpu.VMEM((slots, width), F32),
            page,
            pltpu.VMEM((2, slots, TILE), BF),
            pltpu.VMEM((2, slots, TILE), BF),
            pltpu.VMEM((2, slots, TILE), BF),
            pltpu.VMEM((2, 2, slots, slots), BF),
            pltpu.VMEM((2, width, width), BF),
            pltpu.VMEM((2, width, ffn), BF),
            page,
            pltpu.VMEM((2, down[0] // 2) + down[1:], BF),
            pltpu.VMEM((8, width), F32),
            pltpu.VMEM((2, width, slots), BF),
            pltpu.VMEM((ffn, slots), BF),
            pltpu.SemaphoreType.DMA((copies,)),
            pltpu.SemaphoreType.DMA((copies,)),
            pltpu.SemaphoreType.DMA((len(shards) + 1,)),
            pltpu.SemaphoreType.DMA((64,)),
            pltpu.SemaphoreType.DMA((10,)),
            pltpu.VMEM((nw // 2,) + half, BF),
            pltpu.VMEM((nn, nw // 2) + half, BF),
            pltpu.VMEM((nw // 2, nn * odd_rows, half[1]), BF),
            pltpu.SemaphoreType.DMA((1 + nw // 2,)),
        ],
        compiler_params=pltpu.CompilerParams(
            collective_id=0, has_side_effects=True, vmem_limit_bytes=63 * 2**20
        ),
    )(counts, tokens, rel, lay, cotangent, *shards)


class Scatter:
    def __init__(self, links, chunks, rows, columns, grads, came, slots, base, traded=False):
        self.links, self.chunks, self.rows, self.columns = links, chunks, rows, columns
        self.grads, self.came = grads, came
        (self.held, self.other, self.round, self.out_line, self.in_line, self.load_sem) = slots
        self.base = base
        self.traded = traded
        self.block = rows * links.nn
        self.parts = halves(columns)
        self.core = lax.rem(links.w, 2)
        self.ring = self.held.shape[0]

    def number(self, chunk, kind):
        return self.base + chunk * SCATTER_COPIES + kind

    def core_copy(self, chunk):
        return self.links.copy(
            self.grads.at[chunk, :, 1 - self.core],
            self.came.at[chunk],
            self.number(chunk, 0),
            self.links.wide(1),
        )

    def trade(self, chunk):
        self.core_copy(chunk).start()

    def loads(self, chunk):
        slot, turn = lax.rem(chunk, self.ring), lax.rem(chunk, 2)
        return (
            pltpu.make_async_copy(
                self.grads.at[chunk, :, self.core], self.held.at[slot], self.load_sem.at[turn, 0]
            ),
            pltpu.make_async_copy(
                self.came.at[chunk], self.other.at[turn], self.load_sem.at[turn, 1]
            ),
        )

    def fetch(self, chunk):
        if not self.traded:
            self.core_copy(chunk).wait_recv()
        for load in self.loads(chunk):
            load.start()

    def square(self, mask):
        return jnp.bitwise_xor(self.links.w, mask) // 2

    def hop(self, chunk, p, mask):
        slot = lax.rem(chunk, self.ring)
        low, size, order = self.parts[p]
        bit = order[1] if mask & order[1] else order[0]
        kind = 1 + p * 3 + (X_BIT, Y_BIT, X_BIT | Y_BIT).index(mask)
        return self.links.copy(
            self.held.at[slot, self.square(mask), :, pl.ds(low, size)],
            self.round.at[slot, kind - 1, :, pl.ds(0, size)],
            self.number(chunk, kind),
            self.links.wide(bit),
        )

    def landed(self, chunk, p, mask):
        return self.round.at[
            lax.rem(chunk, self.ring), p * 3 + (X_BIT, Y_BIT, X_BIT | Y_BIT).index(mask)
        ]

    def add_core(self, chunk):
        for load in self.loads(chunk):
            load.wait()
        slot, turn = lax.rem(chunk, self.ring), lax.rem(chunk, 2)

        def one(square, carry):
            self.held[slot, square] = (
                self.held[slot, square].astype(F32) + self.other[turn, square].astype(F32)
            ).astype(BF)
            return carry

        lax.fori_loop(0, self.held.shape[1], one, 0)
        for p, part in enumerate(self.parts):
            self.hop(chunk, p, X_BIT | Y_BIT).start()
        for p, part in enumerate(self.parts):
            self.hop(chunk, p, part[2][1]).start()

    def add_corner(self, chunk):
        slot = lax.rem(chunk, self.ring)
        for p, (low, size, order) in enumerate(self.parts):
            self.hop(chunk, p, X_BIT | Y_BIT).wait_recv()
            square = self.square(order[0])
            came = self.landed(chunk, p, X_BIT | Y_BIT)
            self.held[slot, square, :, low : low + size] = (
                self.held[slot, square, :, low : low + size].astype(F32)
                + came[:, :size].astype(F32)
            ).astype(BF)
        for p, part in enumerate(self.parts):
            self.hop(chunk, p, part[2][0]).start()

    def line_copy(self, chunk, step):
        k = self.links
        slot = lax.rem(chunk, self.ring)
        return k.copy(
            self.out_line.at[slot, lax.rem(k.z + step, k.nn)],
            self.in_line.at[slot, step - 1],
            self.number(chunk, 6 + step),
            k.along(step),
        )

    def add_square(self, chunk):
        slot = lax.rem(chunk, self.ring)
        home = self.square(0)
        for p, (low, size, order) in enumerate(self.parts):
            total = self.held[slot, home, :, low : low + size].astype(F32)
            for mask in order:
                self.hop(chunk, p, mask).wait_recv()
                total = total + self.landed(chunk, p, mask)[:, :size].astype(F32)
            for z in range(self.links.nn):
                self.out_line[slot, z, : self.rows, low : low + size] = total[
                    z * self.rows : (z + 1) * self.rows
                ].astype(BF)
        for step in range(1, self.links.nn):
            self.line_copy(chunk, step).start()
        if not self.traded:
            self.core_copy(chunk).wait_send()
        for p in range(len(self.parts)):
            for mask in (X_BIT, Y_BIT, X_BIT | Y_BIT):
                self.hop(chunk, p, mask).wait_send()

    def total(self, chunk):
        slot = lax.rem(chunk, self.ring)
        total = self.out_line[slot, self.links.z, : self.rows].astype(F32)
        for step in range(1, self.links.nn):
            self.line_copy(chunk, step).wait_recv()
            total = total + self.in_line[slot, step - 1, : self.rows].astype(F32)
        return total

    def pump(self, index, out, made=None):
        index = jnp.int32(index)
        made = self.chunks if made is None else made
        idle = index >= made if made < self.chunks else False
        steps = (self.fetch, self.add_core, self.add_corner, self.add_square, self.finish)
        for lag, action in zip(LAG, steps):
            chunk = index - lag
            ready = jnp.logical_and(chunk >= 0, chunk < self.chunks)
            if made < self.chunks:
                ready = jnp.logical_and(ready, jnp.logical_not(idle))

            @pl.when(ready)
            def _(chunk=chunk, action=action):
                action(chunk, out) if action == self.finish else action(chunk)

    def finish(self, chunk, out):
        out[chunk] = self.total(chunk)
        for step in range(1, self.links.nn):
            self.line_copy(chunk, step).wait_send()


class ScatterSmall:
    def __init__(self, links, grads, out, came, round_in, line_in, mine):
        self.links, self.grads, self.out = links, grads, out
        self.came, self.round, self.line, self.mine = came, round_in, line_in, mine
        self.home = links.w // 2
        self.masks = (X_BIT, Y_BIT, X_BIT | Y_BIT)
        self.core_id = links.fresh()
        self.square_ids = [links.fresh() for _ in self.masks]
        self.line_ids = [links.fresh() for _ in range(1, links.nn)]

    def core_copy(self):
        k = self.links
        return k.copy(self.grads.at[:, 1 - lax.rem(k.w, 2)], self.came, self.core_id, k.wide(1))

    def square_copy(self, index):
        k, mask = self.links, self.masks[index]
        spot = jnp.bitwise_xor(k.w, mask) // 2
        return k.copy(self.mine.at[spot], self.round.at[index], self.square_ids[index], k.wide(mask))

    def line_copy(self, step):
        k = self.links
        rows = pl.ds(pl.multiple_of(lax.rem(k.z + step, k.nn) * 8, 8), 8)
        spot = self.mine.at[self.home, rows]
        return k.copy(spot, self.line.at[step - 1], self.line_ids[step - 1], k.along(step))

    def trade(self):
        self.core_copy().start()

    def spread(self):
        self.core_copy().wait()
        self.mine[...] = self.grads[:, lax.rem(self.links.w, 2)] + self.came[...]
        for index in range(len(self.masks)):
            self.square_copy(index).start()

    def along(self):
        for index in range(len(self.masks)):
            self.square_copy(index).wait()
        total = self.mine[self.home]
        for index in range(len(self.masks)):
            total = total + self.round[index]
        self.mine[self.home] = total
        for step in range(1, self.links.nn):
            self.line_copy(step).start()

    def finish(self):
        total = self.mine[self.home, pl.ds(pl.multiple_of(self.links.z * 8, 8), 8)]
        for step in range(1, self.links.nn):
            self.line_copy(step).wait()
            total = total + self.line[step - 1]
        self.out[...] = total


def padded(rows):
    return (rows + 15) // 16 * 16


def scatter_slots(squares, nn, rows, columns, ring):
    half = columns // 2
    return [
        pltpu.VMEM((ring, squares, nn * rows, columns), BF),
        pltpu.VMEM((2, squares, nn * rows, columns), BF),
        pltpu.VMEM((ring, 6, nn * rows, half), BF),
        pltpu.VMEM((ring, nn, padded(rows), columns), BF),
        pltpu.VMEM((ring, nn - 1, padded(rows), columns), BF),
        pltpu.SemaphoreType.DMA((2, 2)),
    ]


def norm_pull(values, gain, grad):
    scale = lax.rsqrt(jnp.mean(values * values, axis=-1, keepdims=True) + RMS_EPSILON)
    scaled = grad * gain
    along = jnp.mean(scaled * values, axis=-1, keepdims=True)
    share = grad * values * scale
    return scale * scaled - values * (scale * scale * scale * along), share


def fold_rows(values):
    return jnp.sum(values.reshape(values.shape[0] // 8, 8, values.shape[1]), axis=0)


def pack_row(row, first, each, devices):
    total = row.shape[1]
    shape = (128, total)
    pick = jnp.where(iota(shape, 0) == first + lax.rem(iota(shape, 1), each), 1.0, 0.0)
    shape = (devices, total)
    mine = jnp.where(iota(shape, 1) // each == iota(shape, 0), row, 0.0)
    return lax.dot_general(
        mine,
        pick,
        (((1,), (1,)), ((), ())),
        preferred_element_type=F32,
        precision=lax.Precision.HIGHEST,
    )


def backward_kernel(nn, few_facts, many_facts, *refs):
    occupied, refs = refs[0], refs[1:]
    (
        tokens,
        rel_hbm,
        lay_hbm,
        grad_h,
        small_h,
        query_h,
        key_h,
        value_h,
        output_h,
        gate_h,
        up_h,
        down_h,
        na_t,
        q_t,
        k_h,
        v_h,
        att_t,
        hid_h,
        nf_t,
        mix_h,
        probs_h,
        slope_h,
        act_h,
        few_grads,
        few_came,
    ) = refs[:25]
    refs = refs[25:]
    (out_h, rows_out, few_out, many_out, small_out, many_grads, many_came) = refs[:7]
    few_slots, many_slots, refs = refs[7:13], refs[13:19], refs[19:]
    (
        x,
        rel,
        lay,
        small,
        gains,
        grad,
        left,
        acc,
        hid,
        wd_s,
        wgu_s,
        pair,
        slope_s,
        act_s,
        many_stage,
        branch,
        w_one,
        pull,
        pull_t,
        qt,
        k,
        v,
        probs,
        pieces,
        onehot,
        table,
        sums,
        small_grads,
        small_came,
        small_round,
        small_line,
        small_mine,
        send_sem,
        recv_sem,
        local_sem,
        tile_sem,
        stage_sem,
        probs_sem,
    ) = refs
    slots, width = x.shape
    links = Links(nn, send_sem, recv_sem)
    numbers = iter(range(64))

    def move(src, dst):
        copy = pltpu.make_async_copy(src, dst, local_sem.at[next(numbers)])
        copy.start()
        return copy

    few = Scatter(links, *few_facts, few_grads, few_came, few_slots, 0, traded=True)
    base = few_facts[0] * SCATTER_COPIES
    many = Scatter(links, *many_facts, many_grads, many_came, many_slots, base)
    links.used = base + many_facts[0] * SCATTER_COPIES
    little = ScatterSmall(
        links, small_grads, small_out, small_came, small_round, small_line, small_mine
    )
    ffn = mix_h.shape[1]
    tiles = ffn // TILE
    pairs = H // 2
    wide = many.columns
    squares = many_stage.shape[1]
    devices = small.shape[0] // 8
    each = width // devices
    zero = jnp.zeros((8, width), F32)

    def tile_copies(tile):
        turn = lax.rem(tile, 2)
        at = pl.ds(pl.multiple_of(tile * TILE, TILE), TILE)
        return [
            pltpu.make_async_copy(src, dst, tile_sem.at[turn, index])
            for index, (src, dst) in enumerate(
                (
                    (down_h.at[at], wd_s.at[turn]),
                    (gate_h.at[:, at], wgu_s.at[turn, :, pl.ds(0, TILE)]),
                    (up_h.at[:, at], wgu_s.at[turn, :, pl.ds(TILE, TILE)]),
                    (slope_h.at[:, at], slope_s.at[turn]),
                    (act_h.at[:, at], act_s.at[turn]),
                )
            )
        ]

    def many_copy(chunk):
        turn = lax.rem(chunk, 2)
        return pltpu.make_async_copy(many_stage.at[turn], many.grads.at[chunk], stage_sem.at[turn])

    def flush(chunk):
        many_copy(chunk).wait()
        many.trade(chunk)

    def make(chunk, left_rows, right, dot_one):
        found = dot_one(left_rows[...], right())
        many_stage[lax.rem(chunk, 2)] = found.astype(BF).reshape(many_stage.shape[1:])
        many_copy(chunk).start()

    def few_pump(index):
        few.pump(index, few_out)

    def many_pump(index, made=None):
        many.pump(index, many_out, made)

    def ffn_tile(tile, carry):
        turn = lax.rem(tile, 2)

        @pl.when(tile + 1 < tiles)
        def _():
            for copy in tile_copies(tile + 1):
                copy.start()

        for copy in tile_copies(tile):
            copy.wait()
        grad_mixed = dot_nt(grad[...], wd_s[turn])
        pair[:, :TILE] = (grad_mixed * slope_s[turn].astype(F32)).astype(BF)
        pair[:, TILE:] = (grad_mixed * act_s[turn].astype(F32)).astype(BF)
        make(tile, left, lambda: pair[...], dot)

        @pl.when(lax.rem(tile, 2) == 1)
        def _():
            few_pump(tile // 2 + 2)

        acc[...] += dot_nt(pair[...], wgu_s[turn])
        flush(tile)
        many_pump(tile - FFN_LAG)
        return carry

    def unpack():
        rows = small.reshape(devices, 8, 128)[:, 0, :]
        gains[0:1, :] = unpack_row(rows, 0, each, width)
        gains[1:2, :] = unpack_row(rows, each, each, width)

    def norm_two():
        def one(index, total):
            at = pl.ds(pl.multiple_of(index * 64, 64), 64)
            part, share = norm_pull(hid[at, :], gains[1:2, :], acc[at, :])
            whole = grad[at, :].astype(F32) + part
            hid[at, :] = whole
            branch[at, :] = whole.astype(BF)
            return total + fold_rows(share)

        sums[0] = lax.fori_loop(0, slots // 64, one, zero)

    def output_chunk(part):
        make(tiles + part, pull_t, lambda: branch[:, part * wide : (part + 1) * wide], dot)

    def pull_back():
        def one(tile, carry):
            at = pl.ds(pl.multiple_of(tile * WIDE, WIDE), WIDE)
            found = dot_nt(branch[...], w_one[0, at, :]).astype(BF)
            pull[:, at] = found
            pull_t[at, :] = found.T
            return carry

        lax.fori_loop(0, width // WIDE, one, 0)

    def probs_copy(index):
        turn = lax.rem(index, 2)
        return pltpu.make_async_copy(
            probs_h.at[pl.ds(index * 2, 2)], probs.at[turn], probs_sem.at[turn]
        )

    def attend_pair(index, carry):
        @pl.when(index + 1 < pairs)
        def _():
            probs_copy(index + 1).start()

        probs_copy(index).wait()
        turn = lax.rem(index, 2)
        at = pl.ds(pl.multiple_of(index * 128, 128), 128)
        low = iota((slots, 128), 1) < HD
        keys, pulls, values = k[:, at], pull[:, at], v[:, at]
        found = []
        for side in range(2):
            head = index * 2 + side
            mine = jnp.where(low if side == 0 else jnp.logical_not(low), pulls, 0)
            share = probs[turn, side]
            wanted = dot_nt(mine, values)
            share_f = share.astype(F32)
            joint = share_f * wanted
            piece = (joint - share_f * jnp.sum(joint, axis=-1, keepdims=True)).astype(BF)
            pieces[pl.ds(pl.multiple_of(head * slots, slots), slots), :] = piece
            found.append(dot(piece, keys))
            rows = pl.ds(pl.multiple_of(head * HD, HD), HD)
            qt[rows, :] = dot(qt[rows, :], piece).astype(BF)
            pull_t[rows, :] = dot(pull_t[rows, :], share).astype(BF)
        pull[:, at] = jnp.where(low, found[0], found[1]).astype(BF)
        return carry

    def attend(first, last):
        lax.fori_loop(first, last, attend_pair, 0)

    first_head_chunk = tiles + width // wide

    def head_chunk(half, part):
        at = slice(half * wide, (half + 1) * wide)
        chunk = first_head_chunk + half * 3 + part
        if part == 1:
            make(chunk, left, lambda: pull[:, at], dot)
        else:
            grads = qt if part else pull_t
            make(chunk, left, lambda: grads[at, :], dot_nt)
        return chunk

    def head_chunks(half):
        for part in range(3):
            chunk = head_chunk(half, part)
            if part:
                flush(chunk - 1)
        flush(chunk)

    def table_blocks(index, carry):
        sides = []
        for side in range(2):
            block = index * 2 + side
            at = slice(side * slots, (side + 1) * slots)
            for query in range(BACK_QB):
                for which, bucket in enumerate((rel, lay)):
                    row = bucket[pl.ds(block * BACK_QB + query, 1), :]
                    first = (query * 2 + which) * NB
                    onehot[first : first + NB, at] = ones_where(
                        jnp.broadcast_to(row, (NB, slots)) == iota((NB, slots), 0)
                    )
            heads = [
                pieces[pl.ds(pl.multiple_of(head * slots + block * BACK_QB, BACK_QB), BACK_QB), :]
                for head in range(H)
            ]
            sides.append(jnp.concatenate(heads, axis=0))
        table[...] += dot_nt(onehot[...], jnp.concatenate(sides, axis=1))
        return carry

    def add_table(part, parts):
        blocks = slots // BACK_QB // 2
        lax.fori_loop(part * blocks // parts, (part + 1) * blocks // parts, table_blocks, 0)

    whole = ffn // slots
    first_mix = width // slots * ffn

    def output_moves():
        moves = [
            move(down_h.at[:, pl.ds(part * slots, slots)], pieces.at[pl.ds(part * ffn, ffn)])
            for part in range(width // slots)
        ]
        moves += [
            move(
                mix_h.at[:, pl.ds(part * slots, slots)],
                pieces.at[pl.ds(first_mix + part * slots, slots)],
            )
            for part in range(whole)
        ]
        return moves + [move(mix_h.at[:, pl.ds(whole * slots, TILE)], slope_s.at[0])]

    def down_project(part):
        at = slice(part * slots, (part + 1) * slots)
        total = acc[:, at]
        for index in range(whole):
            rows = slice(part * ffn + index * slots, part * ffn + (index + 1) * slots)
            mixed = pieces[first_mix + index * slots : first_mix + (index + 1) * slots, :]
            total = total + dot(mixed, pieces[rows, :])
        total = total + dot(slope_s[0], pieces[part * ffn + whole * slots : (part + 1) * ffn, :])
        valid_rows = iota((slots, 1), 0) < occupied[0] + IMG
        x[:, at] = jnp.where(valid_rows, total, 0.0).astype(BF)

    def turn_back():
        def one(tile, carry):
            at = pl.ds(pl.multiple_of(tile * TILE, TILE), TILE)
            v[:, at] = pull_t[at, :].T
            branch[:, at] = qt[at, :].T
            return carry

        lax.fori_loop(0, width // TILE, one, 0)

    def pull_normed(source, slot, first):
        def one(tile, carry):
            at = pl.ds(pl.multiple_of(tile * WIDE, WIDE), WIDE)
            found = dot_nt(source[...], w_one[slot, at, :])
            acc[:, at] = found if first else acc[:, at] + found
            return carry

        lax.fori_loop(0, width // WIDE, one, 0)

    def norm_one():
        def one(index, total):
            at = pl.ds(pl.multiple_of(index * 64, 64), 64)
            part, share = norm_pull(x[at, :].astype(F32), gains[0:1, :], acc[at, :])
            hid[at, :] += part
            return total + fold_rows(share)

        sums[1] = lax.fori_loop(0, slots // 64, one, zero)

    def pack():
        total = table[...]
        mine = iota(total.shape, 0) // (2 * NB) == lax.rem(iota(total.shape, 1), BACK_QB)
        folded = jnp.sum(
            jnp.where(mine, total, 0.0).reshape(BACK_QB, 2 * NB, H * BACK_QB), axis=0
        )
        packed = [
            pack_row(jnp.sum(sums[1], axis=0, keepdims=True), 0, each, devices),
            pack_row(jnp.sum(sums[0], axis=0, keepdims=True), 0, each, devices),
        ]
        shape = (H * BACK_QB, 128)
        pick = jnp.where(iota(shape, 1) == iota(shape, 0) // BACK_QB, 1.0, 0.0)
        for index in range(2):
            packed.append(
                jnp.dot(
                    folded[index * NB : (index + 1) * NB],
                    pick,
                    preferred_element_type=F32,
                    precision=lax.Precision.HIGHEST,
                )
            )
        small_grads[...] = jnp.zeros_like(small_grads)
        for device in range(devices):
            wide_at, z = divmod(device, nn)
            for index, rows in enumerate(packed):
                at = z * 8 + index
                small_grads[wide_at // 2, wide_at % 2, at : at + 1, :] = rows[device : device + 1]

    few.fetch(jnp.int32(0))
    for copy in tile_copies(0):
        copy.start()
    first_in = [move(grad_h, grad), move(nf_t, left)]
    links.greet()
    few.fetch(jnp.int32(1))
    few.add_core(jnp.int32(0))
    later = [move(hid_h, hid), move(small_h, small), move(att_t, pull_t), move(output_h, w_one.at[0])]
    later += [move(q_t, qt), move(k_h, k), move(v_h, v)]
    last = [move(tokens, x), move(rel_hbm, rel), move(lay_hbm, lay), move(value_h, w_one.at[1])]
    acc[...] = jnp.zeros_like(acc)
    for copy in first_in:
        copy.wait()
    lax.fori_loop(0, tiles, ffn_tile, 0)
    for copy in later:
        copy.wait()
    na_in = move(na_t, left)
    unpack()
    norm_two()
    few_pump(7)
    many_pump(5)
    output_chunk(0)
    output_chunk(1)
    pull_back()
    flush(tiles)
    flush(tiles + 1)
    query_in = move(query_h, w_one.at[0])
    probs_copy(jnp.int32(0)).start()
    few_pump(8)
    many_pump(6)
    attend(0, 2)
    few_pump(9)
    many_pump(7)
    attend(2, 4)
    for copy in last:
        copy.wait()
    na_in.wait()
    many_pump(8)
    head_chunks(0)
    many_pump(9)
    attend(4, 6)
    many_pump(10)
    attend(6, 8)
    many_pump(11)
    head_chunks(1)
    many_pump(12)
    table[...] = jnp.zeros_like(table)
    add_table(0, 3)
    many_pump(13)
    add_table(1, 3)
    many_pump(14)
    add_table(2, 3)
    many_pump(15)
    output_in = output_moves()
    query_in.wait()
    turn_back()
    pull_normed(pull, 0, True)
    key_in = move(key_h, w_one.at[0])
    many_pump(16)
    pull_normed(v, 1, False)
    key_in.wait()
    pull_normed(branch, 0, False)
    many_pump(17)
    norm_one()
    rows_copy = move(hid, rows_out)
    output_in.append(move(hid_h, acc))
    pack()
    little.trade()
    many_pump(18)
    for copy in output_in:
        copy.wait()
    little.spread()
    many_pump(19)
    down_project(0)
    many_pump(20)
    little.along()
    many_pump(21)
    down_project(1)
    out_copy = move(x, out_h)
    many_pump(22)
    many_pump(23)
    many_pump(24)
    little.finish()
    rows_copy.wait()
    out_copy.wait()
    links.finish()


def backward_all(nw, nn, counts, page, weights, saved):
    squares = nw // 2
    devices = nw * nn
    slots, width = page[0].shape
    ffn = weights[5].shape[1]
    few = (width // DOWN_PIECE, ffn // devices, DOWN_PIECE)
    many = (ffn // TILE + 8, width // devices, 2 * TILE)
    outs = [jax.ShapeDtypeStruct((slots, width), BF), jax.ShapeDtypeStruct((slots, width), F32)]
    for chunks, rows, columns in (few, many):
        outs.append(jax.ShapeDtypeStruct((chunks, rows, columns), F32))
    outs.append(jax.ShapeDtypeStruct((8, 128), F32))
    chunks, rows, columns = many
    outs.append(jax.ShapeDtypeStruct((chunks, squares, 2, nn * rows, columns), BF))
    outs.append(jax.ShapeDtypeStruct((chunks, squares, nn * rows, columns), BF))
    copies = (few[0] + many[0]) * SCATTER_COPIES + 16
    vmem = pl.BlockSpec(memory_space=pltpu.VMEM)
    hbm = pl.BlockSpec(memory_space=pl.ANY)
    low = pltpu.VMEM((slots, width), BF)
    turned = pltpu.VMEM((width, slots), BF)
    full = pltpu.VMEM((slots, width), F32)
    inputs = (counts,) + tuple(page) + tuple(weights) + tuple(saved)
    return pl.pallas_call(
        functools.partial(backward_kernel, nn, few, many),
        out_shape=outs,
        in_specs=[pl.BlockSpec(memory_space=pltpu.SMEM)] + [hbm] * (len(inputs) - 1),
        out_specs=[hbm, hbm, vmem, vmem, vmem, hbm, hbm],
        scratch_shapes=scatter_slots(squares, nn, few[1], few[2], few[0])
        + scatter_slots(squares, nn, many[1], many[2], RING)
        + [
            low,
            pltpu.VMEM((slots, slots), jnp.int32),
            pltpu.VMEM((slots, slots), jnp.int32),
            pltpu.VMEM((devices * 8, 128), F32),
            pltpu.VMEM((8, width), F32),
            low,
            turned,
            full,
            full,
            pltpu.VMEM((2, TILE, width), BF),
            pltpu.VMEM((2, width, 2 * TILE), BF),
            pltpu.VMEM((slots, 2 * TILE), BF),
            pltpu.VMEM((2, slots, TILE), BF),
            pltpu.VMEM((2, slots, TILE), BF),
            pltpu.VMEM((2, squares, 2, nn * many[1], many[2]), BF),
            low,
            pltpu.VMEM((2, width, width), BF),
            low,
            turned,
            turned,
            low,
            low,
            pltpu.VMEM((2, 2, slots, slots), BF),
            pltpu.VMEM((H * slots, slots), BF),
            pltpu.VMEM((BACK_QB * 2 * NB, 2 * slots), BF),
            pltpu.VMEM((BACK_QB * 2 * NB, H * BACK_QB), F32),
            pltpu.VMEM((2, 8, width), F32),
            pltpu.VMEM((squares, 2, nn * 8, 128), F32),
            pltpu.VMEM((squares, nn * 8, 128), F32),
            pltpu.VMEM((3, nn * 8, 128), F32),
            pltpu.VMEM((nn - 1, 8, 128), F32),
            pltpu.VMEM((squares, nn * 8, 128), F32),
            pltpu.SemaphoreType.DMA((copies,)),
            pltpu.SemaphoreType.DMA((copies,)),
            pltpu.SemaphoreType.DMA((64,)),
            pltpu.SemaphoreType.DMA((2, 5)),
            pltpu.SemaphoreType.DMA((2,)),
            pltpu.SemaphoreType.DMA((2,)),
        ],
        compiler_params=pltpu.CompilerParams(
            collective_id=1, has_side_effects=True, vmem_limit_bytes=63 * 2**20
        ),
    )(*inputs)[:5]


def place_kernel(few_h, many_h, rows_h, out_h, small, *refs):
    (whole_out, row_out, query, key, value, output, gate, up, down) = refs[:9]
    (gain_attn, gain_ffn, rel, lay) = refs[9:13]
    few, many, rows, whole, in_sem, out_sem = refs[13:]
    tiles = gate.shape[1] // TILE
    wide = many.shape[2]
    part = rows.shape[0] // 8
    arriving = [
        pltpu.make_async_copy(src, dst, in_sem.at[index])
        for index, (src, dst) in enumerate(
            [(many_h, many), (few_h, few), (out_h, whole)]
            + [
                (rows_h.at[pl.ds(index * part, part)], rows.at[pl.ds(index * part, part)])
                for index in range(8)
            ]
        )
    ]
    for copy in arriving:
        copy.start()
    moves = []

    def move(src, dst):
        copy = pltpu.make_async_copy(src, dst, out_sem.at[len(moves)])
        copy.start()
        moves.append(copy)

    for index, target in enumerate((gain_attn, gain_ffn, rel, lay)):
        target[...] = small[index, : target.shape[0]]
    arriving[0].wait()
    for tile in range(tiles):
        at = pl.ds(tile * TILE, TILE)
        move(many.at[tile, :, pl.ds(0, TILE)], gate.at[:, at])
        move(many.at[tile, :, pl.ds(TILE, TILE)], up.at[:, at])
    halves_of = output.shape[1] // wide
    for half in range(halves_of):
        at = pl.ds(half * wide, wide)
        move(many.at[tiles + half], output.at[:, at])
        first = tiles + halves_of + half * 3
        for index, target in enumerate((value, query, key)):
            move(many.at[first + index], target.at[:, at])
    arriving[1].wait()
    for chunk in range(few.shape[0]):
        move(few.at[chunk], down.at[:, pl.ds(chunk * few.shape[2], few.shape[2])])
    arriving[2].wait()
    move(whole, whole_out)
    for index in range(8):
        arriving[3 + index].wait()
        at = pl.ds(index * part, part)
        move(rows.at[at], row_out.at[at])
    for copy in moves:
        copy.wait()


def place_all(few, many, rows, out, small, shapes):
    hbm = pl.BlockSpec(memory_space=pl.ANY)
    vmem = pl.BlockSpec(memory_space=pltpu.VMEM)
    outs = [jax.ShapeDtypeStruct(out.shape, BF), jax.ShapeDtypeStruct(rows.shape, F32)]
    outs += [jax.ShapeDtypeStruct(shape, F32) for shape in shapes]
    return pl.pallas_call(
        place_kernel,
        out_shape=outs,
        in_specs=[hbm] * 4 + [vmem],
        out_specs=[hbm] * 9 + [vmem] * 4,
        scratch_shapes=[
            pltpu.VMEM(few.shape, F32),
            pltpu.VMEM(many.shape, F32),
            pltpu.VMEM(rows.shape, F32),
            pltpu.VMEM(out.shape, BF),
            pltpu.SemaphoreType.DMA((16,)),
            pltpu.SemaphoreType.DMA((64,)),
        ],
        compiler_params=pltpu.CompilerParams(vmem_limit_bytes=63 * 2**20),
    )(few, many, rows, out, small)


def local_fast(
    nw,
    nn,
    tokens,
    w_query,
    w_key,
    w_value,
    w_output,
    w_gate,
    w_up,
    w_down,
    gain_attn,
    gain_ffn,
    rel_table,
    lay_table,
    ocr_counts,
    rel_bucket,
    lay_bucket,
    cotangent,
):
    small = jnp.concatenate([gain_attn, gain_ffn, rel_table, lay_table]).astype(F32)
    small = jnp.pad(small[None], ((0, 7), (0, 128 - small.shape[0])))
    down = jnp.pad(w_down, ((0, padded(w_down.shape[0]) - w_down.shape[0]), (0, 0)))
    page = (tokens, rel_bucket, lay_bucket)
    shards = [small, w_query, w_key, w_value, w_output, w_gate, w_up, down]
    found = forward_all(nw, nn, ocr_counts, *page, cotangent, shards, w_down.shape[0])
    weights, grad, saved = found[: len(shards)], found[len(shards)], found[len(shards) + 1 :]
    output, grad_tokens, few, many, small = backward_all(
        nw, nn, ocr_counts, page + (grad,), weights, saved
    )

    square = w_query.shape
    shapes = [square] * 4 + [w_gate.shape, w_up.shape, w_down.shape]
    shapes += [part.shape for part in (gain_attn, gain_ffn, rel_table, lay_table)]
    return tuple(place_all(few, many, grad_tokens, output, small, shapes))


def local(
    tokens,
    w_query,
    w_key,
    w_value,
    w_output,
    w_gate,
    w_up,
    w_down,
    gain_attn,
    gain_ffn,
    rel_table,
    lay_table,
    ocr_counts,
    rel_bucket,
    lay_bucket,
    cotangent,
):
    slot = tokens.shape[0]
    valid = jnp.arange(slot) < ocr_counts[0] + IMG
    buckets = jnp.arange(NB)
    onehot = jnp.concatenate(
        [
            (rel_bucket[:, :, None] == buckets).astype(jnp.bfloat16),
            (lay_bucket[:, :, None] == buckets).astype(jnp.bfloat16),
        ],
        axis=2,
    )
    tokens_f = tokens.astype(jnp.float32)
    weights = gather_weights(
        w_query,
        w_key,
        w_value,
        w_output,
        w_gate,
        w_up,
        w_down,
        gain_attn,
        gain_ffn,
        rel_table,
        lay_table,
    )
    result, saved = forward_pass(tokens_f, weights, onehot, valid)
    output = jnp.where(valid[:, None], result, 0.0).astype(jnp.bfloat16)
    (
        full_query,
        full_key,
        full_value,
        full_output,
        full_gate,
        full_up,
        full_down,
        full_gain_attn,
        full_gain_ffn,
        full_rel,
        full_lay,
    ) = weights
    (
        normed_attn,
        queries,
        keys_all,
        values_all,
        log_totals,
        attended,
        hidden_one,
        normed_ffn,
        gate_act,
        up_proj,
        mixed,
    ) = saved
    grad_result = jnp.where(valid[:, None], cotangent.astype(jnp.float32), 0.0)
    grad_low = grad_result.astype(jnp.bfloat16)
    grad_down = contract_rows(mixed, grad_low)
    grad_mixed = contract_cols(grad_low, full_down)
    gated_value, gated_pull = jax.vjp(gated_product, gate_act, up_proj)
    grad_gate_act, grad_up_proj = gated_pull(grad_mixed)
    gate_low = grad_gate_act.astype(jnp.bfloat16)
    up_low = grad_up_proj.astype(jnp.bfloat16)
    grad_gate = contract_rows(normed_ffn, gate_low)
    grad_up = contract_rows(normed_ffn, up_low)
    grad_normed_ffn = contract_cols(gate_low, full_gate) + contract_cols(up_low, full_up)
    norm_value, norm_pull = jax.vjp(rms_scale, hidden_one, full_gain_ffn.astype(jnp.float32))
    grad_hidden_part, grad_gain_ffn = norm_pull(grad_normed_ffn)
    grad_hidden = grad_result + grad_hidden_part
    branch_low = grad_hidden.astype(jnp.bfloat16)
    grad_output = contract_rows(attended, branch_low)
    grad_attended = contract_cols(branch_low, full_output).astype(jnp.bfloat16)
    grad_queries, grad_keys, grad_values, grad_table_all = attention_backward(
        queries,
        keys_all,
        values_all,
        log_totals,
        grad_attended,
        table_pair(full_rel, full_lay),
        onehot,
        valid,
    )
    grad_rel = grad_table_all[:NB].reshape(NB * H)
    grad_lay = grad_table_all[NB:].reshape(NB * H)
    grad_query = contract_rows(normed_attn, grad_queries)
    grad_key = contract_rows(normed_attn, grad_keys)
    grad_value = contract_rows(normed_attn, grad_values)
    grad_normed_attn = (
        contract_cols(grad_queries, full_query)
        + contract_cols(grad_keys, full_key)
        + contract_cols(grad_values, full_value)
    )
    input_value, input_pull = jax.vjp(rms_scale, tokens_f, full_gain_attn.astype(jnp.float32))
    grad_input_part, grad_gain_attn = input_pull(grad_normed_attn)
    grad_tokens = grad_hidden + grad_input_part
    owned = (
        lax.psum_scatter(grad_query, ("wide", "narrow"), scatter_dimension=0, tiled=True),
        lax.psum_scatter(grad_key, ("wide", "narrow"), scatter_dimension=0, tiled=True),
        lax.psum_scatter(grad_value, ("wide", "narrow"), scatter_dimension=0, tiled=True),
        lax.psum_scatter(grad_output, ("wide", "narrow"), scatter_dimension=0, tiled=True),
        lax.psum_scatter(grad_gate, ("wide", "narrow"), scatter_dimension=0, tiled=True),
        lax.psum_scatter(grad_up, ("wide", "narrow"), scatter_dimension=0, tiled=True),
        lax.psum_scatter(grad_down, ("wide", "narrow"), scatter_dimension=0, tiled=True),
        lax.psum_scatter(grad_gain_attn, ("wide", "narrow"), scatter_dimension=0, tiled=True),
        lax.psum_scatter(grad_gain_ffn, ("wide", "narrow"), scatter_dimension=0, tiled=True),
        lax.psum_scatter(grad_rel, ("wide", "narrow"), scatter_dimension=0, tiled=True),
        lax.psum_scatter(grad_lay, ("wide", "narrow"), scatter_dimension=0, tiled=True),
    )
    return (
        output,
        grad_tokens,
        owned[0],
        owned[1],
        owned[2],
        owned[3],
        owned[4],
        owned[5],
        owned[6],
        owned[7],
        owned[8],
        owned[9],
        owned[10],
    )


def solution(mesh):
    nw, nn = mesh.shape["wide"], mesh.shape["narrow"]

    def body(*args):
        if nw == 8 and nw * nn == NB and args[1].shape[0] % 16 == 0:
            return local_fast(nw, nn, *args)
        return local(*args)

    placed = (
        P(("wide", "narrow"), None),
        P(("wide", "narrow"), None),
        P(("wide", "narrow"), None),
        P(("wide", "narrow"), None),
        P(("wide", "narrow"), None),
        P(("wide", "narrow"), None),
        P(("wide", "narrow"), None),
        P(("wide", "narrow"), None),
        P(("wide", "narrow")),
        P(("wide", "narrow")),
        P(("wide", "narrow")),
        P(("wide", "narrow")),
        P(("wide", "narrow")),
        P(("wide", "narrow"), None),
        P(("wide", "narrow"), None),
        P(("wide", "narrow"), None),
    )
    return jax.shard_map(
        body,
        mesh=mesh,
        in_specs=placed,
        out_specs=(
            P(("wide", "narrow"), None),
            P(("wide", "narrow"), None),
            P(("wide", "narrow"), None),
            P(("wide", "narrow"), None),
            P(("wide", "narrow"), None),
            P(("wide", "narrow"), None),
            P(("wide", "narrow"), None),
            P(("wide", "narrow"), None),
            P(("wide", "narrow"), None),
            P(("wide", "narrow")),
            P(("wide", "narrow")),
            P(("wide", "narrow")),
            P(("wide", "narrow")),
        ),
        check_vma=False,
    )
```

```python
import functools

import jax
import jax.numpy as jnp
from jax import lax
from jax.experimental import pallas as pl
from jax.experimental.pallas import tpu as pltpu
from jax.sharding import PartitionSpec as P

H = 16
HD = 64
NB = 32
IMG = 196
RING = 6
SCATTER_COPIES = 10
LAG = (0, 1, 2, 4, 8)
LINE_RING = 10
FEW_LAG = (0, 1, 2, 4, 14)
LAGS = LAG[-1]
FFN_LAG = 6
LATE = 2
BACK_QB = 16
WIDE = 512
DOWN_PIECE = 256
REST = 512
UP_TILES = 6
TILE = 256
QB = 8
GELU_SCALE = 0.7978845608028654
GELU_CUBE = 0.044715


RMS_EPSILON = 1e-06
MASK_SCORE = -1000000000.0
HEAD_GROUP = 4


def rms_scale(values, gain):
    return (
        values * lax.rsqrt(jnp.mean(values * values, axis=-1, keepdims=True) + RMS_EPSILON) * gain
    )


def gated_product(gate_act, up_proj):
    return jax.nn.gelu(gate_act, approximate=True) * up_proj


def product(left, right):
    return jnp.dot(left, right, preferred_element_type=jnp.float32)


def contract_rows(left, right):
    return lax.dot_general(
        left, right, (((0,), (0,)), ((), ())), preferred_element_type=jnp.float32
    )


def contract_cols(left, right):
    return lax.dot_general(
        left, right, (((1,), (1,)), ((), ())), preferred_element_type=jnp.float32
    )


def split_heads(matrix):
    return jnp.moveaxis(matrix.reshape(matrix.shape[0], H // HEAD_GROUP, HEAD_GROUP, HD), 1, 0)


def join_heads(stacked):
    return jnp.moveaxis(stacked, 0, 1).reshape(stacked.shape[1], H * HD)


def group_tables(table_all):
    return jnp.moveaxis(table_all.reshape(2 * NB, H // HEAD_GROUP, HEAD_GROUP), 1, 0)


def group_scores(query_group, key_group, table_group, onehot, valid):
    scores = jnp.einsum("ihd,jhd->hij", query_group, key_group, preferred_element_type=jnp.float32)
    scores = scores + jnp.einsum(
        "ijb,bh->hij", onehot, table_group, preferred_element_type=jnp.float32
    )
    return jnp.where(valid[None, None, :], scores, MASK_SCORE)


def gather_weights(
    w_query,
    w_key,
    w_value,
    w_output,
    w_gate,
    w_up,
    w_down,
    gain_attn,
    gain_ffn,
    rel_table,
    lay_table,
):
    return (
        lax.all_gather(w_query, ("wide", "narrow"), axis=0, tiled=True),
        lax.all_gather(w_key, ("wide", "narrow"), axis=0, tiled=True),
        lax.all_gather(w_value, ("wide", "narrow"), axis=0, tiled=True),
        lax.all_gather(w_output, ("wide", "narrow"), axis=0, tiled=True),
        lax.all_gather(w_gate, ("wide", "narrow"), axis=0, tiled=True),
        lax.all_gather(w_up, ("wide", "narrow"), axis=0, tiled=True),
        lax.all_gather(w_down, ("wide", "narrow"), axis=0, tiled=True),
        lax.all_gather(gain_attn, ("wide", "narrow"), axis=0, tiled=True),
        lax.all_gather(gain_ffn, ("wide", "narrow"), axis=0, tiled=True),
        lax.all_gather(rel_table, ("wide", "narrow"), axis=0, tiled=True),
        lax.all_gather(lay_table, ("wide", "narrow"), axis=0, tiled=True),
    )


def table_pair(full_rel, full_lay):
    return jnp.concatenate([full_rel.reshape(NB, H), full_lay.reshape(NB, H)], axis=0)


def forward_pass(tokens_f, weights, onehot, valid):
    (
        full_query,
        full_key,
        full_value,
        full_output,
        full_gate,
        full_up,
        full_down,
        full_gain_attn,
        full_gain_ffn,
        full_rel,
        full_lay,
    ) = weights
    normed_attn = rms_scale(tokens_f, full_gain_attn.astype(jnp.float32)).astype(jnp.bfloat16)
    queries = product(normed_attn, full_query).astype(jnp.bfloat16)
    keys_all = product(normed_attn, full_key).astype(jnp.bfloat16)
    values_all = product(normed_attn, full_value).astype(jnp.bfloat16)

    def forward_one_group(operands):
        query_group, key_group, value_group, table_group = operands
        scores = group_scores(query_group, key_group, table_group, onehot, valid)
        peak = jnp.max(scores, axis=-1, keepdims=True)
        expo = jnp.exp(scores - peak)
        total = jnp.sum(expo, axis=-1, keepdims=True)
        probs_low = (expo / total).astype(jnp.bfloat16)
        attended_group = jnp.einsum(
            "hij,jhd->ihd", probs_low, value_group, preferred_element_type=jnp.float32
        )
        return (attended_group.astype(jnp.bfloat16), (peak + jnp.log(total))[..., 0])

    stacked, log_totals = lax.map(
        forward_one_group,
        (
            split_heads(queries),
            split_heads(keys_all),
            split_heads(values_all),
            group_tables(table_pair(full_rel, full_lay)),
        ),
    )
    attended = join_heads(stacked)
    hidden_one = tokens_f + product(attended, full_output)
    normed_ffn = rms_scale(hidden_one, full_gain_ffn.astype(jnp.float32)).astype(jnp.bfloat16)
    gate_act = product(normed_ffn, full_gate)
    up_proj = product(normed_ffn, full_up)
    mixed = gated_product(gate_act, up_proj).astype(jnp.bfloat16)
    result = hidden_one + product(mixed, full_down)
    return (
        result,
        (
            normed_attn,
            queries,
            keys_all,
            values_all,
            log_totals,
            attended,
            hidden_one,
            normed_ffn,
            gate_act,
            up_proj,
            mixed,
        ),
    )


def attention_backward(
    queries, keys_all, values_all, log_totals, grad_attended, table_all, onehot, valid
):

    def attention_one_group(operands):
        query_group, key_group, value_group, table_group, lse_group, grad_group = operands
        scores = group_scores(query_group, key_group, table_group, onehot, valid)
        probs = jnp.exp(scores - lse_group[..., None])
        probs_low = probs.astype(jnp.bfloat16)
        grad_values = jnp.einsum(
            "hij,ihd->jhd", probs_low, grad_group, preferred_element_type=jnp.float32
        )
        grad_probs = jnp.einsum(
            "ihd,jhd->hij", grad_group, value_group, preferred_element_type=jnp.float32
        )
        grad_scores = (
            probs * (grad_probs - jnp.sum(probs * grad_probs, axis=-1, keepdims=True))
        ).astype(jnp.bfloat16)
        grad_queries = jnp.einsum(
            "hij,jhd->ihd", grad_scores, key_group, preferred_element_type=jnp.float32
        )
        grad_keys = jnp.einsum(
            "hij,ihd->jhd", grad_scores, query_group, preferred_element_type=jnp.float32
        )
        grad_table = jnp.einsum(
            "hij,ijb->bh", grad_scores, onehot, preferred_element_type=jnp.float32
        )
        return (
            grad_queries.astype(jnp.bfloat16),
            grad_keys.astype(jnp.bfloat16),
            grad_values.astype(jnp.bfloat16),
            grad_table,
        )

    grad_q_all, grad_k_all, grad_v_all, grad_tables = lax.map(
        attention_one_group,
        (
            split_heads(queries),
            split_heads(keys_all),
            split_heads(values_all),
            group_tables(table_all),
            log_totals,
            split_heads(grad_attended),
        ),
    )
    grad_table_all = jnp.moveaxis(grad_tables, 0, 1).reshape(2 * NB, H)
    return (join_heads(grad_q_all), join_heads(grad_k_all), join_heads(grad_v_all), grad_table_all)


MESH_ID = pl.DeviceIdType.MESH
BF = jnp.bfloat16
F32 = jnp.float32
X_BIT = 2
Y_BIT = 4
PARTS = ((X_BIT, Y_BIT), (Y_BIT, X_BIT))


class Links:
    def __init__(self, nn, send_sem, recv_sem):
        self.nn = nn
        self.w = lax.axis_index("wide")
        self.z = lax.axis_index("narrow")
        self.send_sem = send_sem
        self.recv_sem = recv_sem
        self.used = 0
        self.sent = []

    def fresh(self):
        self.used += 1
        return self.used - 1

    def wide(self, bit):
        return (jnp.bitwise_xor(self.w, bit), self.z)

    def along(self, step):
        return (self.w, lax.rem(self.z + step, self.nn))

    def copy(self, src, dst, number, device):
        return pltpu.make_async_remote_copy(
            src_ref=src,
            dst_ref=dst,
            send_sem=self.send_sem.at[number],
            recv_sem=self.recv_sem.at[number],
            device_id=device,
            device_id_type=MESH_ID,
        )

    def send(self, src, dst, number, device):
        copy = self.copy(src, dst, number, device)
        copy.start()
        self.sent.append(copy)

    def greet(self):
        barrier = pltpu.get_barrier_semaphore()
        others = [self.wide(bit) for bit in (1, X_BIT, Y_BIT)]
        others += [self.along(step) for step in range(1, self.nn)]
        for other in others:
            pl.semaphore_signal(barrier, inc=1, device_id=other, device_id_type=MESH_ID)
        pl.semaphore_wait(barrier, len(others))

    def finish(self):
        for copy in self.sent:
            copy.wait_send()


class Gather:
    def __init__(self, links, shard, full, rows, window, parts, local_sem, line=None, merged=None):
        self.links, self.shard, self.full, self.rows, self.parts = links, shard, full, rows, parts
        self.window = window
        self.local_sem, self.line, self.merged = local_sem, line, merged
        nn = links.nn
        self.block = rows * nn
        self.line_ids = [links.fresh() for _ in range(1, nn)]
        self.part_ids = {
            (p, mask): links.fresh()
            for p in range(len(parts))
            for mask in (X_BIT, Y_BIT, X_BIT | Y_BIT)
        }
        self.core_ids = {mask: links.fresh() for mask in (0, X_BIT, Y_BIT, X_BIT | Y_BIT)}

    def place(self, w, z):
        if self.line is not None:
            return self.line.at[z]
        return self.full.at[pl.ds((w * self.links.nn + z) * self.rows, self.rows), pl.ds(*self.window)]

    def span(self, mask, part=None):
        rows = pl.ds(jnp.bitwise_xor(self.links.w, mask) * self.block, self.block)
        low, size = self.window if part is None else self.parts[part][:2]
        return self.full.at[rows, pl.ds(low, size)]

    def own(self):
        return pltpu.make_async_copy(
            self.shard, self.place(self.links.w, self.links.z), self.local_sem
        )

    def start(self):
        k = self.links
        self.own().start()
        for step in range(1, k.nn):
            k.send(self.shard, self.place(k.w, k.z), self.line_ids[step - 1], k.along(step))

    def ready(self):
        k = self.links
        self.own().wait()
        for step in range(1, k.nn):
            came = lax.rem(k.z - step + k.nn, k.nn)
            k.copy(
                self.shard, self.place(k.w, came), self.line_ids[step - 1], k.along(step)
            ).wait_recv()
        if self.line is not None:
            whole = jnp.concatenate(
                [self.line[z, : self.rows].astype(F32) for z in range(k.nn)], axis=0
            )
            self.merged[...] = whole.astype(BF)
            move = pltpu.make_async_copy(self.merged, self.span(0), self.local_sem)
            move.start()
            move.wait()

    def spread(self):
        k = self.links
        for p, part in enumerate(self.parts):
            for bit in part[2]:
                k.send(self.span(0, p), self.span(0, p), self.part_ids[p, bit], k.wide(bit))
        k.send(self.span(0), self.span(0), self.core_ids[0], k.wide(1))

    def arrive(self, p, mask):
        k = self.links
        k.copy(
            self.span(mask, p), self.span(mask, p), self.part_ids[p, mask], k.wide(X_BIT)
        ).wait_recv()

    def forward(self):
        k = self.links
        for p, part in enumerate(self.parts):
            first, second = part[2]
            self.arrive(p, first)
            both = first | second
            k.send(self.span(first, p), self.span(first, p), self.part_ids[p, both], k.wide(second))

    def settle(self):
        k = self.links
        for p, part in enumerate(self.parts):
            self.arrive(p, part[2][1])
        for mask in (X_BIT, Y_BIT):
            k.send(self.span(mask), self.span(mask), self.core_ids[mask], k.wide(1))

    def last(self):
        k = self.links
        both = X_BIT | Y_BIT
        for p in range(len(self.parts)):
            self.arrive(p, both)
        k.send(self.span(both), self.span(both), self.core_ids[both], k.wide(1))

    def done(self):
        k = self.links
        for mask, number in self.core_ids.items():
            place = self.span(mask | 1)
            k.copy(place, place, number, k.wide(1)).wait_recv()


def halves(columns, first=0):
    low = columns // 256 * 128
    return ((first, low, PARTS[0]), (first + low, columns - low, PARTS[1]))


class GatherSquare:
    def __init__(self, links, shard, full, rows, window, local_sem, square, lines, merged):
        self.links, self.shard, self.full, self.rows, self.window = links, shard, full, rows, window
        self.square, self.lines, self.merged, self.local_sem = square, lines, merged, local_sem
        self.parts = halves(window[1])
        self.block = rows * links.nn
        self.part_ids = {
            (p, mask): links.fresh()
            for p in range(len(self.parts))
            for mask in (X_BIT, Y_BIT, X_BIT | Y_BIT)
        }
        self.line_ids = [links.fresh() for _ in range(1, links.nn)]
        self.core_ids = [links.fresh() for _ in range(square.shape[0])]

    def spot(self, mask, p):
        low, size = self.parts[p][:2]
        return self.square.at[jnp.bitwise_xor(self.links.w, mask) // 2, :, pl.ds(low, size)]

    def own(self):
        return pltpu.make_async_copy(
            self.shard, self.square.at[self.links.w // 2], self.local_sem.at[0]
        )

    def start(self):
        k = self.links
        self.own().start()
        for p, (low, size, order) in enumerate(self.parts):
            for bit in order:
                k.send(self.shard.at[:, pl.ds(low, size)], self.spot(0, p), self.part_ids[p, bit], k.wide(bit))

    def arrive(self, p, mask):
        k = self.links
        k.copy(self.spot(mask, p), self.spot(mask, p), self.part_ids[p, mask], k.wide(X_BIT)).wait_recv()

    def forward(self):
        k = self.links
        for p, (low, size, (first, second)) in enumerate(self.parts):
            self.arrive(p, first)
            k.send(self.spot(first, p), self.spot(first, p), self.part_ids[p, first | second], k.wide(second))
        for p, (low, size, (first, second)) in enumerate(self.parts):
            self.arrive(p, second)

    def keep(self):
        return pltpu.make_async_copy(self.square, self.lines.at[self.links.z], self.local_sem.at[0])

    def line(self):
        k = self.links
        self.own().wait()
        for p in range(len(self.parts)):
            self.arrive(p, X_BIT | Y_BIT)
        self.keep().start()
        for step in range(1, k.nn):
            k.send(self.square, self.lines.at[k.z], self.line_ids[step - 1], k.along(step))

    def rows_of(self, square, core):
        rows = pl.ds((square * 2 + core) * self.block, self.block)
        return self.full.at[rows, pl.ds(*self.window)]

    def out(self, square):
        core = lax.rem(self.links.w, 2)
        return pltpu.make_async_copy(
            self.merged.at[square], self.rows_of(square, core), self.local_sem.at[1 + square]
        )

    def join(self):
        k = self.links
        self.keep().wait()
        for step in range(1, k.nn):
            came = lax.rem(k.z - step + k.nn, k.nn)
            k.copy(self.square, self.lines.at[came], self.line_ids[step - 1], k.along(step)).wait_recv()

        def one(square, carry):
            whole = jnp.concatenate(
                [self.lines[z, square, : self.rows].astype(F32) for z in range(k.nn)], axis=0
            )
            self.merged[square] = whole.astype(BF)
            return carry

        lax.fori_loop(0, self.merged.shape[0], one, 0)
        core = lax.rem(k.w, 2)
        for square, number in enumerate(self.core_ids):
            self.out(square).start()
            k.send(self.merged.at[square], self.rows_of(square, core), number, k.wide(1))

    def done(self):
        k = self.links
        core = lax.rem(k.w, 2)
        for square, number in enumerate(self.core_ids):
            self.out(square).wait()
            k.copy(self.merged.at[square], self.rows_of(square, 1 - core), number, k.wide(1)).wait_recv()


def dot(left, right):
    return jnp.dot(left, right, preferred_element_type=F32)


def dot_nt(left, right):
    return lax.dot_general(left, right, (((1,), (1,)), ((), ())), preferred_element_type=F32)


def dot_tn(left, right):
    return lax.dot_general(left, right, (((0,), (0,)), ((), ())), preferred_element_type=F32)


def iota(shape, dimension):
    return lax.broadcasted_iota(jnp.int32, shape, dimension)


def ones_where(mask):
    return jnp.where(mask, 1.0, 0.0).astype(BF)


def unpack_row(rows, first, each, total):
    devices = rows.shape[0]
    pick = ones_where(iota((128, total), 0) == first + lax.rem(iota((128, total), 1), each))
    spread = dot(rows.astype(BF), pick)
    mine = iota((devices, total), 1) // each == iota((devices, total), 0)
    return jnp.sum(jnp.where(mine, spread, 0.0), axis=0, keepdims=True)


def table_block(rows, first):
    pick_shape = (H * QB, 128)
    total = None
    for index in range(2):
        lane = first + H * index + iota(pick_shape, 0) // QB
        pick = ones_where(iota(pick_shape, 1) == lane)
        table = dot_nt(pick, rows.astype(BF)).astype(BF)
        wide = (NB, QB * 2 * NB)
        spread = dot(table, ones_where(lax.rem(iota(wide, 1), 2 * NB) == iota(wide, 0) + NB * index))
        total = spread if total is None else total + spread
    shape = (H * QB, QB * 2 * NB)
    mine = lax.rem(iota(shape, 0), QB) == iota(shape, 1) // (2 * NB)
    return jnp.where(mine, total, 0.0).astype(BF)


def bucket_ones(rel, lay, onehot, block):
    width = rel.shape[1]
    rows = iota((NB, width), 0)
    for query in range(QB):
        for index, bucket in enumerate((rel, lay)):
            row = bucket[pl.ds(block * QB + query, 1), :]
            low = (query * 2 + index) * NB
            onehot[low : low + NB, :] = ones_where(jnp.broadcast_to(row, (NB, width)) == rows)


def forward_kernel(nn, shapes, *refs):
    count = len(shapes)
    occupied, tokens, rel_hbm, lay_hbm, cotangent = refs[:5]
    shards = refs[5 : 5 + count]
    refs = refs[5 + count :]
    fulls, refs = refs[:count], refs[count:]
    (grad_h, na_t, q_t, k_h, v_h, att_t, hid_h, nf_t, mix_h, probs_h, slope_h, act_h) = refs[:12]
    down_grads, down_came, refs = refs[12], refs[13], refs[14:]
    (
        line,
        merged,
        x,
        rel,
        lay,
        small,
        lhs,
        onehot,
        bias,
        na,
        q,
        k,
        v,
        att,
        hid,
        nf,
        mix,
        slope,
        act,
        probs,
        w_one,
        w_wide,
        grad,
        down_stage,
        gains,
        turned,
        mixed_t,
        send_sem,
        recv_sem,
        gather_sem,
        local_sem,
        ring_sem,
        rest_square,
        rest_lines,
        rest_merged,
        rest_sem,
    ) = refs
    slots, width = x.shape
    links = Links(nn, send_sem, recv_sem)
    numbers = iter(range(64))

    def move(src, dst):
        copy = pltpu.make_async_copy(src, dst, local_sem.at[next(numbers)])
        copy.start()
        return copy

    arriving = [move(tokens, x), move(rel_hbm, rel), move(lay_hbm, lay)]
    grad_in = move(cotangent, grad)
    links.greet()
    g = []
    first_up = UP_TILES * TILE
    cuts = [(0, columns) for rows, columns in shapes]
    cuts[6:] = [(0, first_up), (first_up, shapes[6][1] - first_up), (0, width - REST)]
    for number, (low, columns) in enumerate(cuts):
        index = min(number, 6) if number < 8 else 7
        rows = shapes[index][0]
        odd = index == 7
        g.append(
            Gather(
                links,
                shards[index].at[:, pl.ds(low, columns)],
                w_wide.at[index - 5] if index in (5, 6) else fulls[index],
                rows,
                (low, columns),
                halves(columns, low) if columns > 128 else ((0, columns, PARTS[0]),),
                gather_sem.at[number],
                line if odd else None,
                merged if odd else None,
            )
        )
    rows, columns = shapes[-1]
    rest = GatherSquare(
        links,
        shards[-1].at[:, pl.ds(columns - REST, REST)],
        fulls[-1],
        rows,
        (columns - REST, REST),
        rest_sem,
        rest_square,
        rest_lines,
        rest_merged,
    )
    down_id = links.used
    small_g, q_g, k_g, v_g, o_g, gate_g, up_g, up_two_g, down_g = g
    leaving = []
    turning = {}
    ffn = mixed_t.shape[0]
    tiles = ffn // TILE
    across = slots // TILE
    pairs = H // 2
    blocks = slots // QB
    block, piece = down_stage.shape[3:]
    chunks = width // piece
    squares = down_stage.shape[1]
    valid = iota((1, slots), 1) < occupied[0] + IMG

    def turn_out(slot, source, target):
        if slot in turning:
            turning[slot].wait()

        def one(tile, carry):
            at = pl.ds(pl.multiple_of(tile * TILE, TILE), TILE)
            turned[slot, at, :] = source[:, at].T
            return carry

        lax.fori_loop(0, width // TILE, one, 0)
        turning[slot] = move(turned.at[slot], target)

    def unpack():
        rows = small.reshape(small.shape[0] // 8, 8, 128)[:, 0, :]
        each = width // rows.shape[0]
        gains[0:1, :] = unpack_row(rows, 0, each, width)
        gains[1:2, :] = unpack_row(rows, each, each, width)
        lhs[...] = table_block(rows, 2 * each)

    def normalise(source, row, target):
        def one(index, carry):
            at = pl.ds(pl.multiple_of(index * 64, 64), 64)
            values = source[at, :].astype(F32)
            scale = lax.rsqrt(jnp.mean(values * values, axis=-1, keepdims=True) + RMS_EPSILON)
            target[at, :] = (values * scale * gains[row : row + 1, :]).astype(BF)
            return carry

        lax.fori_loop(0, slots // 64, one, 0)

    def bias_block(block, carry):
        bucket_ones(rel, lay, onehot, block)
        found = jnp.where(valid, dot(lhs[...], onehot[...]), MASK_SCORE)
        bias[:, pl.ds(pl.multiple_of(block * QB, QB), QB), :] = found.reshape(H, QB, slots)
        return carry

    def add_bias(part, parts):
        lax.fori_loop(part * blocks // parts, (part + 1) * blocks // parts, bias_block, 0)

    def project(slot, target):
        def one(tile, carry):
            at = pl.ds(pl.multiple_of(tile * WIDE, WIDE), WIDE)
            target[:, at] = dot(na[...], w_one[slot, :, at]).astype(BF)
            return carry

        lax.fori_loop(0, width // WIDE, one, 0)

    def probs_out(pair):
        turn = lax.rem(pair, 2)
        return pltpu.make_async_copy(probs.at[turn], probs_h.at[pl.ds(pair * 2, 2)], ring_sem.at[turn])

    def attend_pair(pair, carry):
        @pl.when(pair >= 2)
        def _():
            probs_out(pair - 2).wait()

        at = pl.ds(pl.multiple_of(pair * 128, 128), 128)
        low = iota((slots, 128), 1) < HD
        queries = q[:, at]
        keys = k[:, at]
        found = []
        for side in range(2):
            mine = jnp.where(low if side == 0 else jnp.logical_not(low), queries, 0)
            scores = dot_nt(mine, keys) + bias[pair * 2 + side]
            peak = jnp.max(scores, axis=-1, keepdims=True)
            expo = jnp.exp(scores - peak)
            total = jnp.sum(expo, axis=-1, keepdims=True)
            share = (expo * (1.0 / total)).astype(BF)
            probs[lax.rem(pair, 2), side] = share
            found.append(dot(share, v[:, at]))
        att[:, at] = jnp.where(low, found[0], found[1]).astype(BF)
        probs_out(pair).start()
        return carry

    def attend(first, last):
        lax.fori_loop(first, last, attend_pair, 0)

    def output():
        def one(tile, carry):
            at = pl.ds(pl.multiple_of(tile * WIDE, WIDE), WIDE)
            hid[:, at] = x[:, at].astype(F32) + dot(att[...], w_one[1, :, at])
            return carry

        lax.fori_loop(0, width // WIDE, one, 0)
        leaving.append(move(hid, hid_h))

    def keep_valid():
        valid_rows = iota((slots, 1), 0) < occupied[0] + IMG

        def one(tile, carry):
            at = pl.ds(pl.multiple_of(tile * TILE, TILE), TILE)
            grad[:, at] = jnp.where(valid_rows, grad[:, at].astype(F32), 0.0).astype(BF)
            return carry

        lax.fori_loop(0, width // TILE, one, 0)
        leaving.append(move(grad, grad_h))

    def gate_spot(tile, second):
        at = pl.ds(pl.multiple_of(lax.rem(tile, across) * TILE, TILE), TILE)
        return bias.at[tile // across + second * (-(-tiles // across)), :, at]

    def gate_tile(tile, carry):
        at = pl.ds(pl.multiple_of(tile * TILE, TILE), TILE)
        gate = dot(nf[...], w_wide[0, :, at])
        square = gate * gate
        inner = GELU_SCALE * gate * (1.0 + GELU_CUBE * square)
        bend = jnp.tanh(inner)
        half = 0.5 * (1.0 + bend)
        gate_spot(tile, 0)[...] = gate * half
        gate_spot(tile, 1)[...] = half + 0.5 * gate * (1.0 - bend * bend) * GELU_SCALE * (
            1.0 + 3.0 * GELU_CUBE * square
        )
        return carry

    def ffn_out(tile):
        turn = lax.rem(tile, 2)
        at = pl.ds(pl.multiple_of(tile * TILE, TILE), TILE)
        return (
            pltpu.make_async_copy(slope.at[turn], slope_h.at[:, at], ring_sem.at[2 + turn]),
            pltpu.make_async_copy(act.at[turn], act_h.at[:, at], ring_sem.at[4 + turn]),
            pltpu.make_async_copy(mix.at[turn], mix_h.at[:, at], ring_sem.at[6 + turn]),
        )

    def ffn_tile(tile, carry):
        @pl.when(tile >= 2)
        def _():
            for copy in ffn_out(tile - 2):
                copy.wait()

        at = pl.ds(pl.multiple_of(tile * TILE, TILE), TILE)
        turn = lax.rem(tile, 2)
        up = dot(nf[...], w_wide[1, :, at])
        active = gate_spot(tile, 0)[...]
        rise = gate_spot(tile, 1)[...]
        mixed = (active * up).astype(BF)
        mix[turn] = mixed
        mixed_t[at, :] = mixed.T
        act[turn] = active.astype(BF)
        slope[turn] = (up * rise).astype(BF)
        for copy in ffn_out(tile):
            copy.start()
        return carry

    def down_place(chunk, half):
        return down_grads.at[chunk, pl.ds(half * squares, squares)]

    def down_copy(unit):
        half, chunk, turn = unit // chunks, lax.rem(unit, chunks), lax.rem(unit, 2)
        return pltpu.make_async_copy(down_stage.at[turn], down_place(chunk, half), ring_sem.at[8 + turn])

    def down_trade(unit):
        half, chunk = unit // chunks, lax.rem(unit, chunks)
        core = lax.rem(links.w, 2)
        there = pl.ds(half * squares, squares)
        return links.copy(
            down_grads.at[chunk, there, 1 - core],
            down_came.at[chunk, there],
            down_id + unit,
            links.wide(1),
        )

    def down_unit(unit, carry):
        half, chunk = unit // chunks, lax.rem(unit, chunks)
        size = 2 * squares * block
        rows = pl.ds(pl.multiple_of(half * size, 16), size)
        at = pl.ds(pl.multiple_of(chunk * piece, piece), piece)
        found = dot(mixed_t[rows, :], grad[:, at])
        down_stage[lax.rem(unit, 2)] = found.astype(BF).reshape(down_stage.shape[1:])
        down_copy(unit).start()

        @pl.when(unit >= 1)
        def _():
            down_copy(unit - 1).wait()
            down_trade(unit - 1).start()

        return carry

    def down_units(first, last):
        lax.fori_loop(first, last, down_unit, 0)

    small_g.start()
    q_g.start()
    rest.start()
    small_g.ready()
    small_g.spread()
    k_g.start()
    q_g.ready()
    q_g.spread()
    v_g.start()
    small_g.forward()
    small_g.settle()
    small_g.last()
    small_g.done()
    small_in = move(fulls[0], small)
    rest.forward()
    for copy in arriving:
        copy.wait()
    k_g.ready()
    k_g.spread()
    o_g.start()
    gate_g.start()
    q_g.forward()
    small_in.wait()
    unpack()
    normalise(x, 0, na)
    turn_out(0, na, na_t)
    q_g.settle()
    add_bias(0, 4)
    v_g.ready()
    v_g.spread()
    k_g.forward()
    q_g.last()
    add_bias(1, 4)
    k_g.settle()
    o_g.ready()
    o_g.spread()
    up_g.start()
    v_g.forward()
    add_bias(2, 4)
    k_g.last()
    v_g.settle()
    q_g.done()
    fetch_q = move(fulls[1], w_one.at[0])
    add_bias(3, 4)
    gate_g.ready()
    gate_g.spread()
    up_two_g.start()
    o_g.forward()
    fetch_q.wait()
    project(0, q)
    turn_out(1, q, q_t)
    k_g.done()
    fetch_k = move(fulls[2], w_one.at[1])
    v_g.last()
    fetch_k.wait()
    project(1, k)
    leaving.append(move(k, k_h))
    v_g.done()
    fetch_v = move(fulls[3], w_one.at[0])
    o_g.settle()
    fetch_v.wait()
    project(0, v)
    leaving.append(move(v, v_h))
    attend(0, 3)
    up_g.ready()
    up_g.spread()
    down_g.start()
    o_g.last()
    gate_g.forward()
    o_g.done()
    fetch_o = move(fulls[4], w_one.at[1])
    attend(3, 6)
    gate_g.settle()
    rest.line()
    attend(6, pairs)
    turn_out(0, att, att_t)
    fetch_o.wait()
    output()
    normalise(hid, 1, nf)
    turn_out(1, nf, nf_t)
    up_g.forward()
    up_two_g.ready()
    up_two_g.spread()
    grad_in.wait()
    keep_valid()
    down_g.ready()
    up_g.settle()
    gate_g.last()
    gate_g.done()
    leaving.append(move(w_wide.at[0], fulls[5]))
    lax.fori_loop(0, tiles, gate_tile, 0)
    up_g.last()
    up_two_g.forward()
    down_g.spread()
    up_g.done()
    lax.fori_loop(0, UP_TILES, ffn_tile, 0)
    up_two_g.settle()
    down_units(0, chunks)
    up_two_g.last()
    down_g.forward()
    down_g.settle()
    up_two_g.done()
    leaving.append(move(w_wide.at[1], fulls[6]))
    lax.fori_loop(UP_TILES, tiles, ffn_tile, 0)
    down_g.last()
    rest.join()
    down_units(chunks, 2 * chunks)
    down_copy(jnp.int32(2 * chunks - 1)).wait()
    down_trade(jnp.int32(2 * chunks - 1)).start()
    down_g.done()
    rest.done()
    for unit in range(2 * chunks):
        down_trade(jnp.int32(unit)).wait()
    for copy in leaving + list(turning.values()):
        copy.wait()
    for pair in (pairs - 2, pairs - 1):
        probs_out(pair).wait()
    for tile in (tiles - 2, tiles - 1):
        for copy in ffn_out(tile):
            copy.wait()
    links.finish()


def forward_all(nw, nn, counts, tokens, rel, lay, cotangent, shards, odd_rows):
    devices = nw * nn
    shapes = []
    for index, shard in enumerate(shards):
        rows = odd_rows if index == len(shards) - 1 else shard.shape[0]
        shapes.append((rows, shard.shape[1]))
    slots, width = tokens.shape
    copies = (len(shards) + 2) * (nn - 1 + 6 + nw // 2) + 2 * (width // DOWN_PIECE)
    ffn = shapes[5][1]
    low = jax.ShapeDtypeStruct((slots, width), BF)
    wide = jax.ShapeDtypeStruct((slots, ffn), BF)
    full = jax.ShapeDtypeStruct((slots, width), F32)
    out_shape = [
        jax.ShapeDtypeStruct((rows * devices, columns), shard.dtype)
        for (rows, columns), shard in zip(shapes, shards)
    ]
    low_t = jax.ShapeDtypeStruct((width, slots), BF)
    out_shape += [low, low_t, low_t, low, low, low_t, full, low_t, wide]
    out_shape += [jax.ShapeDtypeStruct((H, slots, slots), BF), wide, wide]
    down = (nw // 2, 2, nn * odd_rows, DOWN_PIECE)
    out_shape += [jax.ShapeDtypeStruct((width // DOWN_PIECE,) + down, BF)]
    out_shape += [jax.ShapeDtypeStruct((width // DOWN_PIECE, nw // 2, nn * odd_rows, DOWN_PIECE), BF)]
    tile_rows = shards[-1].shape[0]
    half = (tile_rows, REST)
    hbm = pl.BlockSpec(memory_space=pl.ANY)
    page = pltpu.VMEM((slots, width), BF)
    return pl.pallas_call(
        functools.partial(forward_kernel, nn, shapes),
        out_shape=out_shape,
        in_specs=[pl.BlockSpec(memory_space=pltpu.SMEM)] + [hbm] * (4 + len(shards)),
        out_specs=[hbm] * len(out_shape),
        scratch_shapes=[
            pltpu.VMEM((nn, tile_rows, width - REST), BF),
            pltpu.VMEM((nn * odd_rows, width - REST), BF),
            page,
            pltpu.VMEM((slots, slots), jnp.int32),
            pltpu.VMEM((slots, slots), jnp.int32),
            pltpu.VMEM((devices * 8, 128), F32),
            pltpu.VMEM((H * QB, QB * 2 * NB), BF),
            pltpu.VMEM((QB * 2 * NB, slots), BF),
            pltpu.VMEM((H, slots, slots), F32),
            page,
            page,
            page,
            page,
            page,
            pltpu.VMEM((slots, width), F32),
            page,
            pltpu.VMEM((2, slots, TILE), BF),
            pltpu.VMEM((2, slots, TILE), BF),
            pltpu.VMEM((2, slots, TILE), BF),
            pltpu.VMEM((2, 2, slots, slots), BF),
            pltpu.VMEM((2, width, width), BF),
            pltpu.VMEM((2, width, ffn), BF),
            page,
            pltpu.VMEM((2, down[0] // 2) + down[1:], BF),
            pltpu.VMEM((8, width), F32),
            pltpu.VMEM((2, width, slots), BF),
            pltpu.VMEM((ffn, slots), BF),
            pltpu.SemaphoreType.DMA((copies,)),
            pltpu.SemaphoreType.DMA((copies,)),
            pltpu.SemaphoreType.DMA((len(shards) + 1,)),
            pltpu.SemaphoreType.DMA((64,)),
            pltpu.SemaphoreType.DMA((10,)),
            pltpu.VMEM((nw // 2,) + half, BF),
            pltpu.VMEM((nn, nw // 2) + half, BF),
            pltpu.VMEM((nw // 2, nn * odd_rows, half[1]), BF),
            pltpu.SemaphoreType.DMA((1 + nw // 2,)),
        ],
        compiler_params=pltpu.CompilerParams(
            collective_id=0, has_side_effects=True, vmem_limit_bytes=63 * 2**20
        ),
    )(counts, tokens, rel, lay, cotangent, *shards)


class Scatter:
    def __init__(self, links, chunks, rows, columns, grads, came, slots, base, traded=False, first=0):
        self.links, self.chunks, self.rows, self.columns = links, chunks, rows, columns
        self.grads, self.came = grads, came
        (self.held, self.other, self.round, self.out_line, self.in_line, self.load_sem) = slots
        self.base = base
        self.traded = traded
        self.first = first
        self.block = rows * links.nn
        self.parts = halves(columns)
        self.core = lax.rem(links.w, 2)
        self.ring = self.held.shape[0]
        self.line_ring = self.out_line.shape[0]

    def number(self, chunk, kind):
        return self.base + chunk * SCATTER_COPIES + kind

    def core_copy(self, chunk):
        return self.links.copy(
            self.grads.at[chunk, :, 1 - self.core],
            self.came.at[chunk],
            self.number(chunk, 0),
            self.links.wide(1),
        )

    def trade(self, chunk):
        self.core_copy(chunk).start()

    def loads(self, chunk):
        slot, turn = lax.rem(chunk, self.ring), lax.rem(chunk, 2)
        return (
            pltpu.make_async_copy(
                self.grads.at[chunk, :, self.core], self.held.at[slot], self.load_sem.at[turn, 0]
            ),
            pltpu.make_async_copy(
                self.came.at[chunk], self.other.at[turn], self.load_sem.at[turn, 1]
            ),
        )

    def fetch(self, chunk):
        if not self.traded:
            self.core_copy(chunk).wait_recv()
        for load in self.loads(chunk):
            load.start()

    def square(self, mask):
        return jnp.bitwise_xor(self.links.w, mask) // 2

    def hop(self, chunk, p, mask):
        slot = lax.rem(chunk, self.ring)
        low, size, order = self.parts[p]
        bit = order[1] if mask & order[1] else order[0]
        kind = 1 + p * 3 + (X_BIT, Y_BIT, X_BIT | Y_BIT).index(mask)
        return self.links.copy(
            self.held.at[slot, self.square(mask), :, pl.ds(low, size)],
            self.round.at[slot, kind - 1, :, pl.ds(0, size)],
            self.number(chunk, kind),
            self.links.wide(bit),
        )

    def landed(self, chunk, p, mask):
        return self.round.at[
            lax.rem(chunk, self.ring), p * 3 + (X_BIT, Y_BIT, X_BIT | Y_BIT).index(mask)
        ]

    def add_core(self, chunk):
        for load in self.loads(chunk):
            load.wait()
        slot, turn = lax.rem(chunk, self.ring), lax.rem(chunk, 2)

        def one(square, carry):
            self.held[slot, square] = (
                self.held[slot, square].astype(F32) + self.other[turn, square].astype(F32)
            ).astype(BF)
            return carry

        lax.fori_loop(0, self.held.shape[1], one, 0)
        for p, part in enumerate(self.parts):
            self.hop(chunk, p, X_BIT | Y_BIT).start()
        for p, part in enumerate(self.parts):
            self.hop(chunk, p, part[2][1]).start()

    def add_corner(self, chunk):
        slot = lax.rem(chunk, self.ring)
        for p, (low, size, order) in enumerate(self.parts):
            self.hop(chunk, p, X_BIT | Y_BIT).wait_recv()
            square = self.square(order[0])
            came = self.landed(chunk, p, X_BIT | Y_BIT)
            self.held[slot, square, :, low : low + size] = (
                self.held[slot, square, :, low : low + size].astype(F32)
                + came[:, :size].astype(F32)
            ).astype(BF)
        for p, part in enumerate(self.parts):
            self.hop(chunk, p, part[2][0]).start()

    def line_copy(self, chunk, step):
        k = self.links
        slot = lax.rem(chunk, self.line_ring)
        return k.copy(
            self.out_line.at[slot, lax.rem(k.z + step, k.nn)],
            self.in_line.at[slot, step - 1],
            self.number(chunk, 6 + step),
            k.along(step),
        )

    def add_square(self, chunk):
        slot, line = lax.rem(chunk, self.ring), lax.rem(chunk, self.line_ring)
        home = self.square(0)
        for p, (low, size, order) in enumerate(self.parts):
            total = self.held[slot, home, :, low : low + size].astype(F32)
            for mask in order:
                self.hop(chunk, p, mask).wait_recv()
                total = total + self.landed(chunk, p, mask)[:, :size].astype(F32)
            for z in range(self.links.nn):
                self.out_line[line, z, : self.rows, low : low + size] = total[
                    z * self.rows : (z + 1) * self.rows
                ].astype(BF)
        for step in range(1, self.links.nn):
            self.line_copy(chunk, step).start()
        if not self.traded:
            self.core_copy(chunk).wait_send()
        for p in range(len(self.parts)):
            for mask in (X_BIT, Y_BIT, X_BIT | Y_BIT):
                self.hop(chunk, p, mask).wait_send()

    def total(self, chunk):
        slot = lax.rem(chunk, self.line_ring)
        total = self.out_line[slot, self.links.z, : self.rows].astype(F32)
        for step in range(1, self.links.nn):
            self.line_copy(chunk, step).wait_recv()
            total = total + self.in_line[slot, step - 1, : self.rows].astype(F32)
        return total

    def pump(self, index, out):
        index = jnp.int32(index)
        steps = (self.fetch, self.add_core, self.add_corner, self.add_square, self.finish)
        for lag, action in zip(FEW_LAG if self.traded else LAG, steps):
            chunk = index - lag + self.first

            @pl.when(jnp.logical_and(chunk >= self.first, chunk < self.chunks))
            def _(chunk=chunk, action=action):
                action(chunk, out) if action == self.finish else action(chunk)

    def finish(self, chunk, out):
        out[chunk] = self.total(chunk)
        for step in range(1, self.links.nn):
            self.line_copy(chunk, step).wait_send()


class ScatterLine:
    def __init__(self, links, rows, columns, grads, came, slots, base):
        self.links, self.rows, self.columns = links, rows, columns
        self.grads, self.came = grads, came
        (self.held, self.other, self.square, self.round, self.in_line, self.load_sem) = slots
        self.base = base
        self.parts = halves(columns)
        self.core = lax.rem(links.w, 2)

    def number(self, chunk, kind):
        return self.base + chunk * SCATTER_COPIES + kind

    def core_copy(self, chunk):
        return self.links.copy(
            self.grads.at[chunk, :, 1 - self.core],
            self.came.at[chunk],
            self.number(chunk, 0),
            self.links.wide(1),
        )

    def loads(self, chunk):
        return (
            pltpu.make_async_copy(
                self.grads.at[chunk, :, self.core], self.held.at[chunk], self.load_sem.at[0]
            ),
            pltpu.make_async_copy(self.came.at[chunk], self.other, self.load_sem.at[1]),
        )

    def fetch(self, chunk):
        self.core_copy(chunk).wait_recv()
        for load in self.loads(chunk):
            load.start()

    def line_copy(self, chunk, step):
        k = self.links
        rows = pl.ds(pl.multiple_of(lax.rem(k.z + step, k.nn) * self.rows, self.rows), self.rows)
        return k.copy(
            self.held.at[chunk, :, rows],
            self.in_line.at[chunk, step - 1],
            self.number(chunk, 6 + step),
            k.along(step),
        )

    def add_core(self, chunk):
        for load in self.loads(chunk):
            load.wait()

        def one(square, carry):
            self.held[chunk, square] = (
                self.held[chunk, square].astype(F32) + self.other[square].astype(F32)
            ).astype(BF)
            return carry

        lax.fori_loop(0, self.held.shape[1], one, 0)
        for step in range(1, self.links.nn):
            self.line_copy(chunk, step).start()

    def spot(self, mask):
        return jnp.bitwise_xor(self.links.w, mask) // 2

    def hop(self, chunk, p, mask):
        low, size, order = self.parts[p]
        bit = order[1] if mask & order[1] else order[0]
        kind = 1 + p * 3 + (X_BIT, Y_BIT, X_BIT | Y_BIT).index(mask)
        return self.links.copy(
            self.square.at[chunk, self.spot(mask), :, pl.ds(low, size)],
            self.round.at[chunk, kind - 1],
            self.number(chunk, kind),
            self.links.wide(bit),
        )

    def landed(self, chunk, p, mask):
        kind = p * 3 + (X_BIT, Y_BIT, X_BIT | Y_BIT).index(mask)
        return self.round[chunk, kind].astype(F32)

    def add_line(self, chunk):
        for step in range(1, self.links.nn):
            self.line_copy(chunk, step).wait_recv()
        rows = pl.ds(pl.multiple_of(self.links.z * self.rows, self.rows), self.rows)
        for square in range(self.held.shape[1]):
            total = self.held[chunk, square, rows, :].astype(F32)
            for step in range(1, self.links.nn):
                total = total + self.in_line[chunk, step - 1, square].astype(F32)
            self.square[chunk, square] = total.astype(BF)
        for p, part in enumerate(self.parts):
            self.hop(chunk, p, X_BIT | Y_BIT).start()
        for p, part in enumerate(self.parts):
            self.hop(chunk, p, part[2][1]).start()

    def add_corner(self, chunk):
        for p, (low, size, order) in enumerate(self.parts):
            self.hop(chunk, p, X_BIT | Y_BIT).wait_recv()
            spot = self.spot(order[0])
            self.square[chunk, spot, :, low : low + size] = (
                self.square[chunk, spot, :, low : low + size].astype(F32)
                + self.landed(chunk, p, X_BIT | Y_BIT)
            ).astype(BF)
        for p, part in enumerate(self.parts):
            self.hop(chunk, p, part[2][0]).start()

    def finish(self, chunk, out):
        for p, (low, size, order) in enumerate(self.parts):
            total = self.square[chunk, self.spot(0), :, low : low + size].astype(F32)
            for mask in order:
                self.hop(chunk, p, mask).wait_recv()
                total = total + self.landed(chunk, p, mask)
            out[chunk, :, low : low + size] = total
        self.core_copy(chunk).wait_send()
        for step in range(1, self.links.nn):
            self.line_copy(chunk, step).wait_send()
        for p in range(len(self.parts)):
            for mask in (X_BIT, Y_BIT, X_BIT | Y_BIT):
                self.hop(chunk, p, mask).wait_send()


class ScatterSmall:
    def __init__(self, links, grads, out, came, round_in, line_in, mine):
        self.links, self.grads, self.out = links, grads, out
        self.came, self.round, self.line, self.mine = came, round_in, line_in, mine
        self.home = links.w // 2
        self.masks = (X_BIT, Y_BIT, X_BIT | Y_BIT)
        self.core_id = links.fresh()
        self.square_ids = [links.fresh() for _ in self.masks]
        self.line_ids = [links.fresh() for _ in range(1, links.nn)]

    def core_copy(self):
        k = self.links
        return k.copy(self.grads.at[:, 1 - lax.rem(k.w, 2)], self.came, self.core_id, k.wide(1))

    def square_copy(self, index):
        k, mask = self.links, self.masks[index]
        spot = jnp.bitwise_xor(k.w, mask) // 2
        return k.copy(self.mine.at[spot], self.round.at[index], self.square_ids[index], k.wide(mask))

    def line_copy(self, step):
        k = self.links
        rows = pl.ds(pl.multiple_of(lax.rem(k.z + step, k.nn) * 8, 8), 8)
        spot = self.mine.at[self.home, rows]
        return k.copy(spot, self.line.at[step - 1], self.line_ids[step - 1], k.along(step))

    def trade(self):
        self.core_copy().start()

    def spread(self):
        self.core_copy().wait()
        self.mine[...] = self.grads[:, lax.rem(self.links.w, 2)] + self.came[...]
        for index in range(len(self.masks)):
            self.square_copy(index).start()

    def along(self):
        for index in range(len(self.masks)):
            self.square_copy(index).wait()
        total = self.mine[self.home]
        for index in range(len(self.masks)):
            total = total + self.round[index]
        self.mine[self.home] = total
        for step in range(1, self.links.nn):
            self.line_copy(step).start()

    def finish(self):
        total = self.mine[self.home, pl.ds(pl.multiple_of(self.links.z * 8, 8), 8)]
        for step in range(1, self.links.nn):
            self.line_copy(step).wait()
            total = total + self.line[step - 1]
        self.out[...] = total


def padded(rows):
    return (rows + 15) // 16 * 16


def scatter_slots(squares, nn, rows, columns, ring, line_ring):
    half = columns // 2
    return [
        pltpu.VMEM((ring, squares, nn * rows, columns), BF),
        pltpu.VMEM((2, squares, nn * rows, columns), BF),
        pltpu.VMEM((ring, 6, nn * rows, half), BF),
        pltpu.VMEM((line_ring, nn, padded(rows), columns), BF),
        pltpu.VMEM((line_ring, nn - 1, padded(rows), columns), BF),
        pltpu.SemaphoreType.DMA((2, 2)),
    ]


def norm_pull(values, gain, grad):
    scale = lax.rsqrt(jnp.mean(values * values, axis=-1, keepdims=True) + RMS_EPSILON)
    scaled = grad * gain
    along = jnp.mean(scaled * values, axis=-1, keepdims=True)
    share = grad * values * scale
    return scale * scaled - values * (scale * scale * scale * along), share


def fold_rows(values):
    return jnp.sum(values.reshape(values.shape[0] // 8, 8, values.shape[1]), axis=0)


def pack_row(row, first, each, devices):
    total = row.shape[1]
    shape = (128, total)
    pick = jnp.where(iota(shape, 0) == first + lax.rem(iota(shape, 1), each), 1.0, 0.0)
    shape = (devices, total)
    mine = jnp.where(iota(shape, 1) // each == iota(shape, 0), row, 0.0)
    return lax.dot_general(
        mine,
        pick,
        (((1,), (1,)), ((), ())),
        preferred_element_type=F32,
        precision=lax.Precision.HIGHEST,
    )


def backward_kernel(nn, few_facts, many_facts, *refs):
    occupied, refs = refs[0], refs[1:]
    (
        tokens,
        rel_hbm,
        lay_hbm,
        grad_h,
        small_h,
        query_h,
        key_h,
        value_h,
        output_h,
        gate_h,
        up_h,
        down_h,
        na_t,
        q_t,
        k_h,
        v_h,
        att_t,
        hid_h,
        nf_t,
        mix_h,
        probs_h,
        slope_h,
        act_h,
        few_grads,
        few_came,
    ) = refs[:25]
    refs = refs[25:]
    (out_h, rows_out, few_out, many_out, small_out, many_grads, many_came) = refs[:7]
    few_slots, many_slots, late_slots, refs = refs[7:13], refs[13:19], refs[19:25], refs[25:]
    (
        x,
        rel,
        lay,
        small,
        gains,
        grad,
        left,
        acc,
        hid,
        wd_s,
        wgu_s,
        pair,
        slope_s,
        act_s,
        many_stage,
        branch,
        w_one,
        pull,
        pull_t,
        qt,
        k,
        v,
        probs,
        pieces,
        onehot,
        table,
        sums,
        small_grads,
        small_came,
        small_round,
        small_line,
        small_mine,
        send_sem,
        recv_sem,
        local_sem,
        tile_sem,
        stage_sem,
        probs_sem,
    ) = refs
    slots, width = x.shape
    links = Links(nn, send_sem, recv_sem)
    numbers = iter(range(64))

    def later_move(src, dst):
        return pltpu.make_async_copy(src, dst, local_sem.at[next(numbers)])

    def move(src, dst):
        copy = later_move(src, dst)
        copy.start()
        return copy

    few = Scatter(links, *few_facts, few_grads, few_came, few_slots, 0, traded=True)
    base = few_facts[0] * SCATTER_COPIES
    many = Scatter(links, *many_facts, many_grads, many_came, many_slots, base, first=LATE)
    late = ScatterLine(links, *many_facts[1:], many_grads, many_came, late_slots, base)
    links.used = base + many_facts[0] * SCATTER_COPIES
    little = ScatterSmall(
        links, small_grads, small_out, small_came, small_round, small_line, small_mine
    )
    ffn = mix_h.shape[1]
    tiles = ffn // TILE
    pairs = H // 2
    wide = many.columns
    squares = many_stage.shape[1]
    devices = small.shape[0] // 8
    each = width // devices
    zero = jnp.zeros((8, width), F32)

    def tile_copies(tile):
        turn = lax.rem(tile, 2)
        at = pl.ds(pl.multiple_of(tile * TILE, TILE), TILE)
        return [
            pltpu.make_async_copy(src, dst, tile_sem.at[turn, index])
            for index, (src, dst) in enumerate(
                (
                    (down_h.at[at], wd_s.at[turn]),
                    (gate_h.at[:, at], wgu_s.at[turn, :, pl.ds(0, TILE)]),
                    (up_h.at[:, at], wgu_s.at[turn, :, pl.ds(TILE, TILE)]),
                    (slope_h.at[:, at], slope_s.at[turn]),
                    (act_h.at[:, at], act_s.at[turn]),
                )
            )
        ]

    def many_copy(chunk):
        turn = lax.rem(chunk, 2)
        return pltpu.make_async_copy(many_stage.at[turn], many.grads.at[chunk], stage_sem.at[turn])

    def flush(chunk):
        many_copy(chunk).wait()
        many.trade(chunk)

    def make(chunk, left_rows, right, dot_one):
        found = dot_one(left_rows[...], right())
        many_stage[lax.rem(chunk, 2)] = found.astype(BF).reshape(many_stage.shape[1:])
        many_copy(chunk).start()

    def few_pump(index):
        few.pump(index, few_out)

    def many_pump(index):
        many.pump(index, many_out)

    def ffn_tile(tile, carry):
        turn = lax.rem(tile, 2)

        @pl.when(tile + 1 < tiles)
        def _():
            for copy in tile_copies(tile + 1):
                copy.start()

        @pl.when(tile == 3)
        def _():
            start(*later)
            start(*last)

        for copy in tile_copies(tile):
            copy.wait()
        grad_mixed = dot_nt(grad[...], wd_s[turn])
        pair[:, :TILE] = (grad_mixed * slope_s[turn].astype(F32)).astype(BF)
        pair[:, TILE:] = (grad_mixed * act_s[turn].astype(F32)).astype(BF)
        make(tile, left, lambda: pair[...], dot)

        @pl.when(lax.rem(tile, 2) == 1)
        def _():
            few_pump(tile // 2 + 2)

        acc[...] += dot_nt(pair[...], wgu_s[turn])
        flush(tile)
        many_pump(tile - FFN_LAG)

        @pl.when(jnp.logical_and(tile >= 2, tile < 2 + LATE))
        def _():
            late.add_core(tile - 2)

        @pl.when(jnp.logical_and(tile >= 1, tile < 1 + LATE))
        def _():
            late.fetch(tile - 1)

        return carry

    def unpack():
        rows = small.reshape(devices, 8, 128)[:, 0, :]
        gains[0:1, :] = unpack_row(rows, 0, each, width)
        gains[1:2, :] = unpack_row(rows, each, each, width)

    def norm_two():
        def one(index, total):
            at = pl.ds(pl.multiple_of(index * 64, 64), 64)
            part, share = norm_pull(hid[at, :], gains[1:2, :], acc[at, :])
            whole = grad[at, :].astype(F32) + part
            hid[at, :] = whole
            branch[at, :] = whole.astype(BF)
            return total + fold_rows(share)

        sums[0] = lax.fori_loop(0, slots // 64, one, zero)

    def output_chunk(part, carry):
        at = pl.ds(pl.multiple_of(part * wide, wide), wide)
        make(tiles + part, pull_t, lambda: branch[:, at], dot)
        return carry

    def pull_back():
        def one(tile, carry):
            at = pl.ds(pl.multiple_of(tile * WIDE, WIDE), WIDE)
            found = dot_nt(branch[...], w_one[0, at, :]).astype(BF)
            pull[:, at] = found
            pull_t[at, :] = found.T
            return carry

        lax.fori_loop(0, width // WIDE, one, 0)

    def probs_copy(index):
        turn = lax.rem(index, 2)
        return pltpu.make_async_copy(
            probs_h.at[pl.ds(index * 2, 2)], probs.at[turn], probs_sem.at[turn]
        )

    def attend_pair(index, carry):
        @pl.when(index + 1 < pairs)
        def _():
            probs_copy(index + 1).start()

        probs_copy(index).wait()
        turn = lax.rem(index, 2)
        at = pl.ds(pl.multiple_of(index * 128, 128), 128)
        low = iota((slots, 128), 1) < HD
        keys, pulls, values = k[:, at], pull[:, at], v[:, at]
        found = []
        for side in range(2):
            head = index * 2 + side
            mine = jnp.where(low if side == 0 else jnp.logical_not(low), pulls, 0)
            share = probs[turn, side]
            wanted = dot_nt(mine, values)
            share_f = share.astype(F32)
            joint = share_f * wanted
            piece = (joint - share_f * jnp.sum(joint, axis=-1, keepdims=True)).astype(BF)
            pieces[pl.ds(pl.multiple_of(head * slots, slots), slots), :] = piece
            found.append(dot(piece, keys))
            rows = pl.ds(pl.multiple_of(head * HD, HD), HD)
            qt[rows, :] = dot(qt[rows, :], piece).astype(BF)
            pull_t[rows, :] = dot(pull_t[rows, :], share).astype(BF)
        pull[:, at] = jnp.where(low, found[0], found[1]).astype(BF)
        return carry

    def attend(first, last):
        lax.fori_loop(first, last, attend_pair, 0)

    first_head_chunk = tiles + width // wide

    def head_chunks(half):
        at = pl.ds(pl.multiple_of(half * wide, wide), wide)
        chunk = first_head_chunk + half * 3

        def turned_chunk(index, carry):
            found = jnp.where(index == 0, pull_t[at, :], qt[at, :])
            make(chunk + 2 * index, left, lambda: found, dot_nt)

            @pl.when(index == 0)
            def _():
                make(chunk + 1, left, lambda: pull[:, at], dot)
                flush(chunk)

            return carry

        lax.fori_loop(0, 2, turned_chunk, 0)
        flush(chunk + 1)
        flush(chunk + 2)

    def table_blocks(index, carry):
        sides = []
        for side in range(2):
            block = index * 2 + side
            at = slice(side * slots, (side + 1) * slots)
            for query in range(BACK_QB):
                for which, bucket in enumerate((rel, lay)):
                    row = bucket[pl.ds(block * BACK_QB + query, 1), :]
                    first = (query * 2 + which) * NB
                    onehot[first : first + NB, at] = ones_where(
                        jnp.broadcast_to(row, (NB, slots)) == iota((NB, slots), 0)
                    )
            heads = [
                pieces[pl.ds(pl.multiple_of(head * slots + block * BACK_QB, BACK_QB), BACK_QB), :]
                for head in range(H)
            ]
            sides.append(jnp.concatenate(heads, axis=0))
        table[...] += dot_nt(onehot[...], jnp.concatenate(sides, axis=1))
        return carry

    def add_table(part, parts):
        blocks = slots // BACK_QB // 2
        lax.fori_loop(part * blocks // parts, (part + 1) * blocks // parts, table_blocks, 0)

    whole = ffn // slots
    first_mix = width // slots * ffn

    def output_moves():
        moves = [
            later_move(down_h.at[:, pl.ds(part * slots, slots)], pieces.at[pl.ds(part * ffn, ffn)])
            for part in range(width // slots)
        ]
        moves += [
            later_move(
                mix_h.at[:, pl.ds(part * slots, slots)],
                pieces.at[pl.ds(first_mix + part * slots, slots)],
            )
            for part in range(whole)
        ]
        return moves + [later_move(mix_h.at[:, pl.ds(whole * slots, TILE)], slope_s.at[0])]

    def down_project(part):
        at = pl.ds(pl.multiple_of(part * slots, slots), slots)

        def one(index, total):
            rows = pl.ds(pl.multiple_of(part * ffn + index * slots, TILE), slots)
            mixed = pl.ds(pl.multiple_of(first_mix + index * slots, TILE), slots)
            acc[:, at] += dot(pieces[mixed, :], pieces[rows, :])
            return total

        lax.fori_loop(0, whole, one, 0)
        rows = pl.ds(pl.multiple_of(part * ffn + whole * slots, TILE), TILE)
        total = acc[:, at] + dot(slope_s[0], pieces[rows, :])
        valid_rows = iota((slots, 1), 0) < occupied[0] + IMG
        x[:, at] = jnp.where(valid_rows, total, 0.0).astype(BF)

    def turn_back():
        def one(tile, carry):
            at = pl.ds(pl.multiple_of(tile * TILE, TILE), TILE)
            v[:, at] = pull_t[at, :].T
            branch[:, at] = qt[at, :].T
            return carry

        lax.fori_loop(0, width // TILE, one, 0)

    def pull_normed(source, slot, first):
        def one(tile, carry):
            at = pl.ds(pl.multiple_of(tile * WIDE, WIDE), WIDE)
            found = dot_nt(source[...], w_one[slot, at, :])
            acc[:, at] = found if first else acc[:, at] + found
            return carry

        lax.fori_loop(0, width // WIDE, one, 0)

    def norm_one():
        def one(index, total):
            at = pl.ds(pl.multiple_of(index * 64, 64), 64)
            part, share = norm_pull(x[at, :].astype(F32), gains[0:1, :], acc[at, :])
            hid[at, :] += part
            return total + fold_rows(share)

        sums[1] = lax.fori_loop(0, slots // 64, one, zero)

    def pack():
        total = table[...]
        mine = iota(total.shape, 0) // (2 * NB) == lax.rem(iota(total.shape, 1), BACK_QB)
        folded = jnp.sum(
            jnp.where(mine, total, 0.0).reshape(BACK_QB, 2 * NB, H * BACK_QB), axis=0
        )
        packed = [
            pack_row(jnp.sum(sums[1], axis=0, keepdims=True), 0, each, devices),
            pack_row(jnp.sum(sums[0], axis=0, keepdims=True), 0, each, devices),
        ]
        shape = (H * BACK_QB, 128)
        pick = jnp.where(iota(shape, 1) == iota(shape, 0) // BACK_QB, 1.0, 0.0)
        for index in range(2):
            packed.append(
                jnp.dot(
                    folded[index * NB : (index + 1) * NB],
                    pick,
                    preferred_element_type=F32,
                    precision=lax.Precision.HIGHEST,
                )
            )
        small_grads[...] = jnp.zeros_like(small_grads)
        for device in range(devices):
            wide_at, z = divmod(device, nn)
            for index, rows in enumerate(packed):
                at = z * 8 + index
                small_grads[wide_at // 2, wide_at % 2, at : at + 1, :] = rows[device : device + 1]

    later = [
        later_move(*pair_of)
        for pair_of in (
            (hid_h, hid),
            (small_h, small),
            (att_t, pull_t),
            (output_h, w_one.at[0]),
            (q_t, qt),
            (k_h, k),
            (v_h, v),
        )
    ]
    last = [
        later_move(*pair_of)
        for pair_of in ((tokens, x), (rel_hbm, rel), (lay_hbm, lay), (value_h, w_one.at[1]))
    ]
    na_in, query_in, key_in = (
        later_move(*pair_of)
        for pair_of in ((na_t, left), (query_h, w_one.at[0]), (key_h, w_one.at[0]))
    )
    rows_copy, out_copy = later_move(hid, rows_out), later_move(x, out_h)
    output_in = output_moves()
    hid_in = later_move(hid_h, acc)

    def start(*copies):
        for copy in copies:
            copy.start()

    def wait(*copies):
        for copy in copies:
            copy.wait()

    few.fetch(jnp.int32(0))
    start(*tile_copies(0))
    first_in = [move(grad_h, grad), move(nf_t, left)]
    links.greet()
    few.fetch(jnp.int32(1))
    few.add_core(jnp.int32(0))
    acc[...] = jnp.zeros_like(acc)
    table[...] = jnp.zeros_like(table)
    wait(*first_in)
    lax.fori_loop(0, tiles, ffn_tile, 0)
    wait(*later)
    na_in.start()
    unpack()
    norm_two()
    def step(index, carry):
        few_pump(index + tiles // 2 + 2)
        many_pump(index + tiles - FFN_LAG)

        for lag, action in ((1, late.add_line), (3, late.add_corner), (5, late.finish)):
            chunk = index - lag

            @pl.when(jnp.logical_and(chunk >= 0, chunk < LATE))
            def _(chunk=chunk, action=action):
                action(chunk, many_out) if action == late.finish else action(chunk)

        @pl.when(index == 0)
        def _():
            lax.fori_loop(0, width // wide, output_chunk, 0)
            pull_back()
            flush(tiles)
            flush(tiles + 1)
            query_in.start()
            probs_copy(jnp.int32(0)).start()

        second = index >= 4
        turn = jnp.where(second, index - 4, index - 1)
        attends = jnp.logical_and(turn >= 0, turn < 2)

        @pl.when(attends)
        def _():
            first = 2 * turn + jnp.where(second, 4, 0)
            attend(first, first + 2)

        @pl.when(index == 3)
        def _():
            wait(*last)
            na_in.wait()

        @pl.when(jnp.logical_or(index == 3, index == 6))
        def _():
            head_chunks(index // 3 - 1)

        @pl.when(jnp.logical_and(index >= 7, index < 10))
        def _():
            add_table(index - 7, 3)

        @pl.when(index == 10)
        def _():
            start(*output_in)
            query_in.wait()
            turn_back()
            pull_normed(pull, 0, True)
            key_in.start()

        @pl.when(index == 11)
        def _():
            pull_normed(v, 1, False)
            key_in.wait()
            pull_normed(branch, 0, False)

        @pl.when(index == 12)
        def _():
            norm_one()
            rows_copy.start()
            hid_in.start()
            pack()
            little.trade()

        @pl.when(index == 13)
        def _():
            wait(*output_in)
            hid_in.wait()
            little.spread()

        @pl.when(index == 15)
        def _():
            little.along()

        @pl.when(jnp.logical_or(index == 14, index == 16))
        def _():
            down_project(index // 2 - 7)

        @pl.when(index == 17)
        def _():
            out_copy.start()

        return carry

    lax.fori_loop(0, many.chunks - LATE + LAGS - (tiles - FFN_LAG) + 1, step, 0)
    little.finish()
    wait(rows_copy, out_copy)
    links.finish()


def backward_all(nw, nn, counts, page, weights, saved):
    squares = nw // 2
    devices = nw * nn
    slots, width = page[0].shape
    ffn = weights[5].shape[1]
    few = (width // DOWN_PIECE, ffn // devices, DOWN_PIECE)
    many = (ffn // TILE + 8, width // devices, 2 * TILE)
    outs = [jax.ShapeDtypeStruct((slots, width), BF), jax.ShapeDtypeStruct((slots, width), F32)]
    for chunks, rows, columns in (few, many):
        outs.append(jax.ShapeDtypeStruct((chunks, rows, columns), F32))
    outs.append(jax.ShapeDtypeStruct((8, 128), F32))
    chunks, rows, columns = many
    outs.append(jax.ShapeDtypeStruct((chunks, squares, 2, nn * rows, columns), BF))
    outs.append(jax.ShapeDtypeStruct((chunks, squares, nn * rows, columns), BF))
    copies = (few[0] + many[0]) * SCATTER_COPIES + 16
    vmem = pl.BlockSpec(memory_space=pltpu.VMEM)
    hbm = pl.BlockSpec(memory_space=pl.ANY)
    low = pltpu.VMEM((slots, width), BF)
    turned = pltpu.VMEM((width, slots), BF)
    full = pltpu.VMEM((slots, width), F32)
    inputs = (counts,) + tuple(page) + tuple(weights) + tuple(saved)
    return pl.pallas_call(
        functools.partial(backward_kernel, nn, few, many),
        out_shape=outs,
        in_specs=[pl.BlockSpec(memory_space=pltpu.SMEM)] + [hbm] * (len(inputs) - 1),
        out_specs=[hbm, hbm, vmem, vmem, vmem, hbm, hbm],
        scratch_shapes=scatter_slots(squares, nn, few[1], few[2], few[0], few[0])
        + scatter_slots(squares, nn, many[1], many[2], RING, LINE_RING)
        + [
            pltpu.VMEM((LATE, squares, nn * many[1], many[2]), BF),
            pltpu.VMEM((squares, nn * many[1], many[2]), BF),
            pltpu.VMEM((LATE, squares, many[1], many[2]), BF),
            pltpu.VMEM((LATE, 6, many[1], many[2] // 2), BF),
            pltpu.VMEM((LATE, nn - 1, squares, many[1], many[2]), BF),
            pltpu.SemaphoreType.DMA((2,)),
        ]
        + [
            low,
            pltpu.VMEM((slots, slots), jnp.int32),
            pltpu.VMEM((slots, slots), jnp.int32),
            pltpu.VMEM((devices * 8, 128), F32),
            pltpu.VMEM((8, width), F32),
            low,
            turned,
            full,
            full,
            pltpu.VMEM((2, TILE, width), BF),
            pltpu.VMEM((2, width, 2 * TILE), BF),
            pltpu.VMEM((slots, 2 * TILE), BF),
            pltpu.VMEM((2, slots, TILE), BF),
            pltpu.VMEM((2, slots, TILE), BF),
            pltpu.VMEM((2, squares, 2, nn * many[1], many[2]), BF),
            low,
            pltpu.VMEM((2, width, width), BF),
            low,
            turned,
            turned,
            low,
            low,
            pltpu.VMEM((2, 2, slots, slots), BF),
            pltpu.VMEM((H * slots, slots), BF),
            pltpu.VMEM((BACK_QB * 2 * NB, 2 * slots), BF),
            pltpu.VMEM((BACK_QB * 2 * NB, H * BACK_QB), F32),
            pltpu.VMEM((2, 8, width), F32),
            pltpu.VMEM((squares, 2, nn * 8, 128), F32),
            pltpu.VMEM((squares, nn * 8, 128), F32),
            pltpu.VMEM((3, nn * 8, 128), F32),
            pltpu.VMEM((nn - 1, 8, 128), F32),
            pltpu.VMEM((squares, nn * 8, 128), F32),
            pltpu.SemaphoreType.DMA((copies,)),
            pltpu.SemaphoreType.DMA((copies,)),
            pltpu.SemaphoreType.DMA((64,)),
            pltpu.SemaphoreType.DMA((2, 5)),
            pltpu.SemaphoreType.DMA((2,)),
            pltpu.SemaphoreType.DMA((2,)),
        ],
        compiler_params=pltpu.CompilerParams(
            collective_id=1, has_side_effects=True, vmem_limit_bytes=63 * 2**20
        ),
    )(*inputs)[:5]


def place_kernel(few_h, many_h, rows_h, out_h, small, *refs):
    (whole_out, row_out, query, key, value, output, gate, up, down) = refs[:9]
    (gain_attn, gain_ffn, rel, lay) = refs[9:13]
    few, many, rows, whole, in_sem, out_sem = refs[13:]
    tiles = gate.shape[1] // TILE
    wide = many.shape[2]
    part = rows.shape[0] // 8
    arriving = [
        pltpu.make_async_copy(src, dst, in_sem.at[index])
        for index, (src, dst) in enumerate(
            [(many_h, many), (few_h, few), (out_h, whole)]
            + [
                (rows_h.at[pl.ds(index * part, part)], rows.at[pl.ds(index * part, part)])
                for index in range(8)
            ]
        )
    ]
    for copy in arriving:
        copy.start()
    moves = []

    def move(src, dst):
        copy = pltpu.make_async_copy(src, dst, out_sem.at[len(moves)])
        copy.start()
        moves.append(copy)

    for index, target in enumerate((gain_attn, gain_ffn, rel, lay)):
        target[...] = small[index, : target.shape[0]]
    arriving[0].wait()
    for tile in range(tiles):
        at = pl.ds(tile * TILE, TILE)
        move(many.at[tile, :, pl.ds(0, TILE)], gate.at[:, at])
        move(many.at[tile, :, pl.ds(TILE, TILE)], up.at[:, at])
    halves_of = output.shape[1] // wide
    for half in range(halves_of):
        at = pl.ds(half * wide, wide)
        move(many.at[tiles + half], output.at[:, at])
        first = tiles + halves_of + half * 3
        for index, target in enumerate((value, query, key)):
            move(many.at[first + index], target.at[:, at])
    arriving[1].wait()
    for chunk in range(few.shape[0]):
        move(few.at[chunk], down.at[:, pl.ds(chunk * few.shape[2], few.shape[2])])
    arriving[2].wait()
    move(whole, whole_out)
    for index in range(8):
        arriving[3 + index].wait()
        at = pl.ds(index * part, part)
        move(rows.at[at], row_out.at[at])
    for copy in moves:
        copy.wait()


def place_all(few, many, rows, out, small, shapes):
    hbm = pl.BlockSpec(memory_space=pl.ANY)
    vmem = pl.BlockSpec(memory_space=pltpu.VMEM)
    outs = [jax.ShapeDtypeStruct(out.shape, BF), jax.ShapeDtypeStruct(rows.shape, F32)]
    outs += [jax.ShapeDtypeStruct(shape, F32) for shape in shapes]
    return pl.pallas_call(
        place_kernel,
        out_shape=outs,
        in_specs=[hbm] * 4 + [vmem],
        out_specs=[hbm] * 9 + [vmem] * 4,
        scratch_shapes=[
            pltpu.VMEM(few.shape, F32),
            pltpu.VMEM(many.shape, F32),
            pltpu.VMEM(rows.shape, F32),
            pltpu.VMEM(out.shape, BF),
            pltpu.SemaphoreType.DMA((16,)),
            pltpu.SemaphoreType.DMA((64,)),
        ],
        compiler_params=pltpu.CompilerParams(vmem_limit_bytes=63 * 2**20),
    )(few, many, rows, out, small)


def local_fast(
    nw,
    nn,
    tokens,
    w_query,
    w_key,
    w_value,
    w_output,
    w_gate,
    w_up,
    w_down,
    gain_attn,
    gain_ffn,
    rel_table,
    lay_table,
    ocr_counts,
    rel_bucket,
    lay_bucket,
    cotangent,
):
    small = jnp.concatenate([gain_attn, gain_ffn, rel_table, lay_table]).astype(F32)
    small = jnp.pad(small[None], ((0, 7), (0, 128 - small.shape[0])))
    down = jnp.pad(w_down, ((0, padded(w_down.shape[0]) - w_down.shape[0]), (0, 0)))
    page = (tokens, rel_bucket, lay_bucket)
    shards = [small, w_query, w_key, w_value, w_output, w_gate, w_up, down]
    found = forward_all(nw, nn, ocr_counts, *page, cotangent, shards, w_down.shape[0])
    weights, grad, saved = found[: len(shards)], found[len(shards)], found[len(shards) + 1 :]
    output, grad_tokens, few, many, small = backward_all(
        nw, nn, ocr_counts, page + (grad,), weights, saved
    )

    square = w_query.shape
    shapes = [square] * 4 + [w_gate.shape, w_up.shape, w_down.shape]
    shapes += [part.shape for part in (gain_attn, gain_ffn, rel_table, lay_table)]
    return tuple(place_all(few, many, grad_tokens, output, small, shapes))


def local(
    tokens,
    w_query,
    w_key,
    w_value,
    w_output,
    w_gate,
    w_up,
    w_down,
    gain_attn,
    gain_ffn,
    rel_table,
    lay_table,
    ocr_counts,
    rel_bucket,
    lay_bucket,
    cotangent,
):
    slot = tokens.shape[0]
    valid = jnp.arange(slot) < ocr_counts[0] + IMG
    buckets = jnp.arange(NB)
    onehot = jnp.concatenate(
        [
            (rel_bucket[:, :, None] == buckets).astype(jnp.bfloat16),
            (lay_bucket[:, :, None] == buckets).astype(jnp.bfloat16),
        ],
        axis=2,
    )
    tokens_f = tokens.astype(jnp.float32)
    weights = gather_weights(
        w_query,
        w_key,
        w_value,
        w_output,
        w_gate,
        w_up,
        w_down,
        gain_attn,
        gain_ffn,
        rel_table,
        lay_table,
    )
    result, saved = forward_pass(tokens_f, weights, onehot, valid)
    output = jnp.where(valid[:, None], result, 0.0).astype(jnp.bfloat16)
    (
        full_query,
        full_key,
        full_value,
        full_output,
        full_gate,
        full_up,
        full_down,
        full_gain_attn,
        full_gain_ffn,
        full_rel,
        full_lay,
    ) = weights
    (
        normed_attn,
        queries,
        keys_all,
        values_all,
        log_totals,
        attended,
        hidden_one,
        normed_ffn,
        gate_act,
        up_proj,
        mixed,
    ) = saved
    grad_result = jnp.where(valid[:, None], cotangent.astype(jnp.float32), 0.0)
    grad_low = grad_result.astype(jnp.bfloat16)
    grad_down = contract_rows(mixed, grad_low)
    grad_mixed = contract_cols(grad_low, full_down)
    gated_value, gated_pull = jax.vjp(gated_product, gate_act, up_proj)
    grad_gate_act, grad_up_proj = gated_pull(grad_mixed)
    gate_low = grad_gate_act.astype(jnp.bfloat16)
    up_low = grad_up_proj.astype(jnp.bfloat16)
    grad_gate = contract_rows(normed_ffn, gate_low)
    grad_up = contract_rows(normed_ffn, up_low)
    grad_normed_ffn = contract_cols(gate_low, full_gate) + contract_cols(up_low, full_up)
    norm_value, norm_pull = jax.vjp(rms_scale, hidden_one, full_gain_ffn.astype(jnp.float32))
    grad_hidden_part, grad_gain_ffn = norm_pull(grad_normed_ffn)
    grad_hidden = grad_result + grad_hidden_part
    branch_low = grad_hidden.astype(jnp.bfloat16)
    grad_output = contract_rows(attended, branch_low)
    grad_attended = contract_cols(branch_low, full_output).astype(jnp.bfloat16)
    grad_queries, grad_keys, grad_values, grad_table_all = attention_backward(
        queries,
        keys_all,
        values_all,
        log_totals,
        grad_attended,
        table_pair(full_rel, full_lay),
        onehot,
        valid,
    )
    grad_rel = grad_table_all[:NB].reshape(NB * H)
    grad_lay = grad_table_all[NB:].reshape(NB * H)
    grad_query = contract_rows(normed_attn, grad_queries)
    grad_key = contract_rows(normed_attn, grad_keys)
    grad_value = contract_rows(normed_attn, grad_values)
    grad_normed_attn = (
        contract_cols(grad_queries, full_query)
        + contract_cols(grad_keys, full_key)
        + contract_cols(grad_values, full_value)
    )
    input_value, input_pull = jax.vjp(rms_scale, tokens_f, full_gain_attn.astype(jnp.float32))
    grad_input_part, grad_gain_attn = input_pull(grad_normed_attn)
    grad_tokens = grad_hidden + grad_input_part
    owned = (
        lax.psum_scatter(grad_query, ("wide", "narrow"), scatter_dimension=0, tiled=True),
        lax.psum_scatter(grad_key, ("wide", "narrow"), scatter_dimension=0, tiled=True),
        lax.psum_scatter(grad_value, ("wide", "narrow"), scatter_dimension=0, tiled=True),
        lax.psum_scatter(grad_output, ("wide", "narrow"), scatter_dimension=0, tiled=True),
        lax.psum_scatter(grad_gate, ("wide", "narrow"), scatter_dimension=0, tiled=True),
        lax.psum_scatter(grad_up, ("wide", "narrow"), scatter_dimension=0, tiled=True),
        lax.psum_scatter(grad_down, ("wide", "narrow"), scatter_dimension=0, tiled=True),
        lax.psum_scatter(grad_gain_attn, ("wide", "narrow"), scatter_dimension=0, tiled=True),
        lax.psum_scatter(grad_gain_ffn, ("wide", "narrow"), scatter_dimension=0, tiled=True),
        lax.psum_scatter(grad_rel, ("wide", "narrow"), scatter_dimension=0, tiled=True),
        lax.psum_scatter(grad_lay, ("wide", "narrow"), scatter_dimension=0, tiled=True),
    )
    return (
        output,
        grad_tokens,
        owned[0],
        owned[1],
        owned[2],
        owned[3],
        owned[4],
        owned[5],
        owned[6],
        owned[7],
        owned[8],
        owned[9],
        owned[10],
    )


def solution(mesh):
    nw, nn = mesh.shape["wide"], mesh.shape["narrow"]

    def body(*args):
        if nw == 8 and nw * nn == NB and args[1].shape[0] % 16 == 0:
            return local_fast(nw, nn, *args)
        return local(*args)

    placed = (
        P(("wide", "narrow"), None),
        P(("wide", "narrow"), None),
        P(("wide", "narrow"), None),
        P(("wide", "narrow"), None),
        P(("wide", "narrow"), None),
        P(("wide", "narrow"), None),
        P(("wide", "narrow"), None),
        P(("wide", "narrow"), None),
        P(("wide", "narrow")),
        P(("wide", "narrow")),
        P(("wide", "narrow")),
        P(("wide", "narrow")),
        P(("wide", "narrow")),
        P(("wide", "narrow"), None),
        P(("wide", "narrow"), None),
        P(("wide", "narrow"), None),
    )
    return jax.shard_map(
        body,
        mesh=mesh,
        in_specs=placed,
        out_specs=(
            P(("wide", "narrow"), None),
            P(("wide", "narrow"), None),
            P(("wide", "narrow"), None),
            P(("wide", "narrow"), None),
            P(("wide", "narrow"), None),
            P(("wide", "narrow"), None),
            P(("wide", "narrow"), None),
            P(("wide", "narrow"), None),
            P(("wide", "narrow"), None),
            P(("wide", "narrow")),
            P(("wide", "narrow")),
            P(("wide", "narrow")),
            P(("wide", "narrow")),
        ),
        check_vma=False,
    )
```

```python
import functools

import jax
import jax.numpy as jnp
from jax import lax
from jax.experimental import pallas as pl
from jax.experimental.pallas import tpu as pltpu
from jax.sharding import PartitionSpec as P

H = 16
HD = 64
NB = 32
IMG = 196
RING = 6
SCATTER_COPIES = 10
LAG = (0, 1, 2, 4, 8)
LINE_RING = 10
FEW_LAG = (0, 1, 2, 4, 14)
LAGS = LAG[-1]
FFN_LAG = 6
LATE = 2
BACK_QB = 16
WIDE = 512
DOWN_PIECE = 256
REST = 512
FIRST = 512
UP_TILES = 6
TILE = 256
QB = 8
GELU_SCALE = 0.7978845608028654
GELU_CUBE = 0.044715


RMS_EPSILON = 1e-06
MASK_SCORE = -1000000000.0
HEAD_GROUP = 4


def rms_scale(values, gain):
    return (
        values * lax.rsqrt(jnp.mean(values * values, axis=-1, keepdims=True) + RMS_EPSILON) * gain
    )


def gated_product(gate_act, up_proj):
    return jax.nn.gelu(gate_act, approximate=True) * up_proj


def product(left, right):
    return jnp.dot(left, right, preferred_element_type=jnp.float32)


def contract_rows(left, right):
    return lax.dot_general(
        left, right, (((0,), (0,)), ((), ())), preferred_element_type=jnp.float32
    )


def contract_cols(left, right):
    return lax.dot_general(
        left, right, (((1,), (1,)), ((), ())), preferred_element_type=jnp.float32
    )


def split_heads(matrix):
    return jnp.moveaxis(matrix.reshape(matrix.shape[0], H // HEAD_GROUP, HEAD_GROUP, HD), 1, 0)


def join_heads(stacked):
    return jnp.moveaxis(stacked, 0, 1).reshape(stacked.shape[1], H * HD)


def group_tables(table_all):
    return jnp.moveaxis(table_all.reshape(2 * NB, H // HEAD_GROUP, HEAD_GROUP), 1, 0)


def group_scores(query_group, key_group, table_group, onehot, valid):
    scores = jnp.einsum("ihd,jhd->hij", query_group, key_group, preferred_element_type=jnp.float32)
    scores = scores + jnp.einsum(
        "ijb,bh->hij", onehot, table_group, preferred_element_type=jnp.float32
    )
    return jnp.where(valid[None, None, :], scores, MASK_SCORE)


def gather_weights(
    w_query,
    w_key,
    w_value,
    w_output,
    w_gate,
    w_up,
    w_down,
    gain_attn,
    gain_ffn,
    rel_table,
    lay_table,
):
    return (
        lax.all_gather(w_query, ("wide", "narrow"), axis=0, tiled=True),
        lax.all_gather(w_key, ("wide", "narrow"), axis=0, tiled=True),
        lax.all_gather(w_value, ("wide", "narrow"), axis=0, tiled=True),
        lax.all_gather(w_output, ("wide", "narrow"), axis=0, tiled=True),
        lax.all_gather(w_gate, ("wide", "narrow"), axis=0, tiled=True),
        lax.all_gather(w_up, ("wide", "narrow"), axis=0, tiled=True),
        lax.all_gather(w_down, ("wide", "narrow"), axis=0, tiled=True),
        lax.all_gather(gain_attn, ("wide", "narrow"), axis=0, tiled=True),
        lax.all_gather(gain_ffn, ("wide", "narrow"), axis=0, tiled=True),
        lax.all_gather(rel_table, ("wide", "narrow"), axis=0, tiled=True),
        lax.all_gather(lay_table, ("wide", "narrow"), axis=0, tiled=True),
    )


def table_pair(full_rel, full_lay):
    return jnp.concatenate([full_rel.reshape(NB, H), full_lay.reshape(NB, H)], axis=0)


def forward_pass(tokens_f, weights, onehot, valid):
    (
        full_query,
        full_key,
        full_value,
        full_output,
        full_gate,
        full_up,
        full_down,
        full_gain_attn,
        full_gain_ffn,
        full_rel,
        full_lay,
    ) = weights
    normed_attn = rms_scale(tokens_f, full_gain_attn.astype(jnp.float32)).astype(jnp.bfloat16)
    queries = product(normed_attn, full_query).astype(jnp.bfloat16)
    keys_all = product(normed_attn, full_key).astype(jnp.bfloat16)
    values_all = product(normed_attn, full_value).astype(jnp.bfloat16)

    def forward_one_group(operands):
        query_group, key_group, value_group, table_group = operands
        scores = group_scores(query_group, key_group, table_group, onehot, valid)
        peak = jnp.max(scores, axis=-1, keepdims=True)
        expo = jnp.exp(scores - peak)
        total = jnp.sum(expo, axis=-1, keepdims=True)
        probs_low = (expo / total).astype(jnp.bfloat16)
        attended_group = jnp.einsum(
            "hij,jhd->ihd", probs_low, value_group, preferred_element_type=jnp.float32
        )
        return (attended_group.astype(jnp.bfloat16), (peak + jnp.log(total))[..., 0])

    stacked, log_totals = lax.map(
        forward_one_group,
        (
            split_heads(queries),
            split_heads(keys_all),
            split_heads(values_all),
            group_tables(table_pair(full_rel, full_lay)),
        ),
    )
    attended = join_heads(stacked)
    hidden_one = tokens_f + product(attended, full_output)
    normed_ffn = rms_scale(hidden_one, full_gain_ffn.astype(jnp.float32)).astype(jnp.bfloat16)
    gate_act = product(normed_ffn, full_gate)
    up_proj = product(normed_ffn, full_up)
    mixed = gated_product(gate_act, up_proj).astype(jnp.bfloat16)
    result = hidden_one + product(mixed, full_down)
    return (
        result,
        (
            normed_attn,
            queries,
            keys_all,
            values_all,
            log_totals,
            attended,
            hidden_one,
            normed_ffn,
            gate_act,
            up_proj,
            mixed,
        ),
    )


def attention_backward(
    queries, keys_all, values_all, log_totals, grad_attended, table_all, onehot, valid
):

    def attention_one_group(operands):
        query_group, key_group, value_group, table_group, lse_group, grad_group = operands
        scores = group_scores(query_group, key_group, table_group, onehot, valid)
        probs = jnp.exp(scores - lse_group[..., None])
        probs_low = probs.astype(jnp.bfloat16)
        grad_values = jnp.einsum(
            "hij,ihd->jhd", probs_low, grad_group, preferred_element_type=jnp.float32
        )
        grad_probs = jnp.einsum(
            "ihd,jhd->hij", grad_group, value_group, preferred_element_type=jnp.float32
        )
        grad_scores = (
            probs * (grad_probs - jnp.sum(probs * grad_probs, axis=-1, keepdims=True))
        ).astype(jnp.bfloat16)
        grad_queries = jnp.einsum(
            "hij,jhd->ihd", grad_scores, key_group, preferred_element_type=jnp.float32
        )
        grad_keys = jnp.einsum(
            "hij,ihd->jhd", grad_scores, query_group, preferred_element_type=jnp.float32
        )
        grad_table = jnp.einsum(
            "hij,ijb->bh", grad_scores, onehot, preferred_element_type=jnp.float32
        )
        return (
            grad_queries.astype(jnp.bfloat16),
            grad_keys.astype(jnp.bfloat16),
            grad_values.astype(jnp.bfloat16),
            grad_table,
        )

    grad_q_all, grad_k_all, grad_v_all, grad_tables = lax.map(
        attention_one_group,
        (
            split_heads(queries),
            split_heads(keys_all),
            split_heads(values_all),
            group_tables(table_all),
            log_totals,
            split_heads(grad_attended),
        ),
    )
    grad_table_all = jnp.moveaxis(grad_tables, 0, 1).reshape(2 * NB, H)
    return (join_heads(grad_q_all), join_heads(grad_k_all), join_heads(grad_v_all), grad_table_all)


MESH_ID = pl.DeviceIdType.MESH
BF = jnp.bfloat16
F32 = jnp.float32
X_BIT = 2
Y_BIT = 4
PARTS = ((X_BIT, Y_BIT), (Y_BIT, X_BIT))


class Links:
    def __init__(self, nn, send_sem, recv_sem):
        self.nn = nn
        self.w = lax.axis_index("wide")
        self.z = lax.axis_index("narrow")
        self.send_sem = send_sem
        self.recv_sem = recv_sem
        self.used = 0
        self.sent = []

    def fresh(self):
        self.used += 1
        return self.used - 1

    def wide(self, bit):
        return (jnp.bitwise_xor(self.w, bit), self.z)

    def along(self, step):
        return (self.w, lax.rem(self.z + step, self.nn))

    def copy(self, src, dst, number, device):
        return pltpu.make_async_remote_copy(
            src_ref=src,
            dst_ref=dst,
            send_sem=self.send_sem.at[number],
            recv_sem=self.recv_sem.at[number],
            device_id=device,
            device_id_type=MESH_ID,
        )

    def send(self, src, dst, number, device):
        copy = self.copy(src, dst, number, device)
        copy.start()
        self.sent.append(copy)

    def greet(self):
        barrier = pltpu.get_barrier_semaphore()
        others = [self.wide(bit) for bit in (1, X_BIT, Y_BIT)]
        others += [self.along(step) for step in range(1, self.nn)]
        for other in others:
            pl.semaphore_signal(barrier, inc=1, device_id=other, device_id_type=MESH_ID)
        pl.semaphore_wait(barrier, len(others))

    def finish(self):
        for copy in self.sent:
            copy.wait_send()


class Gather:
    def __init__(self, links, shard, full, rows, window, parts, local_sem, line=None, merged=None):
        self.links, self.shard, self.full, self.rows, self.parts = links, shard, full, rows, parts
        self.window = window
        self.local_sem, self.line, self.merged = local_sem, line, merged
        nn = links.nn
        self.block = rows * nn
        self.line_ids = [links.fresh() for _ in range(1, nn)]
        self.part_ids = {
            (p, mask): links.fresh()
            for p in range(len(parts))
            for mask in (X_BIT, Y_BIT, X_BIT | Y_BIT)
        }
        self.core_ids = {mask: links.fresh() for mask in (0, X_BIT, Y_BIT, X_BIT | Y_BIT)}

    def place(self, w, z):
        if self.line is not None:
            return self.line.at[z]
        return self.full.at[pl.ds((w * self.links.nn + z) * self.rows, self.rows), pl.ds(*self.window)]

    def span(self, mask, part=None):
        rows = pl.ds(jnp.bitwise_xor(self.links.w, mask) * self.block, self.block)
        low, size = self.window if part is None else self.parts[part][:2]
        return self.full.at[rows, pl.ds(low, size)]

    def own(self):
        return pltpu.make_async_copy(
            self.shard, self.place(self.links.w, self.links.z), self.local_sem
        )

    def start(self):
        k = self.links
        self.own().start()
        for step in range(1, k.nn):
            k.send(self.shard, self.place(k.w, k.z), self.line_ids[step - 1], k.along(step))

    def ready(self):
        k = self.links
        self.own().wait()
        for step in range(1, k.nn):
            came = lax.rem(k.z - step + k.nn, k.nn)
            k.copy(
                self.shard, self.place(k.w, came), self.line_ids[step - 1], k.along(step)
            ).wait_recv()
        if self.line is not None:
            whole = jnp.concatenate(
                [self.line[z, : self.rows].astype(F32) for z in range(k.nn)], axis=0
            )
            self.merged[...] = whole.astype(BF)
            move = pltpu.make_async_copy(self.merged, self.span(0), self.local_sem)
            move.start()
            move.wait()

    def spread(self):
        k = self.links
        for p, part in enumerate(self.parts):
            for bit in part[2]:
                k.send(self.span(0, p), self.span(0, p), self.part_ids[p, bit], k.wide(bit))
        k.send(self.span(0), self.span(0), self.core_ids[0], k.wide(1))

    def arrive(self, p, mask):
        k = self.links
        k.copy(
            self.span(mask, p), self.span(mask, p), self.part_ids[p, mask], k.wide(X_BIT)
        ).wait_recv()

    def forward(self):
        k = self.links
        for p, part in enumerate(self.parts):
            first, second = part[2]
            self.arrive(p, first)
            both = first | second
            k.send(self.span(first, p), self.span(first, p), self.part_ids[p, both], k.wide(second))

    def settle(self):
        k = self.links
        for p, part in enumerate(self.parts):
            self.arrive(p, part[2][1])
        for mask in (X_BIT, Y_BIT):
            k.send(self.span(mask), self.span(mask), self.core_ids[mask], k.wide(1))

    def last(self):
        k = self.links
        both = X_BIT | Y_BIT
        for p in range(len(self.parts)):
            self.arrive(p, both)
        k.send(self.span(both), self.span(both), self.core_ids[both], k.wide(1))

    def done(self):
        k = self.links
        for mask, number in self.core_ids.items():
            place = self.span(mask | 1)
            k.copy(place, place, number, k.wide(1)).wait_recv()


def halves(columns, first=0):
    low = columns // 256 * 128
    return ((first, low, PARTS[0]), (first + low, columns - low, PARTS[1]))


class GatherSquare:
    def __init__(self, links, shard, full, rows, window, local_sem, square, lines, merged):
        self.links, self.shard, self.full, self.rows, self.window = links, shard, full, rows, window
        self.square, self.lines, self.merged, self.local_sem = square, lines, merged, local_sem
        self.parts = halves(window[1])
        self.block = rows * links.nn
        self.part_ids = {
            (p, mask): links.fresh()
            for p in range(len(self.parts))
            for mask in (X_BIT, Y_BIT, X_BIT | Y_BIT)
        }
        self.line_ids = [links.fresh() for _ in range(1, links.nn)]
        self.core_ids = [links.fresh() for _ in range(square.shape[0])]

    def spot(self, mask, p):
        low, size = self.parts[p][:2]
        return self.square.at[jnp.bitwise_xor(self.links.w, mask) // 2, :, pl.ds(low, size)]

    def own(self):
        return pltpu.make_async_copy(
            self.shard, self.square.at[self.links.w // 2], self.local_sem.at[0]
        )

    def start(self):
        k = self.links
        self.own().start()
        for p, (low, size, order) in enumerate(self.parts):
            for bit in order:
                k.send(self.shard.at[:, pl.ds(low, size)], self.spot(0, p), self.part_ids[p, bit], k.wide(bit))

    def arrive(self, p, mask):
        k = self.links
        k.copy(self.spot(mask, p), self.spot(mask, p), self.part_ids[p, mask], k.wide(X_BIT)).wait_recv()

    def forward(self):
        k = self.links
        for p, (low, size, (first, second)) in enumerate(self.parts):
            self.arrive(p, first)
            k.send(self.spot(first, p), self.spot(first, p), self.part_ids[p, first | second], k.wide(second))
        for p, (low, size, (first, second)) in enumerate(self.parts):
            self.arrive(p, second)

    def keep(self):
        return pltpu.make_async_copy(self.square, self.lines.at[self.links.z], self.local_sem.at[0])

    def line(self):
        k = self.links
        self.own().wait()
        for p in range(len(self.parts)):
            self.arrive(p, X_BIT | Y_BIT)
        self.keep().start()
        for step in range(1, k.nn):
            k.send(self.square, self.lines.at[k.z], self.line_ids[step - 1], k.along(step))

    def rows_of(self, square, core):
        rows = pl.ds((square * 2 + core) * self.block, self.block)
        return self.full.at[rows, pl.ds(*self.window)]

    def out(self, square):
        core = lax.rem(self.links.w, 2)
        return pltpu.make_async_copy(
            self.merged.at[square], self.rows_of(square, core), self.local_sem.at[1 + square]
        )

    def join(self):
        k = self.links
        self.keep().wait()
        for step in range(1, k.nn):
            came = lax.rem(k.z - step + k.nn, k.nn)
            k.copy(self.square, self.lines.at[came], self.line_ids[step - 1], k.along(step)).wait_recv()

        def one(square, carry):
            whole = jnp.concatenate(
                [self.lines[z, square, : self.rows].astype(F32) for z in range(k.nn)], axis=0
            )
            self.merged[square] = whole.astype(BF)
            return carry

        lax.fori_loop(0, self.merged.shape[0], one, 0)
        core = lax.rem(k.w, 2)
        for square, number in enumerate(self.core_ids):
            self.out(square).start()
            k.send(self.merged.at[square], self.rows_of(square, core), number, k.wide(1))

    def done(self):
        k = self.links
        core = lax.rem(k.w, 2)
        for square, number in enumerate(self.core_ids):
            self.out(square).wait()
            k.copy(self.merged.at[square], self.rows_of(square, 1 - core), number, k.wide(1)).wait_recv()


def dot(left, right):
    return jnp.dot(left, right, preferred_element_type=F32)


def dot_nt(left, right):
    return lax.dot_general(left, right, (((1,), (1,)), ((), ())), preferred_element_type=F32)


def dot_tn(left, right):
    return lax.dot_general(left, right, (((0,), (0,)), ((), ())), preferred_element_type=F32)


def iota(shape, dimension):
    return lax.broadcasted_iota(jnp.int32, shape, dimension)


def ones_where(mask):
    return jnp.where(mask, 1.0, 0.0).astype(BF)


def small_rows(small, index):
    return small.reshape(small.shape[0] // 8, 8, 128)[:, index, :]


def unpack_row(small, index, total):
    rows = small_rows(small, index)
    devices = rows.shape[0]
    each = total // devices
    pick = ones_where(iota((128, total), 0) == lax.rem(iota((128, total), 1), each))
    spread = dot(rows.astype(BF), pick)
    mine = iota((devices, total), 1) // each == iota((devices, total), 0)
    return jnp.sum(jnp.where(mine, spread, 0.0), axis=0, keepdims=True)


def table_block(small):
    pick_shape = (H * QB, 128)
    total = None
    pick = ones_where(iota(pick_shape, 1) == iota(pick_shape, 0) // QB)
    for index in range(2):
        table = dot_nt(pick, small_rows(small, 2 + index).astype(BF)).astype(BF)
        wide = (NB, QB * 2 * NB)
        spread = dot(table, ones_where(lax.rem(iota(wide, 1), 2 * NB) == iota(wide, 0) + NB * index))
        total = spread if total is None else total + spread
    shape = (H * QB, QB * 2 * NB)
    mine = lax.rem(iota(shape, 0), QB) == iota(shape, 1) // (2 * NB)
    return jnp.where(mine, total, 0.0).astype(BF)


def bucket_ones(rel, lay, onehot, block):
    width = rel.shape[1]
    rows = iota((NB, width), 0)
    for query in range(QB):
        for index, bucket in enumerate((rel, lay)):
            row = bucket[pl.ds(block * QB + query, 1), :]
            low = (query * 2 + index) * NB
            onehot[low : low + NB, :] = ones_where(jnp.broadcast_to(row, (NB, width)) == rows)


def forward_kernel(nn, shapes, *refs):
    count = len(shapes)
    occupied, tokens, rel_hbm, lay_hbm, cotangent = refs[:5]
    parameters, down_shard = refs[5:9], refs[9]
    shards = refs[10 : 8 + count]
    refs = refs[8 + count :]
    fulls, refs = refs[:count], refs[count:]
    (grad_h, na_t, q_t, k_h, v_h, att_t, hid_h, nf_t, mix_h, probs_h, slope_h, act_h) = refs[:12]
    down_grads, down_came, refs = refs[12], refs[13], refs[14:]
    (
        line,
        merged,
        x,
        rel,
        lay,
        small,
        lhs,
        onehot,
        bias,
        na,
        q,
        k,
        v,
        att,
        hid,
        nf,
        mix,
        slope,
        act,
        probs,
        w_one,
        w_wide,
        grad,
        down_stage,
        gains,
        turned,
        mixed_t,
        send_sem,
        recv_sem,
        gather_sem,
        local_sem,
        ring_sem,
        rest_square,
        rest_lines,
        rest_merged,
        rest_sem,
        small_shard,
        down_padded,
    ) = refs
    shards = (small_shard,) + tuple(shards) + (down_padded,)
    slots, width = x.shape
    links = Links(nn, send_sem, recv_sem)
    numbers = iter(range(64))

    def move(src, dst):
        copy = pltpu.make_async_copy(src, dst, local_sem.at[next(numbers)])
        copy.start()
        return copy

    small_shard[...] = jnp.zeros_like(small_shard)
    for index, part in enumerate(parameters):
        small_shard[index : index + 1, : part.shape[0]] = part[...].astype(F32).reshape(1, part.shape[0])
    down_padded[...] = jnp.zeros_like(down_padded)
    down_padded[: down_shard.shape[0], :] = down_shard[...]
    links.greet()
    g = []
    first, wide = UP_TILES * TILE, shapes[5][1]
    cuts = [(0, 0, shapes[0][1]), (1, 0, FIRST), (1, FIRST, width - FIRST)]
    cuts += [(index, 0, width) for index in (2, 3, 4)]
    for index in (5, 6):
        cuts += [(index, 0, first), (index, first, wide - first)]
    cuts.append((7, 0, width - REST))
    for number, (index, low, columns) in enumerate(cuts):
        odd = index == 7
        g.append(
            Gather(
                links,
                shards[index].at[:, pl.ds(low, columns)],
                w_wide.at[index - 5] if index in (5, 6) else fulls[index],
                shapes[index][0],
                (low, columns),
                halves(columns, low) if columns > 128 else ((0, columns, PARTS[0]),),
                gather_sem.at[number],
                line if odd else None,
                merged if odd else None,
            )
        )
    rows, columns = shapes[-1]
    rest = GatherSquare(
        links,
        shards[-1].at[:, pl.ds(columns - REST, REST)],
        fulls[-1],
        rows,
        (columns - REST, REST),
        rest_sem,
        rest_square,
        rest_lines,
        rest_merged,
    )
    down_id = links.used
    small_g, q_g, q_two_g, k_g, v_g, o_g, gate_g, gate_two_g, up_g, up_two_g, down_g = g
    leaving = []
    turning = {}
    ffn = mixed_t.shape[0]
    tiles = ffn // TILE
    across = slots // TILE
    pairs = H // 2
    blocks = slots // QB
    block, piece = down_stage.shape[3:]
    chunks = width // piece
    squares = down_stage.shape[1]
    valid = iota((1, slots), 1) < occupied[0] + IMG

    def turn_out(slot, source, target):
        if slot in turning:
            turning[slot].wait()

        def one(tile, carry):
            at = pl.ds(pl.multiple_of(tile * TILE, TILE), TILE)
            turned[slot, at, :] = source[:, at].T
            return carry

        lax.fori_loop(0, width // TILE, one, 0)
        turning[slot] = move(turned.at[slot], target)

    def unpack():
        gains[0:1, :] = unpack_row(small, 0, width)
        gains[1:2, :] = unpack_row(small, 1, width)
        lhs[...] = table_block(small)

    def normalise(source, row, target):
        def one(index, carry):
            at = pl.ds(pl.multiple_of(index * 64, 64), 64)
            values = source[at, :].astype(F32)
            scale = lax.rsqrt(jnp.mean(values * values, axis=-1, keepdims=True) + RMS_EPSILON)
            target[at, :] = (values * scale * gains[row : row + 1, :]).astype(BF)
            return carry

        lax.fori_loop(0, slots // 64, one, 0)

    def bias_block(block, carry):
        bucket_ones(rel, lay, onehot, block)
        found = jnp.where(valid, dot(lhs[...], onehot[...]), MASK_SCORE)
        bias[:, pl.ds(pl.multiple_of(block * QB, QB), QB), :] = found.reshape(H, QB, slots)
        return carry

    def add_bias(part, parts):
        lax.fori_loop(part * blocks // parts, (part + 1) * blocks // parts, bias_block, 0)

    def project(slot, target):
        def one(tile, carry):
            at = pl.ds(pl.multiple_of(tile * WIDE, WIDE), WIDE)
            target[:, at] = dot(na[...], w_one[slot, :, at]).astype(BF)
            return carry

        lax.fori_loop(0, width // WIDE, one, 0)

    def probs_out(pair):
        turn = lax.rem(pair, 2)
        return pltpu.make_async_copy(probs.at[turn], probs_h.at[pl.ds(pair * 2, 2)], ring_sem.at[turn])

    def attend_pair(pair, carry):
        @pl.when(pair >= 2)
        def _():
            probs_out(pair - 2).wait()

        at = pl.ds(pl.multiple_of(pair * 128, 128), 128)
        low = iota((slots, 128), 1) < HD
        queries = q[:, at]
        keys = k[:, at]
        found = []
        for side in range(2):
            mine = jnp.where(low if side == 0 else jnp.logical_not(low), queries, 0)
            scores = dot_nt(mine, keys) + bias[pair * 2 + side]
            peak = jnp.max(scores, axis=-1, keepdims=True)
            expo = jnp.exp(scores - peak)
            total = jnp.sum(expo, axis=-1, keepdims=True)
            share = (expo * (1.0 / total)).astype(BF)
            probs[lax.rem(pair, 2), side] = share
            found.append(dot(share, v[:, at]))
        att[:, at] = jnp.where(low, found[0], found[1]).astype(BF)
        probs_out(pair).start()
        return carry

    def attend(first, last):
        lax.fori_loop(first, last, attend_pair, 0)

    def output():
        def one(tile, carry):
            at = pl.ds(pl.multiple_of(tile * WIDE, WIDE), WIDE)
            hid[:, at] = x[:, at].astype(F32) + dot(att[...], w_one[1, :, at])
            return carry

        lax.fori_loop(0, width // WIDE, one, 0)
        leaving.append(move(hid, hid_h))

    def keep_valid():
        valid_rows = iota((slots, 1), 0) < occupied[0] + IMG

        def one(tile, carry):
            at = pl.ds(pl.multiple_of(tile * TILE, TILE), TILE)
            grad[:, at] = jnp.where(valid_rows, grad[:, at].astype(F32), 0.0).astype(BF)
            return carry

        lax.fori_loop(0, width // TILE, one, 0)
        leaving.append(move(grad, grad_h))

    def gate_spot(tile, second):
        at = pl.ds(pl.multiple_of(lax.rem(tile, across) * TILE, TILE), TILE)
        return bias.at[tile // across + second * (-(-tiles // across)), :, at]

    def gate_tile(tile, carry):
        at = pl.ds(pl.multiple_of(tile * TILE, TILE), TILE)
        gate = dot(nf[...], w_wide[0, :, at])
        square = gate * gate
        inner = GELU_SCALE * gate * (1.0 + GELU_CUBE * square)
        bend = jnp.tanh(inner)
        half = 0.5 * (1.0 + bend)
        gate_spot(tile, 0)[...] = gate * half
        gate_spot(tile, 1)[...] = half + 0.5 * gate * (1.0 - bend * bend) * GELU_SCALE * (
            1.0 + 3.0 * GELU_CUBE * square
        )
        return carry

    def ffn_out(tile):
        turn = lax.rem(tile, 2)
        at = pl.ds(pl.multiple_of(tile * TILE, TILE), TILE)
        return (
            pltpu.make_async_copy(slope.at[turn], slope_h.at[:, at], ring_sem.at[2 + turn]),
            pltpu.make_async_copy(act.at[turn], act_h.at[:, at], ring_sem.at[4 + turn]),
            pltpu.make_async_copy(mix.at[turn], mix_h.at[:, at], ring_sem.at[6 + turn]),
        )

    def ffn_tile(tile, carry):
        @pl.when(tile >= 2)
        def _():
            for copy in ffn_out(tile - 2):
                copy.wait()

        at = pl.ds(pl.multiple_of(tile * TILE, TILE), TILE)
        turn = lax.rem(tile, 2)
        up = dot(nf[...], w_wide[1, :, at])
        active = gate_spot(tile, 0)[...]
        rise = gate_spot(tile, 1)[...]
        mixed = (active * up).astype(BF)
        mix[turn] = mixed
        mixed_t[at, :] = mixed.T
        act[turn] = active.astype(BF)
        slope[turn] = (up * rise).astype(BF)
        for copy in ffn_out(tile):
            copy.start()
        return carry

    def down_place(chunk, half):
        return down_grads.at[chunk, pl.ds(half * squares, squares)]

    def down_copy(unit):
        half, chunk, turn = unit // chunks, lax.rem(unit, chunks), lax.rem(unit, 2)
        return pltpu.make_async_copy(down_stage.at[turn], down_place(chunk, half), ring_sem.at[8 + turn])

    def down_trade(unit):
        half, chunk = unit // chunks, lax.rem(unit, chunks)
        core = lax.rem(links.w, 2)
        there = pl.ds(half * squares, squares)
        return links.copy(
            down_grads.at[chunk, there, 1 - core],
            down_came.at[chunk, there],
            down_id + unit,
            links.wide(1),
        )

    def down_unit(unit, carry):
        half, chunk = unit // chunks, lax.rem(unit, chunks)
        size = 2 * squares * block
        rows = pl.ds(pl.multiple_of(half * size, 16), size)
        at = pl.ds(pl.multiple_of(chunk * piece, piece), piece)
        found = dot(mixed_t[rows, :], grad[:, at])
        down_stage[lax.rem(unit, 2)] = found.astype(BF).reshape(down_stage.shape[1:])
        down_copy(unit).start()

        @pl.when(unit >= 1)
        def _():
            down_copy(unit - 1).wait()
            down_trade(unit - 1).start()

        return carry

    def down_units(first, last):
        lax.fori_loop(first, last, down_unit, 0)

    small_g.start()
    q_g.start()
    q_two_g.start()
    rest.start()
    arriving = [move(tokens, x), move(rel_hbm, rel), move(lay_hbm, lay)]
    grad_in = move(cotangent, grad)
    q_g.ready()
    q_g.spread()
    k_g.start()
    small_g.ready()
    small_g.spread()
    q_two_g.ready()
    q_two_g.spread()
    v_g.start()
    small_g.forward()
    q_g.forward()
    small_g.settle()
    small_g.last()
    small_g.done()
    small_in = move(fulls[0], small)
    rest.forward()
    k_g.ready()
    k_g.spread()
    o_g.start()
    gate_g.start()
    q_two_g.forward()
    for copy in arriving:
        copy.wait()
    small_in.wait()
    unpack()
    normalise(x, 0, na)
    turn_out(0, na, na_t)
    q_g.settle()
    q_two_g.settle()
    add_bias(0, 4)
    v_g.ready()
    v_g.spread()
    k_g.forward()
    q_g.last()
    q_two_g.last()
    add_bias(1, 4)
    k_g.settle()
    o_g.ready()
    o_g.spread()
    gate_two_g.start()
    v_g.forward()
    add_bias(2, 4)
    k_g.last()
    v_g.settle()
    q_g.done()
    q_two_g.done()
    fetch_q = move(fulls[1], w_one.at[0])
    gate_g.ready()
    gate_g.spread()
    up_g.start()
    o_g.forward()
    add_bias(3, 4)
    fetch_q.wait()
    project(0, q)
    turn_out(1, q, q_t)
    k_g.done()
    fetch_k = move(fulls[2], w_one.at[1])
    v_g.last()
    gate_two_g.ready()
    gate_two_g.spread()
    up_two_g.start()
    fetch_k.wait()
    project(1, k)
    leaving.append(move(k, k_h))
    v_g.done()
    fetch_v = move(fulls[3], w_one.at[0])
    gate_g.forward()
    o_g.settle()
    o_g.last()
    fetch_v.wait()
    project(0, v)
    leaving.append(move(v, v_h))
    o_g.done()
    fetch_o = move(fulls[4], w_one.at[1])
    attend(0, 3)
    gate_two_g.forward()
    up_g.ready()
    up_g.spread()
    down_g.start()
    gate_g.settle()
    attend(3, 6)
    gate_g.last()
    gate_two_g.settle()
    attend(6, pairs)
    turn_out(0, att, att_t)
    down_g.ready()
    rest.line()
    fetch_o.wait()
    output()
    normalise(hid, 1, nf)
    turn_out(1, nf, nf_t)
    up_g.forward()
    up_two_g.ready()
    up_two_g.spread()
    gate_two_g.last()
    gate_g.done()
    grad_in.wait()
    keep_valid()
    lax.fori_loop(0, UP_TILES, gate_tile, 0)
    up_g.settle()
    gate_two_g.done()
    leaving.append(move(w_wide.at[0], fulls[5]))
    lax.fori_loop(UP_TILES, tiles, gate_tile, 0)
    up_g.last()
    up_two_g.forward()
    down_g.spread()
    up_g.done()
    lax.fori_loop(0, UP_TILES, ffn_tile, 0)
    up_two_g.settle()
    down_units(0, chunks)
    up_two_g.last()
    up_two_g.done()
    leaving.append(move(w_wide.at[1], fulls[6]))
    lax.fori_loop(UP_TILES, tiles, ffn_tile, 0)
    down_g.forward()
    down_units(chunks, 2 * chunks)
    down_g.settle()
    rest.join()
    down_g.last()
    down_copy(jnp.int32(2 * chunks - 1)).wait()
    down_trade(jnp.int32(2 * chunks - 1)).start()
    down_g.done()
    rest.done()
    for unit in range(2 * chunks):
        down_trade(jnp.int32(unit)).wait()
    for copy in leaving + list(turning.values()):
        copy.wait()
    for pair in (pairs - 2, pairs - 1):
        probs_out(pair).wait()
    for tile in (tiles - 2, tiles - 1):
        for copy in ffn_out(tile):
            copy.wait()
    links.finish()


def forward_all(nw, nn, counts, tokens, rel, lay, cotangent, parameters, shards):
    devices = nw * nn
    shapes = [(8, 128)] + [shard.shape for shard in shards]
    odd_rows = shards[-1].shape[0]
    tile_rows = padded(odd_rows)
    slots, width = tokens.shape
    copies = (len(shapes) + 4) * (nn - 1 + 6 + nw // 2) + 2 * (width // DOWN_PIECE)
    ffn = shapes[5][1]
    low = jax.ShapeDtypeStruct((slots, width), BF)
    wide = jax.ShapeDtypeStruct((slots, ffn), BF)
    full = jax.ShapeDtypeStruct((slots, width), F32)
    out_shape = [
        jax.ShapeDtypeStruct((rows * devices, columns), BF if index else F32)
        for index, (rows, columns) in enumerate(shapes)
    ]
    low_t = jax.ShapeDtypeStruct((width, slots), BF)
    out_shape += [low, low_t, low_t, low, low, low_t, full, low_t, wide]
    out_shape += [jax.ShapeDtypeStruct((H, slots, slots), BF), wide, wide]
    down = (nw // 2, 2, nn * odd_rows, DOWN_PIECE)
    out_shape += [jax.ShapeDtypeStruct((width // DOWN_PIECE,) + down, BF)]
    out_shape += [jax.ShapeDtypeStruct((width // DOWN_PIECE, nw // 2, nn * odd_rows, DOWN_PIECE), BF)]
    half = (tile_rows, REST)
    hbm = pl.BlockSpec(memory_space=pl.ANY)
    page = pltpu.VMEM((slots, width), BF)
    return pl.pallas_call(
        functools.partial(forward_kernel, nn, shapes),
        out_shape=out_shape,
        in_specs=[pl.BlockSpec(memory_space=pltpu.SMEM)]
        + [hbm] * 4
        + [pl.BlockSpec(memory_space=pltpu.VMEM)] * 5
        + [hbm] * (len(shards) - 1),
        out_specs=[hbm] * len(out_shape),
        scratch_shapes=[
            pltpu.VMEM((nn, tile_rows, width - REST), BF),
            pltpu.VMEM((nn * odd_rows, width - REST), BF),
            page,
            pltpu.VMEM((slots, slots), jnp.int32),
            pltpu.VMEM((slots, slots), jnp.int32),
            pltpu.VMEM((devices * 8, 128), F32),
            pltpu.VMEM((H * QB, QB * 2 * NB), BF),
            pltpu.VMEM((QB * 2 * NB, slots), BF),
            pltpu.VMEM((H, slots, slots), F32),
            page,
            page,
            page,
            page,
            page,
            pltpu.VMEM((slots, width), F32),
            page,
            pltpu.VMEM((2, slots, TILE), BF),
            pltpu.VMEM((2, slots, TILE), BF),
            pltpu.VMEM((2, slots, TILE), BF),
            pltpu.VMEM((2, 2, slots, slots), BF),
            pltpu.VMEM((2, width, width), BF),
            pltpu.VMEM((2, width, ffn), BF),
            page,
            pltpu.VMEM((2, down[0] // 2) + down[1:], BF),
            pltpu.VMEM((8, width), F32),
            pltpu.VMEM((2, width, slots), BF),
            pltpu.VMEM((ffn, slots), BF),
            pltpu.SemaphoreType.DMA((copies,)),
            pltpu.SemaphoreType.DMA((copies,)),
            pltpu.SemaphoreType.DMA((len(shapes) + 3,)),
            pltpu.SemaphoreType.DMA((64,)),
            pltpu.SemaphoreType.DMA((10,)),
            pltpu.VMEM((nw // 2,) + half, BF),
            pltpu.VMEM((nn, nw // 2) + half, BF),
            pltpu.VMEM((nw // 2, nn * odd_rows, half[1]), BF),
            pltpu.SemaphoreType.DMA((1 + nw // 2,)),
            pltpu.VMEM((8, 128), F32),
            pltpu.VMEM((tile_rows, width), BF),
        ],
        compiler_params=pltpu.CompilerParams(
            collective_id=0, has_side_effects=True, vmem_limit_bytes=63 * 2**20
        ),
    )(counts, tokens, rel, lay, cotangent, *parameters, shards[-1], *shards[:-1])


class Scatter:
    def __init__(self, links, chunks, rows, columns, grads, came, slots, base, traded=False, first=0):
        self.links, self.chunks, self.rows, self.columns = links, chunks, rows, columns
        self.grads, self.came = grads, came
        (self.held, self.other, self.round, self.out_line, self.in_line, self.load_sem) = slots
        self.base = base
        self.traded = traded
        self.first = first
        self.block = rows * links.nn
        self.parts = halves(columns)
        self.core = lax.rem(links.w, 2)
        self.ring = self.held.shape[0]
        self.line_ring = self.out_line.shape[0]

    def number(self, chunk, kind):
        return self.base + chunk * SCATTER_COPIES + kind

    def core_copy(self, chunk):
        return self.links.copy(
            self.grads.at[chunk, :, 1 - self.core],
            self.came.at[chunk],
            self.number(chunk, 0),
            self.links.wide(1),
        )

    def trade(self, chunk):
        self.core_copy(chunk).start()

    def loads(self, chunk):
        slot, turn = lax.rem(chunk, self.ring), lax.rem(chunk, 2)
        return (
            pltpu.make_async_copy(
                self.grads.at[chunk, :, self.core], self.held.at[slot], self.load_sem.at[turn, 0]
            ),
            pltpu.make_async_copy(
                self.came.at[chunk], self.other.at[turn], self.load_sem.at[turn, 1]
            ),
        )

    def fetch(self, chunk):
        if not self.traded:
            self.core_copy(chunk).wait_recv()
        for load in self.loads(chunk):
            load.start()

    def square(self, mask):
        return jnp.bitwise_xor(self.links.w, mask) // 2

    def hop(self, chunk, p, mask):
        slot = lax.rem(chunk, self.ring)
        low, size, order = self.parts[p]
        bit = order[1] if mask & order[1] else order[0]
        kind = 1 + p * 3 + (X_BIT, Y_BIT, X_BIT | Y_BIT).index(mask)
        return self.links.copy(
            self.held.at[slot, self.square(mask), :, pl.ds(low, size)],
            self.round.at[slot, kind - 1, :, pl.ds(0, size)],
            self.number(chunk, kind),
            self.links.wide(bit),
        )

    def landed(self, chunk, p, mask):
        return self.round.at[
            lax.rem(chunk, self.ring), p * 3 + (X_BIT, Y_BIT, X_BIT | Y_BIT).index(mask)
        ]

    def add_core(self, chunk):
        for load in self.loads(chunk):
            load.wait()
        slot, turn = lax.rem(chunk, self.ring), lax.rem(chunk, 2)

        def one(square, carry):
            self.held[slot, square] = (
                self.held[slot, square].astype(F32) + self.other[turn, square].astype(F32)
            ).astype(BF)
            return carry

        lax.fori_loop(0, self.held.shape[1], one, 0)
        for p, part in enumerate(self.parts):
            self.hop(chunk, p, X_BIT | Y_BIT).start()
        for p, part in enumerate(self.parts):
            self.hop(chunk, p, part[2][1]).start()

    def add_corner(self, chunk):
        slot = lax.rem(chunk, self.ring)
        for p, (low, size, order) in enumerate(self.parts):
            self.hop(chunk, p, X_BIT | Y_BIT).wait_recv()
            square = self.square(order[0])
            came = self.landed(chunk, p, X_BIT | Y_BIT)
            self.held[slot, square, :, low : low + size] = (
                self.held[slot, square, :, low : low + size].astype(F32)
                + came[:, :size].astype(F32)
            ).astype(BF)
        for p, part in enumerate(self.parts):
            self.hop(chunk, p, part[2][0]).start()

    def line_copy(self, chunk, step):
        k = self.links
        slot = lax.rem(chunk, self.line_ring)
        return k.copy(
            self.out_line.at[slot, lax.rem(k.z + step, k.nn)],
            self.in_line.at[slot, step - 1],
            self.number(chunk, 6 + step),
            k.along(step),
        )

    def add_square(self, chunk):
        slot, line = lax.rem(chunk, self.ring), lax.rem(chunk, self.line_ring)
        home = self.square(0)
        for p, (low, size, order) in enumerate(self.parts):
            total = self.held[slot, home, :, low : low + size].astype(F32)
            for mask in order:
                self.hop(chunk, p, mask).wait_recv()
                total = total + self.landed(chunk, p, mask)[:, :size].astype(F32)
            for z in range(self.links.nn):
                self.out_line[line, z, : self.rows, low : low + size] = total[
                    z * self.rows : (z + 1) * self.rows
                ].astype(BF)
        for step in range(1, self.links.nn):
            self.line_copy(chunk, step).start()
        if not self.traded:
            self.core_copy(chunk).wait_send()
        for p in range(len(self.parts)):
            for mask in (X_BIT, Y_BIT, X_BIT | Y_BIT):
                self.hop(chunk, p, mask).wait_send()

    def total(self, chunk):
        slot = lax.rem(chunk, self.line_ring)
        total = self.out_line[slot, self.links.z, : self.rows].astype(F32)
        for step in range(1, self.links.nn):
            self.line_copy(chunk, step).wait_recv()
            total = total + self.in_line[slot, step - 1, : self.rows].astype(F32)
        return total

    def pump(self, index, out):
        index = jnp.int32(index)
        steps = (self.fetch, self.add_core, self.add_corner, self.add_square, self.finish)
        for lag, action in zip(FEW_LAG if self.traded else LAG, steps):
            chunk = index - lag + self.first

            @pl.when(jnp.logical_and(chunk >= self.first, chunk < self.chunks))
            def _(chunk=chunk, action=action):
                action(chunk, out) if action == self.finish else action(chunk)

    def finish(self, chunk, out):
        out[chunk] = self.total(chunk)
        for step in range(1, self.links.nn):
            self.line_copy(chunk, step).wait_send()


class ScatterLine:
    def __init__(self, links, rows, columns, grads, came, slots, base):
        self.links, self.rows, self.columns = links, rows, columns
        self.grads, self.came = grads, came
        (self.held, self.other, self.square, self.round, self.in_line, self.load_sem) = slots
        self.base = base
        self.parts = halves(columns)
        self.core = lax.rem(links.w, 2)

    def number(self, chunk, kind):
        return self.base + chunk * SCATTER_COPIES + kind

    def core_copy(self, chunk):
        return self.links.copy(
            self.grads.at[chunk, :, 1 - self.core],
            self.came.at[chunk],
            self.number(chunk, 0),
            self.links.wide(1),
        )

    def loads(self, chunk):
        return (
            pltpu.make_async_copy(
                self.grads.at[chunk, :, self.core], self.held.at[chunk], self.load_sem.at[0]
            ),
            pltpu.make_async_copy(self.came.at[chunk], self.other, self.load_sem.at[1]),
        )

    def fetch(self, chunk):
        self.core_copy(chunk).wait_recv()
        for load in self.loads(chunk):
            load.start()

    def line_copy(self, chunk, step):
        k = self.links
        rows = pl.ds(pl.multiple_of(lax.rem(k.z + step, k.nn) * self.rows, self.rows), self.rows)
        return k.copy(
            self.held.at[chunk, :, rows],
            self.in_line.at[chunk, step - 1],
            self.number(chunk, 6 + step),
            k.along(step),
        )

    def add_core(self, chunk):
        for load in self.loads(chunk):
            load.wait()

        def one(square, carry):
            self.held[chunk, square] = (
                self.held[chunk, square].astype(F32) + self.other[square].astype(F32)
            ).astype(BF)
            return carry

        lax.fori_loop(0, self.held.shape[1], one, 0)
        for step in range(1, self.links.nn):
            self.line_copy(chunk, step).start()

    def spot(self, mask):
        return jnp.bitwise_xor(self.links.w, mask) // 2

    def hop(self, chunk, p, mask):
        low, size, order = self.parts[p]
        bit = order[1] if mask & order[1] else order[0]
        kind = 1 + p * 3 + (X_BIT, Y_BIT, X_BIT | Y_BIT).index(mask)
        return self.links.copy(
            self.square.at[chunk, self.spot(mask), :, pl.ds(low, size)],
            self.round.at[chunk, kind - 1],
            self.number(chunk, kind),
            self.links.wide(bit),
        )

    def landed(self, chunk, p, mask):
        kind = p * 3 + (X_BIT, Y_BIT, X_BIT | Y_BIT).index(mask)
        return self.round[chunk, kind].astype(F32)

    def add_line(self, chunk):
        for step in range(1, self.links.nn):
            self.line_copy(chunk, step).wait_recv()
        rows = pl.ds(pl.multiple_of(self.links.z * self.rows, self.rows), self.rows)
        for square in range(self.held.shape[1]):
            total = self.held[chunk, square, rows, :].astype(F32)
            for step in range(1, self.links.nn):
                total = total + self.in_line[chunk, step - 1, square].astype(F32)
            self.square[chunk, square] = total.astype(BF)
        for p, part in enumerate(self.parts):
            self.hop(chunk, p, X_BIT | Y_BIT).start()
        for p, part in enumerate(self.parts):
            self.hop(chunk, p, part[2][1]).start()

    def add_corner(self, chunk):
        for p, (low, size, order) in enumerate(self.parts):
            self.hop(chunk, p, X_BIT | Y_BIT).wait_recv()
            spot = self.spot(order[0])
            self.square[chunk, spot, :, low : low + size] = (
                self.square[chunk, spot, :, low : low + size].astype(F32)
                + self.landed(chunk, p, X_BIT | Y_BIT)
            ).astype(BF)
        for p, part in enumerate(self.parts):
            self.hop(chunk, p, part[2][0]).start()

    def finish(self, chunk, out):
        for p, (low, size, order) in enumerate(self.parts):
            total = self.square[chunk, self.spot(0), :, low : low + size].astype(F32)
            for mask in order:
                self.hop(chunk, p, mask).wait_recv()
                total = total + self.landed(chunk, p, mask)
            out[chunk, :, low : low + size] = total
        self.core_copy(chunk).wait_send()
        for step in range(1, self.links.nn):
            self.line_copy(chunk, step).wait_send()
        for p in range(len(self.parts)):
            for mask in (X_BIT, Y_BIT, X_BIT | Y_BIT):
                self.hop(chunk, p, mask).wait_send()


class ScatterSmall:
    def __init__(self, links, grads, out, came, round_in, line_in, mine):
        self.links, self.grads, self.out = links, grads, out
        self.came, self.round, self.line, self.mine = came, round_in, line_in, mine
        self.home = links.w // 2
        self.masks = (X_BIT, Y_BIT, X_BIT | Y_BIT)
        self.core_id = links.fresh()
        self.square_ids = [links.fresh() for _ in self.masks]
        self.line_ids = [links.fresh() for _ in range(1, links.nn)]

    def core_copy(self):
        k = self.links
        return k.copy(self.grads.at[:, 1 - lax.rem(k.w, 2)], self.came, self.core_id, k.wide(1))

    def square_copy(self, index):
        k, mask = self.links, self.masks[index]
        spot = jnp.bitwise_xor(k.w, mask) // 2
        return k.copy(self.mine.at[spot], self.round.at[index], self.square_ids[index], k.wide(mask))

    def line_copy(self, step):
        k = self.links
        rows = pl.ds(pl.multiple_of(lax.rem(k.z + step, k.nn) * 8, 8), 8)
        spot = self.mine.at[self.home, rows]
        return k.copy(spot, self.line.at[step - 1], self.line_ids[step - 1], k.along(step))

    def trade(self):
        self.core_copy().start()

    def spread(self):
        self.core_copy().wait()
        self.mine[...] = self.grads[:, lax.rem(self.links.w, 2)] + self.came[...]
        for index in range(len(self.masks)):
            self.square_copy(index).start()

    def along(self):
        for index in range(len(self.masks)):
            self.square_copy(index).wait()
        total = self.mine[self.home]
        for index in range(len(self.masks)):
            total = total + self.round[index]
        self.mine[self.home] = total
        for step in range(1, self.links.nn):
            self.line_copy(step).start()

    def finish(self):
        total = self.mine[self.home, pl.ds(pl.multiple_of(self.links.z * 8, 8), 8)]
        for step in range(1, self.links.nn):
            self.line_copy(step).wait()
            total = total + self.line[step - 1]
        self.out[...] = total


def padded(rows):
    return (rows + 15) // 16 * 16


def scatter_slots(squares, nn, rows, columns, ring, line_ring):
    half = columns // 2
    return [
        pltpu.VMEM((ring, squares, nn * rows, columns), BF),
        pltpu.VMEM((2, squares, nn * rows, columns), BF),
        pltpu.VMEM((ring, 6, nn * rows, half), BF),
        pltpu.VMEM((line_ring, nn, padded(rows), columns), BF),
        pltpu.VMEM((line_ring, nn - 1, padded(rows), columns), BF),
        pltpu.SemaphoreType.DMA((2, 2)),
    ]


def norm_pull(values, gain, grad):
    scale = lax.rsqrt(jnp.mean(values * values, axis=-1, keepdims=True) + RMS_EPSILON)
    scaled = grad * gain
    along = jnp.mean(scaled * values, axis=-1, keepdims=True)
    share = grad * values * scale
    return scale * scaled - values * (scale * scale * scale * along), share


def fold_rows(values):
    return jnp.sum(values.reshape(values.shape[0] // 8, 8, values.shape[1]), axis=0)


def pack_row(row, first, each, devices):
    total = row.shape[1]
    shape = (128, total)
    pick = jnp.where(iota(shape, 0) == first + lax.rem(iota(shape, 1), each), 1.0, 0.0)
    shape = (devices, total)
    mine = jnp.where(iota(shape, 1) // each == iota(shape, 0), row, 0.0)
    return lax.dot_general(
        mine,
        pick,
        (((1,), (1,)), ((), ())),
        preferred_element_type=F32,
        precision=lax.Precision.HIGHEST,
    )


def backward_kernel(nn, few_facts, many_facts, *refs):
    occupied, refs = refs[0], refs[1:]
    (
        tokens,
        rel_hbm,
        lay_hbm,
        grad_h,
        small_h,
        query_h,
        key_h,
        value_h,
        output_h,
        gate_h,
        up_h,
        down_h,
        na_t,
        q_t,
        k_h,
        v_h,
        att_t,
        hid_h,
        nf_t,
        mix_h,
        probs_h,
        slope_h,
        act_h,
        few_grads,
        few_came,
    ) = refs[:25]
    refs = refs[25:]
    (out_h, rows_out, few_out, many_out, small_out, many_grads, many_came) = refs[:7]
    few_slots, many_slots, late_slots, refs = refs[7:13], refs[13:19], refs[19:25], refs[25:]
    (
        x,
        rel,
        lay,
        small,
        gains,
        grad,
        left,
        acc,
        hid,
        wd_s,
        wgu_s,
        pair,
        slope_s,
        act_s,
        many_stage,
        branch,
        w_one,
        pull,
        pull_t,
        qt,
        k,
        v,
        probs,
        pieces,
        onehot,
        table,
        sums,
        small_grads,
        small_came,
        small_round,
        small_line,
        small_mine,
        send_sem,
        recv_sem,
        local_sem,
        tile_sem,
        stage_sem,
        probs_sem,
    ) = refs
    slots, width = x.shape
    links = Links(nn, send_sem, recv_sem)
    numbers = iter(range(64))

    def later_move(src, dst):
        return pltpu.make_async_copy(src, dst, local_sem.at[next(numbers)])

    def move(src, dst):
        copy = later_move(src, dst)
        copy.start()
        return copy

    few = Scatter(links, *few_facts, few_grads, few_came, few_slots, 0, traded=True)
    base = few_facts[0] * SCATTER_COPIES
    many = Scatter(links, *many_facts, many_grads, many_came, many_slots, base, first=LATE)
    late = ScatterLine(links, *many_facts[1:], many_grads, many_came, late_slots, base)
    links.used = base + many_facts[0] * SCATTER_COPIES
    little = ScatterSmall(
        links, small_grads, small_out, small_came, small_round, small_line, small_mine
    )
    ffn = mix_h.shape[1]
    tiles = ffn // TILE
    pairs = H // 2
    wide = many.columns
    devices = small.shape[0] // 8
    each = width // devices
    zero = jnp.zeros((8, width), F32)

    def tile_copies(tile):
        turn = lax.rem(tile, 2)
        at = pl.ds(pl.multiple_of(tile * TILE, TILE), TILE)
        return [
            pltpu.make_async_copy(src, dst, tile_sem.at[turn, index])
            for index, (src, dst) in enumerate(
                (
                    (down_h.at[at], wd_s.at[turn]),
                    (gate_h.at[:, at], wgu_s.at[turn, :, pl.ds(0, TILE)]),
                    (up_h.at[:, at], wgu_s.at[turn, :, pl.ds(TILE, TILE)]),
                    (slope_h.at[:, at], slope_s.at[turn]),
                    (act_h.at[:, at], act_s.at[turn]),
                )
            )
        ]

    def many_copy(chunk):
        turn = lax.rem(chunk, 2)
        place = many.grads.at[chunk]
        return pltpu.make_async_copy(many_stage.at[turn].reshape(place.shape), place, stage_sem.at[turn])

    def flush(chunk):
        many_copy(chunk).wait()
        many.trade(chunk)

    def make(chunk, left_rows, right, dot_one):
        found = dot_one(left_rows[...], right())
        many_stage[lax.rem(chunk, 2)] = found.astype(BF)
        many_copy(chunk).start()

    def few_pump(index):
        few.pump(index, few_out)

    def many_pump(index):
        many.pump(index, many_out)

    def ffn_tile(tile, carry):
        turn = lax.rem(tile, 2)

        @pl.when(tile + 1 < tiles)
        def _():
            for copy in tile_copies(tile + 1):
                copy.start()

        for number, copy in enumerate(later + last):
            pl.when(tile == 3 + number // 2)(copy.start)

        for copy in tile_copies(tile):
            copy.wait()
        grad_mixed = dot_nt(grad[...], wd_s[turn])
        pair[:, :TILE] = (grad_mixed * slope_s[turn].astype(F32)).astype(BF)
        pair[:, TILE:] = (grad_mixed * act_s[turn].astype(F32)).astype(BF)
        make(tile, left, lambda: pair[...], dot)

        @pl.when(lax.rem(tile, 2) == 1)
        def _():
            few_pump(tile // 2 + 2)

        acc[...] += dot_nt(pair[...], wgu_s[turn])
        flush(tile)
        many_pump(tile - FFN_LAG)

        @pl.when(jnp.logical_and(tile >= 2, tile < 2 + LATE))
        def _():
            late.add_core(tile - 2)

        @pl.when(jnp.logical_and(tile >= 1, tile < 1 + LATE))
        def _():
            late.fetch(tile - 1)

        return carry

    def unpack():
        gains[0:1, :] = unpack_row(small, 0, width)
        gains[1:2, :] = unpack_row(small, 1, width)

    def norm_two():
        def one(index, total):
            at = pl.ds(pl.multiple_of(index * 64, 64), 64)
            part, share = norm_pull(hid[at, :], gains[1:2, :], acc[at, :])
            whole = grad[at, :].astype(F32) + part
            hid[at, :] = whole
            branch[at, :] = whole.astype(BF)
            return total + fold_rows(share)

        sums[0] = lax.fori_loop(0, slots // 64, one, zero)

    def output_chunk(part, carry):
        at = pl.ds(pl.multiple_of(part * wide, wide), wide)
        make(tiles + part, pull_t, lambda: branch[:, at], dot)
        return carry

    def pull_back():
        def one(tile, carry):
            at = pl.ds(pl.multiple_of(tile * WIDE, WIDE), WIDE)
            found = dot_nt(branch[...], w_one[0, at, :]).astype(BF)
            pull[:, at] = found
            pull_t[at, :] = found.T
            return carry

        lax.fori_loop(0, width // WIDE, one, 0)

    def probs_copy(index):
        turn = lax.rem(index, 2)
        return pltpu.make_async_copy(
            probs_h.at[pl.ds(index * 2, 2)], probs.at[turn], probs_sem.at[turn]
        )

    def attend_pair(index, carry):
        @pl.when(index + 1 < pairs)
        def _():
            probs_copy(index + 1).start()

        probs_copy(index).wait()
        turn = lax.rem(index, 2)
        at = pl.ds(pl.multiple_of(index * 128, 128), 128)
        low = iota((slots, 128), 1) < HD
        keys, pulls, values = k[:, at], pull[:, at], v[:, at]
        found = []
        for side in range(2):
            head = index * 2 + side
            mine = jnp.where(low if side == 0 else jnp.logical_not(low), pulls, 0)
            share = probs[turn, side]
            wanted = dot_nt(mine, values)
            share_f = share.astype(F32)
            joint = share_f * wanted
            piece = (joint - share_f * jnp.sum(joint, axis=-1, keepdims=True)).astype(BF)
            pieces[pl.ds(pl.multiple_of(head * slots, slots), slots), :] = piece
            found.append(dot(piece, keys))
            rows = pl.ds(pl.multiple_of(head * HD, HD), HD)
            qt[rows, :] = dot(qt[rows, :], piece).astype(BF)
            pull_t[rows, :] = dot(pull_t[rows, :], share).astype(BF)
        pull[:, at] = jnp.where(low, found[0], found[1]).astype(BF)
        return carry

    def attend(first, last):
        lax.fori_loop(first, last, attend_pair, 0)

    first_head_chunk = tiles + width // wide

    def head_chunks(half):
        at = pl.ds(pl.multiple_of(half * wide, wide), wide)
        chunk = first_head_chunk + half * 3

        def turned_chunk(index, carry):
            found = jnp.where(index == 0, pull_t[at, :], qt[at, :])
            make(chunk + 2 * index, left, lambda: found, dot_nt)

            @pl.when(index == 0)
            def _():
                make(chunk + 1, left, lambda: pull[:, at], dot)
                flush(chunk)

            return carry

        lax.fori_loop(0, 2, turned_chunk, 0)
        flush(chunk + 1)
        flush(chunk + 2)

    def table_blocks(index, carry):
        sides = []
        for side in range(2):
            block = index * 2 + side
            at = slice(side * slots, (side + 1) * slots)
            for query in range(BACK_QB):
                for which, bucket in enumerate((rel, lay)):
                    row = bucket[pl.ds(block * BACK_QB + query, 1), :]
                    first = (query * 2 + which) * NB
                    onehot[first : first + NB, at] = ones_where(
                        jnp.broadcast_to(row, (NB, slots)) == iota((NB, slots), 0)
                    )
            heads = [
                pieces[pl.ds(pl.multiple_of(head * slots + block * BACK_QB, BACK_QB), BACK_QB), :]
                for head in range(H)
            ]
            sides.append(jnp.concatenate(heads, axis=0))
        table[...] += dot_nt(onehot[...], jnp.concatenate(sides, axis=1))
        return carry

    def add_table(part, parts):
        blocks = slots // BACK_QB // 2
        lax.fori_loop(part * blocks // parts, (part + 1) * blocks // parts, table_blocks, 0)

    whole = ffn // slots
    first_mix = width // slots * ffn

    def output_moves():
        moves = [
            later_move(down_h.at[:, pl.ds(part * slots, slots)], pieces.at[pl.ds(part * ffn, ffn)])
            for part in range(width // slots)
        ]
        moves += [
            later_move(
                mix_h.at[:, pl.ds(part * slots, slots)],
                pieces.at[pl.ds(first_mix + part * slots, slots)],
            )
            for part in range(whole)
        ]
        return moves + [later_move(mix_h.at[:, pl.ds(whole * slots, TILE)], slope_s.at[0])]

    def down_project(part):
        at = pl.ds(pl.multiple_of(part * slots, slots), slots)

        def one(index, total):
            rows = pl.ds(pl.multiple_of(part * ffn + index * slots, TILE), slots)
            mixed = pl.ds(pl.multiple_of(first_mix + index * slots, TILE), slots)
            acc[:, at] += dot(pieces[mixed, :], pieces[rows, :])
            return total

        lax.fori_loop(0, whole, one, 0)
        rows = pl.ds(pl.multiple_of(part * ffn + whole * slots, TILE), TILE)
        total = acc[:, at] + dot(slope_s[0], pieces[rows, :])
        valid_rows = iota((slots, 1), 0) < occupied[0] + IMG
        x[:, at] = jnp.where(valid_rows, total, 0.0).astype(BF)

    def turn_back():
        def one(tile, carry):
            at = pl.ds(pl.multiple_of(tile * TILE, TILE), TILE)
            v[:, at] = pull_t[at, :].T
            branch[:, at] = qt[at, :].T
            return carry

        lax.fori_loop(0, width // TILE, one, 0)

    def pull_normed(source, slot, first):
        def one(tile, carry):
            at = pl.ds(pl.multiple_of(tile * WIDE, WIDE), WIDE)
            found = dot_nt(source[...], w_one[slot, at, :])
            acc[:, at] = found if first else acc[:, at] + found
            return carry

        lax.fori_loop(0, width // WIDE, one, 0)

    def norm_one():
        def one(index, total):
            at = pl.ds(pl.multiple_of(index * 64, 64), 64)
            part, share = norm_pull(x[at, :].astype(F32), gains[0:1, :], acc[at, :])
            hid[at, :] += part
            return total + fold_rows(share)

        sums[1] = lax.fori_loop(0, slots // 64, one, zero)

    def pack():
        total = table[...]
        mine = iota(total.shape, 0) // (2 * NB) == lax.rem(iota(total.shape, 1), BACK_QB)
        folded = jnp.sum(
            jnp.where(mine, total, 0.0).reshape(BACK_QB, 2 * NB, H * BACK_QB), axis=0
        )
        packed = [
            pack_row(jnp.sum(sums[1], axis=0, keepdims=True), 0, each, devices),
            pack_row(jnp.sum(sums[0], axis=0, keepdims=True), 0, each, devices),
        ]
        shape = (H * BACK_QB, 128)
        pick = jnp.where(iota(shape, 1) == iota(shape, 0) // BACK_QB, 1.0, 0.0)
        for index in range(2):
            packed.append(
                jnp.dot(
                    folded[index * NB : (index + 1) * NB],
                    pick,
                    preferred_element_type=F32,
                    precision=lax.Precision.HIGHEST,
                )
            )
        small_grads[...] = jnp.zeros_like(small_grads)
        for device in range(devices):
            wide_at, z = divmod(device, nn)
            for index, rows in enumerate(packed):
                at = z * 8 + index
                small_grads[wide_at // 2, wide_at % 2, at : at + 1, :] = rows[device : device + 1]

    later = [
        later_move(*pair_of)
        for pair_of in (
            (hid_h, hid),
            (small_h, small),
            (att_t, pull_t),
            (output_h, w_one.at[0]),
            (q_t, qt),
            (k_h, k),
            (v_h, v),
        )
    ]
    last = [
        later_move(*pair_of)
        for pair_of in ((tokens, x), (rel_hbm, rel), (lay_hbm, lay), (value_h, w_one.at[1]))
    ]
    na_in, query_in, key_in = (
        later_move(*pair_of)
        for pair_of in ((na_t, left), (query_h, w_one.at[0]), (key_h, w_one.at[0]))
    )
    rows_copy, out_copy = later_move(hid, rows_out), later_move(x, out_h)
    output_in = output_moves()
    hid_in = later_move(hid_h, acc)

    def start(*copies):
        for copy in copies:
            copy.start()

    def wait(*copies):
        for copy in copies:
            copy.wait()

    few.fetch(jnp.int32(0))
    start(*tile_copies(0))
    first_in = [move(grad_h, grad), move(nf_t, left)]
    links.greet()
    few.fetch(jnp.int32(1))
    few.add_core(jnp.int32(0))
    acc[...] = jnp.zeros_like(acc)
    table[...] = jnp.zeros_like(table)
    wait(*first_in)
    lax.fori_loop(0, tiles, ffn_tile, 0)
    wait(*later)
    na_in.start()
    unpack()
    norm_two()
    def step(index, carry):
        few_pump(index + tiles // 2 + 2)
        many_pump(index + tiles - FFN_LAG)

        for lag, action in ((1, late.add_line), (3, late.add_corner), (5, late.finish)):
            chunk = index - lag

            @pl.when(jnp.logical_and(chunk >= 0, chunk < LATE))
            def _(chunk=chunk, action=action):
                action(chunk, many_out) if action == late.finish else action(chunk)

        @pl.when(index == 0)
        def _():
            lax.fori_loop(0, width // wide, output_chunk, 0)
            pull_back()
            flush(tiles)
            flush(tiles + 1)
            query_in.start()
            probs_copy(jnp.int32(0)).start()

        second = index >= 4
        turn = jnp.where(second, index - 4, index - 1)
        attends = jnp.logical_and(turn >= 0, turn < 2)

        @pl.when(attends)
        def _():
            first = 2 * turn + jnp.where(second, 4, 0)
            attend(first, first + 2)

        @pl.when(index == 3)
        def _():
            wait(*last)
            na_in.wait()

        @pl.when(jnp.logical_or(index == 3, index == 6))
        def _():
            head_chunks(index // 3 - 1)

        @pl.when(jnp.logical_and(index >= 7, index < 10))
        def _():
            add_table(index - 7, 3)

        @pl.when(index == 10)
        def _():
            start(*output_in)
            query_in.wait()
            turn_back()
            pull_normed(pull, 0, True)
            key_in.start()

        @pl.when(index == 11)
        def _():
            pull_normed(v, 1, False)
            key_in.wait()
            pull_normed(branch, 0, False)

        @pl.when(index == 12)
        def _():
            norm_one()
            rows_copy.start()
            hid_in.start()
            pack()
            little.trade()

        @pl.when(index == 13)
        def _():
            wait(*output_in)
            hid_in.wait()
            little.spread()

        @pl.when(index == 15)
        def _():
            little.along()

        @pl.when(jnp.logical_or(index == 14, index == 16))
        def _():
            down_project(index // 2 - 7)

        @pl.when(index == 17)
        def _():
            out_copy.start()

        return carry

    lax.fori_loop(0, many.chunks - LATE + LAGS - (tiles - FFN_LAG) + 1, step, 0)
    little.finish()
    wait(rows_copy, out_copy)
    links.finish()


def backward_all(nw, nn, counts, page, weights, saved):
    squares = nw // 2
    devices = nw * nn
    slots, width = page[0].shape
    ffn = weights[5].shape[1]
    few = (width // DOWN_PIECE, ffn // devices, DOWN_PIECE)
    many = (ffn // TILE + 8, width // devices, 2 * TILE)
    outs = [jax.ShapeDtypeStruct((slots, width), BF), jax.ShapeDtypeStruct((slots, width), F32)]
    for chunks, rows, columns in (few, many):
        outs.append(jax.ShapeDtypeStruct((chunks, rows, columns), F32))
    outs.append(jax.ShapeDtypeStruct((8, 128), F32))
    chunks, rows, columns = many
    outs.append(jax.ShapeDtypeStruct((chunks, squares, 2, nn * rows, columns), BF))
    outs.append(jax.ShapeDtypeStruct((chunks, squares, nn * rows, columns), BF))
    copies = (few[0] + many[0]) * SCATTER_COPIES + 16
    vmem = pl.BlockSpec(memory_space=pltpu.VMEM)
    hbm = pl.BlockSpec(memory_space=pl.ANY)
    low = pltpu.VMEM((slots, width), BF)
    turned = pltpu.VMEM((width, slots), BF)
    full = pltpu.VMEM((slots, width), F32)
    inputs = (counts,) + tuple(page) + tuple(weights) + tuple(saved)
    return pl.pallas_call(
        functools.partial(backward_kernel, nn, few, many),
        out_shape=outs,
        in_specs=[pl.BlockSpec(memory_space=pltpu.SMEM)] + [hbm] * (len(inputs) - 1),
        out_specs=[hbm, hbm, vmem, vmem, vmem, hbm, hbm],
        scratch_shapes=scatter_slots(squares, nn, few[1], few[2], few[0], few[0])
        + scatter_slots(squares, nn, many[1], many[2], RING, LINE_RING)
        + [
            pltpu.VMEM((LATE, squares, nn * many[1], many[2]), BF),
            pltpu.VMEM((squares, nn * many[1], many[2]), BF),
            pltpu.VMEM((LATE, squares, many[1], many[2]), BF),
            pltpu.VMEM((LATE, 6, many[1], many[2] // 2), BF),
            pltpu.VMEM((LATE, nn - 1, squares, many[1], many[2]), BF),
            pltpu.SemaphoreType.DMA((2,)),
        ]
        + [
            low,
            pltpu.VMEM((slots, slots), jnp.int32),
            pltpu.VMEM((slots, slots), jnp.int32),
            pltpu.VMEM((devices * 8, 128), F32),
            pltpu.VMEM((8, width), F32),
            low,
            turned,
            full,
            full,
            pltpu.VMEM((2, TILE, width), BF),
            pltpu.VMEM((2, width, 2 * TILE), BF),
            pltpu.VMEM((slots, 2 * TILE), BF),
            pltpu.VMEM((2, slots, TILE), BF),
            pltpu.VMEM((2, slots, TILE), BF),
            pltpu.VMEM((2, width, many[2]), BF),
            low,
            pltpu.VMEM((2, width, width), BF),
            low,
            turned,
            turned,
            low,
            low,
            pltpu.VMEM((2, 2, slots, slots), BF),
            pltpu.VMEM((H * slots, slots), BF),
            pltpu.VMEM((BACK_QB * 2 * NB, 2 * slots), BF),
            pltpu.VMEM((BACK_QB * 2 * NB, H * BACK_QB), F32),
            pltpu.VMEM((2, 8, width), F32),
            pltpu.VMEM((squares, 2, nn * 8, 128), F32),
            pltpu.VMEM((squares, nn * 8, 128), F32),
            pltpu.VMEM((3, nn * 8, 128), F32),
            pltpu.VMEM((nn - 1, 8, 128), F32),
            pltpu.VMEM((squares, nn * 8, 128), F32),
            pltpu.SemaphoreType.DMA((copies,)),
            pltpu.SemaphoreType.DMA((copies,)),
            pltpu.SemaphoreType.DMA((64,)),
            pltpu.SemaphoreType.DMA((2, 5)),
            pltpu.SemaphoreType.DMA((2,)),
            pltpu.SemaphoreType.DMA((2,)),
        ],
        compiler_params=pltpu.CompilerParams(
            collective_id=1, has_side_effects=True, vmem_limit_bytes=63 * 2**20
        ),
    )(*inputs)[:5]


def place_kernel(few_h, many_h, rows_h, out_h, small, *refs):
    (whole_out, row_out, query, key, value, output, gate, up, down) = refs[:9]
    (gain_attn, gain_ffn, rel, lay) = refs[9:13]
    few, many, rows, whole, in_sem, out_sem = refs[13:]
    tiles = gate.shape[1] // TILE
    wide = many.shape[2]
    part = rows.shape[0] // 8
    arriving = [
        pltpu.make_async_copy(src, dst, in_sem.at[index])
        for index, (src, dst) in enumerate(
            [(many_h, many), (few_h, few), (out_h, whole)]
            + [
                (rows_h.at[pl.ds(index * part, part)], rows.at[pl.ds(index * part, part)])
                for index in range(8)
            ]
        )
    ]
    for copy in arriving:
        copy.start()
    moves = []

    def move(src, dst):
        copy = pltpu.make_async_copy(src, dst, out_sem.at[len(moves)])
        copy.start()
        moves.append(copy)

    for index, target in enumerate((gain_attn, gain_ffn, rel, lay)):
        target[...] = small[index, : target.shape[0]]
    arriving[0].wait()
    for tile in range(tiles):
        at = pl.ds(tile * TILE, TILE)
        move(many.at[tile, :, pl.ds(0, TILE)], gate.at[:, at])
        move(many.at[tile, :, pl.ds(TILE, TILE)], up.at[:, at])
    halves_of = output.shape[1] // wide
    for half in range(halves_of):
        at = pl.ds(half * wide, wide)
        move(many.at[tiles + half], output.at[:, at])
        first = tiles + halves_of + half * 3
        for index, target in enumerate((value, query, key)):
            move(many.at[first + index], target.at[:, at])
    arriving[1].wait()
    for chunk in range(few.shape[0]):
        move(few.at[chunk], down.at[:, pl.ds(chunk * few.shape[2], few.shape[2])])
    arriving[2].wait()
    move(whole, whole_out)
    for index in range(8):
        arriving[3 + index].wait()
        at = pl.ds(index * part, part)
        move(rows.at[at], row_out.at[at])
    for copy in moves:
        copy.wait()


def place_all(few, many, rows, out, small, shapes):
    hbm = pl.BlockSpec(memory_space=pl.ANY)
    vmem = pl.BlockSpec(memory_space=pltpu.VMEM)
    outs = [jax.ShapeDtypeStruct(out.shape, BF), jax.ShapeDtypeStruct(rows.shape, F32)]
    outs += [jax.ShapeDtypeStruct(shape, F32) for shape in shapes]
    return pl.pallas_call(
        place_kernel,
        out_shape=outs,
        in_specs=[hbm] * 4 + [vmem],
        out_specs=[hbm] * 9 + [vmem] * 4,
        scratch_shapes=[
            pltpu.VMEM(few.shape, F32),
            pltpu.VMEM(many.shape, F32),
            pltpu.VMEM(rows.shape, F32),
            pltpu.VMEM(out.shape, BF),
            pltpu.SemaphoreType.DMA((16,)),
            pltpu.SemaphoreType.DMA((64,)),
        ],
        compiler_params=pltpu.CompilerParams(vmem_limit_bytes=63 * 2**20),
    )(few, many, rows, out, small)


def local_fast(
    nw,
    nn,
    tokens,
    w_query,
    w_key,
    w_value,
    w_output,
    w_gate,
    w_up,
    w_down,
    gain_attn,
    gain_ffn,
    rel_table,
    lay_table,
    ocr_counts,
    rel_bucket,
    lay_bucket,
    cotangent,
):
    page = (tokens, rel_bucket, lay_bucket)
    parameters = (gain_attn, gain_ffn, rel_table, lay_table)
    shards = (w_query, w_key, w_value, w_output, w_gate, w_up, w_down)
    found = forward_all(nw, nn, ocr_counts, *page, cotangent, parameters, shards)
    count = 1 + len(shards)
    weights, grad, saved = found[:count], found[count], found[count + 1 :]
    output, grad_tokens, few, many, small = backward_all(
        nw, nn, ocr_counts, page + (grad,), weights, saved
    )

    square = w_query.shape
    shapes = [square] * 4 + [w_gate.shape, w_up.shape, w_down.shape]
    shapes += [part.shape for part in (gain_attn, gain_ffn, rel_table, lay_table)]
    return tuple(place_all(few, many, grad_tokens, output, small, shapes))


def local(
    tokens,
    w_query,
    w_key,
    w_value,
    w_output,
    w_gate,
    w_up,
    w_down,
    gain_attn,
    gain_ffn,
    rel_table,
    lay_table,
    ocr_counts,
    rel_bucket,
    lay_bucket,
    cotangent,
):
    slot = tokens.shape[0]
    valid = jnp.arange(slot) < ocr_counts[0] + IMG
    buckets = jnp.arange(NB)
    onehot = jnp.concatenate(
        [
            (rel_bucket[:, :, None] == buckets).astype(jnp.bfloat16),
            (lay_bucket[:, :, None] == buckets).astype(jnp.bfloat16),
        ],
        axis=2,
    )
    tokens_f = tokens.astype(jnp.float32)
    weights = gather_weights(
        w_query,
        w_key,
        w_value,
        w_output,
        w_gate,
        w_up,
        w_down,
        gain_attn,
        gain_ffn,
        rel_table,
        lay_table,
    )
    result, saved = forward_pass(tokens_f, weights, onehot, valid)
    output = jnp.where(valid[:, None], result, 0.0).astype(jnp.bfloat16)
    (
        full_query,
        full_key,
        full_value,
        full_output,
        full_gate,
        full_up,
        full_down,
        full_gain_attn,
        full_gain_ffn,
        full_rel,
        full_lay,
    ) = weights
    (
        normed_attn,
        queries,
        keys_all,
        values_all,
        log_totals,
        attended,
        hidden_one,
        normed_ffn,
        gate_act,
        up_proj,
        mixed,
    ) = saved
    grad_result = jnp.where(valid[:, None], cotangent.astype(jnp.float32), 0.0)
    grad_low = grad_result.astype(jnp.bfloat16)
    grad_down = contract_rows(mixed, grad_low)
    grad_mixed = contract_cols(grad_low, full_down)
    gated_value, gated_pull = jax.vjp(gated_product, gate_act, up_proj)
    grad_gate_act, grad_up_proj = gated_pull(grad_mixed)
    gate_low = grad_gate_act.astype(jnp.bfloat16)
    up_low = grad_up_proj.astype(jnp.bfloat16)
    grad_gate = contract_rows(normed_ffn, gate_low)
    grad_up = contract_rows(normed_ffn, up_low)
    grad_normed_ffn = contract_cols(gate_low, full_gate) + contract_cols(up_low, full_up)
    norm_value, norm_pull = jax.vjp(rms_scale, hidden_one, full_gain_ffn.astype(jnp.float32))
    grad_hidden_part, grad_gain_ffn = norm_pull(grad_normed_ffn)
    grad_hidden = grad_result + grad_hidden_part
    branch_low = grad_hidden.astype(jnp.bfloat16)
    grad_output = contract_rows(attended, branch_low)
    grad_attended = contract_cols(branch_low, full_output).astype(jnp.bfloat16)
    grad_queries, grad_keys, grad_values, grad_table_all = attention_backward(
        queries,
        keys_all,
        values_all,
        log_totals,
        grad_attended,
        table_pair(full_rel, full_lay),
        onehot,
        valid,
    )
    grad_rel = grad_table_all[:NB].reshape(NB * H)
    grad_lay = grad_table_all[NB:].reshape(NB * H)
    grad_query = contract_rows(normed_attn, grad_queries)
    grad_key = contract_rows(normed_attn, grad_keys)
    grad_value = contract_rows(normed_attn, grad_values)
    grad_normed_attn = (
        contract_cols(grad_queries, full_query)
        + contract_cols(grad_keys, full_key)
        + contract_cols(grad_values, full_value)
    )
    input_value, input_pull = jax.vjp(rms_scale, tokens_f, full_gain_attn.astype(jnp.float32))
    grad_input_part, grad_gain_attn = input_pull(grad_normed_attn)
    grad_tokens = grad_hidden + grad_input_part
    owned = (
        lax.psum_scatter(grad_query, ("wide", "narrow"), scatter_dimension=0, tiled=True),
        lax.psum_scatter(grad_key, ("wide", "narrow"), scatter_dimension=0, tiled=True),
        lax.psum_scatter(grad_value, ("wide", "narrow"), scatter_dimension=0, tiled=True),
        lax.psum_scatter(grad_output, ("wide", "narrow"), scatter_dimension=0, tiled=True),
        lax.psum_scatter(grad_gate, ("wide", "narrow"), scatter_dimension=0, tiled=True),
        lax.psum_scatter(grad_up, ("wide", "narrow"), scatter_dimension=0, tiled=True),
        lax.psum_scatter(grad_down, ("wide", "narrow"), scatter_dimension=0, tiled=True),
        lax.psum_scatter(grad_gain_attn, ("wide", "narrow"), scatter_dimension=0, tiled=True),
        lax.psum_scatter(grad_gain_ffn, ("wide", "narrow"), scatter_dimension=0, tiled=True),
        lax.psum_scatter(grad_rel, ("wide", "narrow"), scatter_dimension=0, tiled=True),
        lax.psum_scatter(grad_lay, ("wide", "narrow"), scatter_dimension=0, tiled=True),
    )
    return (
        output,
        grad_tokens,
        owned[0],
        owned[1],
        owned[2],
        owned[3],
        owned[4],
        owned[5],
        owned[6],
        owned[7],
        owned[8],
        owned[9],
        owned[10],
    )


def solution(mesh):
    nw, nn = mesh.shape["wide"], mesh.shape["narrow"]

    def body(*args):
        if nw == 8 and nw * nn == NB and args[1].shape[0] % 16 == 0:
            return local_fast(nw, nn, *args)
        return local(*args)

    placed = (
        P(("wide", "narrow"), None),
        P(("wide", "narrow"), None),
        P(("wide", "narrow"), None),
        P(("wide", "narrow"), None),
        P(("wide", "narrow"), None),
        P(("wide", "narrow"), None),
        P(("wide", "narrow"), None),
        P(("wide", "narrow"), None),
        P(("wide", "narrow")),
        P(("wide", "narrow")),
        P(("wide", "narrow")),
        P(("wide", "narrow")),
        P(("wide", "narrow")),
        P(("wide", "narrow"), None),
        P(("wide", "narrow"), None),
        P(("wide", "narrow"), None),
    )
    return jax.shard_map(
        body,
        mesh=mesh,
        in_specs=placed,
        out_specs=(
            P(("wide", "narrow"), None),
            P(("wide", "narrow"), None),
            P(("wide", "narrow"), None),
            P(("wide", "narrow"), None),
            P(("wide", "narrow"), None),
            P(("wide", "narrow"), None),
            P(("wide", "narrow"), None),
            P(("wide", "narrow"), None),
            P(("wide", "narrow"), None),
            P(("wide", "narrow")),
            P(("wide", "narrow")),
            P(("wide", "narrow")),
            P(("wide", "narrow")),
        ),
        check_vma=False,
    )
```

```python
import functools

import jax
import jax.numpy as jnp
from jax import lax
from jax.experimental import pallas as pl
from jax.experimental.pallas import tpu as pltpu
from jax.sharding import PartitionSpec as P

H = 16
HD = 64
NB = 32
IMG = 196
RING = 6
SCATTER_COPIES = 10
LAG = (0, 1, 2, 4, 8)
LINE_RING = 10
FEW_LAG = (0, 1, 2, 4, 14)
LAGS = LAG[-1]
FFN_LAG = 6
LATE = 2
BACK_QB = 16
WIDE = 512
DOWN_PIECE = 256
REST = 512
FIRST = 512
UP_TILES = 6
TILE = 256
QB = 8
GELU_SCALE = 0.7978845608028654
GELU_CUBE = 0.044715


RMS_EPSILON = 1e-06
MASK_SCORE = -1000000000.0
HEAD_GROUP = 4


def rms_scale(values, gain):
    return (
        values * lax.rsqrt(jnp.mean(values * values, axis=-1, keepdims=True) + RMS_EPSILON) * gain
    )


def gated_product(gate_act, up_proj):
    return jax.nn.gelu(gate_act, approximate=True) * up_proj


def product(left, right):
    return jnp.dot(left, right, preferred_element_type=jnp.float32)


def contract_rows(left, right):
    return lax.dot_general(
        left, right, (((0,), (0,)), ((), ())), preferred_element_type=jnp.float32
    )


def contract_cols(left, right):
    return lax.dot_general(
        left, right, (((1,), (1,)), ((), ())), preferred_element_type=jnp.float32
    )


def split_heads(matrix):
    return jnp.moveaxis(matrix.reshape(matrix.shape[0], H // HEAD_GROUP, HEAD_GROUP, HD), 1, 0)


def join_heads(stacked):
    return jnp.moveaxis(stacked, 0, 1).reshape(stacked.shape[1], H * HD)


def group_tables(table_all):
    return jnp.moveaxis(table_all.reshape(2 * NB, H // HEAD_GROUP, HEAD_GROUP), 1, 0)


def group_scores(query_group, key_group, table_group, onehot, valid):
    scores = jnp.einsum("ihd,jhd->hij", query_group, key_group, preferred_element_type=jnp.float32)
    scores = scores + jnp.einsum(
        "ijb,bh->hij", onehot, table_group, preferred_element_type=jnp.float32
    )
    return jnp.where(valid[None, None, :], scores, MASK_SCORE)


def gather_weights(
    w_query,
    w_key,
    w_value,
    w_output,
    w_gate,
    w_up,
    w_down,
    gain_attn,
    gain_ffn,
    rel_table,
    lay_table,
):
    return (
        lax.all_gather(w_query, ("wide", "narrow"), axis=0, tiled=True),
        lax.all_gather(w_key, ("wide", "narrow"), axis=0, tiled=True),
        lax.all_gather(w_value, ("wide", "narrow"), axis=0, tiled=True),
        lax.all_gather(w_output, ("wide", "narrow"), axis=0, tiled=True),
        lax.all_gather(w_gate, ("wide", "narrow"), axis=0, tiled=True),
        lax.all_gather(w_up, ("wide", "narrow"), axis=0, tiled=True),
        lax.all_gather(w_down, ("wide", "narrow"), axis=0, tiled=True),
        lax.all_gather(gain_attn, ("wide", "narrow"), axis=0, tiled=True),
        lax.all_gather(gain_ffn, ("wide", "narrow"), axis=0, tiled=True),
        lax.all_gather(rel_table, ("wide", "narrow"), axis=0, tiled=True),
        lax.all_gather(lay_table, ("wide", "narrow"), axis=0, tiled=True),
    )


def table_pair(full_rel, full_lay):
    return jnp.concatenate([full_rel.reshape(NB, H), full_lay.reshape(NB, H)], axis=0)


def forward_pass(tokens_f, weights, onehot, valid):
    (
        full_query,
        full_key,
        full_value,
        full_output,
        full_gate,
        full_up,
        full_down,
        full_gain_attn,
        full_gain_ffn,
        full_rel,
        full_lay,
    ) = weights
    normed_attn = rms_scale(tokens_f, full_gain_attn.astype(jnp.float32)).astype(jnp.bfloat16)
    queries = product(normed_attn, full_query).astype(jnp.bfloat16)
    keys_all = product(normed_attn, full_key).astype(jnp.bfloat16)
    values_all = product(normed_attn, full_value).astype(jnp.bfloat16)

    def forward_one_group(operands):
        query_group, key_group, value_group, table_group = operands
        scores = group_scores(query_group, key_group, table_group, onehot, valid)
        peak = jnp.max(scores, axis=-1, keepdims=True)
        expo = jnp.exp(scores - peak)
        total = jnp.sum(expo, axis=-1, keepdims=True)
        probs_low = (expo / total).astype(jnp.bfloat16)
        attended_group = jnp.einsum(
            "hij,jhd->ihd", probs_low, value_group, preferred_element_type=jnp.float32
        )
        return (attended_group.astype(jnp.bfloat16), (peak + jnp.log(total))[..., 0])

    stacked, log_totals = lax.map(
        forward_one_group,
        (
            split_heads(queries),
            split_heads(keys_all),
            split_heads(values_all),
            group_tables(table_pair(full_rel, full_lay)),
        ),
    )
    attended = join_heads(stacked)
    hidden_one = tokens_f + product(attended, full_output)
    normed_ffn = rms_scale(hidden_one, full_gain_ffn.astype(jnp.float32)).astype(jnp.bfloat16)
    gate_act = product(normed_ffn, full_gate)
    up_proj = product(normed_ffn, full_up)
    mixed = gated_product(gate_act, up_proj).astype(jnp.bfloat16)
    result = hidden_one + product(mixed, full_down)
    return (
        result,
        (
            normed_attn,
            queries,
            keys_all,
            values_all,
            log_totals,
            attended,
            hidden_one,
            normed_ffn,
            gate_act,
            up_proj,
            mixed,
        ),
    )


def attention_backward(
    queries, keys_all, values_all, log_totals, grad_attended, table_all, onehot, valid
):

    def attention_one_group(operands):
        query_group, key_group, value_group, table_group, lse_group, grad_group = operands
        scores = group_scores(query_group, key_group, table_group, onehot, valid)
        probs = jnp.exp(scores - lse_group[..., None])
        probs_low = probs.astype(jnp.bfloat16)
        grad_values = jnp.einsum(
            "hij,ihd->jhd", probs_low, grad_group, preferred_element_type=jnp.float32
        )
        grad_probs = jnp.einsum(
            "ihd,jhd->hij", grad_group, value_group, preferred_element_type=jnp.float32
        )
        grad_scores = (
            probs * (grad_probs - jnp.sum(probs * grad_probs, axis=-1, keepdims=True))
        ).astype(jnp.bfloat16)
        grad_queries = jnp.einsum(
            "hij,jhd->ihd", grad_scores, key_group, preferred_element_type=jnp.float32
        )
        grad_keys = jnp.einsum(
            "hij,ihd->jhd", grad_scores, query_group, preferred_element_type=jnp.float32
        )
        grad_table = jnp.einsum(
            "hij,ijb->bh", grad_scores, onehot, preferred_element_type=jnp.float32
        )
        return (
            grad_queries.astype(jnp.bfloat16),
            grad_keys.astype(jnp.bfloat16),
            grad_values.astype(jnp.bfloat16),
            grad_table,
        )

    grad_q_all, grad_k_all, grad_v_all, grad_tables = lax.map(
        attention_one_group,
        (
            split_heads(queries),
            split_heads(keys_all),
            split_heads(values_all),
            group_tables(table_all),
            log_totals,
            split_heads(grad_attended),
        ),
    )
    grad_table_all = jnp.moveaxis(grad_tables, 0, 1).reshape(2 * NB, H)
    return (join_heads(grad_q_all), join_heads(grad_k_all), join_heads(grad_v_all), grad_table_all)


MESH_ID = pl.DeviceIdType.MESH
BF = jnp.bfloat16
F32 = jnp.float32
X_BIT = 2
Y_BIT = 4
PARTS = ((X_BIT, Y_BIT), (Y_BIT, X_BIT))
NEAR = 1
FAR = 2


class Links:
    def __init__(self, nn, send_sem, recv_sem):
        self.nn = nn
        self.w = lax.axis_index("wide")
        self.z = lax.axis_index("narrow")
        self.send_sem = send_sem
        self.recv_sem = recv_sem
        self.used = 0
        self.sent = []

    def fresh(self):
        self.used += 1
        return self.used - 1

    def wide(self, bit):
        return (jnp.bitwise_xor(self.w, bit), self.z)

    def along(self, step):
        return (self.w, lax.rem(self.z + step, self.nn))

    def line(self, bit):
        return (self.w, jnp.bitwise_xor(self.z, bit))

    def copy(self, src, dst, number, device):
        return pltpu.make_async_remote_copy(
            src_ref=src,
            dst_ref=dst,
            send_sem=self.send_sem.at[number],
            recv_sem=self.recv_sem.at[number],
            device_id=device,
            device_id_type=MESH_ID,
        )

    def send(self, src, dst, number, device):
        copy = self.copy(src, dst, number, device)
        copy.start()
        self.sent.append(copy)

    def greet(self):
        barrier = pltpu.get_barrier_semaphore()
        others = [self.wide(bit) for bit in (1, X_BIT, Y_BIT)]
        others += [self.along(step) for step in range(1, self.nn)]
        for other in others:
            pl.semaphore_signal(barrier, inc=1, device_id=other, device_id_type=MESH_ID)
        pl.semaphore_wait(barrier, len(others))

    def finish(self):
        for copy in self.sent:
            copy.wait_send()


class Gather:
    def __init__(self, links, shard, full, rows, window, parts, local_sem, line=None, merged=None):
        self.links, self.shard, self.full, self.rows, self.parts = links, shard, full, rows, parts
        self.window = window
        self.local_sem, self.line, self.merged = local_sem, line, merged
        nn = links.nn
        self.block = rows * nn
        self.line_ids = [links.fresh() for _ in range(1, nn)]
        self.part_ids = {
            (p, mask): links.fresh()
            for p in range(len(parts))
            for mask in (X_BIT, Y_BIT, X_BIT | Y_BIT)
        }
        self.core_ids = {mask: links.fresh() for mask in (0, X_BIT, Y_BIT, X_BIT | Y_BIT)}

    def place(self, w, z):
        if self.line is not None:
            return self.line.at[z]
        return self.full.at[pl.ds((w * self.links.nn + z) * self.rows, self.rows), pl.ds(*self.window)]

    def span(self, mask, part=None):
        rows = pl.ds(jnp.bitwise_xor(self.links.w, mask) * self.block, self.block)
        low, size = self.window if part is None else self.parts[part][:2]
        return self.full.at[rows, pl.ds(low, size)]

    def own(self):
        return pltpu.make_async_copy(
            self.shard, self.place(self.links.w, self.links.z), self.local_sem
        )

    def start(self):
        k = self.links
        self.own().start()
        for bit in (FAR, NEAR):
            k.send(self.shard, self.place(k.w, k.z), self.line_ids[bit - 1], k.line(bit))

    def landed(self, bit):
        k = self.links
        place = self.place(k.w, jnp.bitwise_xor(k.z, bit))
        k.copy(place, place, self.line_ids[bit - 1], k.line(NEAR)).wait_recv()
        return place

    def middle(self):
        place = self.landed(FAR)
        self.links.send(place, place, self.line_ids[2], self.links.line(NEAR))

    def ready(self):
        self.own().wait()
        self.landed(NEAR)
        self.landed(NEAR | FAR)
        k = self.links
        if self.line is not None:
            whole = jnp.concatenate(
                [self.line[z, : self.rows].astype(F32) for z in range(k.nn)], axis=0
            )
            self.merged[...] = whole.astype(BF)
            move = pltpu.make_async_copy(self.merged, self.span(0), self.local_sem)
            move.start()
            move.wait()

    def spread(self):
        k = self.links
        for p, part in enumerate(self.parts):
            for bit in part[2]:
                k.send(self.span(0, p), self.span(0, p), self.part_ids[p, bit], k.wide(bit))
        k.send(self.span(0), self.span(0), self.core_ids[0], k.wide(1))

    def arrive(self, p, mask):
        k = self.links
        k.copy(
            self.span(mask, p), self.span(mask, p), self.part_ids[p, mask], k.wide(X_BIT)
        ).wait_recv()

    def forward(self):
        k = self.links
        for p, part in enumerate(self.parts):
            first, second = part[2]
            self.arrive(p, first)
            both = first | second
            k.send(self.span(first, p), self.span(first, p), self.part_ids[p, both], k.wide(second))

    def settle(self):
        k = self.links
        for p, part in enumerate(self.parts):
            self.arrive(p, part[2][1])
        for mask in (X_BIT, Y_BIT):
            k.send(self.span(mask), self.span(mask), self.core_ids[mask], k.wide(1))

    def last(self):
        k = self.links
        both = X_BIT | Y_BIT
        for p in range(len(self.parts)):
            self.arrive(p, both)
        k.send(self.span(both), self.span(both), self.core_ids[both], k.wide(1))

    def done(self):
        k = self.links
        for mask, number in self.core_ids.items():
            place = self.span(mask | 1)
            k.copy(place, place, number, k.wide(1)).wait_recv()


def halves(columns, first=0):
    low = columns // 256 * 128
    return ((first, low, PARTS[0]), (first + low, columns - low, PARTS[1]))


class GatherSquare:
    def __init__(self, links, shard, full, rows, window, local_sem, square, lines, merged):
        self.links, self.shard, self.full, self.rows, self.window = links, shard, full, rows, window
        self.square, self.lines, self.merged, self.local_sem = square, lines, merged, local_sem
        self.parts = halves(window[1])
        self.block = rows * links.nn
        self.part_ids = {
            (p, mask): links.fresh()
            for p in range(len(self.parts))
            for mask in (X_BIT, Y_BIT, X_BIT | Y_BIT)
        }
        self.line_ids = [links.fresh() for _ in range(1, links.nn)]
        self.core_ids = [links.fresh() for _ in range(square.shape[0])]

    def spot(self, mask, p):
        low, size = self.parts[p][:2]
        return self.square.at[jnp.bitwise_xor(self.links.w, mask) // 2, :, pl.ds(low, size)]

    def own(self):
        return pltpu.make_async_copy(
            self.shard, self.square.at[self.links.w // 2], self.local_sem.at[0]
        )

    def start(self):
        k = self.links
        self.own().start()
        for p, (low, size, order) in enumerate(self.parts):
            for bit in order:
                k.send(self.shard.at[:, pl.ds(low, size)], self.spot(0, p), self.part_ids[p, bit], k.wide(bit))

    def arrive(self, p, mask):
        k = self.links
        k.copy(self.spot(mask, p), self.spot(mask, p), self.part_ids[p, mask], k.wide(X_BIT)).wait_recv()

    def forward(self):
        k = self.links
        for p, (low, size, (first, second)) in enumerate(self.parts):
            self.arrive(p, first)
            k.send(self.spot(first, p), self.spot(first, p), self.part_ids[p, first | second], k.wide(second))
        for p, (low, size, (first, second)) in enumerate(self.parts):
            self.arrive(p, second)

    def keep(self):
        return pltpu.make_async_copy(self.square, self.lines.at[self.links.z], self.local_sem.at[0])

    def line(self):
        k = self.links
        self.own().wait()
        for p in range(len(self.parts)):
            self.arrive(p, X_BIT | Y_BIT)
        self.keep().start()
        for bit in (FAR, NEAR):
            k.send(self.square, self.lines.at[k.z], self.line_ids[bit - 1], k.line(bit))

    def landed(self, bit):
        k = self.links
        place = self.lines.at[jnp.bitwise_xor(k.z, bit)]
        k.copy(place, place, self.line_ids[bit - 1], k.line(NEAR)).wait_recv()
        return place

    def middle(self):
        place = self.landed(FAR)
        self.links.send(place, place, self.line_ids[2], self.links.line(NEAR))

    def rows_of(self, square, core):
        rows = pl.ds((square * 2 + core) * self.block, self.block)
        return self.full.at[rows, pl.ds(*self.window)]

    def out(self, square):
        core = lax.rem(self.links.w, 2)
        return pltpu.make_async_copy(
            self.merged.at[square], self.rows_of(square, core), self.local_sem.at[1 + square]
        )

    def join(self):
        k = self.links
        self.keep().wait()
        self.landed(NEAR)
        self.landed(NEAR | FAR)

        def one(square, carry):
            whole = jnp.concatenate(
                [self.lines[z, square, : self.rows].astype(F32) for z in range(k.nn)], axis=0
            )
            self.merged[square] = whole.astype(BF)
            return carry

        lax.fori_loop(0, self.merged.shape[0], one, 0)
        core = lax.rem(k.w, 2)
        for square, number in enumerate(self.core_ids):
            self.out(square).start()
            k.send(self.merged.at[square], self.rows_of(square, core), number, k.wide(1))

    def done(self):
        k = self.links
        core = lax.rem(k.w, 2)
        for square, number in enumerate(self.core_ids):
            self.out(square).wait()
            k.copy(self.merged.at[square], self.rows_of(square, 1 - core), number, k.wide(1)).wait_recv()


def dot(left, right):
    return jnp.dot(left, right, preferred_element_type=F32)


def dot_nt(left, right):
    return lax.dot_general(left, right, (((1,), (1,)), ((), ())), preferred_element_type=F32)


def dot_tn(left, right):
    return lax.dot_general(left, right, (((0,), (0,)), ((), ())), preferred_element_type=F32)


def iota(shape, dimension):
    return lax.broadcasted_iota(jnp.int32, shape, dimension)


def ones_where(mask):
    return jnp.where(mask, 1.0, 0.0).astype(BF)


def small_rows(small, index):
    return small.reshape(small.shape[0] // 8, 8, 128)[:, index, :]


def unpack_row(small, index, total):
    rows = small_rows(small, index)
    devices = rows.shape[0]
    each = total // devices
    pick = ones_where(iota((128, total), 0) == lax.rem(iota((128, total), 1), each))
    spread = dot(rows.astype(BF), pick)
    mine = iota((devices, total), 1) // each == iota((devices, total), 0)
    return jnp.sum(jnp.where(mine, spread, 0.0), axis=0, keepdims=True)


def table_block(small):
    pick_shape = (H * QB, 128)
    total = None
    pick = ones_where(iota(pick_shape, 1) == iota(pick_shape, 0) // QB)
    for index in range(2):
        table = dot_nt(pick, small_rows(small, 2 + index).astype(BF)).astype(BF)
        wide = (NB, QB * 2 * NB)
        spread = dot(table, ones_where(lax.rem(iota(wide, 1), 2 * NB) == iota(wide, 0) + NB * index))
        total = spread if total is None else total + spread
    shape = (H * QB, QB * 2 * NB)
    mine = lax.rem(iota(shape, 0), QB) == iota(shape, 1) // (2 * NB)
    return jnp.where(mine, total, 0.0).astype(BF)


def bucket_ones(rel, lay, onehot, block):
    width = rel.shape[1]
    rows = iota((NB, width), 0)
    for query in range(QB):
        for index, bucket in enumerate((rel, lay)):
            row = bucket[pl.ds(block * QB + query, 1), :]
            low = (query * 2 + index) * NB
            onehot[low : low + NB, :] = ones_where(jnp.broadcast_to(row, (NB, width)) == rows)


def forward_kernel(nn, shapes, *refs):
    count = len(shapes)
    occupied, tokens, rel_hbm, lay_hbm, cotangent = refs[:5]
    parameters, down_shard = refs[5:9], refs[9]
    shards = refs[10 : 8 + count]
    refs = refs[8 + count :]
    fulls, refs = refs[:count], refs[count:]
    (grad_h, na_t, q_t, k_h, v_h, att_t, hid_h, nf_t, mix_h, probs_h, slope_h, act_h) = refs[:12]
    down_grads, down_came, refs = refs[12], refs[13], refs[14:]
    (
        line,
        merged,
        x,
        rel,
        lay,
        small,
        lhs,
        onehot,
        bias,
        na,
        q,
        k,
        v,
        att,
        hid,
        nf,
        mix,
        slope,
        act,
        probs,
        w_one,
        w_wide,
        grad,
        down_stage,
        gains,
        turned,
        mixed_t,
        send_sem,
        recv_sem,
        gather_sem,
        local_sem,
        ring_sem,
        rest_square,
        rest_lines,
        rest_merged,
        rest_sem,
        small_shard,
        down_padded,
        o_square,
        o_lines,
        o_merged,
        o_sem,
    ) = refs
    shards = (small_shard,) + tuple(shards) + (down_padded,)
    slots, width = x.shape
    links = Links(nn, send_sem, recv_sem)
    numbers = iter(range(64))

    def move(src, dst):
        copy = pltpu.make_async_copy(src, dst, local_sem.at[next(numbers)])
        copy.start()
        return copy

    small_shard[...] = jnp.zeros_like(small_shard)
    for index, part in enumerate(parameters):
        small_shard[index : index + 1, : part.shape[0]] = part[...].astype(F32).reshape(1, part.shape[0])
    down_padded[...] = jnp.zeros_like(down_padded)
    down_padded[: down_shard.shape[0], :] = down_shard[...]
    links.greet()
    g = []
    first, wide = UP_TILES * TILE, shapes[5][1]
    cuts = [(0, 0, shapes[0][1]), (1, 0, FIRST), (1, FIRST, width - FIRST)]
    cuts += [(index, 0, width) for index in (2, 3)]
    for index in (5, 6):
        cuts += [(index, 0, first), (index, first, wide - first)]
    cuts.append((7, 0, width - REST))
    for number, (index, low, columns) in enumerate(cuts):
        odd = index == 7
        g.append(
            Gather(
                links,
                shards[index].at[:, pl.ds(low, columns)],
                w_wide.at[index - 5] if index in (5, 6) else fulls[index],
                shapes[index][0],
                (low, columns),
                halves(columns, low) if columns > 128 else ((0, columns, PARTS[0]),),
                gather_sem.at[number],
                line if odd else None,
                merged if odd else None,
            )
        )
    rows, columns = shapes[-1]
    rest = GatherSquare(
        links,
        shards[-1].at[:, pl.ds(columns - REST, REST)],
        fulls[-1],
        rows,
        (columns - REST, REST),
        rest_sem,
        rest_square,
        rest_lines,
        rest_merged,
    )
    o_g = GatherSquare(
        links, shards[4], fulls[4], shapes[4][0], (0, width), o_sem, o_square, o_lines, o_merged
    )
    down_id = links.used
    small_g, q_g, q_two_g, k_g, v_g, gate_g, gate_two_g, up_g, up_two_g, down_g = g
    leaving = []
    turning = {}
    ffn = mixed_t.shape[0]
    tiles = ffn // TILE
    across = slots // TILE
    pairs = H // 2
    blocks = slots // QB
    block, piece = down_stage.shape[3:]
    chunks = width // piece
    squares = down_stage.shape[1]
    valid = iota((1, slots), 1) < occupied[0] + IMG

    def turn_out(slot, source, target):
        if slot in turning:
            turning[slot].wait()

        def one(tile, carry):
            at = pl.ds(pl.multiple_of(tile * TILE, TILE), TILE)
            turned[slot, at, :] = source[:, at].T
            return carry

        lax.fori_loop(0, width // TILE, one, 0)
        turning[slot] = move(turned.at[slot], target)

    def unpack():
        gains[0:1, :] = unpack_row(small, 0, width)
        gains[1:2, :] = unpack_row(small, 1, width)
        lhs[...] = table_block(small)

    def normalise(source, row, target):
        def one(index, carry):
            at = pl.ds(pl.multiple_of(index * 64, 64), 64)
            values = source[at, :].astype(F32)
            scale = lax.rsqrt(jnp.mean(values * values, axis=-1, keepdims=True) + RMS_EPSILON)
            target[at, :] = (values * scale * gains[row : row + 1, :]).astype(BF)
            return carry

        lax.fori_loop(0, slots // 64, one, 0)

    def bias_block(block, carry):
        bucket_ones(rel, lay, onehot, block)
        found = jnp.where(valid, dot(lhs[...], onehot[...]), MASK_SCORE)
        bias[:, pl.ds(pl.multiple_of(block * QB, QB), QB), :] = found.reshape(H, QB, slots)
        return carry

    def add_bias(part, parts):
        lax.fori_loop(part * blocks // parts, (part + 1) * blocks // parts, bias_block, 0)

    def project(slot, target):
        def one(tile, carry):
            at = pl.ds(pl.multiple_of(tile * WIDE, WIDE), WIDE)
            target[:, at] = dot(na[...], w_one[slot, :, at]).astype(BF)
            return carry

        lax.fori_loop(0, width // WIDE, one, 0)

    def probs_out(pair):
        turn = lax.rem(pair, 2)
        return pltpu.make_async_copy(probs.at[turn], probs_h.at[pl.ds(pair * 2, 2)], ring_sem.at[turn])

    def attend_pair(pair, carry):
        @pl.when(pair >= 2)
        def _():
            probs_out(pair - 2).wait()

        at = pl.ds(pl.multiple_of(pair * 128, 128), 128)
        low = iota((slots, 128), 1) < HD
        queries = q[:, at]
        keys = k[:, at]
        found = []
        for side in range(2):
            mine = jnp.where(low if side == 0 else jnp.logical_not(low), queries, 0)
            scores = dot_nt(mine, keys) + bias[pair * 2 + side]
            peak = jnp.max(scores, axis=-1, keepdims=True)
            expo = jnp.exp(scores - peak)
            total = jnp.sum(expo, axis=-1, keepdims=True)
            share = (expo * (1.0 / total)).astype(BF)
            probs[lax.rem(pair, 2), side] = share
            found.append(dot(share, v[:, at]))
        att[:, at] = jnp.where(low, found[0], found[1]).astype(BF)
        probs_out(pair).start()
        return carry

    def attend(first, last):
        lax.fori_loop(first, last, attend_pair, 0)

    def output():
        def one(tile, carry):
            at = pl.ds(pl.multiple_of(tile * WIDE, WIDE), WIDE)
            hid[:, at] = x[:, at].astype(F32) + dot(att[...], w_one[1, :, at])
            return carry

        lax.fori_loop(0, width // WIDE, one, 0)
        leaving.append(move(hid, hid_h))

    def keep_valid():
        valid_rows = iota((slots, 1), 0) < occupied[0] + IMG

        def one(tile, carry):
            at = pl.ds(pl.multiple_of(tile * TILE, TILE), TILE)
            grad[:, at] = jnp.where(valid_rows, grad[:, at].astype(F32), 0.0).astype(BF)
            return carry

        lax.fori_loop(0, width // TILE, one, 0)
        leaving.append(move(grad, grad_h))

    def gate_spot(tile, second):
        at = pl.ds(pl.multiple_of(lax.rem(tile, across) * TILE, TILE), TILE)
        return bias.at[tile // across + second * (-(-tiles // across)), :, at]

    def gate_tile(tile, carry):
        at = pl.ds(pl.multiple_of(tile * TILE, TILE), TILE)
        gate = dot(nf[...], w_wide[0, :, at])
        square = gate * gate
        inner = GELU_SCALE * gate * (1.0 + GELU_CUBE * square)
        bend = jnp.tanh(inner)
        half = 0.5 * (1.0 + bend)
        gate_spot(tile, 0)[...] = gate * half
        gate_spot(tile, 1)[...] = half + 0.5 * gate * (1.0 - bend * bend) * GELU_SCALE * (
            1.0 + 3.0 * GELU_CUBE * square
        )
        return carry

    def ffn_out(tile):
        turn = lax.rem(tile, 2)
        at = pl.ds(pl.multiple_of(tile * TILE, TILE), TILE)
        return (
            pltpu.make_async_copy(slope.at[turn], slope_h.at[:, at], ring_sem.at[2 + turn]),
            pltpu.make_async_copy(act.at[turn], act_h.at[:, at], ring_sem.at[4 + turn]),
            pltpu.make_async_copy(mix.at[turn], mix_h.at[:, at], ring_sem.at[6 + turn]),
        )

    def ffn_tile(tile, carry):
        @pl.when(tile >= 2)
        def _():
            for copy in ffn_out(tile - 2):
                copy.wait()

        at = pl.ds(pl.multiple_of(tile * TILE, TILE), TILE)
        turn = lax.rem(tile, 2)
        up = dot(nf[...], w_wide[1, :, at])
        active = gate_spot(tile, 0)[...]
        rise = gate_spot(tile, 1)[...]
        mixed = (active * up).astype(BF)
        mix[turn] = mixed
        mixed_t[at, :] = mixed.T
        act[turn] = active.astype(BF)
        slope[turn] = (up * rise).astype(BF)
        for copy in ffn_out(tile):
            copy.start()
        return carry

    def down_place(chunk, half):
        return down_grads.at[chunk, pl.ds(half * squares, squares)]

    def down_copy(unit):
        half, chunk, turn = unit // chunks, lax.rem(unit, chunks), lax.rem(unit, 2)
        return pltpu.make_async_copy(down_stage.at[turn], down_place(chunk, half), ring_sem.at[8 + turn])

    def down_trade(unit):
        half, chunk = unit // chunks, lax.rem(unit, chunks)
        core = lax.rem(links.w, 2)
        there = pl.ds(half * squares, squares)
        return links.copy(
            down_grads.at[chunk, there, 1 - core],
            down_came.at[chunk, there],
            down_id + unit,
            links.wide(1),
        )

    def down_unit(unit, carry):
        half, chunk = unit // chunks, lax.rem(unit, chunks)
        size = 2 * squares * block
        rows = pl.ds(pl.multiple_of(half * size, 16), size)
        at = pl.ds(pl.multiple_of(chunk * piece, piece), piece)
        found = dot(mixed_t[rows, :], grad[:, at])
        down_stage[lax.rem(unit, 2)] = found.astype(BF).reshape(down_stage.shape[1:])
        down_copy(unit).start()

        @pl.when(unit >= 1)
        def _():
            down_copy(unit - 1).wait()
            down_trade(unit - 1).start()

        return carry

    def down_units(first, last):
        lax.fori_loop(first, last, down_unit, 0)

    small_g.start()
    q_g.start()
    q_two_g.start()
    o_g.start()
    rest.start()
    arriving = [move(tokens, x), move(rel_hbm, rel), move(lay_hbm, lay)]
    grad_in = move(cotangent, grad)
    small_g.middle()
    q_g.middle()
    q_two_g.middle()
    k_g.start()
    q_g.ready()
    q_g.spread()
    small_g.ready()
    small_g.spread()
    q_two_g.ready()
    q_two_g.spread()
    k_g.middle()
    v_g.start()
    small_g.forward()
    q_g.forward()
    small_g.settle()
    small_g.last()
    small_g.done()
    small_in = move(fulls[0], small)
    o_g.forward()
    rest.forward()
    k_g.ready()
    k_g.spread()
    v_g.middle()
    gate_g.start()
    q_two_g.forward()
    for copy in arriving:
        copy.wait()
    small_in.wait()
    unpack()
    normalise(x, 0, na)
    turn_out(0, na, na_t)
    q_g.settle()
    q_two_g.settle()
    v_g.ready()
    v_g.spread()
    k_g.forward()
    gate_g.middle()
    gate_two_g.start()
    q_g.last()
    q_two_g.last()
    add_bias(0, 4)
    k_g.settle()
    gate_g.ready()
    gate_g.spread()
    gate_two_g.middle()
    up_g.start()
    v_g.forward()
    add_bias(1, 4)
    k_g.last()
    q_g.done()
    q_two_g.done()
    fetch_q = move(fulls[1], w_one.at[0])
    v_g.settle()
    up_g.middle()
    up_two_g.start()
    add_bias(2, 4)
    k_g.done()
    fetch_k = move(fulls[2], w_one.at[1])
    gate_two_g.ready()
    gate_two_g.spread()
    gate_g.forward()
    up_two_g.middle()
    o_g.line()
    add_bias(3, 4)
    v_g.last()
    fetch_q.wait()
    project(0, q)
    turn_out(1, q, q_t)
    v_g.done()
    fetch_v = move(fulls[3], w_one.at[0])
    fetch_k.wait()
    project(1, k)
    leaving.append(move(k, k_h))
    fetch_v.wait()
    project(0, v)
    leaving.append(move(v, v_h))
    up_g.ready()
    up_g.spread()
    gate_g.settle()
    attend(0, 3)
    gate_two_g.forward()
    o_g.middle()
    down_g.start()
    attend(3, 6)
    gate_g.last()
    gate_two_g.settle()
    attend(6, pairs)
    turn_out(0, att, att_t)
    o_g.join()
    down_g.middle()
    up_g.forward()
    up_two_g.ready()
    up_two_g.spread()
    o_g.done()
    fetch_o = move(fulls[4], w_one.at[1])
    down_g.ready()
    rest.line()
    fetch_o.wait()
    output()
    normalise(hid, 1, nf)
    turn_out(1, nf, nf_t)
    gate_two_g.last()
    gate_g.done()
    grad_in.wait()
    keep_valid()
    lax.fori_loop(0, UP_TILES, gate_tile, 0)
    up_g.settle()
    gate_two_g.done()
    leaving.append(move(w_wide.at[0], fulls[5]))
    lax.fori_loop(UP_TILES, tiles, gate_tile, 0)
    up_g.last()
    up_two_g.forward()
    down_g.spread()
    up_g.done()
    lax.fori_loop(0, UP_TILES, ffn_tile, 0)
    up_two_g.settle()
    down_units(0, chunks)
    rest.middle()
    up_two_g.last()
    up_two_g.done()
    leaving.append(move(w_wide.at[1], fulls[6]))
    lax.fori_loop(UP_TILES, tiles, ffn_tile, 0)
    down_g.forward()
    down_units(chunks, 2 * chunks)
    down_g.settle()
    rest.join()
    down_g.last()
    down_copy(jnp.int32(2 * chunks - 1)).wait()
    down_trade(jnp.int32(2 * chunks - 1)).start()
    down_g.done()
    rest.done()
    for unit in range(2 * chunks):
        down_trade(jnp.int32(unit)).wait()
    for copy in leaving + list(turning.values()):
        copy.wait()
    for pair in (pairs - 2, pairs - 1):
        probs_out(pair).wait()
    for tile in (tiles - 2, tiles - 1):
        for copy in ffn_out(tile):
            copy.wait()
    links.finish()


def forward_all(nw, nn, counts, tokens, rel, lay, cotangent, parameters, shards):
    devices = nw * nn
    shapes = [(8, 128)] + [shard.shape for shard in shards]
    odd_rows = shards[-1].shape[0]
    tile_rows = padded(odd_rows)
    slots, width = tokens.shape
    copies = (len(shapes) + 4) * (nn - 1 + 6 + nw // 2) + 2 * (width // DOWN_PIECE)
    ffn = shapes[5][1]
    low = jax.ShapeDtypeStruct((slots, width), BF)
    wide = jax.ShapeDtypeStruct((slots, ffn), BF)
    full = jax.ShapeDtypeStruct((slots, width), F32)
    out_shape = [
        jax.ShapeDtypeStruct((rows * devices, columns), BF if index else F32)
        for index, (rows, columns) in enumerate(shapes)
    ]
    low_t = jax.ShapeDtypeStruct((width, slots), BF)
    out_shape += [low, low_t, low_t, low, low, low_t, full, low_t, wide]
    out_shape += [jax.ShapeDtypeStruct((H, slots, slots), BF), wide, wide]
    down = (nw // 2, 2, nn * odd_rows, DOWN_PIECE)
    out_shape += [jax.ShapeDtypeStruct((width // DOWN_PIECE,) + down, BF)]
    out_shape += [jax.ShapeDtypeStruct((width // DOWN_PIECE, nw // 2, nn * odd_rows, DOWN_PIECE), BF)]
    half = (tile_rows, REST)
    hbm = pl.BlockSpec(memory_space=pl.ANY)
    page = pltpu.VMEM((slots, width), BF)
    return pl.pallas_call(
        functools.partial(forward_kernel, nn, shapes),
        out_shape=out_shape,
        in_specs=[pl.BlockSpec(memory_space=pltpu.SMEM)]
        + [hbm] * 4
        + [pl.BlockSpec(memory_space=pltpu.VMEM)] * 5
        + [hbm] * (len(shards) - 1),
        out_specs=[hbm] * len(out_shape),
        scratch_shapes=[
            pltpu.VMEM((nn, tile_rows, width - REST), BF),
            pltpu.VMEM((nn * odd_rows, width - REST), BF),
            page,
            pltpu.VMEM((slots, slots), jnp.int32),
            pltpu.VMEM((slots, slots), jnp.int32),
            pltpu.VMEM((devices * 8, 128), F32),
            pltpu.VMEM((H * QB, QB * 2 * NB), BF),
            pltpu.VMEM((QB * 2 * NB, slots), BF),
            pltpu.VMEM((H, slots, slots), F32),
            page,
            page,
            page,
            page,
            page,
            pltpu.VMEM((slots, width), F32),
            page,
            pltpu.VMEM((2, slots, TILE), BF),
            pltpu.VMEM((2, slots, TILE), BF),
            pltpu.VMEM((2, slots, TILE), BF),
            pltpu.VMEM((2, 2, slots, slots), BF),
            pltpu.VMEM((2, width, width), BF),
            pltpu.VMEM((2, width, ffn), BF),
            page,
            pltpu.VMEM((2, down[0] // 2) + down[1:], BF),
            pltpu.VMEM((8, width), F32),
            pltpu.VMEM((2, width, slots), BF),
            pltpu.VMEM((ffn, slots), BF),
            pltpu.SemaphoreType.DMA((copies,)),
            pltpu.SemaphoreType.DMA((copies,)),
            pltpu.SemaphoreType.DMA((len(shapes) + 3,)),
            pltpu.SemaphoreType.DMA((64,)),
            pltpu.SemaphoreType.DMA((10,)),
            pltpu.VMEM((nw // 2,) + half, BF),
            pltpu.VMEM((nn, nw // 2) + half, BF),
            pltpu.VMEM((nw // 2, nn * odd_rows, half[1]), BF),
            pltpu.SemaphoreType.DMA((1 + nw // 2,)),
            pltpu.VMEM((8, 128), F32),
            pltpu.VMEM((tile_rows, width), BF),
            pltpu.VMEM((nw // 2,) + shards[3].shape, BF),
            pltpu.VMEM((nn, nw // 2) + shards[3].shape, BF),
            pltpu.VMEM((nw // 2, nn * shards[3].shape[0], width), BF),
            pltpu.SemaphoreType.DMA((1 + nw // 2,)),
        ],
        compiler_params=pltpu.CompilerParams(
            collective_id=0, has_side_effects=True, vmem_limit_bytes=63 * 2**20
        ),
    )(counts, tokens, rel, lay, cotangent, *parameters, shards[-1], *shards[:-1])


class Scatter:
    def __init__(self, links, chunks, rows, columns, grads, came, slots, base, traded=False, first=0):
        self.links, self.chunks, self.rows, self.columns = links, chunks, rows, columns
        self.grads, self.came = grads, came
        (self.held, self.other, self.round, self.out_line, self.in_line, self.load_sem) = slots
        self.base = base
        self.traded = traded
        self.first = first
        self.block = rows * links.nn
        self.parts = halves(columns)
        self.core = lax.rem(links.w, 2)
        self.ring = self.held.shape[0]
        self.line_ring = self.out_line.shape[0]

    def number(self, chunk, kind):
        return self.base + chunk * SCATTER_COPIES + kind

    def core_copy(self, chunk):
        return self.links.copy(
            self.grads.at[chunk, :, 1 - self.core],
            self.came.at[chunk],
            self.number(chunk, 0),
            self.links.wide(1),
        )

    def trade(self, chunk):
        self.core_copy(chunk).start()

    def loads(self, chunk):
        slot, turn = lax.rem(chunk, self.ring), lax.rem(chunk, 2)
        return (
            pltpu.make_async_copy(
                self.grads.at[chunk, :, self.core], self.held.at[slot], self.load_sem.at[turn, 0]
            ),
            pltpu.make_async_copy(
                self.came.at[chunk], self.other.at[turn], self.load_sem.at[turn, 1]
            ),
        )

    def fetch(self, chunk):
        if not self.traded:
            self.core_copy(chunk).wait_recv()
        for load in self.loads(chunk):
            load.start()

    def square(self, mask):
        return jnp.bitwise_xor(self.links.w, mask) // 2

    def hop(self, chunk, p, mask):
        slot = lax.rem(chunk, self.ring)
        low, size, order = self.parts[p]
        bit = order[1] if mask & order[1] else order[0]
        kind = 1 + p * 3 + (X_BIT, Y_BIT, X_BIT | Y_BIT).index(mask)
        return self.links.copy(
            self.held.at[slot, self.square(mask), :, pl.ds(low, size)],
            self.round.at[slot, kind - 1, :, pl.ds(0, size)],
            self.number(chunk, kind),
            self.links.wide(bit),
        )

    def landed(self, chunk, p, mask):
        return self.round.at[
            lax.rem(chunk, self.ring), p * 3 + (X_BIT, Y_BIT, X_BIT | Y_BIT).index(mask)
        ]

    def add_core(self, chunk):
        for load in self.loads(chunk):
            load.wait()
        slot, turn = lax.rem(chunk, self.ring), lax.rem(chunk, 2)

        def one(square, carry):
            self.held[slot, square] = (
                self.held[slot, square].astype(F32) + self.other[turn, square].astype(F32)
            ).astype(BF)
            return carry

        lax.fori_loop(0, self.held.shape[1], one, 0)
        for p, part in enumerate(self.parts):
            self.hop(chunk, p, X_BIT | Y_BIT).start()
        for p, part in enumerate(self.parts):
            self.hop(chunk, p, part[2][1]).start()

    def add_corner(self, chunk):
        slot = lax.rem(chunk, self.ring)
        for p, (low, size, order) in enumerate(self.parts):
            self.hop(chunk, p, X_BIT | Y_BIT).wait_recv()
            square = self.square(order[0])
            came = self.landed(chunk, p, X_BIT | Y_BIT)
            self.held[slot, square, :, low : low + size] = (
                self.held[slot, square, :, low : low + size].astype(F32)
                + came[:, :size].astype(F32)
            ).astype(BF)
        for p, part in enumerate(self.parts):
            self.hop(chunk, p, part[2][0]).start()

    def line_copy(self, chunk, step):
        k = self.links
        slot = lax.rem(chunk, self.line_ring)
        return k.copy(
            self.out_line.at[slot, lax.rem(k.z + step, k.nn)],
            self.in_line.at[slot, step - 1],
            self.number(chunk, 6 + step),
            k.along(step),
        )

    def add_square(self, chunk):
        slot, line = lax.rem(chunk, self.ring), lax.rem(chunk, self.line_ring)
        home = self.square(0)
        for p, (low, size, order) in enumerate(self.parts):
            total = self.held[slot, home, :, low : low + size].astype(F32)
            for mask in order:
                self.hop(chunk, p, mask).wait_recv()
                total = total + self.landed(chunk, p, mask)[:, :size].astype(F32)
            for z in range(self.links.nn):
                self.out_line[line, z, : self.rows, low : low + size] = total[
                    z * self.rows : (z + 1) * self.rows
                ].astype(BF)
        for step in range(1, self.links.nn):
            self.line_copy(chunk, step).start()
        if not self.traded:
            self.core_copy(chunk).wait_send()
        for p in range(len(self.parts)):
            for mask in (X_BIT, Y_BIT, X_BIT | Y_BIT):
                self.hop(chunk, p, mask).wait_send()

    def total(self, chunk):
        slot = lax.rem(chunk, self.line_ring)
        total = self.out_line[slot, self.links.z, : self.rows].astype(F32)
        for step in range(1, self.links.nn):
            self.line_copy(chunk, step).wait_recv()
            total = total + self.in_line[slot, step - 1, : self.rows].astype(F32)
        return total

    def pump(self, index, out):
        index = jnp.int32(index)
        steps = (self.fetch, self.add_core, self.add_corner, self.add_square, self.finish)
        for lag, action in zip(FEW_LAG if self.traded else LAG, steps):
            chunk = index - lag + self.first

            @pl.when(jnp.logical_and(chunk >= self.first, chunk < self.chunks))
            def _(chunk=chunk, action=action):
                action(chunk, out) if action == self.finish else action(chunk)

    def finish(self, chunk, out):
        out[chunk] = self.total(chunk)
        for step in range(1, self.links.nn):
            self.line_copy(chunk, step).wait_send()


class ScatterLine:
    def __init__(self, links, rows, columns, grads, came, slots, base):
        self.links, self.rows, self.columns = links, rows, columns
        self.grads, self.came = grads, came
        (self.held, self.other, self.square, self.round, self.in_line, self.load_sem) = slots
        self.base = base
        self.parts = halves(columns)
        self.core = lax.rem(links.w, 2)

    def number(self, chunk, kind):
        return self.base + chunk * SCATTER_COPIES + kind

    def core_copy(self, chunk):
        return self.links.copy(
            self.grads.at[chunk, :, 1 - self.core],
            self.came.at[chunk],
            self.number(chunk, 0),
            self.links.wide(1),
        )

    def loads(self, chunk):
        return (
            pltpu.make_async_copy(
                self.grads.at[chunk, :, self.core], self.held.at[chunk], self.load_sem.at[0]
            ),
            pltpu.make_async_copy(self.came.at[chunk], self.other, self.load_sem.at[1]),
        )

    def fetch(self, chunk):
        self.core_copy(chunk).wait_recv()
        for load in self.loads(chunk):
            load.start()

    def line_copy(self, chunk, step):
        k = self.links
        rows = pl.ds(pl.multiple_of(lax.rem(k.z + step, k.nn) * self.rows, self.rows), self.rows)
        return k.copy(
            self.held.at[chunk, :, rows],
            self.in_line.at[chunk, step - 1],
            self.number(chunk, 6 + step),
            k.along(step),
        )

    def add_core(self, chunk):
        for load in self.loads(chunk):
            load.wait()

        def one(square, carry):
            self.held[chunk, square] = (
                self.held[chunk, square].astype(F32) + self.other[square].astype(F32)
            ).astype(BF)
            return carry

        lax.fori_loop(0, self.held.shape[1], one, 0)
        for step in range(1, self.links.nn):
            self.line_copy(chunk, step).start()

    def spot(self, mask):
        return jnp.bitwise_xor(self.links.w, mask) // 2

    def hop(self, chunk, p, mask):
        low, size, order = self.parts[p]
        bit = order[1] if mask & order[1] else order[0]
        kind = 1 + p * 3 + (X_BIT, Y_BIT, X_BIT | Y_BIT).index(mask)
        return self.links.copy(
            self.square.at[chunk, self.spot(mask), :, pl.ds(low, size)],
            self.round.at[chunk, kind - 1],
            self.number(chunk, kind),
            self.links.wide(bit),
        )

    def landed(self, chunk, p, mask):
        kind = p * 3 + (X_BIT, Y_BIT, X_BIT | Y_BIT).index(mask)
        return self.round[chunk, kind].astype(F32)

    def add_line(self, chunk):
        for step in range(1, self.links.nn):
            self.line_copy(chunk, step).wait_recv()
        rows = pl.ds(pl.multiple_of(self.links.z * self.rows, self.rows), self.rows)
        for square in range(self.held.shape[1]):
            total = self.held[chunk, square, rows, :].astype(F32)
            for step in range(1, self.links.nn):
                total = total + self.in_line[chunk, step - 1, square].astype(F32)
            self.square[chunk, square] = total.astype(BF)
        for p, part in enumerate(self.parts):
            self.hop(chunk, p, X_BIT | Y_BIT).start()
        for p, part in enumerate(self.parts):
            self.hop(chunk, p, part[2][1]).start()

    def add_corner(self, chunk):
        for p, (low, size, order) in enumerate(self.parts):
            self.hop(chunk, p, X_BIT | Y_BIT).wait_recv()
            spot = self.spot(order[0])
            self.square[chunk, spot, :, low : low + size] = (
                self.square[chunk, spot, :, low : low + size].astype(F32)
                + self.landed(chunk, p, X_BIT | Y_BIT)
            ).astype(BF)
        for p, part in enumerate(self.parts):
            self.hop(chunk, p, part[2][0]).start()

    def finish(self, chunk, out):
        for p, (low, size, order) in enumerate(self.parts):
            total = self.square[chunk, self.spot(0), :, low : low + size].astype(F32)
            for mask in order:
                self.hop(chunk, p, mask).wait_recv()
                total = total + self.landed(chunk, p, mask)
            out[chunk, :, low : low + size] = total
        self.core_copy(chunk).wait_send()
        for step in range(1, self.links.nn):
            self.line_copy(chunk, step).wait_send()
        for p in range(len(self.parts)):
            for mask in (X_BIT, Y_BIT, X_BIT | Y_BIT):
                self.hop(chunk, p, mask).wait_send()


class ScatterSmall:
    def __init__(self, links, grads, out, came, round_in, line_in, mine):
        self.links, self.grads, self.out = links, grads, out
        self.came, self.round, self.line, self.mine = came, round_in, line_in, mine
        self.home = links.w // 2
        self.masks = (X_BIT, Y_BIT, X_BIT | Y_BIT)
        self.core_id = links.fresh()
        self.square_ids = [links.fresh() for _ in self.masks]
        self.line_ids = [links.fresh() for _ in range(1, links.nn)]

    def core_copy(self):
        k = self.links
        return k.copy(self.grads.at[:, 1 - lax.rem(k.w, 2)], self.came, self.core_id, k.wide(1))

    def square_copy(self, index):
        k, mask = self.links, self.masks[index]
        spot = jnp.bitwise_xor(k.w, mask) // 2
        return k.copy(self.mine.at[spot], self.round.at[index], self.square_ids[index], k.wide(mask))

    def line_copy(self, step):
        k = self.links
        rows = pl.ds(pl.multiple_of(lax.rem(k.z + step, k.nn) * 8, 8), 8)
        spot = self.mine.at[self.home, rows]
        return k.copy(spot, self.line.at[step - 1], self.line_ids[step - 1], k.along(step))

    def trade(self):
        self.core_copy().start()

    def spread(self):
        self.core_copy().wait()
        self.mine[...] = self.grads[:, lax.rem(self.links.w, 2)] + self.came[...]
        for index in range(len(self.masks)):
            self.square_copy(index).start()

    def along(self):
        for index in range(len(self.masks)):
            self.square_copy(index).wait()
        total = self.mine[self.home]
        for index in range(len(self.masks)):
            total = total + self.round[index]
        self.mine[self.home] = total
        for step in range(1, self.links.nn):
            self.line_copy(step).start()

    def finish(self):
        total = self.mine[self.home, pl.ds(pl.multiple_of(self.links.z * 8, 8), 8)]
        for step in range(1, self.links.nn):
            self.line_copy(step).wait()
            total = total + self.line[step - 1]
        self.out[...] = total


def padded(rows):
    return (rows + 15) // 16 * 16


def scatter_slots(squares, nn, rows, columns, ring, line_ring):
    half = columns // 2
    return [
        pltpu.VMEM((ring, squares, nn * rows, columns), BF),
        pltpu.VMEM((2, squares, nn * rows, columns), BF),
        pltpu.VMEM((ring, 6, nn * rows, half), BF),
        pltpu.VMEM((line_ring, nn, padded(rows), columns), BF),
        pltpu.VMEM((line_ring, nn - 1, padded(rows), columns), BF),
        pltpu.SemaphoreType.DMA((2, 2)),
    ]


def norm_pull(values, gain, grad):
    scale = lax.rsqrt(jnp.mean(values * values, axis=-1, keepdims=True) + RMS_EPSILON)
    scaled = grad * gain
    along = jnp.mean(scaled * values, axis=-1, keepdims=True)
    share = grad * values * scale
    return scale * scaled - values * (scale * scale * scale * along), share


def fold_rows(values):
    return jnp.sum(values.reshape(values.shape[0] // 8, 8, values.shape[1]), axis=0)


def pack_row(row, first, each, devices):
    total = row.shape[1]
    shape = (128, total)
    pick = jnp.where(iota(shape, 0) == first + lax.rem(iota(shape, 1), each), 1.0, 0.0)
    shape = (devices, total)
    mine = jnp.where(iota(shape, 1) // each == iota(shape, 0), row, 0.0)
    return lax.dot_general(
        mine,
        pick,
        (((1,), (1,)), ((), ())),
        preferred_element_type=F32,
        precision=lax.Precision.HIGHEST,
    )


def backward_kernel(nn, few_facts, many_facts, *refs):
    occupied, refs = refs[0], refs[1:]
    (
        tokens,
        rel_hbm,
        lay_hbm,
        grad_h,
        small_h,
        query_h,
        key_h,
        value_h,
        output_h,
        gate_h,
        up_h,
        down_h,
        na_t,
        q_t,
        k_h,
        v_h,
        att_t,
        hid_h,
        nf_t,
        mix_h,
        probs_h,
        slope_h,
        act_h,
        few_grads,
        few_came,
    ) = refs[:25]
    refs = refs[25:]
    (out_h, rows_out, few_out, many_out, small_out, many_grads, many_came) = refs[:7]
    few_slots, many_slots, late_slots, refs = refs[7:13], refs[13:19], refs[19:25], refs[25:]
    (
        x,
        rel,
        lay,
        small,
        gains,
        grad,
        left,
        acc,
        hid,
        wd_s,
        wgu_s,
        pair,
        slope_s,
        act_s,
        many_stage,
        branch,
        w_one,
        pull,
        pull_t,
        qt,
        k,
        v,
        probs,
        pieces,
        onehot,
        table,
        sums,
        small_grads,
        small_came,
        small_round,
        small_line,
        small_mine,
        send_sem,
        recv_sem,
        local_sem,
        tile_sem,
        stage_sem,
        probs_sem,
    ) = refs
    slots, width = x.shape
    links = Links(nn, send_sem, recv_sem)
    numbers = iter(range(64))

    def later_move(src, dst):
        return pltpu.make_async_copy(src, dst, local_sem.at[next(numbers)])

    def move(src, dst):
        copy = later_move(src, dst)
        copy.start()
        return copy

    few = Scatter(links, *few_facts, few_grads, few_came, few_slots, 0, traded=True)
    base = few_facts[0] * SCATTER_COPIES
    many = Scatter(links, *many_facts, many_grads, many_came, many_slots, base, first=LATE)
    late = ScatterLine(links, *many_facts[1:], many_grads, many_came, late_slots, base)
    links.used = base + many_facts[0] * SCATTER_COPIES
    little = ScatterSmall(
        links, small_grads, small_out, small_came, small_round, small_line, small_mine
    )
    ffn = mix_h.shape[1]
    tiles = ffn // TILE
    pairs = H // 2
    wide = many.columns
    devices = small.shape[0] // 8
    each = width // devices
    zero = jnp.zeros((8, width), F32)

    def tile_copies(tile):
        turn = lax.rem(tile, 2)
        at = pl.ds(pl.multiple_of(tile * TILE, TILE), TILE)
        return [
            pltpu.make_async_copy(src, dst, tile_sem.at[turn, index])
            for index, (src, dst) in enumerate(
                (
                    (down_h.at[at], wd_s.at[turn]),
                    (gate_h.at[:, at], wgu_s.at[turn, :, pl.ds(0, TILE)]),
                    (up_h.at[:, at], wgu_s.at[turn, :, pl.ds(TILE, TILE)]),
                    (slope_h.at[:, at], slope_s.at[turn]),
                    (act_h.at[:, at], act_s.at[turn]),
                )
            )
        ]

    def many_copy(chunk):
        turn = lax.rem(chunk, 2)
        place = many.grads.at[chunk]
        return pltpu.make_async_copy(many_stage.at[turn].reshape(place.shape), place, stage_sem.at[turn])

    def flush(chunk):
        many_copy(chunk).wait()
        many.trade(chunk)

    def make(chunk, left_rows, right, dot_one):
        found = dot_one(left_rows[...], right())
        many_stage[lax.rem(chunk, 2)] = found.astype(BF)
        many_copy(chunk).start()

    def few_pump(index):
        few.pump(index, few_out)

    def many_pump(index):
        many.pump(index, many_out)

    def ffn_tile(tile, carry):
        turn = lax.rem(tile, 2)

        @pl.when(tile + 1 < tiles)
        def _():
            for copy in tile_copies(tile + 1):
                copy.start()

        for number, copy in enumerate(later + last):
            pl.when(tile == 3 + number // 2)(copy.start)

        for copy in tile_copies(tile):
            copy.wait()
        grad_mixed = dot_nt(grad[...], wd_s[turn])
        pair[:, :TILE] = (grad_mixed * slope_s[turn].astype(F32)).astype(BF)
        pair[:, TILE:] = (grad_mixed * act_s[turn].astype(F32)).astype(BF)
        make(tile, left, lambda: pair[...], dot)

        @pl.when(lax.rem(tile, 2) == 1)
        def _():
            few_pump(tile // 2 + 2)

        acc[...] += dot_nt(pair[...], wgu_s[turn])
        flush(tile)
        many_pump(tile - FFN_LAG)

        @pl.when(jnp.logical_and(tile >= 2, tile < 2 + LATE))
        def _():
            late.add_core(tile - 2)

        @pl.when(jnp.logical_and(tile >= 1, tile < 1 + LATE))
        def _():
            late.fetch(tile - 1)

        return carry

    def unpack():
        gains[0:1, :] = unpack_row(small, 0, width)
        gains[1:2, :] = unpack_row(small, 1, width)

    def norm_two():
        def one(index, total):
            at = pl.ds(pl.multiple_of(index * 64, 64), 64)
            part, share = norm_pull(hid[at, :], gains[1:2, :], acc[at, :])
            whole = grad[at, :].astype(F32) + part
            hid[at, :] = whole
            branch[at, :] = whole.astype(BF)
            return total + fold_rows(share)

        sums[0] = lax.fori_loop(0, slots // 64, one, zero)

    def output_chunk(part, carry):
        at = pl.ds(pl.multiple_of(part * wide, wide), wide)
        make(tiles + part, pull_t, lambda: branch[:, at], dot)
        return carry

    def pull_back():
        def one(tile, carry):
            at = pl.ds(pl.multiple_of(tile * WIDE, WIDE), WIDE)
            found = dot_nt(branch[...], w_one[0, at, :]).astype(BF)
            pull[:, at] = found
            pull_t[at, :] = found.T
            return carry

        lax.fori_loop(0, width // WIDE, one, 0)

    def probs_copy(index):
        turn = lax.rem(index, 2)
        return pltpu.make_async_copy(
            probs_h.at[pl.ds(index * 2, 2)], probs.at[turn], probs_sem.at[turn]
        )

    def attend_pair(index, carry):
        @pl.when(index + 1 < pairs)
        def _():
            probs_copy(index + 1).start()

        probs_copy(index).wait()
        turn = lax.rem(index, 2)
        at = pl.ds(pl.multiple_of(index * 128, 128), 128)
        low = iota((slots, 128), 1) < HD
        keys, pulls, values = k[:, at], pull[:, at], v[:, at]
        found = []
        for side in range(2):
            head = index * 2 + side
            mine = jnp.where(low if side == 0 else jnp.logical_not(low), pulls, 0)
            share = probs[turn, side]
            wanted = dot_nt(mine, values)
            share_f = share.astype(F32)
            joint = share_f * wanted
            piece = (joint - share_f * jnp.sum(joint, axis=-1, keepdims=True)).astype(BF)
            pieces[pl.ds(pl.multiple_of(head * slots, slots), slots), :] = piece
            found.append(dot(piece, keys))
            rows = pl.ds(pl.multiple_of(head * HD, HD), HD)
            qt[rows, :] = dot(qt[rows, :], piece).astype(BF)
            pull_t[rows, :] = dot(pull_t[rows, :], share).astype(BF)
        pull[:, at] = jnp.where(low, found[0], found[1]).astype(BF)
        return carry

    def attend(first, last):
        lax.fori_loop(first, last, attend_pair, 0)

    first_head_chunk = tiles + width // wide

    def head_chunks(half):
        at = pl.ds(pl.multiple_of(half * wide, wide), wide)
        chunk = first_head_chunk + half * 3

        def turned_chunk(index, carry):
            found = jnp.where(index == 0, pull_t[at, :], qt[at, :])
            make(chunk + 2 * index, left, lambda: found, dot_nt)

            @pl.when(index == 0)
            def _():
                make(chunk + 1, left, lambda: pull[:, at], dot)
                flush(chunk)

            return carry

        lax.fori_loop(0, 2, turned_chunk, 0)
        flush(chunk + 1)
        flush(chunk + 2)

    def table_blocks(index, carry):
        sides = []
        for side in range(2):
            block = index * 2 + side
            at = slice(side * slots, (side + 1) * slots)
            for query in range(BACK_QB):
                for which, bucket in enumerate((rel, lay)):
                    row = bucket[pl.ds(block * BACK_QB + query, 1), :]
                    first = (query * 2 + which) * NB
                    onehot[first : first + NB, at] = ones_where(
                        jnp.broadcast_to(row, (NB, slots)) == iota((NB, slots), 0)
                    )
            heads = [
                pieces[pl.ds(pl.multiple_of(head * slots + block * BACK_QB, BACK_QB), BACK_QB), :]
                for head in range(H)
            ]
            sides.append(jnp.concatenate(heads, axis=0))
        table[...] += dot_nt(onehot[...], jnp.concatenate(sides, axis=1))
        return carry

    def add_table(part, parts):
        blocks = slots // BACK_QB // 2
        lax.fori_loop(part * blocks // parts, (part + 1) * blocks // parts, table_blocks, 0)

    whole = ffn // slots
    first_mix = width // slots * ffn

    def output_moves():
        moves = [
            later_move(down_h.at[:, pl.ds(part * slots, slots)], pieces.at[pl.ds(part * ffn, ffn)])
            for part in range(width // slots)
        ]
        moves += [
            later_move(
                mix_h.at[:, pl.ds(part * slots, slots)],
                pieces.at[pl.ds(first_mix + part * slots, slots)],
            )
            for part in range(whole)
        ]
        return moves + [later_move(mix_h.at[:, pl.ds(whole * slots, TILE)], slope_s.at[0])]

    def down_project(part):
        at = pl.ds(pl.multiple_of(part * slots, slots), slots)

        def one(index, total):
            rows = pl.ds(pl.multiple_of(part * ffn + index * slots, TILE), slots)
            mixed = pl.ds(pl.multiple_of(first_mix + index * slots, TILE), slots)
            acc[:, at] += dot(pieces[mixed, :], pieces[rows, :])
            return total

        lax.fori_loop(0, whole, one, 0)
        rows = pl.ds(pl.multiple_of(part * ffn + whole * slots, TILE), TILE)
        total = acc[:, at] + dot(slope_s[0], pieces[rows, :])
        valid_rows = iota((slots, 1), 0) < occupied[0] + IMG
        x[:, at] = jnp.where(valid_rows, total, 0.0).astype(BF)

    def turn_back():
        def one(tile, carry):
            at = pl.ds(pl.multiple_of(tile * TILE, TILE), TILE)
            v[:, at] = pull_t[at, :].T
            branch[:, at] = qt[at, :].T
            return carry

        lax.fori_loop(0, width // TILE, one, 0)

    def pull_normed(source, slot, first):
        def one(tile, carry):
            at = pl.ds(pl.multiple_of(tile * WIDE, WIDE), WIDE)
            found = dot_nt(source[...], w_one[slot, at, :])
            acc[:, at] = found if first else acc[:, at] + found
            return carry

        lax.fori_loop(0, width // WIDE, one, 0)

    def norm_one():
        def one(index, total):
            at = pl.ds(pl.multiple_of(index * 64, 64), 64)
            part, share = norm_pull(x[at, :].astype(F32), gains[0:1, :], acc[at, :])
            hid[at, :] += part
            return total + fold_rows(share)

        sums[1] = lax.fori_loop(0, slots // 64, one, zero)

    def pack():
        total = table[...]
        mine = iota(total.shape, 0) // (2 * NB) == lax.rem(iota(total.shape, 1), BACK_QB)
        folded = jnp.sum(
            jnp.where(mine, total, 0.0).reshape(BACK_QB, 2 * NB, H * BACK_QB), axis=0
        )
        packed = [
            pack_row(jnp.sum(sums[1], axis=0, keepdims=True), 0, each, devices),
            pack_row(jnp.sum(sums[0], axis=0, keepdims=True), 0, each, devices),
        ]
        shape = (H * BACK_QB, 128)
        pick = jnp.where(iota(shape, 1) == iota(shape, 0) // BACK_QB, 1.0, 0.0)
        for index in range(2):
            packed.append(
                jnp.dot(
                    folded[index * NB : (index + 1) * NB],
                    pick,
                    preferred_element_type=F32,
                    precision=lax.Precision.HIGHEST,
                )
            )
        small_grads[...] = jnp.zeros_like(small_grads)
        for device in range(devices):
            wide_at, z = divmod(device, nn)
            for index, rows in enumerate(packed):
                at = z * 8 + index
                small_grads[wide_at // 2, wide_at % 2, at : at + 1, :] = rows[device : device + 1]

    later = [
        later_move(*pair_of)
        for pair_of in (
            (hid_h, hid),
            (small_h, small),
            (att_t, pull_t),
            (output_h, w_one.at[0]),
            (q_t, qt),
            (k_h, k),
            (v_h, v),
        )
    ]
    last = [
        later_move(*pair_of)
        for pair_of in ((tokens, x), (rel_hbm, rel), (lay_hbm, lay), (value_h, w_one.at[1]))
    ]
    na_in, query_in, key_in = (
        later_move(*pair_of)
        for pair_of in ((na_t, left), (query_h, w_one.at[0]), (key_h, w_one.at[0]))
    )
    rows_copy, out_copy = later_move(hid, rows_out), later_move(x, out_h)
    output_in = output_moves()
    hid_in = later_move(hid_h, acc)

    def start(*copies):
        for copy in copies:
            copy.start()

    def wait(*copies):
        for copy in copies:
            copy.wait()

    few.fetch(jnp.int32(0))
    start(*tile_copies(0))
    first_in = [move(grad_h, grad), move(nf_t, left)]
    links.greet()
    few.fetch(jnp.int32(1))
    few.add_core(jnp.int32(0))
    acc[...] = jnp.zeros_like(acc)
    table[...] = jnp.zeros_like(table)
    wait(*first_in)
    lax.fori_loop(0, tiles, ffn_tile, 0)
    wait(*later)
    na_in.start()
    unpack()
    norm_two()
    def step(index, carry):
        few_pump(index + tiles // 2 + 2)
        many_pump(index + tiles - FFN_LAG)

        for lag, action in ((1, late.add_line), (3, late.add_corner), (5, late.finish)):
            chunk = index - lag

            @pl.when(jnp.logical_and(chunk >= 0, chunk < LATE))
            def _(chunk=chunk, action=action):
                action(chunk, many_out) if action == late.finish else action(chunk)

        @pl.when(index == 0)
        def _():
            lax.fori_loop(0, width // wide, output_chunk, 0)
            pull_back()
            flush(tiles)
            flush(tiles + 1)
            query_in.start()
            probs_copy(jnp.int32(0)).start()

        second = index >= 4
        turn = jnp.where(second, index - 4, index - 1)
        attends = jnp.logical_and(turn >= 0, turn < 2)

        @pl.when(attends)
        def _():
            first = 2 * turn + jnp.where(second, 4, 0)
            attend(first, first + 2)

        @pl.when(index == 3)
        def _():
            wait(*last)
            na_in.wait()

        @pl.when(jnp.logical_or(index == 3, index == 6))
        def _():
            head_chunks(index // 3 - 1)

        @pl.when(jnp.logical_and(index >= 7, index < 10))
        def _():
            add_table(index - 7, 3)

        @pl.when(index == 10)
        def _():
            start(*output_in)
            query_in.wait()
            turn_back()
            pull_normed(pull, 0, True)
            key_in.start()

        @pl.when(index == 11)
        def _():
            pull_normed(v, 1, False)
            key_in.wait()
            pull_normed(branch, 0, False)

        @pl.when(index == 12)
        def _():
            norm_one()
            rows_copy.start()
            hid_in.start()
            pack()
            little.trade()

        @pl.when(index == 13)
        def _():
            wait(*output_in)
            hid_in.wait()
            little.spread()

        @pl.when(index == 15)
        def _():
            little.along()

        @pl.when(jnp.logical_or(index == 14, index == 16))
        def _():
            down_project(index // 2 - 7)

        @pl.when(index == 17)
        def _():
            out_copy.start()

        return carry

    lax.fori_loop(0, many.chunks - LATE + LAGS - (tiles - FFN_LAG) + 1, step, 0)
    little.finish()
    wait(rows_copy, out_copy)
    links.finish()


def backward_all(nw, nn, counts, page, weights, saved):
    squares = nw // 2
    devices = nw * nn
    slots, width = page[0].shape
    ffn = weights[5].shape[1]
    few = (width // DOWN_PIECE, ffn // devices, DOWN_PIECE)
    many = (ffn // TILE + 8, width // devices, 2 * TILE)
    outs = [jax.ShapeDtypeStruct((slots, width), BF), jax.ShapeDtypeStruct((slots, width), F32)]
    for chunks, rows, columns in (few, many):
        outs.append(jax.ShapeDtypeStruct((chunks, rows, columns), F32))
    outs.append(jax.ShapeDtypeStruct((8, 128), F32))
    chunks, rows, columns = many
    outs.append(jax.ShapeDtypeStruct((chunks, squares, 2, nn * rows, columns), BF))
    outs.append(jax.ShapeDtypeStruct((chunks, squares, nn * rows, columns), BF))
    copies = (few[0] + many[0]) * SCATTER_COPIES + 16
    vmem = pl.BlockSpec(memory_space=pltpu.VMEM)
    hbm = pl.BlockSpec(memory_space=pl.ANY)
    low = pltpu.VMEM((slots, width), BF)
    turned = pltpu.VMEM((width, slots), BF)
    full = pltpu.VMEM((slots, width), F32)
    inputs = (counts,) + tuple(page) + tuple(weights) + tuple(saved)
    return pl.pallas_call(
        functools.partial(backward_kernel, nn, few, many),
        out_shape=outs,
        in_specs=[pl.BlockSpec(memory_space=pltpu.SMEM)] + [hbm] * (len(inputs) - 1),
        out_specs=[hbm, hbm, vmem, vmem, vmem, hbm, hbm],
        scratch_shapes=scatter_slots(squares, nn, few[1], few[2], few[0], few[0])
        + scatter_slots(squares, nn, many[1], many[2], RING, LINE_RING)
        + [
            pltpu.VMEM((LATE, squares, nn * many[1], many[2]), BF),
            pltpu.VMEM((squares, nn * many[1], many[2]), BF),
            pltpu.VMEM((LATE, squares, many[1], many[2]), BF),
            pltpu.VMEM((LATE, 6, many[1], many[2] // 2), BF),
            pltpu.VMEM((LATE, nn - 1, squares, many[1], many[2]), BF),
            pltpu.SemaphoreType.DMA((2,)),
        ]
        + [
            low,
            pltpu.VMEM((slots, slots), jnp.int32),
            pltpu.VMEM((slots, slots), jnp.int32),
            pltpu.VMEM((devices * 8, 128), F32),
            pltpu.VMEM((8, width), F32),
            low,
            turned,
            full,
            full,
            pltpu.VMEM((2, TILE, width), BF),
            pltpu.VMEM((2, width, 2 * TILE), BF),
            pltpu.VMEM((slots, 2 * TILE), BF),
            pltpu.VMEM((2, slots, TILE), BF),
            pltpu.VMEM((2, slots, TILE), BF),
            pltpu.VMEM((2, width, many[2]), BF),
            low,
            pltpu.VMEM((2, width, width), BF),
            low,
            turned,
            turned,
            low,
            low,
            pltpu.VMEM((2, 2, slots, slots), BF),
            pltpu.VMEM((H * slots, slots), BF),
            pltpu.VMEM((BACK_QB * 2 * NB, 2 * slots), BF),
            pltpu.VMEM((BACK_QB * 2 * NB, H * BACK_QB), F32),
            pltpu.VMEM((2, 8, width), F32),
            pltpu.VMEM((squares, 2, nn * 8, 128), F32),
            pltpu.VMEM((squares, nn * 8, 128), F32),
            pltpu.VMEM((3, nn * 8, 128), F32),
            pltpu.VMEM((nn - 1, 8, 128), F32),
            pltpu.VMEM((squares, nn * 8, 128), F32),
            pltpu.SemaphoreType.DMA((copies,)),
            pltpu.SemaphoreType.DMA((copies,)),
            pltpu.SemaphoreType.DMA((64,)),
            pltpu.SemaphoreType.DMA((2, 5)),
            pltpu.SemaphoreType.DMA((2,)),
            pltpu.SemaphoreType.DMA((2,)),
        ],
        compiler_params=pltpu.CompilerParams(
            collective_id=1, has_side_effects=True, vmem_limit_bytes=63 * 2**20
        ),
    )(*inputs)[:5]


def place_kernel(few_h, many_h, rows_h, out_h, small, *refs):
    (whole_out, row_out, query, key, value, output, gate, up, down) = refs[:9]
    (gain_attn, gain_ffn, rel, lay) = refs[9:13]
    few, many, rows, whole, in_sem, out_sem = refs[13:]
    tiles = gate.shape[1] // TILE
    wide = many.shape[2]
    part = rows.shape[0] // 8
    arriving = [
        pltpu.make_async_copy(src, dst, in_sem.at[index])
        for index, (src, dst) in enumerate(
            [(many_h, many), (few_h, few), (out_h, whole)]
            + [
                (rows_h.at[pl.ds(index * part, part)], rows.at[pl.ds(index * part, part)])
                for index in range(8)
            ]
        )
    ]
    for copy in arriving:
        copy.start()
    moves = []

    def move(src, dst):
        copy = pltpu.make_async_copy(src, dst, out_sem.at[len(moves)])
        copy.start()
        moves.append(copy)

    for index, target in enumerate((gain_attn, gain_ffn, rel, lay)):
        target[...] = small[index, : target.shape[0]]
    arriving[0].wait()
    for tile in range(tiles):
        at = pl.ds(tile * TILE, TILE)
        move(many.at[tile, :, pl.ds(0, TILE)], gate.at[:, at])
        move(many.at[tile, :, pl.ds(TILE, TILE)], up.at[:, at])
    halves_of = output.shape[1] // wide
    for half in range(halves_of):
        at = pl.ds(half * wide, wide)
        move(many.at[tiles + half], output.at[:, at])
        first = tiles + halves_of + half * 3
        for index, target in enumerate((value, query, key)):
            move(many.at[first + index], target.at[:, at])
    arriving[1].wait()
    for chunk in range(few.shape[0]):
        move(few.at[chunk], down.at[:, pl.ds(chunk * few.shape[2], few.shape[2])])
    arriving[2].wait()
    move(whole, whole_out)
    for index in range(8):
        arriving[3 + index].wait()
        at = pl.ds(index * part, part)
        move(rows.at[at], row_out.at[at])
    for copy in moves:
        copy.wait()


def place_all(few, many, rows, out, small, shapes):
    hbm = pl.BlockSpec(memory_space=pl.ANY)
    vmem = pl.BlockSpec(memory_space=pltpu.VMEM)
    outs = [jax.ShapeDtypeStruct(out.shape, BF), jax.ShapeDtypeStruct(rows.shape, F32)]
    outs += [jax.ShapeDtypeStruct(shape, F32) for shape in shapes]
    return pl.pallas_call(
        place_kernel,
        out_shape=outs,
        in_specs=[hbm] * 4 + [vmem],
        out_specs=[hbm] * 9 + [vmem] * 4,
        scratch_shapes=[
            pltpu.VMEM(few.shape, F32),
            pltpu.VMEM(many.shape, F32),
            pltpu.VMEM(rows.shape, F32),
            pltpu.VMEM(out.shape, BF),
            pltpu.SemaphoreType.DMA((16,)),
            pltpu.SemaphoreType.DMA((64,)),
        ],
        compiler_params=pltpu.CompilerParams(vmem_limit_bytes=63 * 2**20),
    )(few, many, rows, out, small)


def local_fast(
    nw,
    nn,
    tokens,
    w_query,
    w_key,
    w_value,
    w_output,
    w_gate,
    w_up,
    w_down,
    gain_attn,
    gain_ffn,
    rel_table,
    lay_table,
    ocr_counts,
    rel_bucket,
    lay_bucket,
    cotangent,
):
    page = (tokens, rel_bucket, lay_bucket)
    parameters = (gain_attn, gain_ffn, rel_table, lay_table)
    shards = (w_query, w_key, w_value, w_output, w_gate, w_up, w_down)
    found = forward_all(nw, nn, ocr_counts, *page, cotangent, parameters, shards)
    count = 1 + len(shards)
    weights, grad, saved = found[:count], found[count], found[count + 1 :]
    output, grad_tokens, few, many, small = backward_all(
        nw, nn, ocr_counts, page + (grad,), weights, saved
    )

    square = w_query.shape
    shapes = [square] * 4 + [w_gate.shape, w_up.shape, w_down.shape]
    shapes += [part.shape for part in (gain_attn, gain_ffn, rel_table, lay_table)]
    return tuple(place_all(few, many, grad_tokens, output, small, shapes))


def local(
    tokens,
    w_query,
    w_key,
    w_value,
    w_output,
    w_gate,
    w_up,
    w_down,
    gain_attn,
    gain_ffn,
    rel_table,
    lay_table,
    ocr_counts,
    rel_bucket,
    lay_bucket,
    cotangent,
):
    slot = tokens.shape[0]
    valid = jnp.arange(slot) < ocr_counts[0] + IMG
    buckets = jnp.arange(NB)
    onehot = jnp.concatenate(
        [
            (rel_bucket[:, :, None] == buckets).astype(jnp.bfloat16),
            (lay_bucket[:, :, None] == buckets).astype(jnp.bfloat16),
        ],
        axis=2,
    )
    tokens_f = tokens.astype(jnp.float32)
    weights = gather_weights(
        w_query,
        w_key,
        w_value,
        w_output,
        w_gate,
        w_up,
        w_down,
        gain_attn,
        gain_ffn,
        rel_table,
        lay_table,
    )
    result, saved = forward_pass(tokens_f, weights, onehot, valid)
    output = jnp.where(valid[:, None], result, 0.0).astype(jnp.bfloat16)
    (
        full_query,
        full_key,
        full_value,
        full_output,
        full_gate,
        full_up,
        full_down,
        full_gain_attn,
        full_gain_ffn,
        full_rel,
        full_lay,
    ) = weights
    (
        normed_attn,
        queries,
        keys_all,
        values_all,
        log_totals,
        attended,
        hidden_one,
        normed_ffn,
        gate_act,
        up_proj,
        mixed,
    ) = saved
    grad_result = jnp.where(valid[:, None], cotangent.astype(jnp.float32), 0.0)
    grad_low = grad_result.astype(jnp.bfloat16)
    grad_down = contract_rows(mixed, grad_low)
    grad_mixed = contract_cols(grad_low, full_down)
    gated_value, gated_pull = jax.vjp(gated_product, gate_act, up_proj)
    grad_gate_act, grad_up_proj = gated_pull(grad_mixed)
    gate_low = grad_gate_act.astype(jnp.bfloat16)
    up_low = grad_up_proj.astype(jnp.bfloat16)
    grad_gate = contract_rows(normed_ffn, gate_low)
    grad_up = contract_rows(normed_ffn, up_low)
    grad_normed_ffn = contract_cols(gate_low, full_gate) + contract_cols(up_low, full_up)
    norm_value, norm_pull = jax.vjp(rms_scale, hidden_one, full_gain_ffn.astype(jnp.float32))
    grad_hidden_part, grad_gain_ffn = norm_pull(grad_normed_ffn)
    grad_hidden = grad_result + grad_hidden_part
    branch_low = grad_hidden.astype(jnp.bfloat16)
    grad_output = contract_rows(attended, branch_low)
    grad_attended = contract_cols(branch_low, full_output).astype(jnp.bfloat16)
    grad_queries, grad_keys, grad_values, grad_table_all = attention_backward(
        queries,
        keys_all,
        values_all,
        log_totals,
        grad_attended,
        table_pair(full_rel, full_lay),
        onehot,
        valid,
    )
    grad_rel = grad_table_all[:NB].reshape(NB * H)
    grad_lay = grad_table_all[NB:].reshape(NB * H)
    grad_query = contract_rows(normed_attn, grad_queries)
    grad_key = contract_rows(normed_attn, grad_keys)
    grad_value = contract_rows(normed_attn, grad_values)
    grad_normed_attn = (
        contract_cols(grad_queries, full_query)
        + contract_cols(grad_keys, full_key)
        + contract_cols(grad_values, full_value)
    )
    input_value, input_pull = jax.vjp(rms_scale, tokens_f, full_gain_attn.astype(jnp.float32))
    grad_input_part, grad_gain_attn = input_pull(grad_normed_attn)
    grad_tokens = grad_hidden + grad_input_part
    owned = (
        lax.psum_scatter(grad_query, ("wide", "narrow"), scatter_dimension=0, tiled=True),
        lax.psum_scatter(grad_key, ("wide", "narrow"), scatter_dimension=0, tiled=True),
        lax.psum_scatter(grad_value, ("wide", "narrow"), scatter_dimension=0, tiled=True),
        lax.psum_scatter(grad_output, ("wide", "narrow"), scatter_dimension=0, tiled=True),
        lax.psum_scatter(grad_gate, ("wide", "narrow"), scatter_dimension=0, tiled=True),
        lax.psum_scatter(grad_up, ("wide", "narrow"), scatter_dimension=0, tiled=True),
        lax.psum_scatter(grad_down, ("wide", "narrow"), scatter_dimension=0, tiled=True),
        lax.psum_scatter(grad_gain_attn, ("wide", "narrow"), scatter_dimension=0, tiled=True),
        lax.psum_scatter(grad_gain_ffn, ("wide", "narrow"), scatter_dimension=0, tiled=True),
        lax.psum_scatter(grad_rel, ("wide", "narrow"), scatter_dimension=0, tiled=True),
        lax.psum_scatter(grad_lay, ("wide", "narrow"), scatter_dimension=0, tiled=True),
    )
    return (
        output,
        grad_tokens,
        owned[0],
        owned[1],
        owned[2],
        owned[3],
        owned[4],
        owned[5],
        owned[6],
        owned[7],
        owned[8],
        owned[9],
        owned[10],
    )


def solution(mesh):
    nw, nn = mesh.shape["wide"], mesh.shape["narrow"]

    def body(*args):
        if nw == 8 and nw * nn == NB and args[1].shape[0] % 16 == 0:
            return local_fast(nw, nn, *args)
        return local(*args)

    placed = (
        P(("wide", "narrow"), None),
        P(("wide", "narrow"), None),
        P(("wide", "narrow"), None),
        P(("wide", "narrow"), None),
        P(("wide", "narrow"), None),
        P(("wide", "narrow"), None),
        P(("wide", "narrow"), None),
        P(("wide", "narrow"), None),
        P(("wide", "narrow")),
        P(("wide", "narrow")),
        P(("wide", "narrow")),
        P(("wide", "narrow")),
        P(("wide", "narrow")),
        P(("wide", "narrow"), None),
        P(("wide", "narrow"), None),
        P(("wide", "narrow"), None),
    )
    return jax.shard_map(
        body,
        mesh=mesh,
        in_specs=placed,
        out_specs=(
            P(("wide", "narrow"), None),
            P(("wide", "narrow"), None),
            P(("wide", "narrow"), None),
            P(("wide", "narrow"), None),
            P(("wide", "narrow"), None),
            P(("wide", "narrow"), None),
            P(("wide", "narrow"), None),
            P(("wide", "narrow"), None),
            P(("wide", "narrow"), None),
            P(("wide", "narrow")),
            P(("wide", "narrow")),
            P(("wide", "narrow")),
            P(("wide", "narrow")),
        ),
        check_vma=False,
    )
```
